32 devices in a mesh: grp: 2 (over y), blk: 4 (over z), cls: 2 (over x), rot: 2 (over core).
Axes of the slice: x: 2, y: 2, z: 4, core: 2. Of those that a mesh axis runs over, the one named last changes fastest.
Arguments:
- particles: bfloat16 [2304, 128, 128], P(('grp', 'blk'), 'rot'), parts along dimension 0, may hold values from -48 to 48
- references: bfloat16 [16, 128, 128], P(('grp', 'blk', 'cls'), 'rot'), parts along dimension 0, may hold values from -6 to 6
- noise_inv: float32 [64], replicated, may hold values from 0.5 to 2
- prior_rot: int32 [2304], P(('grp', 'blk')), parts along dimension 0, may hold values from 0 to 255
Outputs:
- class_means: float32 [16, 128, 128], P(('grp', 'blk', 'cls'), 'rot'), parts along dimension 0
- log_evidence: float32 [2304], P(('grp', 'blk', 'rot')), parts along dimension 0
The draws below stay inside these ranges and needn't reach their ends.
There are 2 independent parts, one for each index of `grp`. The reference program is written for one: setup_inputs(seed, part) draws one part's arguments, and reference() takes and returns one part's arrays. A program takes and returns all parts, laid end to end along the dimension named above; an argument that names none is the same for every part. Nothing has to cross between parts.
All inputs are finite; a program needn't handle non-finite values.
Results may differ from the reference program's by a relative error of at most 0.0036.
Values may be sent and summed in bfloat16 or wider, within the bound.
No kernel may reach another device: no remote copies, remote signals or barrier semaphores. Data moves between devices by JAX's collectives and lax.ppermute only.
A program may use at most 128 MiB of HBM per device.

```python
import math
import jax
import jax.numpy as jnp
from jax import lax

RAD = 64
D = 128
ANG = 256
F = 128
K = 8
P_SIZE = 1152
ITERS = 2
SIGMA = 32


def class_images(key):
    return jnp.clip(jax.random.normal(key, (K, F, D), jnp.float32), -6.0, 6.0)


def draw_references(key, part):
    images = class_images(key)
    return images.astype(jnp.bfloat16)


def draw_particles(key, part):
    key = jax.random.fold_in(key, 23)
    keys = jax.random.split(key, 1)
    noise = jax.random.normal(keys[0], (P_SIZE, F, D), jnp.float32)
    return jnp.clip(noise, -6.0, 6.0).astype(jnp.bfloat16)


def plant(entries, rng, low, top_value):
    longest = entries.shape.index(max(entries.shape))
    spots = []
    for shift in (0, 1):
        where = [jax.random.randint(jax.random.fold_in(rng, axis), (), 0, length) for axis, length in enumerate(entries.shape)]
        where[longest] = (where[longest] + shift) % entries.shape[longest]
        spots.append(tuple(where))
    return entries.at[spots[0]].set(low).at[spots[1]].set(top_value)


def setup_inputs(seed: int = 0, part: int = 0) -> dict:
    streams_of = jax.random.split(jax.random.key(seed), 5)
    part_splits = jax.random.split(jax.random.fold_in(streams_of[4], part), 5)
    return {
        "particles": draw_particles(jax.random.fold_in(jax.random.fold_in(streams_of[4], part), 71), part),
        "references": draw_references(jax.random.fold_in(jax.random.fold_in(streams_of[4], part), 71), part),
        "noise_inv": jnp.clip(jnp.exp(jax.random.uniform(streams_of[2], (RAD,), jnp.float32, math.log(0.5), math.log(2.0))), 0.5, 2.0),
        "prior_rot": plant(jax.random.randint(part_splits[3], (P_SIZE,), 0, ANG), jax.random.fold_in(part_splits[3], 1), 0, ANG - 1).astype(jnp.int32),
    }


shrinkage = 1.0


def freq_scale(freq):
    return jnp.where(freq == 0, 1.0, 2.0).astype(jnp.float32) / ANG


def turn_angle(first, second):
    product = (first[:, None] * second[None, :]) % ANG
    return product.astype(jnp.float32) * (2.0 * math.pi / ANG)


def iteration(particles, references, paired, doubled, inverse, forward, prior_rot):
    scale_freq = freq_scale(jnp.arange(F, dtype=jnp.int32))
    weighted = (references.astype(jnp.float32) * doubled).astype(jnp.bfloat16)
    turned = jnp.concatenate([-weighted[..., RAD:], weighted[..., :RAD]], -1)
    stacked = jnp.stack([weighted, turned], 1).astype(jnp.float32)
    energy = jnp.sum(references.astype(jnp.float32) ** 2 * doubled * scale_freq[None, :, None], axis=(1, 2))
    span = math.gcd(P_SIZE, 256)
    count_blocks = P_SIZE // span
    turns = jnp.arange(ANG, dtype=jnp.int32)

    def one_block(carry, inputs):
        totals, counts = carry
        block, pair_block, prior_block = inputs
        correlation = jnp.einsum("pfd,kcfd->pkcf", block.astype(jnp.float32), stacked,
                                 precision=lax.Precision.HIGHEST)
        inner = jnp.dot(correlation.reshape(span * K, 2 * F), inverse,
                        precision=lax.Precision.HIGHEST, preferred_element_type=jnp.float32)
        offset = jnp.abs(turns[None, :] - prior_block[:, None])
        distance = jnp.minimum(offset, ANG - offset).astype(jnp.float32)
        prior_term = -distance * distance / (2.0 * SIGMA * SIGMA)
        scores = inner.reshape(span, K, ANG) - 0.5 * energy[None, :, None] + prior_term[:, None, :]
        summit = jnp.max(scores, axis=(1, 2))
        evidence = summit + jnp.log(jnp.sum(jnp.exp(scores - summit[:, None, None]), axis=(1, 2)))
        posterior = jnp.exp(scores - evidence[:, None, None])
        counts = counts + jnp.sum(posterior, axis=(0, 2))
        rounded = posterior.astype(jnp.bfloat16)
        spectrum = jnp.dot(rounded.reshape(span * K, ANG).astype(jnp.float32), forward,
                           precision=lax.Precision.HIGHEST, preferred_element_type=jnp.float32)
        spectrum = spectrum.astype(jnp.bfloat16).reshape(span, K, 2, F)
        totals = totals + jnp.einsum("pkcf,pcfd->kfd", spectrum.astype(jnp.float32),
                                     pair_block.astype(jnp.float32), precision=lax.Precision.HIGHEST)
        return (totals, counts), evidence

    start = (jnp.zeros((K, F, D), jnp.float32), jnp.zeros((K,), jnp.float32))
    inputs = (particles.reshape(count_blocks, span, F, D),
              paired.reshape(count_blocks, span, 2, F, D),
              prior_rot.reshape(count_blocks, span))
    (totals, counts), evidence = lax.scan(one_block, start, inputs)
    means = totals / (counts + shrinkage)[:, None, None]
    return means, evidence.reshape(P_SIZE)


def reference(particles, references, noise_inv, prior_rot):
    doubled = jnp.concatenate([noise_inv, noise_inv]).astype(jnp.float32)
    freq = jnp.arange(F, dtype=jnp.int32)
    turns = jnp.arange(ANG, dtype=jnp.int32)
    angles = turn_angle(freq, turns)
    scale = freq_scale(freq)[:, None]
    inverse = jnp.concatenate([scale * jnp.cos(angles), -scale * jnp.sin(angles)], 0)
    back_angles = turn_angle(turns, freq)
    forward = jnp.concatenate([jnp.cos(back_angles), jnp.sin(back_angles)], 1)
    flipped = jnp.concatenate([-particles[..., RAD:], particles[..., :RAD]], -1)
    paired = jnp.stack([particles, flipped], 1)
    current = references
    for step in range(ITERS):
        means, evidence = iteration(particles, current, paired, doubled, inverse, forward, prior_rot)
        current = means.astype(jnp.bfloat16)
    return means, evidence
```

```python
import functools
import math

import jax
import jax.numpy as jnp
import numpy as np
from jax import lax
from jax.experimental import pallas as pl
from jax.experimental.pallas import tpu as pltpu
from jax.sharding import PartitionSpec as P

ANG = 256
ITERS = 2
SIGMA = 32

shrinkage = 1.0

F32 = jnp.float32
BF16 = jnp.bfloat16
PAD = 16


def tables(freqs):
    freq = np.arange(freqs)
    turn = np.arange(ANG)
    angle = (turn[:, None] * freq[None, :] % ANG) * (2.0 * math.pi / ANG)
    scale = np.where(freq == 0, 1.0, 2.0) / ANG
    inverse = np.concatenate([scale * np.cos(angle), -scale * np.sin(angle)], 1).astype(np.float32)
    forward = np.concatenate([np.cos(angle), np.sin(angle)], 1).T.astype(np.float32)

    def split(x):
        high = x.astype(BF16)
        return high, (x - high.astype(np.float32)).astype(BF16)

    return split(inverse) + split(forward)


def loop(count, body, unroll):
    while count % unroll:
        unroll -= 1
    if unroll == count:
        for i in range(count):
            body(i)
        return

    def step(outer, carry):
        for inner in range(unroll):
            body(outer * unroll + inner)
        return carry

    lax.fori_loop(0, count // unroll, step, 0)


def params(*shapes):
    total = 0
    for shape, dtype in shapes:
        size = jnp.dtype(dtype).itemsize
        dims = [1, 1, *shape]
        rows = -(-dims[-2] // 16) * 16
        lanes = -(-dims[-1] // 128) * 128
        total += math.prod(dims[:-2]) * rows * lanes * size
    return pltpu.CompilerParams(vmem_limit_bytes=min(total + (4 << 20), 62 << 20))


def vmem(count):
    return [pl.BlockSpec(memory_space=pltpu.VMEM)] * count


def prep_kernel(share, groups, start_ref, particles_ref, *rest):
    outs, (held, wide, sems) = rest[:groups], rest[groups:]
    freqs = particles_ref.shape[1]
    copies = []
    for g in range(groups):
        rows = pl.ds(start_ref[g], share)
        copy = pltpu.make_async_copy(particles_ref.at[rows], held.at[g], sems.at[g])
        copy.start()
        copies.append(copy)
    for g in reversed(range(groups)):
        copies[g].wait()

        def widen(p, g=g):
            wide[pl.ds(pl.multiple_of(p * freqs, 8), freqs), :] = held[g, p].astype(F32)

        loop(share, widen, 8)

        def turn(f, g=g):
            outs[g][f] = wide[pl.ds(f, share, stride=freqs), :].astype(BF16)

        loop(freqs, turn, 8)


def prep(particles, start, share, groups):
    _, freqs, depth = particles.shape
    shape = (freqs, share, depth)
    return pl.pallas_call(
        functools.partial(prep_kernel, share, groups),
        out_shape=[jax.ShapeDtypeStruct(shape, BF16)] * groups,
        in_specs=[pl.BlockSpec(memory_space=pltpu.SMEM), pl.BlockSpec(memory_space=pl.ANY)],
        out_specs=vmem(groups),
        scratch_shapes=[
            pltpu.VMEM((groups, share, freqs, depth), BF16),
            pltpu.VMEM((share * freqs, depth), F32),
            pltpu.SemaphoreType.DMA((groups,)),
        ],
        compiler_params=params(*[(shape, BF16)] * (2 * groups), ((share * freqs, depth), F32)),
        cost_estimate=pl.CostEstimate(
            flops=0, bytes_accessed=4 * groups * math.prod(shape), transcendentals=0
        ),
    )(start, particles)


def em_kernel(groups, sides, blocks, send_type, *refs):
    peers = sides * groups
    refs = list(refs)
    take = lambda n: [refs.pop(0) for _ in range(n)]
    (index_ref,) = take(1)
    particles = take(groups)
    pieces = take(peers)
    doubled_ref, prior_ref, inv_hi, inv_lo, fwd_hi, fwd_lo = take(6)
    outs = take(peers)
    (evidence_ref,) = take(1)
    image, field, energy_ref, count_ref = take(4)
    freqs, share, depth = particles[0].shape
    every = freqs * groups
    classes = sides * blocks
    radii = depth // 2
    start = [
        pl.multiple_of(lax.rem(index_ref[0] + g, groups) * freqs, freqs) for g in range(groups)
    ]
    lane = lax.broadcasted_iota(jnp.int32, (freqs, depth), 1)
    sign = jnp.where(lane < radii, -1.0, 1.0).astype(F32)
    doubled = doubled_ref[...]
    row = lax.broadcasted_iota(jnp.int32, (freqs, depth), 0)

    for side in range(sides):

        def weigh(i, side=side):
            k = side * blocks + i
            energy = jnp.zeros((freqs, depth), F32)
            for g in range(groups):
                plain = pieces[side * groups + g][i].astype(F32)
                scale = jnp.where(row + start[g] == 0, 1.0 / ANG, 2.0 / ANG).astype(F32)
                energy = energy + plain * plain * doubled * scale
                weighted = (plain * doubled).astype(BF16).astype(F32)
                base = k * 2 * every + start[g]
                image[pl.ds(pl.multiple_of(base, 8), freqs), :] = weighted
                image[pl.ds(pl.multiple_of(base + every, 8), freqs), :] = sign * pltpu.roll(
                    weighted, radii, 1
                )
            total = jnp.sum(jnp.sum(energy, axis=0, keepdims=True), axis=1, keepdims=True)
            energy_ref[pl.ds(k, 1), :] = jnp.broadcast_to(total, (1, share))

        loop(blocks, weigh, 4)

    for g in range(groups):

        def correlate(f, g=g):
            rows = pl.ds(start[g] + f, 2 * classes, stride=every)
            field[rows, :] = lax.dot_general(
                image[rows, :].astype(BF16),
                particles[g][f],
                (((1,), (1,)), ((), ())),
                preferred_element_type=F32,
            )

        loop(freqs, correlate, 16)

    turns = lax.broadcasted_iota(jnp.int32, (ANG, share), 0)
    offset = jnp.abs(turns - prior_ref[...])
    distance = jnp.minimum(offset, ANG - offset).astype(F32)
    prior_term = -distance * distance / (2.0 * SIGMA * SIGMA)
    dot = functools.partial(jnp.dot, preferred_element_type=F32)

    def class_rows(k):
        return pl.ds(pl.multiple_of(k * ANG, ANG), ANG)

    def score(k, peak):
        value = field[class_rows(k), :]
        high = value.astype(BF16)
        low = (value - high.astype(F32)).astype(BF16)
        inner = dot(inv_hi[...], high) + (dot(inv_hi[...], low) + dot(inv_lo[...], high))
        scores = inner - 0.5 * energy_ref[pl.ds(k, 1), :] + prior_term
        field[class_rows(k), :] = scores
        return jnp.maximum(peak, jnp.max(scores, axis=0, keepdims=True))

    def weight(k, total):
        value = jnp.exp(field[class_rows(k), :] - peak)
        field[class_rows(k), :] = value
        return total + jnp.sum(value, axis=0, keepdims=True)

    def spectrum(k, carry):
        value = field[class_rows(k), :] * inverse_total
        count = jnp.sum(jnp.sum(value, axis=0, keepdims=True), axis=1, keepdims=True)
        count_ref[pl.ds(k, 1), :] = jnp.broadcast_to(count, (1, depth))
        rounded = value.astype(BF16)
        turned = dot(fwd_hi[...], rounded) + dot(fwd_lo[...], rounded)
        field[class_rows(k), :] = turned
        return carry

    def each(body, init):
        if classes <= 8:
            for k in range(classes):
                init = body(k, init)
            return init
        return lax.fori_loop(0, classes, body, init)

    peak = each(score, jnp.full((1, share), -jnp.inf, F32))
    total = each(weight, jnp.zeros((1, share), F32))
    evidence_ref[...] = peak + jnp.log(total)
    inverse_total = 1.0 / total
    each(spectrum, 0)

    for g in range(groups):

        def accumulate(f, g=g):
            rows = pl.ds(start[g] + f, 2 * classes, stride=every)
            image[rows, :] = dot(field[rows, :].astype(BF16), particles[g][f])

        loop(freqs, accumulate, 16)

    for side in range(sides):

        def finish(i, side=side):
            k = side * blocks + i
            count = count_ref[pl.ds(k, 1), :]
            high = count.astype(BF16).astype(F32)
            spare = lax.broadcasted_iota(jnp.int32, (PAD, depth), 0)
            for g in range(groups):
                out = outs[side * groups + g]
                base = k * 2 * every + start[g]
                plain = image[pl.ds(pl.multiple_of(base, 8), freqs), :]
                other = image[pl.ds(pl.multiple_of(base + every, 8), freqs), :]
                value = plain + sign * pltpu.roll(other, radii, 1)
                out[i, pl.ds(0, freqs), :] = value.astype(out.dtype)
                tail = jnp.where(spare == 0, high, jnp.where(spare == 1, count - high, 0.0))
                out[i, pl.ds(freqs, PAD), :] = tail.astype(out.dtype)

        loop(blocks, finish, 4)


def em(index, particles, pieces, doubled, prior, constants, sides, send_type):
    groups = len(particles)
    freqs, share, depth = particles[0].shape
    blocks = pieces[0].shape[0]
    classes = sides * blocks
    every = freqs * groups
    piece = (blocks, freqs + PAD, depth)
    kinds = [F32] + [send_type] * (sides * groups - 1)
    scratch = [
        ((2 * every * classes, depth), F32),
        ((2 * every * classes, share), F32),
        ((classes, share), F32),
        ((classes, depth), F32),
    ]
    buffers = scratch + [(x.shape, x.dtype) for x in (*particles, *pieces, *constants)]
    return pl.pallas_call(
        functools.partial(em_kernel, groups, sides, blocks, send_type),
        out_shape=[jax.ShapeDtypeStruct(piece, kind) for kind in kinds]
        + [jax.ShapeDtypeStruct((1, share), F32)],
        in_specs=[pl.BlockSpec(memory_space=pltpu.SMEM)]
        + vmem(groups + len(pieces) + 2 + len(constants)),
        out_specs=vmem(len(kinds) + 1),
        scratch_shapes=[pltpu.VMEM(*entry) for entry in scratch],
        compiler_params=params(*buffers, *[(piece, kind) for kind in kinds]),
        cost_estimate=pl.CostEstimate(
            flops=8 * classes * share * every * (depth + 3 * ANG),
            bytes_accessed=2 * every * share * depth,
            transcendentals=classes * share * ANG,
        ),
    )(index, *particles, *pieces, doubled, prior, *constants)


def combine_kernel(count, *refs):
    ins, outs = refs[:count], refs[count:]
    for i, out in enumerate(outs):
        total = ins[0][i].astype(F32)
        for ref in ins[1:]:
            total = total + ref[i].astype(F32)
        out[...] = total


def combine(parts):
    blocks, rows, depth = parts[0].shape
    return pl.pallas_call(
        functools.partial(combine_kernel, len(parts)),
        out_shape=[jax.ShapeDtypeStruct((rows, depth), F32)] * blocks,
        in_specs=vmem(len(parts)),
        out_specs=vmem(blocks),
        compiler_params=params(*[(x.shape, F32) for x in parts], (parts[0].shape, F32)),
    )(*parts)


def means_kernel(count, freqs, *refs):
    ins, (out,) = refs[:count], refs[count:]
    total = ins[0][...]
    for ref in ins[1:]:
        total = total + ref[...]
    counts = total[freqs : freqs + 1, :] + total[freqs + 1 : freqs + 2, :]
    out[0] = (total[:freqs, :] / (counts + shrinkage)).astype(out.dtype)


def class_means(parts, dtype):
    rows, depth = parts[0].shape
    freqs = rows - PAD
    return pl.pallas_call(
        functools.partial(means_kernel, len(parts), freqs),
        out_shape=jax.ShapeDtypeStruct((1, freqs, depth), dtype),
        in_specs=vmem(len(parts)),
        out_specs=pl.BlockSpec(memory_space=pltpu.VMEM),
        compiler_params=params(*[(x.shape, F32) for x in parts], (parts[0].shape, F32)),
    )(*parts)


def shift(value, axes, sizes, step):
    if not any(step):
        return value
    pairs = []
    for there in np.ndindex(*sizes):
        here = tuple((t - s) % n for t, s, n in zip(there, step, sizes))
        pairs.append((int(np.ravel_multi_index(there, sizes)), int(np.ravel_multi_index(here, sizes))))
    return lax.ppermute(value, axes, pairs)


def shards(particles, references, noise_inv, prior_rot):
    batch, freqs, depth = particles.shape
    sides = lax.axis_size("cls")
    groups = lax.axis_size("rot")
    blocks = lax.axis_size("blk")
    side = lax.axis_index("cls")
    group = lax.axis_index("rot")
    half = batch // groups
    share = half // sides
    axes, sizes = ("cls", "rot"), (sides, groups)
    steps = list(np.ndindex(*sizes))

    constants = [jnp.asarray(x) for x in tables(freqs * groups)]
    doubled = jnp.concatenate([noise_inv, noise_inv]).reshape(1, depth)
    index = group.astype(jnp.int32).reshape(1)
    start = (group + jnp.arange(groups, dtype=jnp.int32)) % groups * half + side * share
    prior = lax.dynamic_slice_in_dim(prior_rot, start[0], share, 0).reshape(1, share)

    cut = prep(particles, start, share, groups)
    own = [cut[0]]
    for g in range(1, groups):
        own.append(shift(cut[-g % groups], ("rot",), (groups,), (g,)))

    current = references
    for step in range(ITERS):
        last = step == ITERS - 1
        column = [shift(current, ("blk",), (blocks,), (i,)) for i in range(blocks)]
        column = jnp.concatenate(column, 0)
        pieces = [shift(column, axes, sizes, s) for s in steps]
        *sums, evidence = em(
            index, own, pieces, doubled, prior, constants, sides, F32 if last else BF16
        )
        parts = [shift(x, axes, sizes, tuple(-i for i in s)) for x, s in zip(sums, steps)]
        mine = combine(parts)
        mine = [shift(x, ("blk",), (blocks,), (-i,)) for i, x in enumerate(mine)]
        current = class_means(mine, F32 if last else BF16)
    gathered = jnp.concatenate([shift(evidence, ("cls",), (sides,), (i,)) for i in range(sides)], 0)
    evidence = jnp.roll(gathered, side, 0).reshape(half)
    return current, evidence


def solution(mesh):
    in_specs = (
        P(("grp", "blk"), "rot", None),
        P(("grp", "blk", "cls"), "rot", None),
        P(),
        P(("grp", "blk")),
    )
    out_specs = (P(("grp", "blk", "cls"), "rot", None), P(("grp", "blk", "rot")))
    return jax.shard_map(shards, mesh=mesh, in_specs=in_specs, out_specs=out_specs, check_vma=False)
```

```python
import functools
import math

import jax
import jax.numpy as jnp
import numpy as np
from jax import lax
from jax.experimental import pallas as pl
from jax.experimental.pallas import tpu as pltpu
from jax.sharding import PartitionSpec as P

ANG = 256
ITERS = 2
SIGMA = 32

shrinkage = 1.0

F32 = jnp.float32
BF16 = jnp.bfloat16


def tables(freqs):
    freq = np.arange(freqs)
    turn = np.arange(ANG)
    angle = (turn[:, None] * freq[None, :] % ANG) * (2.0 * math.pi / ANG)
    scale = np.where(freq == 0, 1.0, 2.0) / ANG
    inverse = np.concatenate([scale * np.cos(angle), -scale * np.sin(angle)], 1).astype(np.float32)
    forward = np.concatenate([np.cos(angle), np.sin(angle)], 1).T.astype(np.float32)

    def split(x):
        high = x.astype(BF16)
        return high, (x - high.astype(np.float32)).astype(BF16)

    return split(inverse) + split(forward)


def loop(count, body, unroll):
    while count % unroll:
        unroll -= 1
    if unroll == count:
        for i in range(count):
            body(i)
        return

    def step(outer, carry):
        for inner in range(unroll):
            body(outer * unroll + inner)
        return carry

    lax.fori_loop(0, count // unroll, step, 0)


def params(*shapes):
    total = 0
    for shape, dtype in shapes:
        size = jnp.dtype(dtype).itemsize
        dims = [1, 1, *shape]
        rows = -(-dims[-2] // 16) * 16
        lanes = -(-dims[-1] // 128) * 128
        total += math.prod(dims[:-2]) * rows * lanes * size
    return pltpu.CompilerParams(vmem_limit_bytes=min(total + (4 << 20), 62 << 20))


def vmem(count):
    return [pl.BlockSpec(memory_space=pltpu.VMEM)] * count


def prep_kernel(share, groups, start_ref, particles_ref, *rest):
    outs, (held, wide, sems) = rest[:groups], rest[groups:]
    freqs, depth = held.shape[2:]
    pitch = wide.shape[0] // share
    copies = []
    for g in reversed(range(groups)):
        rows = pl.ds(start_ref[g], share)
        copy = pltpu.make_async_copy(particles_ref.at[rows], held.at[g], sems.at[g])
        copy.start()
        copies.append((g, copy))
    for g, copy in copies:
        copy.wait()

        def widen(p, g=g):
            wide[pl.ds(pl.multiple_of(p * pitch, 8), freqs), :] = held[g, p].astype(F32)

        loop(share, widen, 8)

        def turn(f, g=g):
            for part in range(2):
                rows = pl.ds(2 * f + part, share, stride=pitch)
                outs[g][f, :, pl.ds(part * depth, depth)] = wide[rows, :].astype(BF16)

        loop(freqs // 2, turn, 8)


def prep(particles, start, share, groups):
    _, freqs, depth = particles.shape
    shape = (freqs // 2, share, 2 * depth)
    held = (groups, share, freqs, depth)
    wide = (share * (freqs + 8), depth)
    return pl.pallas_call(
        functools.partial(prep_kernel, share, groups),
        out_shape=[jax.ShapeDtypeStruct(shape, BF16)] * groups,
        in_specs=[
            pl.BlockSpec(memory_space=pltpu.SMEM),
            pl.BlockSpec(memory_space=pltpu.MemorySpace.HBM),
        ],
        out_specs=vmem(groups),
        scratch_shapes=[
            pltpu.VMEM(held, BF16),
            pltpu.VMEM(wide, F32),
            pltpu.SemaphoreType.DMA((groups,)),
        ],
        compiler_params=params(*[(shape, BF16)] * groups, (held, BF16), (wide, F32)),
        cost_estimate=pl.CostEstimate(
            flops=0, bytes_accessed=4 * groups * math.prod(shape), transcendentals=0
        ),
    )(start, particles)


def em_kernel(groups, sides, blocks, *refs):
    refs = list(refs)
    take = lambda n: [refs.pop(0) for _ in range(n)]
    (index_ref,) = take(1)
    particles = take(groups)
    pieces_ref, doubled_ref, prior_ref, inv_hi, inv_lo, fwd_hi, fwd_lo = take(7)
    out, evidence_ref = take(2)
    image, field, energy_ref, count_ref = take(4)
    pairs, share, twice = particles[0].shape
    freqs, depth = 2 * pairs, twice // 2
    every = freqs * groups
    classes = sides * blocks
    radii = depth // 2
    pitch = image.shape[0] // (2 * classes)
    start = [
        pl.multiple_of(lax.rem(index_ref[0] + g, groups) * freqs, freqs) for g in range(groups)
    ]
    lane = lax.broadcasted_iota(jnp.int32, (freqs, depth), 1)
    sign = jnp.where(lane < radii, -1.0, 1.0).astype(F32)
    doubled = doubled_ref[...]
    row = lax.broadcasted_iota(jnp.int32, (freqs, depth), 0)
    dot = functools.partial(jnp.dot, preferred_element_type=F32)

    def rows(base, count):
        return pl.ds(pl.multiple_of(base, 8), count)

    def weigh(k):
        energy = jnp.zeros((freqs, depth), F32)
        for g in range(groups):
            plain = pieces_ref[k * groups + g].astype(F32)
            scale = jnp.where(row + g * freqs == 0, 1.0 / ANG, 2.0 / ANG).astype(F32)
            energy = energy + plain * plain * doubled * scale
            weighted = (plain * doubled).astype(BF16).astype(F32)
            base = k * 2 * pitch + g * freqs
            image[rows(base, freqs), :] = weighted
            image[rows(base + pitch, freqs), :] = sign * pltpu.roll(weighted, radii, 1)
        total = jnp.sum(jnp.sum(energy, axis=0, keepdims=True), axis=1, keepdims=True)
        energy_ref[pl.ds(k, 1), :] = jnp.broadcast_to(total, (1, share))

    loop(classes, weigh, 8)

    none = jnp.zeros((2 * classes, depth), BF16)
    for g in range(groups):

        def correlate(f, g=g):
            where = [
                pl.ds(start[g] + 2 * f + part, 2 * classes, stride=pitch) for part in range(2)
            ]
            first, second = [image[at, :].astype(BF16) for at in where]
            left = jnp.concatenate(
                [
                    jnp.concatenate([first, none], 1),
                    jnp.concatenate([none, second], 1),
                ],
                0,
            )
            value = lax.dot_general(
                left, particles[g][f], (((1,), (1,)), ((), ())), preferred_element_type=F32
            )
            for part, at in enumerate(where):
                field[at, :] = value[part * 2 * classes : (part + 1) * 2 * classes]

        loop(pairs, correlate, 8)

    turns = lax.broadcasted_iota(jnp.int32, (ANG, share), 0)
    offset = jnp.abs(turns - prior_ref[...])
    distance = jnp.minimum(offset, ANG - offset).astype(F32)
    prior_term = -distance * distance / (2.0 * SIGMA * SIGMA)

    def load(k):
        return jnp.concatenate(
            [field[rows((2 * k + part) * pitch, every), :] for part in range(2)], 0
        )

    def store(k, value):
        for part in range(2):
            field[rows((2 * k + part) * pitch, every), :] = value[part * every : (part + 1) * every]

    def score(k, peak):
        value = load(k)
        high = value.astype(BF16)
        low = (value - high.astype(F32)).astype(BF16)
        inner = dot(inv_hi[...], high) + (dot(inv_hi[...], low) + dot(inv_lo[...], high))
        scores = inner - 0.5 * energy_ref[pl.ds(k, 1), :] + prior_term
        store(k, scores)
        return jnp.maximum(peak, jnp.max(scores, axis=0, keepdims=True))

    def weight(k, total):
        value = jnp.exp(load(k) - peak)
        store(k, value)
        return total + jnp.sum(value, axis=0, keepdims=True)

    def spectrum(k, carry):
        value = load(k) * inverse_total
        count = jnp.sum(jnp.sum(value, axis=0, keepdims=True), axis=1, keepdims=True)
        count_ref[pl.ds(k, 1), :] = jnp.broadcast_to(count, (1, depth))
        rounded = value.astype(BF16)
        store(k, dot(fwd_hi[...], rounded) + dot(fwd_lo[...], rounded))
        return carry

    def each(body, init):
        if classes <= 8:
            for k in range(classes):
                init = body(k, init)
            return init
        return lax.fori_loop(0, classes, body, init)

    peak = each(score, jnp.full((1, share), -jnp.inf, F32))
    total = each(weight, jnp.zeros((1, share), F32))
    evidence = peak + jnp.log(total)
    evidence_ref[...] = evidence
    inverse_total = 1.0 / total
    each(spectrum, 0)

    for g in range(groups):

        def accumulate(f, g=g):
            where = [
                pl.ds(start[g] + 2 * f + part, 2 * classes, stride=pitch) for part in range(2)
            ]
            left = jnp.concatenate([field[at, :].astype(BF16) for at in where], 0)
            value = dot(left, particles[g][f])
            for part, at in enumerate(where):
                image[at, :] = value[
                    part * 2 * classes : (part + 1) * 2 * classes,
                    part * depth : (part + 1) * depth,
                ]

        loop(pairs, accumulate, 8)

    spare = lax.broadcasted_iota(jnp.int32, (out.shape[2] - freqs, depth), 0)
    for side in range(sides):

        def finish(i, side=side):
            k = i * sides + side
            count = count_ref[pl.ds(k, 1), :]
            high = count.astype(BF16).astype(F32)
            tail = jnp.where(spare == 0, high, jnp.where(spare == 1, count - high, 0.0))
            for g in range(groups):
                base = k * 2 * pitch + g * freqs
                other = pltpu.roll(image[rows(base + pitch, freqs), :], radii, 1)
                value = image[rows(base, freqs), :] + sign * other
                out[side * groups + g, i, pl.ds(0, freqs), :] = value.astype(out.dtype)
                out[side * groups + g, i, pl.ds(freqs, tail.shape[0]), :] = tail.astype(out.dtype)

        loop(blocks, finish, 4)


def em(index, particles, pieces, doubled, prior, constants, sides, send_type):
    groups = len(particles)
    pairs, share, twice = particles[0].shape
    freqs, depth = 2 * pairs, twice // 2
    classes = pieces.shape[0] // groups
    blocks = classes // sides
    every = freqs * groups
    sums = (sides * groups, blocks, freqs + (8 if send_type == F32 else 16), depth)
    scratch = [
        ((2 * (every + 8) * classes, depth), F32),
        ((2 * (every + 8) * classes, share), F32),
        ((classes, share), F32),
        ((classes, depth), F32),
    ]
    buffers = scratch + [(x.shape, x.dtype) for x in (*particles, pieces, *constants)]
    return pl.pallas_call(
        functools.partial(em_kernel, groups, sides, blocks),
        out_shape=[jax.ShapeDtypeStruct(sums, send_type), jax.ShapeDtypeStruct((1, share), F32)],
        in_specs=[pl.BlockSpec(memory_space=pltpu.SMEM)] + vmem(groups + 3 + len(constants)),
        out_specs=vmem(2),
        scratch_shapes=[pltpu.VMEM(*entry) for entry in scratch],
        compiler_params=params(*buffers, (sums, send_type)),
        cost_estimate=pl.CostEstimate(
            flops=8 * classes * share * every * (depth + 3 * ANG),
            bytes_accessed=2 * every * share * depth,
            transcendentals=classes * share * ANG,
        ),
    )(index, *particles, pieces, doubled, prior, *constants)


def combine_kernel(parts_ref, out):
    rows = out.shape[1]
    for i in range(out.shape[0]):
        total = parts_ref[0, i].astype(F32)
        for j in range(1, parts_ref.shape[0]):
            total = total + parts_ref[j, i].astype(F32)
        out[i] = total[:rows]


def combine(parts, freqs):
    _, blocks, _, depth = parts.shape
    shape = (blocks, freqs + 8, depth)
    return pl.pallas_call(
        combine_kernel,
        out_shape=jax.ShapeDtypeStruct(shape, F32),
        in_specs=vmem(1),
        out_specs=pl.BlockSpec(memory_space=pltpu.VMEM),
        compiler_params=params((parts.shape, F32), (shape, F32)),
    )(parts)


def means_kernel(parts_ref, out):
    freqs = out.shape[1]
    total = parts_ref[0]
    for i in range(1, parts_ref.shape[0]):
        total = total + parts_ref[i]
    counts = total[freqs : freqs + 1, :] + total[freqs + 1 : freqs + 2, :]
    value = (total[:freqs, :] / (counts + shrinkage)).astype(out.dtype)
    for i in range(out.shape[0]):
        out[i] = value


def class_means(parts, copies, dtype):
    _, rows, depth = parts.shape
    shape = (copies, rows - 8, depth)
    return pl.pallas_call(
        means_kernel,
        out_shape=jax.ShapeDtypeStruct(shape, dtype),
        in_specs=vmem(1),
        out_specs=pl.BlockSpec(memory_space=pltpu.VMEM),
        compiler_params=params((parts.shape, F32), (shape, dtype)),
    )(parts)


def shift(value, axes, sizes, step):
    if not any(step):
        return value
    pairs = []
    for there in np.ndindex(*sizes):
        here = tuple((t - s) % n for t, s, n in zip(there, step, sizes))
        pairs.append((int(np.ravel_multi_index(there, sizes)), int(np.ravel_multi_index(here, sizes))))
    return lax.ppermute(value, axes, pairs)


def shards(particles, references, noise_inv, prior_rot):
    batch, freqs, depth = particles.shape
    sides = lax.axis_size("cls")
    groups = lax.axis_size("rot")
    blocks = lax.axis_size("blk")
    side = lax.axis_index("cls")
    group = lax.axis_index("rot")
    half = batch // groups
    share = half // sides
    members = blocks * sides * groups

    constants = [jnp.asarray(x) for x in tables(freqs * groups)]
    doubled = jnp.concatenate([noise_inv, noise_inv]).reshape(1, depth)
    index = group.astype(jnp.int32).reshape(1)
    start = (group + jnp.arange(groups, dtype=jnp.int32)) % groups * half + side * share
    prior = lax.dynamic_slice_in_dim(prior_rot, start[0], share, 0).reshape(1, share)

    cut = prep(particles, start, share, groups)
    own = [cut[0]]
    for g in range(1, groups):
        own.append(shift(cut[-g % groups], ("rot",), (groups,), (g,)))

    exchange = functools.partial(lax.all_to_all, split_axis=0, concat_axis=0, tiled=True)
    current = jnp.broadcast_to(references, (members, freqs, depth))
    for step in range(ITERS):
        last = step == ITERS - 1
        pieces = exchange(current, ("blk", "cls", "rot"))
        sums, evidence = em(
            index, own, pieces, doubled, prior, constants, sides, F32 if last else BF16
        )
        if last:
            gathered = [shift(evidence, ("cls",), (sides,), (i,)) for i in range(sides)]
        mine = combine(exchange(sums, ("cls", "rot")), freqs)
        mine = exchange(mine, "blk")
        current = class_means(mine, 1, F32) if last else class_means(mine, members, BF16)
    evidence = jnp.roll(jnp.concatenate(gathered, 0), side, 0).reshape(half)
    return current, evidence


def solution(mesh):
    in_specs = (
        P(("grp", "blk"), "rot", None),
        P(("grp", "blk", "cls"), "rot", None),
        P(),
        P(("grp", "blk")),
    )
    out_specs = (P(("grp", "blk", "cls"), "rot", None), P(("grp", "blk", "rot")))
    return jax.shard_map(shards, mesh=mesh, in_specs=in_specs, out_specs=out_specs, check_vma=False)
```

```python
import functools
import math

import jax
import jax.numpy as jnp
import numpy as np
from jax import lax
from jax.experimental import pallas as pl
from jax.experimental.pallas import tpu as pltpu
from jax.sharding import PartitionSpec as P

ANG = 256
ITERS = 2
SIGMA = 32

shrinkage = 1.0

F32 = jnp.float32
BF16 = jnp.bfloat16
SPARE = 8
LONG_SPARE = 16

dot = functools.partial(jnp.dot, preferred_element_type=F32)


def split(x):
    high = x.astype(BF16)
    return high, (x - high.astype(F32)).astype(BF16)


def tables(half_freq):
    turn = np.arange(ANG)
    inverse, forward = [], []
    for group in range(2):
        sides = {}
        for which in range(2):
            freq = which * half_freq + np.arange(half_freq)
            angle = (turn[:, None] * freq[None, :] % ANG) * (2.0 * math.pi / ANG)
            scale = np.where(freq == 0, 1.0, 2.0) / ANG
            sides[which] = (
                np.concatenate([scale * np.cos(angle), -scale * np.sin(angle)], 1),
                np.concatenate([np.cos(angle), np.sin(angle)], 1).T,
            )
        inverse.append(np.concatenate([sides[group][0], sides[1 - group][0]], 1))
        forward.append(np.concatenate([sides[1 - group][1], sides[group][1]], 0))
    result = []
    for table in (inverse, forward):
        table = np.stack(table).astype(np.float32)
        high = table.astype(BF16)
        result += [high, (table - high.astype(np.float32)).astype(BF16)]
    return [jnp.asarray(x) for x in result]


def loop(count, body, unroll):
    while count % unroll:
        unroll -= 1
    if unroll == count:
        for i in range(count):
            body(i)
        return

    def step(outer, carry):
        for inner in range(unroll):
            body(outer * unroll + inner)
        return carry

    lax.fori_loop(0, count // unroll, step, 0)


def each(count, body, init):
    if count <= 8:
        for k in range(count):
            init = body(k, init)
        return init
    return lax.fori_loop(0, count, body, init)


def rows(base, count):
    return pl.ds(pl.multiple_of(base, 8), count)


def call(kernel, ins, outs, scratch=(), flops=0, scalar=False):
    total = 0
    buffers = [(x.shape, x.dtype) for x in ins] + list(outs) + list(scratch)
    for shape, dtype in buffers:
        dims = [1, 1, *shape]
        lines = -(-dims[-2] // 16) * 16
        lanes = -(-dims[-1] // 128) * 128
        total += math.prod(dims[:-2]) * lines * lanes * jnp.dtype(dtype).itemsize
    kinds = [pltpu.SMEM if scalar and i == 0 else pltpu.VMEM for i in range(len(ins))]
    return pl.pallas_call(
        kernel,
        out_shape=[jax.ShapeDtypeStruct(*x) for x in outs],
        in_specs=[pl.BlockSpec(memory_space=kind) for kind in kinds],
        out_specs=[pl.BlockSpec(memory_space=pltpu.VMEM)] * len(outs),
        scratch_shapes=[pltpu.VMEM(*x) for x in scratch],
        compiler_params=pltpu.CompilerParams(
            vmem_limit_bytes=min(total + (4 << 20), 62 << 20)
        ),
        cost_estimate=pl.CostEstimate(flops=flops, bytes_accessed=total, transcendentals=0),
    )(*ins)


def prep_kernel(share, start_ref, particles_ref, out, wide):
    freqs, depth = particles_ref.shape[1:]
    pitch = wide.shape[0] // share
    first = start_ref[0]

    def widen(p):
        wide[rows(p * pitch, freqs), :] = particles_ref[first + p].astype(F32)

    loop(share, widen, 8)

    def turn(f):
        for part in range(2):
            at = pl.ds(2 * f + part, share, stride=pitch)
            out[f, :, pl.ds(part * depth, depth)] = wide[at, :].astype(BF16)

    loop(freqs // 2, turn, 8)


def prep(particles, start, share):
    _, freqs, depth = particles.shape
    return call(
        functools.partial(prep_kernel, share),
        [start.reshape(1), particles],
        [((freqs // 2, share, 2 * depth), BF16)],
        [((share * (freqs + SPARE), depth), F32)],
        flops=1 << 30,
        scalar=True,
    )[0]


def weigh_kernel(fresh, positions, *refs):
    index_ref, first_ref, second_ref, doubled_ref, particles, out, energy_ref, left_ref, image = refs
    pairs, share, twice = particles.shape
    freqs, depth = 2 * pairs, twice // 2
    classes, lanes = energy_ref.shape
    pitch = freqs + SPARE
    radii = depth // 2
    lane = lax.broadcasted_iota(jnp.int32, (freqs, depth), 1)
    sign = jnp.where(lane < radii, -1.0, 1.0).astype(F32)
    doubled = doubled_ref[...]
    row = lax.broadcasted_iota(jnp.int32, (freqs, depth), 0) + index_ref[0] * freqs
    scale = jnp.where(row == 0, 1.0 / ANG, 2.0 / ANG).astype(F32) * doubled

    for k in range(classes):
        if fresh:
            half = classes // 2
            plain = (first_ref if k < half else second_ref)[k % half].astype(F32)
        else:
            total = first_ref[k].astype(F32) + second_ref[positions[k]].astype(F32)
            counts = total[freqs : freqs + 1, :] + total[freqs + 1 : freqs + 2, :]
            plain = (total[:freqs, :] / (counts + shrinkage)).astype(BF16).astype(F32)
        weighted = (plain * doubled).astype(BF16).astype(F32)
        image[rows(2 * k * pitch, freqs), :] = weighted
        image[rows((2 * k + 1) * pitch, freqs), :] = sign * pltpu.roll(weighted, radii, 1)
        energy = jnp.sum(plain * plain * scale, axis=0, keepdims=True)
        energy = jnp.broadcast_to(jnp.sum(energy, axis=1, keepdims=True), (SPARE, lanes))
        energy_ref[pl.ds(k, 1), :] = energy[:1]
        out[0, rows(2 * k * pitch + freqs, SPARE), :] = energy[:, : out.shape[2]]

    none = jnp.zeros((2 * classes, depth), BF16)

    def correlate(f):
        first, second = [
            image[pl.ds(2 * f + part, 2 * classes, stride=pitch), :].astype(BF16)
            for part in range(2)
        ]
        left = jnp.concatenate(
            [jnp.concatenate([first, none], 1), jnp.concatenate([none, second], 1)], 0
        )
        left_ref[f] = left
        place(out, f, times(left, particles[f]), classes, pitch)

    loop(pairs, correlate, 8)


def times(left, particles):
    return lax.dot_general(left, particles, (((1,), (1,)), ((), ())), preferred_element_type=F32)


def place(out, f, value, classes, pitch):
    tiles, _, width = out.shape
    spare = jnp.zeros((value.shape[0], tiles * width - value.shape[1]), F32)
    value = jnp.concatenate([value, spare], 1) if spare.size else value
    for part in range(2):
        at = pl.ds(2 * f + part, 2 * classes, stride=pitch)
        for tile in range(tiles):
            out[tile, at, :] = value[
                part * 2 * classes : (part + 1) * 2 * classes, tile * width : (tile + 1) * width
            ]


def lane_tiles(share):
    return -(-share // 128)


def weigh(index, first, second, doubled, particles, fresh, positions):
    pairs, share, twice = particles.shape
    classes = len(positions)
    lines = 2 * classes * (2 * pairs + SPARE)
    tiles = lane_tiles(share)
    return call(
        functools.partial(weigh_kernel, fresh, positions),
        [index, first, second, doubled, particles],
        [
            ((tiles, lines, 128), F32),
            ((classes, tiles * 128), F32),
            ((pairs, 4 * classes, twice), BF16),
        ],
        [((lines, twice // 2), F32)],
        flops=8 * classes * share * pairs * twice * 4,
        scalar=True,
    )


def correlate_kernel(left_ref, particles, out):
    pairs = left_ref.shape[0]
    classes = left_ref.shape[1] // 4

    def body(f):
        place(out, f, times(left_ref[f], particles[f]), classes, 2 * pairs + SPARE)

    loop(pairs, body, 8)


def correlate(left, particles):
    pairs, share, twice = particles.shape
    lines = left.shape[1] // 2 * (2 * pairs + SPARE)
    return call(
        correlate_kernel,
        [left, particles],
        [((lane_tiles(share), lines, 128), F32)],
        flops=2 * left.shape[1] * share * pairs * twice * 8,
    )[0]


def across(ref, at):
    return jnp.concatenate([ref[tile, at, :] for tile in range(ref.shape[0])], 1)


def score_kernel(index_ref, own, other, energy_ref, prior_ref, inv_hi, inv_lo, *refs):
    weights, peaks, sums, field = refs
    classes, share = energy_ref.shape
    tiles, lines, width = own.shape
    pitch = lines // (2 * classes)
    freqs = pitch - SPARE
    which = index_ref[0]
    turns = lax.broadcasted_iota(jnp.int32, (ANG, share), 0)
    offset = jnp.abs(turns - prior_ref[...])
    distance = jnp.minimum(offset, ANG - offset).astype(F32)
    prior_term = -distance * distance / (2.0 * SIGMA * SIGMA)

    def score(k, peak):
        value = jnp.concatenate(
            [
                across(ref, rows((2 * k + part) * pitch, freqs))
                for ref in (own, other)
                for part in (0, 1)
            ],
            0,
        )
        high, low = split(value)
        inner = dot(inv_hi[which], high) + (dot(inv_hi[which], low) + dot(inv_lo[which], high))
        far = other[0, rows(2 * k * pitch + freqs, SPARE), :][:1]
        energy = energy_ref[pl.ds(k, 1), :] + jnp.concatenate([far] * tiles, 1)
        scores = inner - 0.5 * energy + prior_term
        field[rows(k * ANG, ANG), :] = scores
        return jnp.maximum(peak, jnp.max(scores, axis=0, keepdims=True))

    peak = each(classes, score, jnp.full((1, share), -jnp.inf, F32))

    def weight(k, total):
        value = jnp.exp(field[rows(k * ANG, ANG), :] - peak)
        weights[k] = value.astype(BF16)
        part = jnp.sum(value, axis=0, keepdims=True)
        sums[pl.ds(k, 1), :] = part
        return total + part

    total = each(classes, weight, jnp.zeros((1, share), F32))
    line = lax.broadcasted_iota(jnp.int32, peaks.shape, 0)
    peaks[...] = jnp.where(line == 0, peak, total)


def scores(index, own, other, energy, prior, inv_hi, inv_lo):
    classes, share = energy.shape
    return call(
        score_kernel,
        [index, own, other, energy, prior, inv_hi, inv_lo],
        [((classes, ANG, share), BF16), ((8, share), F32), ((classes, share), F32)],
        [((classes * ANG, share), F32)],
        flops=6 * classes * share * ANG * ANG,
        scalar=True,
    )


def merge(first, second):
    top = jnp.maximum(first[0:1], second[0:1])
    total = first[1:2] * jnp.exp(first[0:1] - top) + second[1:2] * jnp.exp(second[0:1] - top)
    return top, total


def merge_kernel(first, second, out):
    top, total = merge(first[...], second[...])
    line = lax.broadcasted_iota(jnp.int32, out.shape, 0)
    out[...] = jnp.where(line == 0, top, total)


def turn_kernel(index_ref, weights, fwd_hi, fwd_lo, other, own):
    classes = weights.shape[0]
    tiles, lines, width = own.shape
    pitch = lines // (2 * classes)
    freqs = pitch - SPARE
    which = index_ref[0]

    def body(k, carry):
        value = dot(fwd_hi[which], weights[k]) + dot(fwd_lo[which], weights[k])
        for i, ref in enumerate((other, own)):
            for part in range(2):
                start = (2 * i + part) * freqs
                for tile in range(tiles):
                    ref[tile, rows((2 * k + part) * pitch, freqs), :] = value[
                        start : start + freqs, tile * width : (tile + 1) * width
                    ]
        return carry

    each(classes, body, 0)


def turn(index, weights, fwd_hi, fwd_lo, freqs):
    classes, _, share = weights.shape
    shape = (share // 128, 2 * classes * (freqs + SPARE), 128)
    return call(
        turn_kernel,
        [index, weights, fwd_hi, fwd_lo],
        [(shape, F32), (shape, F32)],
        flops=4 * classes * share * ANG * ANG,
        scalar=True,
    )


def scale_kernel(here, first, second, sums, other, own, send, keep, evidence_ref):
    classes, lanes = sums.shape
    share = evidence_ref.shape[1]
    pitch = own.shape[1] // (2 * classes)
    pairs = (pitch - SPARE) // 2
    top, total = merge(first[...], second[...])
    evidence_ref[...] = (top + jnp.log(total))[:, :share]
    factor = jnp.exp(here[0:1, :] - top) / total
    lane = lax.broadcasted_iota(jnp.int32, (1, lanes), 1)
    factor = jnp.where(lane < share, factor, 0.0)

    def body(f):
        for ref, out in ((other, send), (own, keep)):
            parts = [
                across(ref, pl.ds(2 * f + part, 2 * classes, stride=pitch)) * factor
                for part in range(2)
            ]
            out[f] = jnp.concatenate(parts, 0).astype(BF16)[:, :share]

    loop(pairs, body, 8)
    counts = jnp.sum(sums[...] * factor, axis=1, keepdims=True)
    high = counts.astype(BF16).astype(F32)
    column = jnp.concatenate([high, counts - high, high, high], 0)
    column = jnp.broadcast_to(column, (4 * classes, share)).astype(BF16)
    send[pairs] = column
    keep[pairs] = column


def scale(here, first, second, sums, other, own, share):
    classes = sums.shape[0]
    pairs = (own.shape[1] // (2 * classes) - SPARE) // 2
    shape = (pairs + 1, 4 * classes, share)
    return call(
        scale_kernel,
        [here, first, second, sums, other, own],
        [(shape, BF16), (shape, BF16), ((1, share), F32)],
    )


def gather_kernel(spectrum, particles, image):
    pairs, _, twice = particles.shape
    classes = spectrum.shape[1] // 4

    def body(f):
        value = dot(spectrum[f], particles[f])
        take_in(image, f, value, classes, False)

    loop(pairs, body, 8)


def take_in(image, f, value, classes, add):
    lines, depth = image.shape
    for part in range(2):
        at = pl.ds(2 * f + part, 2 * classes, stride=lines // (2 * classes))
        new = value[
            part * 2 * classes : (part + 1) * 2 * classes, part * depth : (part + 1) * depth
        ]
        image[at, :] = image[at, :] + new if add else new


def gather(spectrum, particles):
    pairs, _, twice = particles.shape
    lines = spectrum.shape[1] // 2 * (2 * pairs + SPARE)
    return call(
        gather_kernel,
        [spectrum, particles],
        [((lines, twice // 2), F32)],
        flops=2 * math.prod(spectrum.shape) * twice * 8,
    )[0]


def finish_kernel(image, mine, spectrum, particles, *refs):
    outs, held = refs[:-1], refs[-1]
    pairs, _, twice = particles.shape
    classes = spectrum.shape[1] // 4
    freqs, depth = 2 * pairs, twice // 2
    radii = depth // 2
    pitch = freqs + SPARE

    def body(f):
        value = dot(spectrum[f], particles[f])
        take_in(held, f, value, classes, False)

    loop(pairs, body, 8)
    counts = mine[pairs].astype(F32) + spectrum[pairs].astype(F32)
    lane = lax.broadcasted_iota(jnp.int32, (freqs, depth), 1)
    sign = jnp.where(lane < radii, -1.0, 1.0).astype(F32)
    each_out = classes // len(outs)
    for k in range(classes):
        out = outs[k // each_out]
        plain, turned = [
            image[rows((2 * k + part) * pitch, freqs), :]
            + held[rows((2 * k + part) * pitch, freqs), :]
            for part in range(2)
        ]
        value = plain + sign * pltpu.roll(turned, radii, 1)
        out[k % each_out, pl.ds(0, freqs), :] = value.astype(out.dtype)
        count = counts[k : k + 1, :depth] + counts[classes + k : classes + k + 1, :depth]
        out[k % each_out, pl.ds(freqs, out.shape[1] - freqs), :] = tail(count, freqs, out)


def tail(count, freqs, out):
    shape = (out.shape[1] - freqs, out.shape[2])
    line = lax.broadcasted_iota(jnp.int32, shape, 0)
    high = count.astype(BF16).astype(F32)
    return jnp.where(line == 0, high, jnp.where(line == 1, count - high, 0.0)).astype(out.dtype)


def finish(image, mine, spectrum, particles, last):
    pairs, _, twice = particles.shape
    classes = spectrum.shape[1] // 4
    depth = twice // 2
    if last:
        outs = [((classes // 2, 2 * pairs + SPARE, depth), F32)] * 2
    else:
        outs = [((classes, 2 * pairs + LONG_SPARE, depth), BF16)]
    return call(
        finish_kernel,
        [image, mine, spectrum, particles],
        outs,
        [(image.shape, F32)],
        flops=2 * math.prod(spectrum.shape) * twice * 8,
    )


def add_kernel(positions, freqs, own, other, out):
    for k, position in enumerate(positions):
        total = own[k].astype(F32) + other[position].astype(F32)
        count = total[freqs : freqs + 1, :] + total[freqs + 1 : freqs + 2, :]
        out[k, pl.ds(0, freqs), :] = total[:freqs, :].astype(out.dtype)
        out[k, pl.ds(freqs, out.shape[1] - freqs), :] = tail(count, freqs, out)


def halve_kernel(own, other, keep, send):
    half = keep.shape[0]
    for k in range(half):
        keep[k] = own[k] + other[k]
        send[k] = own[half + k] + other[half + k]


def means_kernel(own, other, out):
    freqs = out.shape[1]
    total = own[0] + other[0]
    counts = total[freqs : freqs + 1, :] + total[freqs + 1 : freqs + 2, :]
    out[0] = total[:freqs, :] / (counts + shrinkage)


def swap(value, axis, size, bit):
    return lax.ppermute(value, axis, [(i, i ^ bit) for i in range(size)])


def bits(size):
    assert size > 1 and size & (size - 1) == 0
    return [1 << i for i in range(size.bit_length() - 1)]


def shards(particles, references, noise_inv, prior_rot):
    batch, freqs, depth = particles.shape
    sides = lax.axis_size("cls")
    groups = lax.axis_size("rot")
    blocks = lax.axis_size("blk")
    assert groups == 2 and 2 * groups * freqs == ANG
    group = lax.axis_index("rot").astype(jnp.int32)
    share = batch // groups
    order = [0]
    for bit in reversed(bits(blocks)):
        order = order + [o ^ bit for o in order]
    inv_hi, inv_lo, fwd_hi, fwd_lo = tables(freqs)
    doubled = jnp.concatenate([noise_inv, noise_inv]).reshape(1, depth)
    index = group.reshape(1)
    prior = lax.dynamic_slice_in_dim(prior_rot, group * share, share, 0)
    prior = jnp.pad(prior, (0, -share % 128)).reshape(1, -1)

    other_images = prep(particles, (1 - group) * share, share)
    own_images = prep(particles, group * share, share)
    first = references
    for bit in reversed(bits(blocks)):
        second = swap(first, "blk", blocks, bit)
        if bit > 1:
            first = jnp.concatenate([first, second], 0)
    positions = list(range(blocks))
    for step in range(ITERS):
        last = step == ITERS - 1
        message, energy, left = weigh(
            index, first, second, doubled, other_images, step == 0, positions
        )
        message = swap(message, "rot", groups, 1)
        own = correlate(left, own_images)
        weights, here, sums = scores(index, own, message, energy, prior, inv_hi, inv_lo)
        first = here
        for bit in bits(sides):
            second = swap(first, "cls", sides, bit)
            if 2 * bit < sides:
                (first,) = call(merge_kernel, [first, second], [(here.shape, F32)])
        other, own = turn(index, weights, fwd_hi, fwd_lo, freqs)
        send, keep, evidence = scale(here, first, second, sums, other, own, share)
        message = swap(send, "rot", groups, 1)
        image = gather(keep, own_images)
        if not last:
            (first,) = finish(image, keep, message, other_images, last)
            for bit in bits(blocks):
                second = swap(first, "blk", blocks, bit)
                positions = [order.index(o ^ bit) for o in order]
                if 2 * bit < blocks:
                    (first,) = call(
                        functools.partial(add_kernel, positions, freqs),
                        [first, second],
                        [(first.shape, first.dtype)],
                    )
        else:
            first, second = finish(image, keep, message, other_images, last)
            for bit in bits(blocks):
                second = swap(second, "blk", blocks, bit)
                if 2 * bit < blocks:
                    shape = (first.shape[0] // 2, *first.shape[1:])
                    first, second = call(halve_kernel, [first, second], [(shape, F32)] * 2)
    (means,) = call(means_kernel, [first, second], [((1, freqs, depth), F32)])
    return means, evidence.reshape(share)


def solution(mesh):
    in_specs = (
        P(("grp", "blk"), "rot", None),
        P(("grp", "blk", "cls"), "rot", None),
        P(),
        P(("grp", "blk")),
    )
    out_specs = (P(("grp", "blk", "cls"), "rot", None), P(("grp", "blk", "rot")))
    return jax.shard_map(shards, mesh=mesh, in_specs=in_specs, out_specs=out_specs, check_vma=False)
```

```python
import functools
import math

import jax
import jax.numpy as jnp
import numpy as np
from jax import lax
from jax.experimental import pallas as pl
from jax.experimental.pallas import tpu as pltpu
from jax.sharding import PartitionSpec as P

ANG = 256
ITERS = 2
SIGMA = 32

shrinkage = 1.0

F32 = jnp.float32
BF16 = jnp.bfloat16
SPARE = 8

dot = functools.partial(jnp.dot, preferred_element_type=F32)


def split(x):
    high = x.astype(BF16)
    return high, (x - high.astype(F32)).astype(BF16)


def tables(half_freq):
    turn = np.arange(ANG)
    inverse, forward = [], []
    for group in range(2):
        sides = {}
        for which in range(2):
            freq = which * half_freq + np.arange(half_freq)
            angle = (turn[:, None] * freq[None, :] % ANG) * (2.0 * math.pi / ANG)
            scale = np.where(freq == 0, 1.0, 2.0) / ANG
            sides[which] = (
                np.concatenate([scale * np.cos(angle), -scale * np.sin(angle)], 1),
                np.concatenate([np.cos(angle), np.sin(angle)], 1).T,
            )
        inverse.append(np.concatenate([sides[group][0], sides[1 - group][0]], 1))
        forward.append(np.concatenate([sides[1 - group][1], sides[group][1]], 0))
    result = []
    for table in (inverse, forward):
        table = np.stack(table).astype(np.float32)
        high = table.astype(BF16)
        result += [high, (table - high.astype(np.float32)).astype(BF16)]
    return [jnp.asarray(x.reshape(-1, ANG)) for x in result]


def loop(count, body, unroll):
    while count % unroll:
        unroll -= 1
    if unroll == count:
        for i in range(count):
            body(i)
        return

    def step(outer, carry):
        for inner in range(unroll):
            body(outer * unroll + inner)
        return carry

    lax.fori_loop(0, count // unroll, step, 0)


def each(count, body, init):
    if count <= 8:
        for k in range(count):
            init = body(k, init)
        return init
    return lax.fori_loop(0, count, body, init)


def rows(base, count):
    return pl.ds(pl.multiple_of(base, 8), count)


def call(kernel, ins, outs, scratch=(), flops=0, scalar=False, far=(), room=4 << 20):
    total = 0
    buffers = [(x.shape, x.dtype) for i, x in enumerate(ins) if i not in far]
    for shape, dtype in buffers + list(outs) + [x for x in scratch if isinstance(x, tuple)]:
        dims = [1, 1, *shape]
        lines = -(-dims[-2] // 16) * 16
        lanes = -(-dims[-1] // 128) * 128
        total += math.prod(dims[:-2]) * lines * lanes * jnp.dtype(dtype).itemsize
    kinds = [pltpu.VMEM] * len(ins)
    if scalar:
        kinds[0] = pltpu.SMEM
    for i in far:
        kinds[i] = pltpu.MemorySpace.HBM
    return pl.pallas_call(
        kernel,
        out_shape=[jax.ShapeDtypeStruct(*x) for x in outs],
        in_specs=[pl.BlockSpec(memory_space=kind) for kind in kinds],
        out_specs=[pl.BlockSpec(memory_space=pltpu.VMEM)] * len(outs),
        scratch_shapes=[pltpu.VMEM(*x) if isinstance(x, tuple) else x for x in scratch],
        compiler_params=pltpu.CompilerParams(vmem_limit_bytes=min(total + room, 56 << 20)),
        cost_estimate=pl.CostEstimate(flops=flops, bytes_accessed=total, transcendentals=0),
    )(*ins)


def prep_kernel(share, start_ref, particles_ref, other, own, held, wide, sems):
    chunk, freqs, depth = held.shape[1:]
    pitch = wide.shape[0] // chunk
    steps = share // chunk
    copies = []
    for i in range(2 * steps):
        first = start_ref[i // steps] + i % steps * chunk
        copy = pltpu.make_async_copy(particles_ref.at[pl.ds(first, chunk)], held.at[i], sems.at[i])
        copy.start()
        copies.append(copy)
    for i in range(2 * steps):
        out = (other, own)[i // steps]
        to = pl.ds(i % steps * chunk, chunk)
        copies[i].wait()

        def widen(p):
            wide[rows(p * pitch, freqs), :] = held[i, p].astype(F32)

        loop(chunk, widen, 8)

        def turn(f):
            for part in range(2):
                at = pl.ds(2 * f + part, chunk, stride=pitch)
                out[f, to, pl.ds(part * depth, depth)] = wide[at, :].astype(BF16)

        loop(freqs // 2, turn, 8)


def prep(particles, start, share):
    _, freqs, depth = particles.shape
    chunk = max([n for n in (16, 32, 48) if share % n == 0], default=share)
    steps = 2 * share // chunk
    return call(
        functools.partial(prep_kernel, share),
        [start, particles],
        [((freqs // 2, share, 2 * depth), BF16)] * 2,
        [
            ((steps, chunk, freqs, depth), BF16),
            ((chunk * (freqs + SPARE), depth), F32),
            pltpu.SemaphoreType.DMA((steps,)),
        ],
        flops=1 << 31,
        scalar=True,
        far=(1,),
        room=56 << 20,
    )


def tree(values):
    values = list(values)
    while len(values) > 1:
        values = [a + b for a, b in zip(values[::2], values[1::2])]
    return values[0]


def weigh_kernel(fresh, count, *refs):
    index_ref, *sources = refs[: count + 1]
    doubled_ref, particles, out, energy_ref, left_ref, image = refs[count + 1 :]
    pairs, share, twice = particles.shape
    freqs, depth = 2 * pairs, twice // 2
    classes, lanes = energy_ref.shape
    pitch = freqs + SPARE
    radii = depth // 2
    lane = lax.broadcasted_iota(jnp.int32, (freqs, depth), 1)
    sign = jnp.where(lane < radii, -1.0, 1.0).astype(F32)
    doubled = jnp.concatenate([doubled_ref[...]] * 2, 1)
    row = lax.broadcasted_iota(jnp.int32, (freqs, depth), 0) + index_ref[0] * freqs
    scale = jnp.where(row == 0, 1.0 / ANG, 2.0 / ANG).astype(F32) * doubled

    for k in range(classes):
        if fresh:
            plain = sources[k][0].astype(F32)
        else:
            sums, highs, lows = [
                tree(
                    source[pl.ds(base + (k ^ i) * step, step), :].astype(F32)
                    for i, source in enumerate(sources)
                )
                for base, step in ((0, freqs), (classes * freqs, 1), (classes * (freqs + 1), 1))
            ]
            plain = (sums / (highs + lows + shrinkage)).astype(BF16).astype(F32)
        weighted = (plain * doubled).astype(BF16).astype(F32)
        image[rows(2 * k * pitch, freqs), :] = weighted
        image[rows((2 * k + 1) * pitch, freqs), :] = sign * pltpu.roll(weighted, radii, 1)
        energy = jnp.sum(plain * plain * scale, axis=0, keepdims=True)
        energy = jnp.broadcast_to(jnp.sum(energy, axis=1, keepdims=True), (SPARE, lanes))
        energy_ref[pl.ds(k, 1), :] = energy[:1]
        out[0, rows(2 * k * pitch + freqs, SPARE), :] = energy[:, : out.shape[2]]

    none = jnp.zeros((2 * classes, depth), BF16)

    def correlate(f):
        first, second = [
            image[pl.ds(2 * f + part, 2 * classes, stride=pitch), :].astype(BF16)
            for part in range(2)
        ]
        left = jnp.concatenate(
            [jnp.concatenate([first, none], 1), jnp.concatenate([none, second], 1)], 0
        )
        left_ref[f] = left
        place(out, f, times(left, particles[f]), classes, pitch)

    loop(pairs, correlate, 8)


def times(left, particles):
    return lax.dot_general(left, particles, (((1,), (1,)), ((), ())), preferred_element_type=F32)


def place(out, f, value, classes, pitch):
    tiles, _, width = out.shape
    spare = jnp.zeros((value.shape[0], tiles * width - value.shape[1]), F32)
    value = jnp.concatenate([value, spare], 1) if spare.size else value
    for part in range(2):
        at = pl.ds(2 * f + part, 2 * classes, stride=pitch)
        for tile in range(tiles):
            out[tile, at, :] = value[
                part * 2 * classes : (part + 1) * 2 * classes, tile * width : (tile + 1) * width
            ]


def lane_tiles(share):
    return -(-share // 128)


def weigh(index, sources, inverse_noise, particles, fresh):
    pairs, share, twice = particles.shape
    classes = len(sources)
    lines = 2 * classes * (2 * pairs + SPARE)
    tiles = lane_tiles(share)
    return call(
        functools.partial(weigh_kernel, fresh, classes),
        [index, *sources, inverse_noise, particles],
        [
            ((tiles, lines, 128), F32),
            ((classes, tiles * 128), F32),
            ((pairs, 4 * classes, twice), BF16),
        ],
        [((lines, twice // 2), F32)],
        flops=8 * classes * share * pairs * twice * 4,
        scalar=True,
    )


def correlate_kernel(left_ref, particles, out):
    pairs = left_ref.shape[0]
    classes = left_ref.shape[1] // 4

    def body(f):
        place(out, f, times(left_ref[f], particles[f]), classes, 2 * pairs + SPARE)

    loop(pairs, body, 8)


def correlate(left, particles):
    pairs, share, twice = particles.shape
    lines = left.shape[1] // 2 * (2 * pairs + SPARE)
    return call(
        correlate_kernel,
        [left, particles],
        [((lane_tiles(share), lines, 128), F32)],
        flops=2 * left.shape[1] * share * pairs * twice * 8,
    )[0]


def across(ref, at):
    return jnp.concatenate([ref[tile, at, :] for tile in range(ref.shape[0])], 1)


def table_rows(index_ref, base, count):
    return pl.ds(pl.multiple_of(index_ref[0] * ANG + base, 128), count)


def score_kernel(index_ref, own, other, energy_ref, prior_ref, inv_hi, inv_lo, *refs):
    weights, peaks = refs
    classes, share = energy_ref.shape
    tiles, lines, width = own.shape
    pitch = lines // (2 * classes)
    freqs = pitch - SPARE
    which = table_rows(index_ref, 0, ANG)
    turns = lax.broadcasted_iota(jnp.int32, (ANG, share), 0)
    offset = jnp.abs(turns - prior_ref[...])
    distance = jnp.minimum(offset, ANG - offset).astype(F32)
    prior_term = -distance * distance / (2.0 * SIGMA * SIGMA)

    def score(k, peak):
        value = jnp.concatenate(
            [
                across(ref, rows((2 * k + part) * pitch, freqs))
                for ref in (own, other)
                for part in (0, 1)
            ],
            0,
        )
        high, low = split(value)
        inner = dot(inv_hi[which, :], high) + (
            dot(inv_hi[which, :], low) + dot(inv_lo[which, :], high)
        )
        far = other[0, rows(2 * k * pitch + freqs, SPARE), :][:1]
        energy = energy_ref[pl.ds(k, 1), :] + jnp.concatenate([far] * tiles, 1)
        scores = inner - 0.5 * energy + prior_term
        weights[k] = scores
        return jnp.maximum(peak, jnp.max(scores, axis=0, keepdims=True))

    peak = each(classes, score, jnp.full((1, share), -jnp.inf, F32))

    def weight(k, total):
        value = jnp.exp(weights[k] - peak)
        weights[k] = value
        return total + jnp.sum(value, axis=0, keepdims=True)

    total = each(classes, weight, jnp.zeros((1, share), F32))
    line = lax.broadcasted_iota(jnp.int32, peaks.shape, 0)
    peaks[...] = jnp.where(line == 0, peak, total)


def scores(index, own, other, energy, prior, inv_hi, inv_lo):
    classes, share = energy.shape
    return call(
        score_kernel,
        [index, own, other, energy, prior, inv_hi, inv_lo],
        [((classes, ANG, share), F32), ((8, share), F32)],
        flops=6 * classes * share * ANG * ANG,
        scalar=True,
    )


def merge(first, second):
    top = jnp.maximum(first[0:1], second[0:1])
    total = first[1:2] * jnp.exp(first[0:1] - top) + second[1:2] * jnp.exp(second[0:1] - top)
    return top, total


def merge_kernel(first, second, out):
    top, total = merge(first[...], second[...])
    line = lax.broadcasted_iota(jnp.int32, out.shape, 0)
    out[...] = jnp.where(line == 0, top, total)


def turn_kernel(index_ref, weights, here, first, second, fwd_hi, fwd_lo, *refs):
    rounded_ref, send, evidence_ref, held = refs
    classes, _, lanes = weights.shape
    share = evidence_ref.shape[1]
    pairs = send.shape[0] - 1
    top, total = merge(first[...], second[...])
    evidence_ref[...] = (top + jnp.log(total))[:, :share]
    factor = jnp.exp(here[0:1, :] - top) / total
    lane = lax.broadcasted_iota(jnp.int32, (1, lanes), 1)
    factor = jnp.where(lane < share, factor, 0.0)
    which = table_rows(index_ref, 0, ANG // 2)
    line = lax.broadcasted_iota(jnp.int32, (4 * classes, share), 0)

    def body(k, column):
        value = weights[k] * factor
        count = jnp.sum(jnp.sum(value, axis=0, keepdims=True), axis=1, keepdims=True)
        rounded = value.astype(BF16)
        rounded_ref[k] = rounded
        spread(held, k, dot(fwd_hi[which, :], rounded) + dot(fwd_lo[which, :], rounded))
        high = count.astype(BF16).astype(F32)
        return jnp.where(line == k, high, jnp.where(line == classes + k, count - high, column))

    column = each(classes, body, jnp.zeros((4 * classes, share), F32))
    send[pairs] = column.astype(BF16)

    def rearrange(f):
        send[f] = pick(held, f, classes, share)

    loop(pairs, rearrange, 8)


def spread(held, k, value):
    tiles, lines, width = held.shape
    freqs = value.shape[0] // 2
    for part in range(2):
        for tile in range(tiles):
            held[tile, rows((2 * k + part) * (freqs + SPARE), freqs), :] = value[
                part * freqs : (part + 1) * freqs, tile * width : (tile + 1) * width
            ]


def pick(held, f, classes, share):
    pitch = held.shape[1] // (2 * classes)
    parts = [
        across(held, pl.ds(2 * f + part, 2 * classes, stride=pitch)).astype(BF16)
        for part in range(2)
    ]
    return jnp.concatenate(parts, 0)[:, :share]


def turn(index, weights, here, first, second, fwd_hi, fwd_lo, freqs, share):
    classes, _, lanes = weights.shape
    return call(
        turn_kernel,
        [index, weights, here, first, second, fwd_hi, fwd_lo],
        [
            ((classes, ANG, lanes), BF16),
            ((freqs // 2 + 1, 4 * classes, share), BF16),
            ((1, share), F32),
        ],
        [((lanes // 128, 2 * classes * (freqs + SPARE), 128), F32)],
        flops=4 * classes * lanes * ANG * ANG,
        scalar=True,
    )


def gather_kernel(index_ref, rounded_ref, fwd_hi, fwd_lo, particles, image, held):
    classes = rounded_ref.shape[0]
    pairs, share, _ = particles.shape
    which = table_rows(index_ref, ANG // 2, ANG // 2)

    def body(k, carry):
        rounded = rounded_ref[k]
        spread(held, k, dot(fwd_hi[which, :], rounded) + dot(fwd_lo[which, :], rounded))
        return carry

    each(classes, body, 0)

    def accumulate(f):
        take_in(image, f, dot(pick(held, f, classes, share), particles[f]), classes)

    loop(pairs, accumulate, 8)


def gather(index, rounded, fwd_hi, fwd_lo, particles):
    pairs, share, twice = particles.shape
    classes, _, lanes = rounded.shape
    lines = 2 * classes * (2 * pairs + SPARE)
    return call(
        gather_kernel,
        [index, rounded, fwd_hi, fwd_lo, particles],
        [((lines, twice // 2), F32)],
        [((lanes // 128, lines, 128), F32)],
        flops=4 * classes * lanes * ANG * ANG,
        scalar=True,
    )[0]


def take_in(image, f, value, classes):
    lines, depth = image.shape
    for part in range(2):
        at = pl.ds(2 * f + part, 2 * classes, stride=lines // (2 * classes))
        image[at, :] = value[
            part * 2 * classes : (part + 1) * 2 * classes, part * depth : (part + 1) * depth
        ]


def finish_kernel(image, mine, spectrum, particles, *refs):
    outs, held = refs[:-1], refs[-1]
    pairs, _, twice = particles.shape
    classes = spectrum.shape[1] // 4
    freqs, depth = 2 * pairs, twice // 2
    radii = depth // 2
    pitch = freqs + SPARE

    def body(f):
        take_in(held, f, dot(spectrum[f], particles[f]), classes)

    loop(pairs, body, 8)
    counts = (mine[pairs].astype(F32) + spectrum[pairs].astype(F32))[:, :depth]
    counts = counts[:classes] + counts[classes : 2 * classes]
    lane = lax.broadcasted_iota(jnp.int32, (freqs, depth), 1)
    sign = jnp.where(lane < radii, -1.0, 1.0).astype(F32)
    for k in range(classes):
        plain, turned = [
            image[rows((2 * k + part) * pitch, freqs), :]
            + held[rows((2 * k + part) * pitch, freqs), :]
            for part in range(2)
        ]
        value = plain + sign * pltpu.roll(turned, radii, 1)
        if len(outs) == 1:
            outs[0][pl.ds(k * freqs, freqs), :] = value.astype(BF16)
        else:
            outs[k][pl.ds(0, freqs), :] = value
            outs[k][pl.ds(freqs, SPARE), :] = jnp.broadcast_to(counts[k : k + 1], (SPARE, depth))
    if len(outs) == 1:
        end = outs[0].shape[0] - classes * freqs
        high, low = split(counts)
        spare = [jnp.zeros((end - 2 * classes, depth), F32)] if end > 2 * classes else []
        tail = jnp.concatenate([high.astype(F32), low.astype(F32), *spare], 0)
        outs[0][pl.ds(classes * freqs, end), :] = tail.astype(BF16)


def finish(image, mine, spectrum, particles, last):
    pairs, _, twice = particles.shape
    classes = spectrum.shape[1] // 4
    freqs, depth = 2 * pairs, twice // 2
    if last:
        outs = [((freqs + SPARE, depth), F32)] * classes
    else:
        outs = [((classes * freqs + -(-2 * classes // 16) * 16, depth), BF16)]
    return call(
        finish_kernel,
        [image, mine, spectrum, particles],
        outs,
        [(image.shape, F32)],
        flops=2 * math.prod(spectrum.shape) * twice * 8,
    )


def means_kernel(*refs):
    parts, out = refs[:-1], refs[-1]
    freqs = out.shape[1]
    total = tree(ref[...] for ref in parts)
    out[0] = total[:freqs, :] / (total[freqs : freqs + 1, :] + shrinkage)


def swap(value, axis, size, bit):
    if not bit:
        return value
    return lax.ppermute(value, axis, [(i, i ^ bit) for i in range(size)])


def bits(size):
    assert size > 1 and size & (size - 1) == 0
    return [1 << i for i in range(size.bit_length() - 1)]


def shards(particles, references, noise_inv, prior_rot):
    batch, freqs, depth = particles.shape
    sides = lax.axis_size("cls")
    groups = lax.axis_size("rot")
    blocks = lax.axis_size("blk")
    assert groups == 2 and 2 * groups * freqs == ANG
    group = lax.axis_index("rot").astype(jnp.int32)
    share = batch // groups
    inv_hi, inv_lo, fwd_hi, fwd_lo = tables(freqs)
    inverse_noise = noise_inv.reshape(1, depth // 2)
    index = group.reshape(1)
    prior = lax.dynamic_slice_in_dim(prior_rot, group * share, share, 0)
    prior = jnp.pad(prior, (0, -share % 128)).reshape(1, -1)
    assert blocks & (blocks - 1) == 0

    sources = [swap(references, "blk", blocks, i) for i in range(blocks)]
    other_images, own_images = prep(particles, jnp.stack([1 - group, group]) * share, share)
    for step in range(ITERS):
        last = step == ITERS - 1
        message, energy, left = weigh(index, sources, inverse_noise, other_images, step == 0)
        message = swap(message, "rot", groups, 1)
        own = correlate(left, own_images)
        weights, here = scores(index, own, message, energy, prior, inv_hi, inv_lo)
        first = here
        for bit in bits(sides):
            second = swap(first, "cls", sides, bit)
            if 2 * bit < sides:
                (first,) = call(merge_kernel, [first, second], [(here.shape, F32)])
        rounded, send, evidence = turn(
            index, weights, here, first, second, fwd_hi, fwd_lo, freqs, share
        )
        message = swap(send, "rot", groups, 1)
        image = gather(index, rounded, fwd_hi, fwd_lo, own_images)
        sums = finish(image, send, message, other_images, last)
        sums = sums if last else sums * blocks
        sources = [swap(x, "blk", blocks, i) for i, x in enumerate(sums)]
    (means,) = call(means_kernel, sources, [((1, freqs, depth), F32)])
    return means, evidence.reshape(share)


def solution(mesh):
    in_specs = (
        P(("grp", "blk"), "rot", None),
        P(("grp", "blk", "cls"), "rot", None),
        P(),
        P(("grp", "blk")),
    )
    out_specs = (P(("grp", "blk", "cls"), "rot", None), P(("grp", "blk", "rot")))
    return jax.shard_map(shards, mesh=mesh, in_specs=in_specs, out_specs=out_specs, check_vma=False)
```

```python
import functools
import math

import jax
import jax.numpy as jnp
import numpy as np
from jax import lax
from jax.experimental import pallas as pl
from jax.experimental.pallas import tpu as pltpu
from jax.sharding import PartitionSpec as P

ANG = 256
ITERS = 2
SIGMA = 32

shrinkage = 1.0

F32 = jnp.float32
BF16 = jnp.bfloat16
SPARE = 8

dot = functools.partial(jnp.dot, preferred_element_type=F32)


def split(x):
    high = x.astype(BF16)
    return high, (x - high.astype(F32)).astype(BF16)


def tables(half_freq):
    turn = np.arange(ANG)
    inverse, forward = [], []
    for group in range(2):
        sides = {}
        for which in range(2):
            freq = which * half_freq + np.arange(half_freq)
            angle = (turn[:, None] * freq[None, :] % ANG) * (2.0 * math.pi / ANG)
            scale = np.where(freq == 0, 1.0, 2.0) / ANG
            sides[which] = (
                np.concatenate([scale * np.cos(angle), -scale * np.sin(angle)], 1),
                np.concatenate([np.cos(angle), np.sin(angle)], 1).T,
            )
        inverse.append(np.concatenate([sides[group][0], sides[1 - group][0]], 1))
        forward.append(np.concatenate([sides[1 - group][1], sides[group][1]], 0))
    result = []
    for table in (inverse, forward):
        table = np.stack(table).astype(np.float32)
        high = table.astype(BF16)
        result += [high, (table - high.astype(np.float32)).astype(BF16)]
    return [jnp.asarray(x.reshape(-1, ANG)) for x in result]


def loop(count, body, unroll):
    while count % unroll:
        unroll -= 1
    if unroll == count:
        for i in range(count):
            body(i)
        return

    def step(outer, carry):
        for inner in range(unroll):
            body(outer * unroll + inner)
        return carry

    lax.fori_loop(0, count // unroll, step, 0)


def each(count, body, init):
    if count <= 8:
        for k in range(count):
            init = body(k, init)
        return init
    return lax.fori_loop(0, count, body, init)


def rows(base, count):
    return pl.ds(pl.multiple_of(base, 8), count)


def call(kernel, ins, outs, scratch=(), flops=0, far=(), room=4 << 20):
    total = 0
    buffers = [(x.shape, x.dtype) for i, x in enumerate(ins) if i not in far]
    for shape, dtype in buffers + list(outs) + [x for x in scratch if isinstance(x, tuple)]:
        dims = [1, 1, *shape]
        lines = -(-dims[-2] // 16) * 16
        lanes = -(-dims[-1] // 128) * 128
        total += math.prod(dims[:-2]) * lines * lanes * jnp.dtype(dtype).itemsize
    kinds = [pltpu.VMEM] * len(ins)
    for i in far:
        kinds[i] = pltpu.MemorySpace.HBM
    return pl.pallas_call(
        kernel,
        out_shape=[jax.ShapeDtypeStruct(*x) for x in outs],
        in_specs=[pl.BlockSpec(memory_space=kind) for kind in kinds],
        out_specs=[pl.BlockSpec(memory_space=pltpu.VMEM)] * len(outs),
        scratch_shapes=[pltpu.VMEM(*x) if isinstance(x, tuple) else x for x in scratch],
        compiler_params=pltpu.CompilerParams(vmem_limit_bytes=min(total + room, 56 << 20)),
        cost_estimate=pl.CostEstimate(flops=flops, bytes_accessed=total, transcendentals=0),
    )(*ins)


def prep_kernel(share, particles_ref, other, own, held, wide, sems):
    chunk, freqs, depth = held.shape[1:]
    pitch = wide.shape[0] // chunk
    steps = share // chunk
    group = lax.axis_index("rot")
    copies = []
    for i in range(2 * steps):
        first = jnp.where(i < steps, 1 - group, group) * share + i % steps * chunk
        copy = pltpu.make_async_copy(particles_ref.at[pl.ds(first, chunk)], held.at[i], sems.at[i])
        copy.start()
        copies.append(copy)
    for i in range(2 * steps):
        out = (other, own)[i // steps]
        to = pl.ds(i % steps * chunk, chunk)
        copies[i].wait()

        def widen(p):
            wide[rows(p * pitch, freqs), :] = held[i, p].astype(F32)

        loop(chunk, widen, 8)

        def turn(f):
            for part in range(2):
                at = pl.ds(2 * f + part, chunk, stride=pitch)
                out[f, to, pl.ds(part * depth, depth)] = wide[at, :].astype(BF16)

        loop(freqs // 2, turn, 8)


def prep(particles, share):
    _, freqs, depth = particles.shape
    chunk = max([n for n in (16, 32, 48) if share % n == 0], default=share)
    steps = 2 * share // chunk
    return call(
        functools.partial(prep_kernel, share),
        [particles],
        [((freqs // 2, share, 2 * depth), BF16)] * 2,
        [
            ((steps, chunk, freqs, depth), BF16),
            ((chunk * (freqs + SPARE), depth), F32),
            pltpu.SemaphoreType.DMA((steps,)),
        ],
        flops=1 << 31,
        far=(0,),
        room=36 << 20,
    )


def tree(values):
    values = list(values)
    while len(values) > 1:
        values = [a + b for a, b in zip(values[::2], values[1::2])]
    return values[0]


def weigh_kernel(fresh, count, *refs):
    sources = refs[:count]
    doubled_ref, particles, out, energy_ref, left_ref, image = refs[count:]
    pairs, share, twice = particles.shape
    freqs, depth = 2 * pairs, twice // 2
    classes, lanes = energy_ref.shape
    pitch = freqs + SPARE
    radii = depth // 2
    lane = lax.broadcasted_iota(jnp.int32, (freqs, depth), 1)
    sign = jnp.where(lane < radii, -1.0, 1.0).astype(F32)
    doubled = jnp.concatenate([doubled_ref[...]] * 2, 1)
    row = lax.broadcasted_iota(jnp.int32, (freqs, depth), 0) + lax.axis_index("rot") * freqs
    scale = jnp.where(row == 0, 1.0 / ANG, 2.0 / ANG).astype(F32) * doubled

    for k in range(classes):
        if fresh:
            plain = sources[k][0].astype(F32)
        else:
            sums, highs, lows = [
                tree(
                    source[pl.ds(base + (k ^ i) * step, step), :].astype(F32)
                    for i, source in enumerate(sources)
                )
                for base, step in ((0, freqs), (classes * freqs, 1), (classes * (freqs + 1), 1))
            ]
            plain = (sums / (highs + lows + shrinkage)).astype(BF16).astype(F32)
        weighted = (plain * doubled).astype(BF16).astype(F32)
        image[rows(2 * k * pitch, freqs), :] = weighted
        image[rows((2 * k + 1) * pitch, freqs), :] = sign * pltpu.roll(weighted, radii, 1)
        energy = jnp.sum(plain * plain * scale, axis=0, keepdims=True)
        energy = jnp.broadcast_to(jnp.sum(energy, axis=1, keepdims=True), (SPARE, lanes))
        energy_ref[pl.ds(k, 1), :] = energy[:1]
        out[0, rows(2 * k * pitch + freqs, SPARE), :] = energy[:, : out.shape[2]]

    none = jnp.zeros((2 * classes, depth), BF16)

    def correlate(f):
        first, second = [
            image[pl.ds(2 * f + part, 2 * classes, stride=pitch), :].astype(BF16)
            for part in range(2)
        ]
        left = jnp.concatenate(
            [jnp.concatenate([first, none], 1), jnp.concatenate([none, second], 1)], 0
        )
        left_ref[f] = left
        place(out, f, times(left, particles[f]), classes, pitch)

    loop(pairs, correlate, 8)


def times(left, particles):
    return lax.dot_general(left, particles, (((1,), (1,)), ((), ())), preferred_element_type=F32)


def place(out, f, value, classes, pitch):
    tiles, _, width = out.shape
    spare = jnp.zeros((value.shape[0], tiles * width - value.shape[1]), F32)
    value = jnp.concatenate([value, spare], 1) if spare.size else value
    for part in range(2):
        at = pl.ds(2 * f + part, 2 * classes, stride=pitch)
        for tile in range(tiles):
            out[tile, at, :] = value[
                part * 2 * classes : (part + 1) * 2 * classes, tile * width : (tile + 1) * width
            ]


def lane_tiles(share):
    return -(-share // 128)


def weigh(sources, inverse_noise, particles, fresh):
    pairs, share, twice = particles.shape
    classes = len(sources)
    lines = 2 * classes * (2 * pairs + SPARE)
    tiles = lane_tiles(share)
    return call(
        functools.partial(weigh_kernel, fresh, classes),
        [*sources, inverse_noise, particles],
        [
            ((tiles, lines, 128), F32),
            ((classes, tiles * 128), F32),
            ((pairs, 4 * classes, twice), BF16),
        ],
        [((lines, twice // 2), F32)],
        flops=8 * classes * share * pairs * twice * 4,
    )


def correlate_kernel(left_ref, particles, out):
    pairs = left_ref.shape[0]
    classes = left_ref.shape[1] // 4

    def body(f):
        place(out, f, times(left_ref[f], particles[f]), classes, 2 * pairs + SPARE)

    loop(pairs, body, 8)


def correlate(left, particles):
    pairs, share, twice = particles.shape
    lines = left.shape[1] // 2 * (2 * pairs + SPARE)
    return call(
        correlate_kernel,
        [left, particles],
        [((lane_tiles(share), lines, 128), F32)],
        flops=2 * left.shape[1] * share * pairs * twice * 8,
    )[0]


def across(ref, at):
    return jnp.concatenate([ref[tile, at, :] for tile in range(ref.shape[0])], 1)


def table_rows(base, count):
    return pl.ds(pl.multiple_of(lax.axis_index("rot") * ANG + base, 128), count)


def score_kernel(own, other, energy_ref, prior_ref, inv_hi, inv_lo, *refs):
    weights, peaks = refs
    classes, share = energy_ref.shape
    tiles, lines, width = own.shape
    pitch = lines // (2 * classes)
    freqs = pitch - SPARE
    which = table_rows(0, ANG)
    turns = lax.broadcasted_iota(jnp.int32, (ANG, share), 0)
    offset = jnp.abs(turns - prior_ref[...])
    distance = jnp.minimum(offset, ANG - offset).astype(F32)
    prior_term = -distance * distance / (2.0 * SIGMA * SIGMA)

    def score(k, peak):
        value = jnp.concatenate(
            [
                across(ref, rows((2 * k + part) * pitch, freqs))
                for ref in (own, other)
                for part in (0, 1)
            ],
            0,
        )
        high, low = split(value)
        inner = dot(inv_hi[which, :], high) + (
            dot(inv_hi[which, :], low) + dot(inv_lo[which, :], high)
        )
        far = other[0, rows(2 * k * pitch + freqs, SPARE), :][:1]
        energy = energy_ref[pl.ds(k, 1), :] + jnp.concatenate([far] * tiles, 1)
        scores = inner - 0.5 * energy + prior_term
        weights[k] = scores
        return jnp.maximum(peak, jnp.max(scores, axis=0, keepdims=True))

    peak = each(classes, score, jnp.full((1, share), -jnp.inf, F32))

    def weight(k, total):
        value = jnp.exp(weights[k] - peak)
        weights[k] = value
        return total + jnp.sum(value, axis=0, keepdims=True)

    total = each(classes, weight, jnp.zeros((1, share), F32))
    line = lax.broadcasted_iota(jnp.int32, peaks.shape, 0)
    peaks[...] = jnp.where(line == 0, peak, total)


def scores(own, other, energy, prior, inv_hi, inv_lo):
    classes, share = energy.shape
    return call(
        score_kernel,
        [own, other, energy, prior, inv_hi, inv_lo],
        [((classes, ANG, share), F32), ((8, share), F32)],
        flops=6 * classes * share * ANG * ANG,
    )


def merge(first, second):
    top = jnp.maximum(first[0:1], second[0:1])
    total = first[1:2] * jnp.exp(first[0:1] - top) + second[1:2] * jnp.exp(second[0:1] - top)
    return top, total


def merge_kernel(first, second, out):
    top, total = merge(first[...], second[...])
    line = lax.broadcasted_iota(jnp.int32, out.shape, 0)
    out[...] = jnp.where(line == 0, top, total)


def turn_kernel(weights, here, first, second, fwd_hi, fwd_lo, *refs):
    rounded_ref, send, evidence_ref, held = refs
    classes, _, lanes = weights.shape
    share = evidence_ref.shape[1]
    pairs = send.shape[0] - 1
    top, total = merge(first[...], second[...])
    evidence_ref[...] = (top + jnp.log(total))[:, :share]
    factor = jnp.exp(here[0:1, :] - top) / total
    lane = lax.broadcasted_iota(jnp.int32, (1, lanes), 1)
    factor = jnp.where(lane < share, factor, 0.0)
    which = table_rows(0, ANG // 2)
    line = lax.broadcasted_iota(jnp.int32, (4 * classes, share), 0)

    def body(k, column):
        value = weights[k] * factor
        count = jnp.sum(jnp.sum(value, axis=0, keepdims=True), axis=1, keepdims=True)
        rounded = value.astype(BF16)
        rounded_ref[k] = rounded
        spread(held, k, dot(fwd_hi[which, :], rounded) + dot(fwd_lo[which, :], rounded))
        high = count.astype(BF16).astype(F32)
        return jnp.where(line == k, high, jnp.where(line == classes + k, count - high, column))

    column = each(classes, body, jnp.zeros((4 * classes, share), F32))
    send[pairs] = column.astype(BF16)

    def rearrange(f):
        send[f] = pick(held, f, classes, share)

    loop(pairs, rearrange, 8)


def spread(held, k, value):
    tiles, lines, width = held.shape
    freqs = value.shape[0] // 2
    for part in range(2):
        for tile in range(tiles):
            held[tile, rows((2 * k + part) * (freqs + SPARE), freqs), :] = value[
                part * freqs : (part + 1) * freqs, tile * width : (tile + 1) * width
            ]


def pick(held, f, classes, share):
    pitch = held.shape[1] // (2 * classes)
    parts = [
        across(held, pl.ds(2 * f + part, 2 * classes, stride=pitch)).astype(BF16)
        for part in range(2)
    ]
    return jnp.concatenate(parts, 0)[:, :share]


def turn(weights, here, first, second, fwd_hi, fwd_lo, freqs, share):
    classes, _, lanes = weights.shape
    return call(
        turn_kernel,
        [weights, here, first, second, fwd_hi, fwd_lo],
        [
            ((classes, ANG, lanes), BF16),
            ((freqs // 2 + 1, 4 * classes, share), BF16),
            ((1, share), F32),
        ],
        [((lanes // 128, 2 * classes * (freqs + SPARE), 128), F32)],
        flops=4 * classes * lanes * ANG * ANG,
    )


def gather_kernel(rounded_ref, fwd_hi, fwd_lo, particles, image, held):
    classes = rounded_ref.shape[0]
    pairs, share, _ = particles.shape
    which = table_rows(ANG // 2, ANG // 2)

    def body(k, carry):
        rounded = rounded_ref[k]
        spread(held, k, dot(fwd_hi[which, :], rounded) + dot(fwd_lo[which, :], rounded))
        return carry

    each(classes, body, 0)

    def accumulate(f):
        take_in(image, f, dot(pick(held, f, classes, share), particles[f]), classes)

    loop(pairs, accumulate, 8)


def gather(rounded, fwd_hi, fwd_lo, particles):
    pairs, share, twice = particles.shape
    classes, _, lanes = rounded.shape
    lines = 2 * classes * (2 * pairs + SPARE)
    return call(
        gather_kernel,
        [rounded, fwd_hi, fwd_lo, particles],
        [((lines, twice // 2), F32)],
        [((lanes // 128, lines, 128), F32)],
        flops=4 * classes * lanes * ANG * ANG,
    )[0]


def take_in(image, f, value, classes):
    lines, depth = image.shape
    for part in range(2):
        at = pl.ds(2 * f + part, 2 * classes, stride=lines // (2 * classes))
        image[at, :] = value[
            part * 2 * classes : (part + 1) * 2 * classes, part * depth : (part + 1) * depth
        ]


def finish_kernel(image, mine, spectrum, particles, *refs):
    outs, held = refs[:-1], refs[-1]
    pairs, _, twice = particles.shape
    classes = spectrum.shape[1] // 4
    freqs, depth = 2 * pairs, twice // 2
    radii = depth // 2
    pitch = freqs + SPARE

    def body(f):
        take_in(held, f, dot(spectrum[f], particles[f]), classes)

    loop(pairs, body, 8)
    counts = (mine[pairs].astype(F32) + spectrum[pairs].astype(F32))[:, :depth]
    counts = counts[:classes] + counts[classes : 2 * classes]
    lane = lax.broadcasted_iota(jnp.int32, (freqs, depth), 1)
    sign = jnp.where(lane < radii, -1.0, 1.0).astype(F32)
    for k in range(classes):
        plain, turned = [
            image[rows((2 * k + part) * pitch, freqs), :]
            + held[rows((2 * k + part) * pitch, freqs), :]
            for part in range(2)
        ]
        value = plain + sign * pltpu.roll(turned, radii, 1)
        if len(outs) == 1:
            outs[0][pl.ds(k * freqs, freqs), :] = value.astype(BF16)
        else:
            outs[k][pl.ds(0, freqs), :] = value
            outs[k][pl.ds(freqs, SPARE), :] = jnp.broadcast_to(counts[k : k + 1], (SPARE, depth))
    if len(outs) == 1:
        end = outs[0].shape[0] - classes * freqs
        high, low = split(counts)
        spare = [jnp.zeros((end - 2 * classes, depth), F32)] if end > 2 * classes else []
        tail = jnp.concatenate([high.astype(F32), low.astype(F32), *spare], 0)
        outs[0][pl.ds(classes * freqs, end), :] = tail.astype(BF16)


def finish(image, mine, spectrum, particles, last):
    pairs, _, twice = particles.shape
    classes = spectrum.shape[1] // 4
    freqs, depth = 2 * pairs, twice // 2
    if last:
        outs = [((freqs + SPARE, depth), F32)] * classes
    else:
        outs = [((classes * freqs + -(-2 * classes // 16) * 16, depth), BF16)]
    return call(
        finish_kernel,
        [image, mine, spectrum, particles],
        outs,
        [(image.shape, F32)],
        flops=2 * math.prod(spectrum.shape) * twice * 8,
    )


def means_kernel(*refs):
    *parts, evidence_ref, out, last_ref = refs
    last_ref[...] = evidence_ref[...]
    freqs = out.shape[1]
    total = tree(ref[...] for ref in parts)
    out[0] = total[:freqs, :] / (total[freqs : freqs + 1, :] + shrinkage)


def swap(value, axis, size, bit):
    if not bit:
        return value
    return lax.ppermute(value, axis, [(i, i ^ bit) for i in range(size)])


def bits(size):
    assert size > 1 and size & (size - 1) == 0
    return [1 << i for i in range(size.bit_length() - 1)]


def shards(particles, references, noise_inv, prior_rot):
    batch, freqs, depth = particles.shape
    sides = lax.axis_size("cls")
    groups = lax.axis_size("rot")
    blocks = lax.axis_size("blk")
    assert groups == 2 and 2 * groups * freqs == ANG
    group = lax.axis_index("rot").astype(jnp.int32)
    share = batch // groups
    inv_hi, inv_lo, fwd_hi, fwd_lo = tables(freqs)
    inverse_noise = noise_inv.reshape(1, depth // 2)
    prior = lax.dynamic_slice_in_dim(prior_rot, group * share, share, 0)
    prior = jnp.pad(prior, (0, -share % 128)).reshape(1, -1)
    assert blocks & (blocks - 1) == 0

    sources = [swap(references, "blk", blocks, i) for i in range(blocks)]
    other_images, own_images = prep(particles, share)
    for step in range(ITERS):
        last = step == ITERS - 1
        message, energy, left = weigh(sources, inverse_noise, other_images, step == 0)
        message = swap(message, "rot", groups, 1)
        own = correlate(left, own_images)
        weights, here = scores(own, message, energy, prior, inv_hi, inv_lo)
        first = here
        for bit in bits(sides):
            second = swap(first, "cls", sides, bit)
            if 2 * bit < sides:
                (first,) = call(merge_kernel, [first, second], [(here.shape, F32)])
        rounded, send, evidence = turn(weights, here, first, second, fwd_hi, fwd_lo, freqs, share)
        message = swap(send, "rot", groups, 1)
        image = gather(rounded, fwd_hi, fwd_lo, own_images)
        sums = finish(image, send, message, other_images, last)
        sums = sums if last else sums * blocks
        sources = [swap(x, "blk", blocks, i) for i, x in enumerate(sums)]
    means, evidence = call(
        means_kernel, [*sources, evidence], [((1, freqs, depth), F32), (evidence.shape, F32)]
    )
    return means, evidence.reshape(share)


def solution(mesh):
    in_specs = (
        P(("grp", "blk"), "rot", None),
        P(("grp", "blk", "cls"), "rot", None),
        P(),
        P(("grp", "blk")),
    )
    out_specs = (P(("grp", "blk", "cls"), "rot", None), P(("grp", "blk", "rot")))
    return jax.shard_map(shards, mesh=mesh, in_specs=in_specs, out_specs=out_specs, check_vma=False)
```

```python
import functools
import math

import jax
import jax.numpy as jnp
import numpy as np
from jax import lax
from jax.experimental import pallas as pl
from jax.experimental.pallas import tpu as pltpu
from jax.sharding import PartitionSpec as P

ANG = 256
ITERS = 2
SIGMA = 32

shrinkage = 1.0

F32 = jnp.float32
BF16 = jnp.bfloat16
SPARE = 8

dot = functools.partial(jnp.dot, preferred_element_type=F32)


def split(x):
    high = x.astype(BF16)
    return high, (x - high.astype(F32)).astype(BF16)


def tables(half_freq):
    turn = np.arange(ANG)
    inverse, forward = [], []
    for group in range(2):
        sides = {}
        for which in range(2):
            freq = which * half_freq + np.arange(half_freq)
            angle = (turn[:, None] * freq[None, :] % ANG) * (2.0 * math.pi / ANG)
            scale = np.where(freq == 0, 1.0, 2.0) / ANG
            sides[which] = (
                np.concatenate([scale * np.cos(angle), -scale * np.sin(angle)], 1),
                np.concatenate([np.cos(angle), np.sin(angle)], 1).T,
            )
        inverse.append(np.concatenate([sides[group][0], sides[1 - group][0]], 1))
        forward.append(np.concatenate([sides[1 - group][1], sides[group][1]], 0))
    result = []
    for table in (inverse, forward):
        table = np.stack(table).astype(np.float32)
        high = table.astype(BF16)
        result += [high, (table - high.astype(np.float32)).astype(BF16)]
    return [jnp.asarray(x.reshape(-1, ANG)) for x in result]


def loop(count, body, unroll):
    while count % unroll:
        unroll -= 1
    if unroll == count:
        for i in range(count):
            body(i)
        return

    def step(outer, carry):
        for inner in range(unroll):
            body(outer * unroll + inner)
        return carry

    lax.fori_loop(0, count // unroll, step, 0)


def each(count, body, init):
    if count <= 8:
        for k in range(count):
            init = body(k, init)
        return init
    return lax.fori_loop(0, count, body, init)


def rows(base, count):
    return pl.ds(pl.multiple_of(base, 8), count)


def call(kernel, ins, outs, scratch=(), flops=0, far=(), room=4 << 20):
    total = 0
    buffers = [(x.shape, x.dtype) for i, x in enumerate(ins) if i not in far]
    for shape, dtype in buffers + list(outs) + [x for x in scratch if isinstance(x, tuple)]:
        dims = [1, 1, *shape]
        lines = -(-dims[-2] // 16) * 16
        lanes = -(-dims[-1] // 128) * 128
        total += math.prod(dims[:-2]) * lines * lanes * jnp.dtype(dtype).itemsize
    kinds = [pltpu.VMEM] * len(ins)
    for i in far:
        kinds[i] = pltpu.MemorySpace.HBM
    return pl.pallas_call(
        kernel,
        out_shape=[jax.ShapeDtypeStruct(*x) for x in outs],
        in_specs=[pl.BlockSpec(memory_space=kind) for kind in kinds],
        out_specs=[pl.BlockSpec(memory_space=pltpu.VMEM)] * len(outs),
        scratch_shapes=[pltpu.VMEM(*x) if isinstance(x, tuple) else x for x in scratch],
        compiler_params=pltpu.CompilerParams(vmem_limit_bytes=min(total + room, 56 << 20)),
        cost_estimate=pl.CostEstimate(flops=flops, bytes_accessed=total, transcendentals=0),
    )(*ins)


def prep_kernel(share, particles_ref, other, own, held, sems):
    steps, chunk, freqs, depth = held.shape
    steps //= 2
    group = lax.axis_index("rot")
    copies = []
    for i in range(2 * steps):
        first = jnp.where(i < steps, 1 - group, group) * share + i % steps * chunk
        copy = pltpu.make_async_copy(particles_ref.at[pl.ds(first, chunk)], held.at[i], sems.at[i])
        copy.start()
        copies.append(copy)
    to = lax.broadcasted_iota(jnp.int32, (256, 256), 0)
    at = lax.broadcasted_iota(jnp.int32, (256, 256), 1)
    permutation = ((to // 16 == at % 16) & (to % 16 == at // 16)).astype(F32).astype(BF16)
    for i in range(2 * steps):
        out = (other, own)[i // steps]
        copies[i].wait()
        for p in range(0, chunk, 16):
            for f in range(0, freqs, 32):
                blocks = [
                    jnp.concatenate(
                        [held[i, p + j, pl.ds(f + half, 16), :] for j in range(16)], 0
                    )
                    for half in (0, 16)
                ]
                turned = dot(permutation, jnp.concatenate(blocks, 1)).astype(BF16)
                for half in range(2):
                    for j in range(16):
                        pair, part = divmod(f + 16 * half + j, 2)
                        out[
                            pair,
                            pl.ds(i % steps * chunk + p, 16),
                            pl.ds(part * depth, depth),
                        ] = turned[16 * j : 16 * j + 16, half * depth : (half + 1) * depth]


def prep(particles, share):
    _, freqs, depth = particles.shape
    assert share % 16 == 0 and freqs % 32 == 0
    chunk = max(n for n in (16, 32, 48) if share % n == 0)
    steps = 2 * share // chunk
    return call(
        functools.partial(prep_kernel, share),
        [particles],
        [((freqs // 2, share, 2 * depth), BF16)] * 2,
        [((steps, chunk, freqs, depth), BF16), pltpu.SemaphoreType.DMA((steps,))],
        flops=1 << 31,
        far=(0,),
        room=38 << 20,
    )


def tree(values):
    values = list(values)
    while len(values) > 1:
        values = [a + b for a, b in zip(values[::2], values[1::2])]
    return values[0]


def weigh_kernel(fresh, count, *refs):
    sources = refs[:count]
    doubled_ref, particles, out, energy_ref, left_ref, image = refs[count:]
    pairs, share, twice = particles.shape
    freqs, depth = 2 * pairs, twice // 2
    classes, lanes = energy_ref.shape
    pitch = freqs + SPARE
    radii = depth // 2
    lane = lax.broadcasted_iota(jnp.int32, (freqs, depth), 1)
    sign = jnp.where(lane < radii, -1.0, 1.0).astype(F32)
    doubled = jnp.concatenate([doubled_ref[...]] * 2, 1)
    row = lax.broadcasted_iota(jnp.int32, (freqs, depth), 0) + lax.axis_index("rot") * freqs
    scale = jnp.where(row == 0, 1.0 / ANG, 2.0 / ANG).astype(F32) * doubled

    for k in range(classes):
        if fresh:
            plain = sources[k][0].astype(F32)
        else:
            sums, highs, lows = [
                tree(
                    source[pl.ds(base + (k ^ i) * step, step), :].astype(F32)
                    for i, source in enumerate(sources)
                )
                for base, step in ((0, freqs), (classes * freqs, 1), (classes * (freqs + 1), 1))
            ]
            plain = (sums / (highs + lows + shrinkage)).astype(BF16).astype(F32)
        weighted = (plain * doubled).astype(BF16).astype(F32)
        image[rows(2 * k * pitch, freqs), :] = weighted
        image[rows((2 * k + 1) * pitch, freqs), :] = sign * pltpu.roll(weighted, radii, 1)
        energy = jnp.sum(plain * plain * scale, axis=0, keepdims=True)
        energy = jnp.broadcast_to(jnp.sum(energy, axis=1, keepdims=True), (SPARE, lanes))
        energy_ref[pl.ds(k, 1), :] = energy[:1]
        out[0, rows(2 * k * pitch + freqs, SPARE), :] = energy[:, : out.shape[2]]

    none = jnp.zeros((2 * classes, depth), BF16)

    def correlate(f):
        first, second = [
            image[pl.ds(2 * f + part, 2 * classes, stride=pitch), :].astype(BF16)
            for part in range(2)
        ]
        left = jnp.concatenate(
            [jnp.concatenate([first, none], 1), jnp.concatenate([none, second], 1)], 0
        )
        left_ref[f] = left
        place(out, f, times(left, particles[f]), classes, pitch)

    loop(pairs, correlate, 8)


def times(left, particles):
    return lax.dot_general(left, particles, (((1,), (1,)), ((), ())), preferred_element_type=F32)


def place(out, f, value, classes, pitch):
    tiles, _, width = out.shape
    spare = jnp.zeros((value.shape[0], tiles * width - value.shape[1]), F32)
    value = jnp.concatenate([value, spare], 1) if spare.size else value
    for part in range(2):
        at = pl.ds(2 * f + part, 2 * classes, stride=pitch)
        for tile in range(tiles):
            out[tile, at, :] = value[
                part * 2 * classes : (part + 1) * 2 * classes, tile * width : (tile + 1) * width
            ]


def lane_tiles(share):
    return -(-share // 128)


def weigh(sources, inverse_noise, particles, fresh):
    pairs, share, twice = particles.shape
    classes = len(sources)
    lines = 2 * classes * (2 * pairs + SPARE)
    tiles = lane_tiles(share)
    return call(
        functools.partial(weigh_kernel, fresh, classes),
        [*sources, inverse_noise, particles],
        [
            ((tiles, lines, 128), F32),
            ((classes, tiles * 128), F32),
            ((pairs, 4 * classes, twice), BF16),
        ],
        [((lines, twice // 2), F32)],
        flops=8 * classes * share * pairs * twice * 4,
    )


def correlate_kernel(left_ref, particles, out):
    pairs = left_ref.shape[0]
    classes = left_ref.shape[1] // 4

    def body(f):
        place(out, f, times(left_ref[f], particles[f]), classes, 2 * pairs + SPARE)

    loop(pairs, body, 8)


def correlate(left, particles):
    pairs, share, twice = particles.shape
    lines = left.shape[1] // 2 * (2 * pairs + SPARE)
    return call(
        correlate_kernel,
        [left, particles],
        [((lane_tiles(share), lines, 128), F32)],
        flops=2 * left.shape[1] * share * pairs * twice * 8,
    )[0]


def across(ref, at):
    return jnp.concatenate([ref[tile, at, :] for tile in range(ref.shape[0])], 1)


def table_rows(base, count):
    return pl.ds(pl.multiple_of(lax.axis_index("rot") * ANG + base, 128), count)


def score_kernel(own, other, energy_ref, prior_ref, inv_hi, inv_lo, *refs):
    weights, peaks = refs
    classes, share = energy_ref.shape
    tiles, lines, width = own.shape
    pitch = lines // (2 * classes)
    freqs = pitch - SPARE
    which = table_rows(0, ANG)
    turns = lax.broadcasted_iota(jnp.int32, (ANG, share), 0)
    lane = lax.broadcasted_iota(jnp.int32, (1, share), 1)
    priors = prior_ref[...].reshape(1, -1)
    half = priors.shape[1] // 2
    first, second = [
        jnp.concatenate([priors[:, i * half : (i + 1) * half], lane[:, half:]], 1)
        for i in range(2)
    ]
    offset = jnp.abs(turns - jnp.where(lax.axis_index("rot") == 0, first, second))
    distance = jnp.minimum(offset, ANG - offset).astype(F32)
    prior_term = -distance * distance / (2.0 * SIGMA * SIGMA)

    def score(k, peak):
        value = jnp.concatenate(
            [
                across(ref, rows((2 * k + part) * pitch, freqs))
                for ref in (own, other)
                for part in (0, 1)
            ],
            0,
        )
        high, low = split(value)
        inner = dot(inv_hi[which, :], high) + (
            dot(inv_hi[which, :], low) + dot(inv_lo[which, :], high)
        )
        far = other[0, rows(2 * k * pitch + freqs, SPARE), :][:1]
        energy = energy_ref[pl.ds(k, 1), :] + jnp.concatenate([far] * tiles, 1)
        scores = inner - 0.5 * energy + prior_term
        weights[k] = scores
        return jnp.maximum(peak, jnp.max(scores, axis=0, keepdims=True))

    peak = each(classes, score, jnp.full((1, share), -jnp.inf, F32))

    def weight(k, total):
        value = jnp.exp(weights[k] - peak)
        weights[k] = value
        return total + jnp.sum(value, axis=0, keepdims=True)

    total = each(classes, weight, jnp.zeros((1, share), F32))
    line = lax.broadcasted_iota(jnp.int32, peaks.shape, 0)
    peaks[...] = jnp.where(line == 0, peak, total)


def scores(own, other, energy, prior, inv_hi, inv_lo):
    classes, share = energy.shape
    return call(
        score_kernel,
        [own, other, energy, prior, inv_hi, inv_lo],
        [((classes, ANG, share), F32), ((8, share), F32)],
        flops=6 * classes * share * ANG * ANG,
    )


def merge(first, second):
    top = jnp.maximum(first[0:1], second[0:1])
    total = first[1:2] * jnp.exp(first[0:1] - top) + second[1:2] * jnp.exp(second[0:1] - top)
    return top, total


def merge_kernel(first, second, out):
    top, total = merge(first[...], second[...])
    line = lax.broadcasted_iota(jnp.int32, out.shape, 0)
    out[...] = jnp.where(line == 0, top, total)


def turn_kernel(weights, here, first, second, fwd_hi, fwd_lo, *refs):
    rounded_ref, send, *evidence_ref, held = refs
    classes, _, lanes = weights.shape
    share = send.shape[2]
    pairs = send.shape[0] - 1
    top, total = merge(first[...], second[...])
    for ref in evidence_ref:
        ref[...] = (top + jnp.log(total))[:, :share]
    factor = jnp.exp(here[0:1, :] - top) / total
    lane = lax.broadcasted_iota(jnp.int32, (1, lanes), 1)
    factor = jnp.where(lane < share, factor, 0.0)
    which = table_rows(0, ANG // 2)
    line = lax.broadcasted_iota(jnp.int32, (4 * classes, share), 0)

    def body(k, column):
        value = weights[k] * factor
        count = jnp.sum(jnp.sum(value, axis=0, keepdims=True), axis=1, keepdims=True)
        rounded = value.astype(BF16)
        rounded_ref[k] = rounded
        spread(held, k, dot(fwd_hi[which, :], rounded) + dot(fwd_lo[which, :], rounded))
        high = count.astype(BF16).astype(F32)
        return jnp.where(line == k, high, jnp.where(line == classes + k, count - high, column))

    column = each(classes, body, jnp.zeros((4 * classes, share), F32))
    send[pairs] = column.astype(BF16)

    def rearrange(f):
        send[f] = pick(held, f, classes, share)

    loop(pairs, rearrange, 8)


def spread(held, k, value):
    tiles, lines, width = held.shape
    freqs = value.shape[0] // 2
    for part in range(2):
        for tile in range(tiles):
            held[tile, rows((2 * k + part) * (freqs + SPARE), freqs), :] = value[
                part * freqs : (part + 1) * freqs, tile * width : (tile + 1) * width
            ]


def pick(held, f, classes, share):
    pitch = held.shape[1] // (2 * classes)
    parts = [
        across(held, pl.ds(2 * f + part, 2 * classes, stride=pitch)).astype(BF16)
        for part in range(2)
    ]
    return jnp.concatenate(parts, 0)[:, :share]


def turn(weights, here, first, second, fwd_hi, fwd_lo, freqs, share, last):
    classes, _, lanes = weights.shape
    return call(
        turn_kernel,
        [weights, here, first, second, fwd_hi, fwd_lo],
        [
            ((classes, ANG, lanes), BF16),
            ((freqs // 2 + 1, 4 * classes, share), BF16),
            *([((1, share), F32)] if last else []),
        ],
        [((lanes // 128, 2 * classes * (freqs + SPARE), 128), F32)],
        flops=4 * classes * lanes * ANG * ANG,
    )


def gather_kernel(rounded_ref, fwd_hi, fwd_lo, particles, image, held):
    classes = rounded_ref.shape[0]
    pairs, share, _ = particles.shape
    which = table_rows(ANG // 2, ANG // 2)

    def body(k, carry):
        rounded = rounded_ref[k]
        spread(held, k, dot(fwd_hi[which, :], rounded) + dot(fwd_lo[which, :], rounded))
        return carry

    each(classes, body, 0)

    def accumulate(f):
        take_in(image, f, dot(pick(held, f, classes, share), particles[f]), classes)

    loop(pairs, accumulate, 8)


def gather(rounded, fwd_hi, fwd_lo, particles):
    pairs, share, twice = particles.shape
    classes, _, lanes = rounded.shape
    lines = 2 * classes * (2 * pairs + SPARE)
    return call(
        gather_kernel,
        [rounded, fwd_hi, fwd_lo, particles],
        [((lines, twice // 2), F32)],
        [((lanes // 128, lines, 128), F32)],
        flops=4 * classes * lanes * ANG * ANG,
    )[0]


def take_in(image, f, value, classes):
    lines, depth = image.shape
    for part in range(2):
        at = pl.ds(2 * f + part, 2 * classes, stride=lines // (2 * classes))
        image[at, :] = value[
            part * 2 * classes : (part + 1) * 2 * classes, part * depth : (part + 1) * depth
        ]


def finish_kernel(image, mine, spectrum, particles, *refs):
    outs, held = refs[:-1], refs[-1]
    pairs, _, twice = particles.shape
    classes = spectrum.shape[1] // 4
    freqs, depth = 2 * pairs, twice // 2
    radii = depth // 2
    pitch = freqs + SPARE

    def body(f):
        take_in(held, f, dot(spectrum[f], particles[f]), classes)

    loop(pairs, body, 8)
    counts = (mine[pairs].astype(F32) + spectrum[pairs].astype(F32))[:, :depth]
    counts = counts[:classes] + counts[classes : 2 * classes]
    lane = lax.broadcasted_iota(jnp.int32, (freqs, depth), 1)
    sign = jnp.where(lane < radii, -1.0, 1.0).astype(F32)
    for k in range(classes):
        plain, turned = [
            image[rows((2 * k + part) * pitch, freqs), :]
            + held[rows((2 * k + part) * pitch, freqs), :]
            for part in range(2)
        ]
        value = plain + sign * pltpu.roll(turned, radii, 1)
        if len(outs) == 1:
            outs[0][pl.ds(k * freqs, freqs), :] = value.astype(BF16)
        else:
            outs[k][pl.ds(0, freqs), :] = value
            outs[k][pl.ds(freqs, SPARE), :] = jnp.broadcast_to(counts[k : k + 1], (SPARE, depth))
    if len(outs) == 1:
        end = outs[0].shape[0] - classes * freqs
        high, low = split(counts)
        spare = [jnp.zeros((end - 2 * classes, depth), F32)] if end > 2 * classes else []
        tail = jnp.concatenate([high.astype(F32), low.astype(F32), *spare], 0)
        outs[0][pl.ds(classes * freqs, end), :] = tail.astype(BF16)


def finish(image, mine, spectrum, particles, last):
    pairs, _, twice = particles.shape
    classes = spectrum.shape[1] // 4
    freqs, depth = 2 * pairs, twice // 2
    if last:
        outs = [((freqs + SPARE, depth), F32)] * classes
    else:
        outs = [((classes * freqs + -(-2 * classes // 16) * 16, depth), BF16)]
    return call(
        finish_kernel,
        [image, mine, spectrum, particles],
        outs,
        [(image.shape, F32)],
        flops=2 * math.prod(spectrum.shape) * twice * 8,
    )


def means_kernel(*refs):
    *parts, evidence_ref, out, last_ref = refs
    last_ref[...] = evidence_ref[...]
    freqs = out.shape[1]
    total = tree(ref[...] for ref in parts)
    out[0] = total[:freqs, :] / (total[freqs : freqs + 1, :] + shrinkage)


def swap(value, axis, size, bit):
    if not bit:
        return value
    return lax.ppermute(value, axis, [(i, i ^ bit) for i in range(size)])


def bits(size):
    assert size > 1 and size & (size - 1) == 0
    return [1 << i for i in range(size.bit_length() - 1)]


def shards(particles, references, noise_inv, prior_rot):
    batch, freqs, depth = particles.shape
    sides = lax.axis_size("cls")
    groups = lax.axis_size("rot")
    blocks = lax.axis_size("blk")
    assert groups == 2 and 2 * groups * freqs == ANG
    share = batch // groups
    inv_hi, inv_lo, fwd_hi, fwd_lo = tables(freqs)
    inverse_noise = noise_inv.reshape(1, depth // 2)
    assert blocks & (blocks - 1) == 0

    sources = [swap(references, "blk", blocks, i) for i in range(blocks)]
    other_images, own_images = prep(particles, share)
    for step in range(ITERS):
        last = step == ITERS - 1
        message, energy, left = weigh(sources, inverse_noise, other_images, step == 0)
        message = swap(message, "rot", groups, 1)
        own = correlate(left, own_images)
        weights, here = scores(own, message, energy, prior_rot, inv_hi, inv_lo)
        first = here
        for bit in bits(sides):
            second = swap(first, "cls", sides, bit)
            if 2 * bit < sides:
                (first,) = call(merge_kernel, [first, second], [(here.shape, F32)])
        rounded, send, *evidence = turn(
            weights, here, first, second, fwd_hi, fwd_lo, freqs, share, last
        )
        message = swap(send, "rot", groups, 1)
        image = gather(rounded, fwd_hi, fwd_lo, own_images)
        sums = finish(image, send, message, other_images, last)
        sums = sums if last else sums * blocks
        sources = [swap(sums[i], "blk", blocks, i) for i in reversed(range(blocks))][::-1]
    means, evidence = call(
        means_kernel, [*sources[::-1], *evidence], [((1, freqs, depth), F32), ((1, share), F32)]
    )
    return means, evidence.reshape(share)


def solution(mesh):
    in_specs = (
        P(("grp", "blk"), "rot", None),
        P(("grp", "blk", "cls"), "rot", None),
        P(),
        P(("grp", "blk")),
    )
    out_specs = (P(("grp", "blk", "cls"), "rot", None), P(("grp", "blk", "rot")))
    return jax.shard_map(shards, mesh=mesh, in_specs=in_specs, out_specs=out_specs, check_vma=False)
```

```python
import functools
import math

import jax
import jax.numpy as jnp
import numpy as np
from jax import lax
from jax.experimental import pallas as pl
from jax.experimental.pallas import tpu as pltpu
from jax.sharding import PartitionSpec as P

ANG = 256
ITERS = 2
SIGMA = 32

shrinkage = 1.0

F32 = jnp.float32
BF16 = jnp.bfloat16
SPARE = 8

dot = functools.partial(jnp.dot, preferred_element_type=F32)


def split(x):
    high = x.astype(BF16)
    return high, (x - high.astype(F32)).astype(BF16)


def tables(half_freq):
    turn = np.arange(ANG)
    inverse, forward = [], []
    for group in range(2):
        sides = {}
        for which in range(2):
            freq = which * half_freq + np.arange(half_freq)
            angle = (turn[:, None] * freq[None, :] % ANG) * (2.0 * math.pi / ANG)
            scale = np.where(freq == 0, 1.0, 2.0) / ANG
            sides[which] = (
                np.concatenate([scale * np.cos(angle), -scale * np.sin(angle)], 1),
                np.concatenate([np.cos(angle), np.sin(angle)], 1).T,
            )
        inverse.append(np.concatenate([sides[group][0], sides[1 - group][0]], 1))
        forward.append(np.concatenate([sides[1 - group][1], sides[group][1]], 0))
    result = []
    for table in (inverse, forward):
        table = np.stack(table).astype(np.float32)
        high = table.astype(BF16)
        result += [high, (table - high.astype(np.float32)).astype(BF16)]
    return [jnp.asarray(x.reshape(-1, ANG)) for x in result]


def loop(count, body, unroll):
    while count % unroll:
        unroll -= 1
    if unroll == count:
        for i in range(count):
            body(i)
        return

    def step(outer, carry):
        for inner in range(unroll):
            body(outer * unroll + inner)
        return carry

    lax.fori_loop(0, count // unroll, step, 0)


def each(count, body, init):
    if count <= 8:
        for k in range(count):
            init = body(k, init)
        return init
    return lax.fori_loop(0, count, body, init)


def rows(base, count):
    return pl.ds(pl.multiple_of(base, 8), count)


def call(kernel, ins, outs, scratch=(), flops=0, far=(), room=4 << 20):
    total = 0
    buffers = [(x.shape, x.dtype) for i, x in enumerate(ins) if i not in far]
    for shape, dtype in buffers + list(outs) + [x for x in scratch if isinstance(x, tuple)]:
        dims = [1, 1, *shape]
        lines = -(-dims[-2] // 16) * 16
        lanes = -(-dims[-1] // 128) * 128
        total += math.prod(dims[:-2]) * lines * lanes * jnp.dtype(dtype).itemsize
    kinds = [pltpu.VMEM] * len(ins)
    for i in far:
        kinds[i] = pltpu.MemorySpace.HBM
    return pl.pallas_call(
        kernel,
        out_shape=[jax.ShapeDtypeStruct(*x) for x in outs],
        in_specs=[pl.BlockSpec(memory_space=kind) for kind in kinds],
        out_specs=[pl.BlockSpec(memory_space=pltpu.VMEM)] * len(outs),
        scratch_shapes=[pltpu.VMEM(*x) if isinstance(x, tuple) else x for x in scratch],
        compiler_params=pltpu.CompilerParams(vmem_limit_bytes=min(total + room, 56 << 20)),
        cost_estimate=pl.CostEstimate(flops=flops, bytes_accessed=total, transcendentals=0),
    )(*ins)


def prior_kernel(prior_ref, references_ref, prior_term, out):
    out[...] = references_ref[...]
    turns = lax.broadcasted_iota(jnp.int32, prior_term.shape, 0)
    lane = lax.broadcasted_iota(jnp.int32, (1, prior_term.shape[1]), 1)
    priors = prior_ref[...].reshape(1, -1)
    half = priors.shape[1] // 2
    first, second = [
        jnp.concatenate([priors[:, i * half : (i + 1) * half], lane[:, half:]], 1)
        for i in range(2)
    ]
    offset = jnp.abs(turns - jnp.where(lax.axis_index("rot") == 0, first, second))
    distance = jnp.minimum(offset, ANG - offset).astype(F32)
    prior_term[...] = -distance * distance / (2.0 * SIGMA * SIGMA)


def prep_kernel(share, particles_ref, other, own):
    freqs, depth = particles_ref.shape[1:]
    group = lax.axis_index("rot")
    to = lax.broadcasted_iota(jnp.int32, (256, 256), 0)
    at = lax.broadcasted_iota(jnp.int32, (256, 256), 1)
    permutation = ((to // 16 == at % 16) & (to % 16 == at // 16)).astype(F32).astype(BF16)
    for out, first in ((other, (1 - group) * share), (own, group * share)):
        for p in range(0, share, 16):
            for f in range(0, freqs, 32):
                blocks = [
                    jnp.concatenate(
                        [particles_ref[first + p + j, pl.ds(f + half, 16), :] for j in range(16)],
                        0,
                    )
                    for half in (0, 16)
                ]
                turned = dot(permutation, jnp.concatenate(blocks, 1)).astype(BF16)
                for half in range(2):
                    for j in range(16):
                        pair, part = divmod(f + 16 * half + j, 2)
                        out[pair, pl.ds(p, 16), pl.ds(part * depth, depth)] = turned[
                            16 * j : 16 * j + 16, half * depth : (half + 1) * depth
                        ]


def prep(particles, share):
    _, freqs, depth = particles.shape
    assert share % 16 == 0 and freqs % 32 == 0
    return call(
        functools.partial(prep_kernel, share),
        [particles],
        [((freqs // 2, share, 2 * depth), BF16)] * 2,
        flops=1 << 31,
    )


def tree(values):
    values = list(values)
    while len(values) > 1:
        values = [a + b for a, b in zip(values[::2], values[1::2])]
    return values[0]


def weigh_kernel(fresh, count, *refs):
    sources = refs[:count]
    doubled_ref, particles, out, energy_ref, left_ref, image = refs[count:]
    pairs, share, twice = particles.shape
    freqs, depth = 2 * pairs, twice // 2
    classes, lanes = energy_ref.shape
    pitch = freqs + SPARE
    radii = depth // 2
    lane = lax.broadcasted_iota(jnp.int32, (freqs, depth), 1)
    sign = jnp.where(lane < radii, -1.0, 1.0).astype(F32)
    doubled = jnp.concatenate([doubled_ref[...]] * 2, 1)
    row = lax.broadcasted_iota(jnp.int32, (freqs, depth), 0) + lax.axis_index("rot") * freqs
    scale = jnp.where(row == 0, 1.0 / ANG, 2.0 / ANG).astype(F32) * doubled

    for k in range(classes):
        if fresh:
            plain = sources[k][0].astype(F32)
        else:
            sums, highs, lows = [
                tree(
                    source[pl.ds(base + (k ^ i) * step, step), :].astype(F32)
                    for i, source in enumerate(sources)
                )
                for base, step in ((0, freqs), (classes * freqs, 1), (classes * (freqs + 1), 1))
            ]
            plain = (sums / (highs + lows + shrinkage)).astype(BF16).astype(F32)
        weighted = (plain * doubled).astype(BF16).astype(F32)
        image[rows(2 * k * pitch, freqs), :] = weighted
        image[rows((2 * k + 1) * pitch, freqs), :] = sign * pltpu.roll(weighted, radii, 1)
        energy = jnp.sum(plain * plain * scale, axis=0, keepdims=True)
        energy = jnp.broadcast_to(jnp.sum(energy, axis=1, keepdims=True), (SPARE, lanes))
        energy_ref[pl.ds(k, 1), :] = energy[:1]
        out[0, rows(2 * k * pitch + freqs, SPARE), :] = energy[:, : out.shape[2]]

    none = jnp.zeros((2 * classes, depth), BF16)

    def correlate(f):
        first, second = [
            image[pl.ds(2 * f + part, 2 * classes, stride=pitch), :].astype(BF16)
            for part in range(2)
        ]
        left = jnp.concatenate(
            [jnp.concatenate([first, none], 1), jnp.concatenate([none, second], 1)], 0
        )
        left_ref[f] = left
        place(out, f, times(left, particles[f]), classes, pitch)

    loop(pairs, correlate, 8)


def times(left, particles):
    return lax.dot_general(left, particles, (((1,), (1,)), ((), ())), preferred_element_type=F32)


def place(out, f, value, classes, pitch):
    tiles, _, width = out.shape
    spare = jnp.zeros((value.shape[0], tiles * width - value.shape[1]), F32)
    value = jnp.concatenate([value, spare], 1) if spare.size else value
    for part in range(2):
        at = pl.ds(2 * f + part, 2 * classes, stride=pitch)
        for tile in range(tiles):
            out[tile, at, :] = value[
                part * 2 * classes : (part + 1) * 2 * classes, tile * width : (tile + 1) * width
            ]


def lane_tiles(share):
    return -(-share // 128)


def weigh(sources, inverse_noise, particles, fresh):
    pairs, share, twice = particles.shape
    classes = len(sources)
    lines = 2 * classes * (2 * pairs + SPARE)
    tiles = lane_tiles(share)
    return call(
        functools.partial(weigh_kernel, fresh, classes),
        [*sources, inverse_noise, particles],
        [
            ((tiles, lines, 128), F32),
            ((classes, tiles * 128), F32),
            ((pairs, 4 * classes, twice), BF16),
        ],
        [((lines, twice // 2), F32)],
        flops=8 * classes * share * pairs * twice * 4,
    )


def correlate_kernel(left_ref, particles, out):
    pairs = left_ref.shape[0]
    classes = left_ref.shape[1] // 4

    def body(f):
        place(out, f, times(left_ref[f], particles[f]), classes, 2 * pairs + SPARE)

    loop(pairs, body, 8)


def correlate(left, particles):
    pairs, share, twice = particles.shape
    lines = left.shape[1] // 2 * (2 * pairs + SPARE)
    return call(
        correlate_kernel,
        [left, particles],
        [((lane_tiles(share), lines, 128), F32)],
        flops=2 * left.shape[1] * share * pairs * twice * 8,
    )[0]


def across(ref, at):
    return jnp.concatenate([ref[tile, at, :] for tile in range(ref.shape[0])], 1)


def table_rows(base, count):
    return pl.ds(pl.multiple_of(lax.axis_index("rot") * ANG + base, 128), count)


def score_kernel(own, other, energy_ref, prior_term, inv_hi, inv_lo, *refs):
    weights, peaks = refs
    classes, share = energy_ref.shape
    tiles, lines, width = own.shape
    pitch = lines // (2 * classes)
    freqs = pitch - SPARE
    which = table_rows(0, ANG)
    def score(k, peak):
        value = jnp.concatenate(
            [
                across(ref, rows((2 * k + part) * pitch, freqs))
                for ref in (own, other)
                for part in (0, 1)
            ],
            0,
        )
        high, low = split(value)
        inner = dot(inv_hi[which, :], high) + (
            dot(inv_hi[which, :], low) + dot(inv_lo[which, :], high)
        )
        far = other[0, rows(2 * k * pitch + freqs, SPARE), :][:1]
        energy = energy_ref[pl.ds(k, 1), :] + jnp.concatenate([far] * tiles, 1)
        scores = inner - 0.5 * energy + prior_term[...]
        weights[k] = scores
        return jnp.maximum(peak, jnp.max(scores, axis=0, keepdims=True))

    peak = each(classes, score, jnp.full((1, share), -jnp.inf, F32))

    def weight(k, total):
        value = jnp.exp(weights[k] - peak)
        weights[k] = value
        return total + jnp.sum(value, axis=0, keepdims=True)

    total = each(classes, weight, jnp.zeros((1, share), F32))
    line = lax.broadcasted_iota(jnp.int32, peaks.shape, 0)
    peaks[...] = jnp.where(line == 0, peak, total)


def scores(own, other, energy, prior_term, inv_hi, inv_lo):
    classes, share = energy.shape
    return call(
        score_kernel,
        [own, other, energy, prior_term, inv_hi, inv_lo],
        [((classes, ANG, share), F32), ((8, share), F32)],
        flops=6 * classes * share * ANG * ANG,
    )


def merge(first, second):
    top = jnp.maximum(first[0:1], second[0:1])
    total = first[1:2] * jnp.exp(first[0:1] - top) + second[1:2] * jnp.exp(second[0:1] - top)
    return top, total


def merge_kernel(first, second, out):
    top, total = merge(first[...], second[...])
    line = lax.broadcasted_iota(jnp.int32, out.shape, 0)
    out[...] = jnp.where(line == 0, top, total)


def turn_kernel(weights, here, first, second, fwd_hi, fwd_lo, *refs):
    rounded_ref, send, *evidence_ref, held = refs
    classes, _, lanes = weights.shape
    share = send.shape[2]
    pairs = send.shape[0] - 1
    top, total = merge(first[...], second[...])
    for ref in evidence_ref:
        ref[...] = (top + jnp.log(total))[:, :share]
    factor = jnp.exp(here[0:1, :] - top) / total
    lane = lax.broadcasted_iota(jnp.int32, (1, lanes), 1)
    factor = jnp.where(lane < share, factor, 0.0)
    which = table_rows(0, ANG // 2)
    line = lax.broadcasted_iota(jnp.int32, (4 * classes, share), 0)

    def body(k, column):
        value = weights[k] * factor
        count = jnp.sum(jnp.sum(value, axis=0, keepdims=True), axis=1, keepdims=True)
        rounded = value.astype(BF16)
        rounded_ref[k] = rounded
        spread(held, k, dot(fwd_hi[which, :], rounded) + dot(fwd_lo[which, :], rounded))
        high = count.astype(BF16).astype(F32)
        return jnp.where(line == k, high, jnp.where(line == classes + k, count - high, column))

    column = each(classes, body, jnp.zeros((4 * classes, share), F32))
    send[pairs] = column.astype(BF16)

    def rearrange(f):
        send[f] = pick(held, f, classes, share)

    loop(pairs, rearrange, 8)


def spread(held, k, value):
    tiles, lines, width = held.shape
    freqs = value.shape[0] // 2
    for part in range(2):
        for tile in range(tiles):
            held[tile, rows((2 * k + part) * (freqs + SPARE), freqs), :] = value[
                part * freqs : (part + 1) * freqs, tile * width : (tile + 1) * width
            ]


def pick(held, f, classes, share):
    pitch = held.shape[1] // (2 * classes)
    parts = [
        across(held, pl.ds(2 * f + part, 2 * classes, stride=pitch)).astype(BF16)
        for part in range(2)
    ]
    return jnp.concatenate(parts, 0)[:, :share]


def turn(weights, here, first, second, fwd_hi, fwd_lo, freqs, share, last):
    classes, _, lanes = weights.shape
    return call(
        turn_kernel,
        [weights, here, first, second, fwd_hi, fwd_lo],
        [
            ((classes, ANG, lanes), BF16),
            ((freqs // 2 + 1, 4 * classes, share), BF16),
            *([((1, share), F32)] if last else []),
        ],
        [((lanes // 128, 2 * classes * (freqs + SPARE), 128), F32)],
        flops=4 * classes * lanes * ANG * ANG,
    )


def gather_kernel(rounded_ref, fwd_hi, fwd_lo, particles, image, held):
    classes = rounded_ref.shape[0]
    pairs, share, _ = particles.shape
    which = table_rows(ANG // 2, ANG // 2)

    def body(k, carry):
        rounded = rounded_ref[k]
        spread(held, k, dot(fwd_hi[which, :], rounded) + dot(fwd_lo[which, :], rounded))
        return carry

    each(classes, body, 0)

    def accumulate(f):
        take_in(image, f, dot(pick(held, f, classes, share), particles[f]), classes)

    loop(pairs, accumulate, 8)


def gather(rounded, fwd_hi, fwd_lo, particles):
    pairs, share, twice = particles.shape
    classes, _, lanes = rounded.shape
    lines = 2 * classes * (2 * pairs + SPARE)
    return call(
        gather_kernel,
        [rounded, fwd_hi, fwd_lo, particles],
        [((lines, twice // 2), F32)],
        [((lanes // 128, lines, 128), F32)],
        flops=4 * classes * lanes * ANG * ANG,
    )[0]


def take_in(image, f, value, classes):
    lines, depth = image.shape
    for part in range(2):
        at = pl.ds(2 * f + part, 2 * classes, stride=lines // (2 * classes))
        image[at, :] = value[
            part * 2 * classes : (part + 1) * 2 * classes, part * depth : (part + 1) * depth
        ]


def finish_kernel(image, mine, spectrum, particles, *refs):
    outs, held = refs[:-1], refs[-1]
    pairs, _, twice = particles.shape
    classes = spectrum.shape[1] // 4
    freqs, depth = 2 * pairs, twice // 2
    radii = depth // 2
    pitch = freqs + SPARE

    def body(f):
        take_in(held, f, dot(spectrum[f], particles[f]), classes)

    loop(pairs, body, 8)
    counts = (mine[pairs].astype(F32) + spectrum[pairs].astype(F32))[:, :depth]
    counts = counts[:classes] + counts[classes : 2 * classes]
    lane = lax.broadcasted_iota(jnp.int32, (freqs, depth), 1)
    sign = jnp.where(lane < radii, -1.0, 1.0).astype(F32)
    for k in range(classes):
        plain, turned = [
            image[rows((2 * k + part) * pitch, freqs), :]
            + held[rows((2 * k + part) * pitch, freqs), :]
            for part in range(2)
        ]
        value = plain + sign * pltpu.roll(turned, radii, 1)
        if len(outs) == 1:
            outs[0][pl.ds(k * freqs, freqs), :] = value.astype(BF16)
        else:
            outs[k][pl.ds(0, freqs), :] = value
            outs[k][pl.ds(freqs, SPARE), :] = jnp.broadcast_to(counts[k : k + 1], (SPARE, depth))
    if len(outs) == 1:
        end = outs[0].shape[0] - classes * freqs
        high, low = split(counts)
        spare = [jnp.zeros((end - 2 * classes, depth), F32)] if end > 2 * classes else []
        tail = jnp.concatenate([high.astype(F32), low.astype(F32), *spare], 0)
        outs[0][pl.ds(classes * freqs, end), :] = tail.astype(BF16)


def finish(image, mine, spectrum, particles, last):
    pairs, _, twice = particles.shape
    classes = spectrum.shape[1] // 4
    freqs, depth = 2 * pairs, twice // 2
    if last:
        outs = [((freqs + SPARE, depth), F32)] * classes
    else:
        outs = [((classes * freqs + -(-2 * classes // 16) * 16, depth), BF16)]
    return call(
        finish_kernel,
        [image, mine, spectrum, particles],
        outs,
        [(image.shape, F32)],
        flops=2 * math.prod(spectrum.shape) * twice * 8,
    )


def means_kernel(*refs):
    *parts, evidence_ref, out, last_ref = refs
    last_ref[...] = evidence_ref[...]
    freqs = out.shape[1]
    total = tree(ref[...] for ref in parts)
    out[0] = total[:freqs, :] / (total[freqs : freqs + 1, :] + shrinkage)


def swap(value, axis, size, bit):
    if not bit:
        return value
    return lax.ppermute(value, axis, [(i, i ^ bit) for i in range(size)])


def bits(size):
    assert size > 1 and size & (size - 1) == 0
    return [1 << i for i in range(size.bit_length() - 1)]


def shards(particles, references, noise_inv, prior_rot):
    batch, freqs, depth = particles.shape
    sides = lax.axis_size("cls")
    groups = lax.axis_size("rot")
    blocks = lax.axis_size("blk")
    assert groups == 2 and 2 * groups * freqs == ANG
    share = batch // groups
    inv_hi, inv_lo, fwd_hi, fwd_lo = tables(freqs)
    inverse_noise = noise_inv.reshape(1, depth // 2)
    assert blocks & (blocks - 1) == 0

    prior_term, first = call(
        prior_kernel,
        [prior_rot, references],
        [((ANG, lane_tiles(share) * 128), F32), (references.shape, BF16)],
        flops=1 << 32,
    )
    sources = [swap(first, "blk", blocks, i) for i in reversed(range(blocks))][::-1]
    other_images, own_images = prep(particles, share)
    for step in range(ITERS):
        last = step == ITERS - 1
        message, energy, left = weigh(sources, inverse_noise, other_images, step == 0)
        message = swap(message, "rot", groups, 1)
        own = correlate(left, own_images)
        weights, here = scores(own, message, energy, prior_term, inv_hi, inv_lo)
        first = here
        for bit in bits(sides):
            second = swap(first, "cls", sides, bit)
            if 2 * bit < sides:
                (first,) = call(merge_kernel, [first, second], [(here.shape, F32)])
        rounded, send, *evidence = turn(
            weights, here, first, second, fwd_hi, fwd_lo, freqs, share, last
        )
        message = swap(send, "rot", groups, 1)
        image = gather(rounded, fwd_hi, fwd_lo, own_images)
        sums = finish(image, send, message, other_images, last)
        sums = sums if last else sums * blocks
        sources = [swap(sums[i], "blk", blocks, i) for i in reversed(range(blocks))][::-1]
    means, evidence = call(
        means_kernel, [*sources[::-1], *evidence], [((1, freqs, depth), F32), ((1, share), F32)]
    )
    return means, evidence.reshape(share)


def solution(mesh):
    in_specs = (
        P(("grp", "blk"), "rot", None),
        P(("grp", "blk", "cls"), "rot", None),
        P(),
        P(("grp", "blk")),
    )
    out_specs = (P(("grp", "blk", "cls"), "rot", None), P(("grp", "blk", "rot")))
    return jax.shard_map(shards, mesh=mesh, in_specs=in_specs, out_specs=out_specs, check_vma=False)
```

```python
import functools
import math

import jax
import jax.numpy as jnp
import numpy as np
from jax import lax
from jax.experimental import pallas as pl
from jax.experimental.pallas import tpu as pltpu
from jax.sharding import PartitionSpec as P

ANG = 256
ITERS = 2
SIGMA = 32

shrinkage = 1.0

F32 = jnp.float32
BF16 = jnp.bfloat16
SPARE = 8

dot = functools.partial(jnp.dot, preferred_element_type=F32)


def split(x):
    high = x.astype(BF16)
    return high, (x - high.astype(F32)).astype(BF16)


def tables(half_freq):
    turn = np.arange(ANG)
    inverse, forward = [], []
    for group in range(2):
        sides = {}
        for which in range(2):
            freq = which * half_freq + np.arange(half_freq)
            angle = (turn[:, None] * freq[None, :] % ANG) * (2.0 * math.pi / ANG)
            scale = np.where(freq == 0, 1.0, 2.0) / ANG
            sides[which] = (
                np.concatenate([scale * np.cos(angle), -scale * np.sin(angle)], 1),
                np.concatenate([np.cos(angle), np.sin(angle)], 1).T,
            )
        inverse.append(np.concatenate([sides[group][0], sides[1 - group][0]], 1))
        forward.append(np.concatenate([sides[1 - group][1], sides[group][1]], 0))
    result = []
    for table in (inverse, forward):
        table = np.stack(table).astype(np.float32)
        high = table.astype(BF16)
        result += [high, (table - high.astype(np.float32)).astype(BF16)]
    return [jnp.asarray(x.reshape(-1, ANG)) for x in result]


def loop(count, body, unroll):
    while count % unroll:
        unroll -= 1
    if unroll == count:
        for i in range(count):
            body(i)
        return

    def step(outer, carry):
        for inner in range(unroll):
            body(outer * unroll + inner)
        return carry

    lax.fori_loop(0, count // unroll, step, 0)


def each(count, body, init):
    if count <= 8:
        for k in range(count):
            init = body(k, init)
        return init
    return lax.fori_loop(0, count, body, init)


def rows(base, count):
    return pl.ds(pl.multiple_of(base, 8), count)


def call(kernel, ins, outs, scratch=(), flops=0, far=(), room=4 << 20):
    total = 0
    buffers = [(x.shape, x.dtype) for i, x in enumerate(ins) if i not in far]
    for shape, dtype in buffers + list(outs) + [x for x in scratch if isinstance(x, tuple)]:
        dims = [1, 1, *shape]
        lines = -(-dims[-2] // 16) * 16
        lanes = -(-dims[-1] // 128) * 128
        total += math.prod(dims[:-2]) * lines * lanes * jnp.dtype(dtype).itemsize
    kinds = [pltpu.VMEM] * len(ins)
    for i in far:
        kinds[i] = pltpu.MemorySpace.HBM
    return pl.pallas_call(
        kernel,
        out_shape=[jax.ShapeDtypeStruct(*x) for x in outs],
        in_specs=[pl.BlockSpec(memory_space=kind) for kind in kinds],
        out_specs=[pl.BlockSpec(memory_space=pltpu.VMEM)] * len(outs),
        scratch_shapes=[pltpu.VMEM(*x) if isinstance(x, tuple) else x for x in scratch],
        compiler_params=pltpu.CompilerParams(vmem_limit_bytes=min(total + room, 56 << 20)),
        cost_estimate=pl.CostEstimate(flops=flops, bytes_accessed=total, transcendentals=0),
    )(*ins)


def permutation_kernel(out):
    to = lax.broadcasted_iota(jnp.int32, out.shape, 0)
    at = lax.broadcasted_iota(jnp.int32, out.shape, 1)
    out[...] = ((to // 16 == at % 16) & (to % 16 == at // 16)).astype(F32).astype(BF16)


def prior_kernel(prior_ref, prior_term):
    turns = lax.broadcasted_iota(jnp.int32, prior_term.shape, 0)
    lane = lax.broadcasted_iota(jnp.int32, (1, prior_term.shape[1]), 1)
    priors = prior_ref[...].reshape(1, -1)
    half = priors.shape[1] // 2
    first, second = [
        jnp.concatenate([priors[:, i * half : (i + 1) * half], lane[:, half:]], 1)
        for i in range(2)
    ]
    offset = jnp.abs(turns - jnp.where(lax.axis_index("rot") == 0, first, second))
    distance = jnp.minimum(offset, ANG - offset).astype(F32)
    prior_term[...] = -distance * distance / (2.0 * SIGMA * SIGMA)


def prep_kernel(share, particles_ref, permutation_ref, other, own):
    freqs, depth = particles_ref.shape[1:]
    group = lax.axis_index("rot")
    permutation = permutation_ref[...]
    for out, first in ((other, (1 - group) * share), (own, group * share)):
        for p in range(0, share, 16):
            for f in range(0, freqs, 32):
                blocks = [
                    jnp.concatenate(
                        [particles_ref[first + p + j, pl.ds(f + half, 16), :] for j in range(16)],
                        0,
                    )
                    for half in (0, 16)
                ]
                turned = dot(permutation, jnp.concatenate(blocks, 1)).astype(BF16)
                for half in range(2):
                    for j in range(16):
                        pair, part = divmod(f + 16 * half + j, 2)
                        out[pair, pl.ds(p, 16), pl.ds(part * depth, depth)] = turned[
                            16 * j : 16 * j + 16, half * depth : (half + 1) * depth
                        ]


def prep(particles, permutation, share):
    _, freqs, depth = particles.shape
    assert share % 16 == 0 and freqs % 32 == 0
    return call(
        functools.partial(prep_kernel, share),
        [particles, permutation],
        [((freqs // 2, share, 2 * depth), BF16)] * 2,
        flops=1 << 31,
    )


def tree(values):
    values = list(values)
    while len(values) > 1:
        values = [a + b for a, b in zip(values[::2], values[1::2])]
    return values[0]


def weigh_kernel(fresh, count, *refs):
    sources = refs[:count]
    doubled_ref, particles, out, energy_ref, left_ref, image = refs[count:]
    pairs, share, twice = particles.shape
    freqs, depth = 2 * pairs, twice // 2
    classes, lanes = energy_ref.shape
    pitch = freqs + SPARE
    radii = depth // 2
    lane = lax.broadcasted_iota(jnp.int32, (freqs, depth), 1)
    sign = jnp.where(lane < radii, -1.0, 1.0).astype(F32)
    doubled = jnp.concatenate([doubled_ref[...]] * 2, 1)
    row = lax.broadcasted_iota(jnp.int32, (freqs, depth), 0) + lax.axis_index("rot") * freqs
    scale = jnp.where(row == 0, 1.0 / ANG, 2.0 / ANG).astype(F32) * doubled

    for k in range(classes):
        if fresh:
            plain = sources[k][0].astype(F32)
        else:
            sums, highs, lows = [
                tree(
                    source[pl.ds(base + (k ^ i) * step, step), :].astype(F32)
                    for i, source in enumerate(sources)
                )
                for base, step in ((0, freqs), (classes * freqs, 1), (classes * (freqs + 1), 1))
            ]
            plain = (sums / (highs + lows + shrinkage)).astype(BF16).astype(F32)
        weighted = (plain * doubled).astype(BF16).astype(F32)
        image[rows(2 * k * pitch, freqs), :] = weighted
        image[rows((2 * k + 1) * pitch, freqs), :] = sign * pltpu.roll(weighted, radii, 1)
        energy = jnp.sum(plain * plain * scale, axis=0, keepdims=True)
        energy = jnp.broadcast_to(jnp.sum(energy, axis=1, keepdims=True), (SPARE, lanes))
        energy_ref[pl.ds(k, 1), :] = energy[:1]
        out[0, rows(2 * k * pitch + freqs, SPARE), :] = energy[:, : out.shape[2]]

    none = jnp.zeros((2 * classes, depth), BF16)

    def correlate(f):
        first, second = [
            image[pl.ds(2 * f + part, 2 * classes, stride=pitch), :].astype(BF16)
            for part in range(2)
        ]
        left = jnp.concatenate(
            [jnp.concatenate([first, none], 1), jnp.concatenate([none, second], 1)], 0
        )
        left_ref[f] = left
        place(out, f, times(left, particles[f]), classes, pitch)

    loop(pairs, correlate, 8)


def times(left, particles):
    return lax.dot_general(left, particles, (((1,), (1,)), ((), ())), preferred_element_type=F32)


def place(out, f, value, classes, pitch):
    tiles, _, width = out.shape
    spare = jnp.zeros((value.shape[0], tiles * width - value.shape[1]), F32)
    value = jnp.concatenate([value, spare], 1) if spare.size else value
    for part in range(2):
        at = pl.ds(2 * f + part, 2 * classes, stride=pitch)
        for tile in range(tiles):
            out[tile, at, :] = value[
                part * 2 * classes : (part + 1) * 2 * classes, tile * width : (tile + 1) * width
            ]


def lane_tiles(share):
    return -(-share // 128)


def weigh(sources, inverse_noise, particles, fresh):
    pairs, share, twice = particles.shape
    classes = len(sources)
    lines = 2 * classes * (2 * pairs + SPARE)
    tiles = lane_tiles(share)
    return call(
        functools.partial(weigh_kernel, fresh, classes),
        [*sources, inverse_noise, particles],
        [
            ((tiles, lines, 128), F32),
            ((classes, tiles * 128), F32),
            ((pairs, 4 * classes, twice), BF16),
        ],
        [((lines, twice // 2), F32)],
        flops=8 * classes * share * pairs * twice * 4,
    )


def correlate_kernel(left_ref, particles, out):
    pairs = left_ref.shape[0]
    classes = left_ref.shape[1] // 4

    def body(f):
        place(out, f, times(left_ref[f], particles[f]), classes, 2 * pairs + SPARE)

    loop(pairs, body, 8)


def correlate(left, particles):
    pairs, share, twice = particles.shape
    lines = left.shape[1] // 2 * (2 * pairs + SPARE)
    return call(
        correlate_kernel,
        [left, particles],
        [((lane_tiles(share), lines, 128), F32)],
        flops=2 * left.shape[1] * share * pairs * twice * 8,
    )[0]


def across(ref, at):
    return jnp.concatenate([ref[tile, at, :] for tile in range(ref.shape[0])], 1)


def table_rows(base, count):
    return pl.ds(pl.multiple_of(lax.axis_index("rot") * ANG + base, 128), count)


def score_kernel(own, other, energy_ref, prior_term, inv_hi, inv_lo, *refs):
    weights, peaks = refs
    classes, share = energy_ref.shape
    tiles, lines, width = own.shape
    pitch = lines // (2 * classes)
    freqs = pitch - SPARE
    which = table_rows(0, ANG)
    def score(k, peak):
        value = jnp.concatenate(
            [
                across(ref, rows((2 * k + part) * pitch, freqs))
                for ref in (own, other)
                for part in (0, 1)
            ],
            0,
        )
        high, low = split(value)
        inner = dot(inv_hi[which, :], high) + (
            dot(inv_hi[which, :], low) + dot(inv_lo[which, :], high)
        )
        far = other[0, rows(2 * k * pitch + freqs, SPARE), :][:1]
        energy = energy_ref[pl.ds(k, 1), :] + jnp.concatenate([far] * tiles, 1)
        scores = inner - 0.5 * energy + prior_term[...]
        weights[k] = scores
        return jnp.maximum(peak, jnp.max(scores, axis=0, keepdims=True))

    peak = each(classes, score, jnp.full((1, share), -jnp.inf, F32))

    def weight(k, total):
        value = jnp.exp(weights[k] - peak)
        weights[k] = value
        return total + jnp.sum(value, axis=0, keepdims=True)

    total = each(classes, weight, jnp.zeros((1, share), F32))
    line = lax.broadcasted_iota(jnp.int32, peaks.shape, 0)
    peaks[...] = jnp.where(line == 0, peak, total)


def scores(own, other, energy, prior_term, inv_hi, inv_lo):
    classes, share = energy.shape
    return call(
        score_kernel,
        [own, other, energy, prior_term, inv_hi, inv_lo],
        [((classes, ANG, share), F32), ((8, share), F32)],
        flops=6 * classes * share * ANG * ANG,
    )


def merge(first, second):
    top = jnp.maximum(first[0:1], second[0:1])
    total = first[1:2] * jnp.exp(first[0:1] - top) + second[1:2] * jnp.exp(second[0:1] - top)
    return top, total


def merge_kernel(first, second, out):
    top, total = merge(first[...], second[...])
    line = lax.broadcasted_iota(jnp.int32, out.shape, 0)
    out[...] = jnp.where(line == 0, top, total)


def turn_kernel(weights, here, first, second, fwd_hi, fwd_lo, *refs):
    rounded_ref, send, *evidence_ref, held = refs
    classes, _, lanes = weights.shape
    share = send.shape[2]
    pairs = send.shape[0] - 1
    top, total = merge(first[...], second[...])
    for ref in evidence_ref:
        ref[...] = (top + jnp.log(total))[:, :share]
    factor = jnp.exp(here[0:1, :] - top) / total
    lane = lax.broadcasted_iota(jnp.int32, (1, lanes), 1)
    factor = jnp.where(lane < share, factor, 0.0)
    which = table_rows(0, ANG // 2)
    line = lax.broadcasted_iota(jnp.int32, (4 * classes, share), 0)

    def body(k, column):
        value = weights[k] * factor
        count = jnp.sum(jnp.sum(value, axis=0, keepdims=True), axis=1, keepdims=True)
        rounded = value.astype(BF16)
        rounded_ref[k] = rounded
        spread(held, k, dot(fwd_hi[which, :], rounded) + dot(fwd_lo[which, :], rounded))
        high = count.astype(BF16).astype(F32)
        return jnp.where(line == k, high, jnp.where(line == classes + k, count - high, column))

    column = each(classes, body, jnp.zeros((4 * classes, share), F32))
    send[pairs] = column.astype(BF16)

    def rearrange(f):
        send[f] = pick(held, f, classes, share)

    loop(pairs, rearrange, 8)


def spread(held, k, value):
    tiles, lines, width = held.shape
    freqs = value.shape[0] // 2
    for part in range(2):
        for tile in range(tiles):
            held[tile, rows((2 * k + part) * (freqs + SPARE), freqs), :] = value[
                part * freqs : (part + 1) * freqs, tile * width : (tile + 1) * width
            ]


def pick(held, f, classes, share):
    pitch = held.shape[1] // (2 * classes)
    parts = [
        across(held, pl.ds(2 * f + part, 2 * classes, stride=pitch)).astype(BF16)
        for part in range(2)
    ]
    return jnp.concatenate(parts, 0)[:, :share]


def turn(weights, here, first, second, fwd_hi, fwd_lo, freqs, share, last):
    classes, _, lanes = weights.shape
    return call(
        turn_kernel,
        [weights, here, first, second, fwd_hi, fwd_lo],
        [
            ((classes, ANG, lanes), BF16),
            ((freqs // 2 + 1, 4 * classes, share), BF16),
            *([((1, share), F32)] if last else []),
        ],
        [((lanes // 128, 2 * classes * (freqs + SPARE), 128), F32)],
        flops=4 * classes * lanes * ANG * ANG,
    )


def gather_kernel(rounded_ref, fwd_hi, fwd_lo, particles, image, held):
    classes = rounded_ref.shape[0]
    pairs, share, _ = particles.shape
    which = table_rows(ANG // 2, ANG // 2)

    def body(k, carry):
        rounded = rounded_ref[k]
        spread(held, k, dot(fwd_hi[which, :], rounded) + dot(fwd_lo[which, :], rounded))
        return carry

    each(classes, body, 0)

    def accumulate(f):
        take_in(image, f, dot(pick(held, f, classes, share), particles[f]), classes)

    loop(pairs, accumulate, 8)


def gather(rounded, fwd_hi, fwd_lo, particles):
    pairs, share, twice = particles.shape
    classes, _, lanes = rounded.shape
    lines = 2 * classes * (2 * pairs + SPARE)
    return call(
        gather_kernel,
        [rounded, fwd_hi, fwd_lo, particles],
        [((lines, twice // 2), F32)],
        [((lanes // 128, lines, 128), F32)],
        flops=4 * classes * lanes * ANG * ANG,
    )[0]


def take_in(image, f, value, classes):
    lines, depth = image.shape
    for part in range(2):
        at = pl.ds(2 * f + part, 2 * classes, stride=lines // (2 * classes))
        image[at, :] = value[
            part * 2 * classes : (part + 1) * 2 * classes, part * depth : (part + 1) * depth
        ]


def finish_kernel(image, mine, spectrum, particles, *refs):
    outs, held = refs[:-1], refs[-1]
    pairs, _, twice = particles.shape
    classes = spectrum.shape[1] // 4
    freqs, depth = 2 * pairs, twice // 2
    radii = depth // 2
    pitch = freqs + SPARE

    def body(f):
        take_in(held, f, dot(spectrum[f], particles[f]), classes)

    loop(pairs, body, 8)
    counts = (mine[pairs].astype(F32) + spectrum[pairs].astype(F32))[:, :depth]
    counts = counts[:classes] + counts[classes : 2 * classes]
    lane = lax.broadcasted_iota(jnp.int32, (freqs, depth), 1)
    sign = jnp.where(lane < radii, -1.0, 1.0).astype(F32)
    for k in range(classes):
        plain, turned = [
            image[rows((2 * k + part) * pitch, freqs), :]
            + held[rows((2 * k + part) * pitch, freqs), :]
            for part in range(2)
        ]
        value = plain + sign * pltpu.roll(turned, radii, 1)
        if len(outs) == 1:
            outs[0][pl.ds(k * freqs, freqs), :] = value.astype(BF16)
        else:
            outs[k][pl.ds(0, freqs), :] = value
            outs[k][pl.ds(freqs, SPARE), :] = jnp.broadcast_to(counts[k : k + 1], (SPARE, depth))
    if len(outs) == 1:
        end = outs[0].shape[0] - classes * freqs
        high, low = split(counts)
        spare = [jnp.zeros((end - 2 * classes, depth), F32)] if end > 2 * classes else []
        tail = jnp.concatenate([high.astype(F32), low.astype(F32), *spare], 0)
        outs[0][pl.ds(classes * freqs, end), :] = tail.astype(BF16)


def finish(image, mine, spectrum, particles, last):
    pairs, _, twice = particles.shape
    classes = spectrum.shape[1] // 4
    freqs, depth = 2 * pairs, twice // 2
    if last:
        outs = [((freqs + SPARE, depth), F32)] * classes
    else:
        outs = [((classes * freqs + -(-2 * classes // 16) * 16, depth), BF16)]
    return call(
        finish_kernel,
        [image, mine, spectrum, particles],
        outs,
        [(image.shape, F32)],
        flops=2 * math.prod(spectrum.shape) * twice * 8,
    )


def means_kernel(*refs):
    *parts, evidence_ref, out, last_ref = refs
    last_ref[...] = evidence_ref[...]
    freqs = out.shape[1]
    total = tree(ref[...] for ref in parts)
    out[0] = total[:freqs, :] / (total[freqs : freqs + 1, :] + shrinkage)


def swap(value, axis, size, bit):
    if not bit:
        return value
    return lax.ppermute(value, axis, [(i, i ^ bit) for i in range(size)])


def bits(size):
    assert size > 1 and size & (size - 1) == 0
    return [1 << i for i in range(size.bit_length() - 1)]


def shards(particles, references, noise_inv, prior_rot):
    batch, freqs, depth = particles.shape
    sides = lax.axis_size("cls")
    groups = lax.axis_size("rot")
    blocks = lax.axis_size("blk")
    assert groups == 2 and 2 * groups * freqs == ANG
    share = batch // groups
    inv_hi, inv_lo, fwd_hi, fwd_lo = tables(freqs)
    inverse_noise = noise_inv.reshape(1, depth // 2)
    assert blocks & (blocks - 1) == 0

    (permutation,) = call(permutation_kernel, [], [((256, 256), BF16)], flops=1 << 32)
    first, permutation = lax.optimization_barrier((references, permutation))
    (prior_term,) = call(
        prior_kernel, [prior_rot], [((ANG, lane_tiles(share) * 128), F32)], flops=1 << 26
    )
    sources = [swap(first, "blk", blocks, i) for i in reversed(range(blocks))][::-1]
    other_images, own_images = prep(particles, permutation, share)
    for step in range(ITERS):
        last = step == ITERS - 1
        message, energy, left = weigh(sources, inverse_noise, other_images, step == 0)
        message = swap(message, "rot", groups, 1)
        own = correlate(left, own_images)
        weights, here = scores(own, message, energy, prior_term, inv_hi, inv_lo)
        first = here
        for bit in bits(sides):
            second = swap(first, "cls", sides, bit)
            if 2 * bit < sides:
                (first,) = call(merge_kernel, [first, second], [(here.shape, F32)])
        rounded, send, *evidence = turn(
            weights, here, first, second, fwd_hi, fwd_lo, freqs, share, last
        )
        message = swap(send, "rot", groups, 1)
        image = gather(rounded, fwd_hi, fwd_lo, own_images)
        sums = finish(image, send, message, other_images, last)
        sums = sums if last else sums * blocks
        sources = [swap(sums[i], "blk", blocks, i) for i in reversed(range(blocks))][::-1]
    means, evidence = call(
        means_kernel, [*sources[::-1], *evidence], [((1, freqs, depth), F32), ((1, share), F32)]
    )
    return means, evidence.reshape(share)


def solution(mesh):
    in_specs = (
        P(("grp", "blk"), "rot", None),
        P(("grp", "blk", "cls"), "rot", None),
        P(),
        P(("grp", "blk")),
    )
    out_specs = (P(("grp", "blk", "cls"), "rot", None), P(("grp", "blk", "rot")))
    return jax.shard_map(shards, mesh=mesh, in_specs=in_specs, out_specs=out_specs, check_vma=False)
```

```python
import functools
import math

import jax
import jax.numpy as jnp
import numpy as np
from jax import lax
from jax.experimental import pallas as pl
from jax.experimental.pallas import tpu as pltpu
from jax.sharding import PartitionSpec as P

ANG = 256
ITERS = 2
SIGMA = 32

shrinkage = 1.0

F32 = jnp.float32
BF16 = jnp.bfloat16
SPARE = 8

dot = functools.partial(jnp.dot, preferred_element_type=F32)


def split(x):
    high = x.astype(BF16)
    return high, (x - high.astype(F32)).astype(BF16)


def tables(half_freq):
    turn = np.arange(ANG)
    inverse, forward = [], []
    for group in range(2):
        sides = {}
        for which in range(2):
            freq = which * half_freq + np.arange(half_freq)
            angle = (turn[:, None] * freq[None, :] % ANG) * (2.0 * math.pi / ANG)
            scale = np.where(freq == 0, 1.0, 2.0) / ANG
            sides[which] = (
                np.concatenate([scale * np.cos(angle), -scale * np.sin(angle)], 1),
                np.concatenate([np.cos(angle), np.sin(angle)], 1).T,
            )
        inverse.append(np.concatenate([sides[group][0], sides[1 - group][0]], 1))
        forward.append(np.concatenate([sides[1 - group][1], sides[group][1]], 0))
    result = []
    for table in (inverse, forward):
        table = np.stack(table).astype(np.float32)
        high = table.astype(BF16)
        result += [high, (table - high.astype(np.float32)).astype(BF16)]
    return [jnp.asarray(x.reshape(-1, ANG)) for x in result]


def loop(count, body, unroll):
    while count % unroll:
        unroll -= 1
    if unroll == count:
        for i in range(count):
            body(i)
        return

    def step(outer, carry):
        for inner in range(unroll):
            body(outer * unroll + inner)
        return carry

    lax.fori_loop(0, count // unroll, step, 0)


def each(count, body, init):
    if count <= 8:
        for k in range(count):
            init = body(k, init)
        return init
    return lax.fori_loop(0, count, body, init)


def rows(base, count):
    return pl.ds(pl.multiple_of(base, 8), count)


def call(kernel, ins, outs, scratch=(), flops=0, far=(), room=4 << 20):
    total = 0
    buffers = [(x.shape, x.dtype) for i, x in enumerate(ins) if i not in far]
    for shape, dtype in buffers + list(outs) + [x for x in scratch if isinstance(x, tuple)]:
        dims = [1, 1, *shape]
        lines = -(-dims[-2] // 16) * 16
        lanes = -(-dims[-1] // 128) * 128
        total += math.prod(dims[:-2]) * lines * lanes * jnp.dtype(dtype).itemsize
    kinds = [pltpu.VMEM] * len(ins)
    for i in far:
        kinds[i] = pltpu.MemorySpace.HBM
    return pl.pallas_call(
        kernel,
        out_shape=[jax.ShapeDtypeStruct(*x) for x in outs],
        in_specs=[pl.BlockSpec(memory_space=kind) for kind in kinds],
        out_specs=[pl.BlockSpec(memory_space=pltpu.VMEM)] * len(outs),
        scratch_shapes=[pltpu.VMEM(*x) if isinstance(x, tuple) else x for x in scratch],
        compiler_params=pltpu.CompilerParams(vmem_limit_bytes=min(total + room, 56 << 20)),
        cost_estimate=pl.CostEstimate(flops=flops, bytes_accessed=total, transcendentals=0),
    )(*ins)


def permutation_kernel(out):
    to = lax.broadcasted_iota(jnp.int32, out.shape, 0)
    at = lax.broadcasted_iota(jnp.int32, out.shape, 1)
    out[...] = ((to // 16 == at % 16) & (to % 16 == at // 16)).astype(F32).astype(BF16)


def prior_kernel(prior_ref, prior_term):
    turns = lax.broadcasted_iota(jnp.int32, prior_term.shape, 0)
    lane = lax.broadcasted_iota(jnp.int32, (1, prior_term.shape[1]), 1)
    priors = prior_ref[...].reshape(1, -1)
    half = priors.shape[1] // 2
    first, second = [
        jnp.concatenate([priors[:, i * half : (i + 1) * half], lane[:, half:]], 1)
        for i in range(2)
    ]
    offset = jnp.abs(turns - jnp.where(lax.axis_index("rot") == 0, first, second))
    distance = jnp.minimum(offset, ANG - offset).astype(F32)
    prior_term[...] = -distance * distance / (2.0 * SIGMA * SIGMA)


def prep_kernel(share, particles_ref, permutation_ref, other, own):
    freqs, depth = particles_ref.shape[1:]
    group = lax.axis_index("rot")
    permutation = permutation_ref[...]
    for out, first in ((other, (1 - group) * share), (own, group * share)):
        for p in range(0, share, 16):
            for f in range(0, freqs, 32):
                blocks = [
                    jnp.concatenate(
                        [particles_ref[first + p + j, pl.ds(f + half, 16), :] for j in range(16)],
                        0,
                    )
                    for half in (0, 16)
                ]
                turned = dot(permutation, jnp.concatenate(blocks, 1)).astype(BF16)
                for half in range(2):
                    for j in range(16):
                        pair, part = divmod(f + 16 * half + j, 2)
                        out[pair, pl.ds(p, 16), pl.ds(part * depth, depth)] = turned[
                            16 * j : 16 * j + 16, half * depth : (half + 1) * depth
                        ]


def prep(particles, permutation, share):
    _, freqs, depth = particles.shape
    assert share % 16 == 0 and freqs % 32 == 0
    return call(
        functools.partial(prep_kernel, share),
        [particles, permutation],
        [((freqs // 2, share, 2 * depth), BF16)] * 2,
        flops=1 << 31,
    )


def tree(values):
    values = list(values)
    while len(values) > 1:
        values = [a + b for a, b in zip(values[::2], values[1::2])]
    return values[0]


def weigh_kernel(fresh, count, *refs):
    sources = refs[:count]
    doubled_ref, particles, out, energy_ref, left_ref, image, *rest = refs[count:]
    pairs, share, twice = particles.shape
    freqs, depth = 2 * pairs, twice // 2
    classes, lanes = energy_ref.shape
    pitch = freqs + SPARE
    radii = depth // 2
    lane = lax.broadcasted_iota(jnp.int32, (freqs, depth), 1)
    sign = jnp.where(lane < radii, -1.0, 1.0).astype(F32)
    doubled = jnp.concatenate([doubled_ref[...]] * 2, 1)
    row = lax.broadcasted_iota(jnp.int32, (freqs, depth), 0) + lax.axis_index("rot") * freqs
    scale = jnp.where(row == 0, 1.0 / ANG, 2.0 / ANG).astype(F32) * doubled

    for k in range(classes):
        if fresh:
            plain = sources[k][0].astype(F32)
        else:
            sums, highs, lows = [
                tree(
                    source[pl.ds(base + (k ^ i) * step, step), :].astype(F32)
                    for i, source in enumerate(sources)
                )
                for base, step in ((0, freqs), (classes * freqs, 1), (classes * (freqs + 1), 1))
            ]
            plain = (sums / (highs + lows + shrinkage)).astype(BF16).astype(F32)
        weighted = (plain * doubled).astype(BF16).astype(F32)
        image[rows(2 * k * pitch, freqs), :] = weighted
        image[rows((2 * k + 1) * pitch, freqs), :] = sign * pltpu.roll(weighted, radii, 1)
        energy = jnp.sum(plain * plain * scale, axis=0, keepdims=True)
        energy = jnp.broadcast_to(jnp.sum(energy, axis=1, keepdims=True), (SPARE, lanes))
        energy_ref[pl.ds(k, 1), :] = energy[:1]
        out[rows(2 * k * pitch + freqs, SPARE), :] = energy[:, : out.shape[1]]

    none = jnp.zeros((2 * classes, depth), BF16)

    def correlate(f):
        first, second = [
            image[pl.ds(2 * f + part, 2 * classes, stride=pitch), :].astype(BF16)
            for part in range(2)
        ]
        left = jnp.concatenate(
            [jnp.concatenate([first, none], 1), jnp.concatenate([none, second], 1)], 0
        )
        left_ref[f] = left
        place([out, *rest], f, times(left, particles[f]), classes, pitch)

    loop(pairs, correlate, 8)
    for ref in rest:
        width = share - 128
        for pack in range(-(-2 * classes * width // 128)):
            total = 0.0
            for i in range(min(128 // width, 2 * classes - pack * (128 // width))):
                group = ref[rows((pack * (128 // width) + i) * pitch, pitch), :]
                total = total + (pltpu.roll(group, i * width, 1) if i else group)
            out[rows((2 * classes + pack) * pitch, pitch), :] = total


def times(left, particles):
    return lax.dot_general(left, particles, (((1,), (1,)), ((), ())), preferred_element_type=F32)


def place(outs, f, value, classes, pitch):
    spare = jnp.zeros((value.shape[0], len(outs) * 128 - value.shape[1]), F32)
    value = jnp.concatenate([value, spare], 1) if spare.size else value
    for part in range(2):
        at = pl.ds(2 * f + part, 2 * classes, stride=pitch)
        for tile, out in enumerate(outs):
            out[at, :] = value[
                part * 2 * classes : (part + 1) * 2 * classes, tile * 128 : (tile + 1) * 128
            ]


def lane_tiles(share):
    return -(-share // 128)


def weigh(sources, inverse_noise, particles, fresh):
    pairs, share, twice = particles.shape
    classes = len(sources)
    pitch = 2 * pairs + SPARE
    tiles = lane_tiles(share)
    assert tiles == 1 or tiles == 2 and 128 % (share - 128) == 0
    packs = -(-2 * classes * (share - 128) // 128) if tiles == 2 else 0
    return call(
        functools.partial(weigh_kernel, fresh, classes),
        [*sources, inverse_noise, particles],
        [
            (((2 * classes + packs) * pitch, 128), F32),
            ((classes, tiles * 128), F32),
            ((pairs, 4 * classes, twice), BF16),
        ],
        [((2 * classes * pitch, twice // 2), F32)]
        + [((2 * classes * pitch, 128), F32)] * (tiles - 1),
        flops=8 * classes * share * pairs * twice * 4,
    )


def correlate_kernel(left_ref, particles, out):
    pairs = left_ref.shape[0]
    classes = left_ref.shape[1] // 4

    def body(f):
        outs = [out.at[tile] for tile in range(out.shape[0])]
        place(outs, f, times(left_ref[f], particles[f]), classes, 2 * pairs + SPARE)

    loop(pairs, body, 8)


def correlate(left, particles):
    pairs, share, twice = particles.shape
    lines = left.shape[1] // 2 * (2 * pairs + SPARE)
    return call(
        correlate_kernel,
        [left, particles],
        [((lane_tiles(share), lines, 128), F32)],
        flops=2 * left.shape[1] * share * pairs * twice * 8,
    )[0]


def across(ref, at):
    return jnp.concatenate([ref[tile, at, :] for tile in range(ref.shape[0])], 1)


def table_rows(base, count):
    return pl.ds(pl.multiple_of(lax.axis_index("rot") * ANG + base, 128), count)


def score_kernel(particles, own, other, energy_ref, prior_term, inv_hi, inv_lo, *refs):
    weights, peaks = refs
    classes, share = energy_ref.shape
    tiles, lines, width = own.shape
    pitch = lines // (2 * classes)
    freqs = pitch - SPARE
    which = table_rows(0, ANG)
    def unpacked(group):
        first = other[rows(group * pitch, freqs), :]
        if tiles == 1:
            return first
        width = particles - 128
        bundle = 128 // width
        packed = other[rows((2 * classes + group // bundle) * pitch, freqs), :]
        back = (bundle - group % bundle) % bundle * width
        return jnp.concatenate([first, pltpu.roll(packed, back, 1)], 1)

    def score(k, peak):
        near = [across(own, rows((2 * k + part) * pitch, freqs)) for part in range(2)]
        far = [unpacked(2 * k + part) for part in range(2)]
        value = jnp.concatenate(near + far, 0)
        high, low = split(value)
        inner = dot(inv_hi[which, :], high) + (
            dot(inv_hi[which, :], low) + dot(inv_lo[which, :], high)
        )
        far = other[rows(2 * k * pitch + freqs, SPARE), :][:1]
        energy = energy_ref[pl.ds(k, 1), :] + jnp.concatenate([far] * tiles, 1)
        scores = inner - 0.5 * energy + prior_term[...]
        weights[k] = scores
        return jnp.maximum(peak, jnp.max(scores, axis=0, keepdims=True))

    peak = each(classes, score, jnp.full((1, share), -jnp.inf, F32))

    def weight(k, total):
        value = jnp.exp(weights[k] - peak)
        weights[k] = value
        return total + jnp.sum(value, axis=0, keepdims=True)

    total = each(classes, weight, jnp.zeros((1, share), F32))
    line = lax.broadcasted_iota(jnp.int32, peaks.shape, 0)
    peaks[...] = jnp.where(line == 0, peak, total)


def scores(own, other, energy, prior_term, inv_hi, inv_lo, particles):
    classes, share = energy.shape
    return call(
        functools.partial(score_kernel, particles),
        [own, other, energy, prior_term, inv_hi, inv_lo],
        [((classes, ANG, share), F32), ((8, share), F32)],
        flops=6 * classes * share * ANG * ANG,
    )


def merge(first, second):
    top = jnp.maximum(first[0:1], second[0:1])
    total = first[1:2] * jnp.exp(first[0:1] - top) + second[1:2] * jnp.exp(second[0:1] - top)
    return top, total


def merge_kernel(first, second, out):
    top, total = merge(first[...], second[...])
    line = lax.broadcasted_iota(jnp.int32, out.shape, 0)
    out[...] = jnp.where(line == 0, top, total)


def turn_kernel(share, weights, here, first, second, fwd_hi, fwd_lo, *refs):
    rounded_ref, send, *evidence_ref, held = refs
    classes, _, lanes = weights.shape
    pairs = (held.shape[1] // (2 * classes) - SPARE) // 2
    top, total = merge(first[...], second[...])
    for ref in evidence_ref:
        ref[...] = (top + jnp.log(total))[:, :share]
    factor = jnp.exp(here[0:1, :] - top) / total
    lane = lax.broadcasted_iota(jnp.int32, (1, lanes), 1)
    factor = jnp.where(lane < share, factor, 0.0)
    which = table_rows(0, ANG // 2)
    line = lax.broadcasted_iota(jnp.int32, (4 * classes, 128), 0)

    def body(k, column):
        value = weights[k] * factor
        count = jnp.sum(jnp.sum(value, axis=0, keepdims=True), axis=1, keepdims=True)
        rounded = value.astype(BF16)
        rounded_ref[k] = rounded
        spread(held, k, dot(fwd_hi[which, :], rounded) + dot(fwd_lo[which, :], rounded))
        high = count.astype(BF16).astype(F32)
        return jnp.where(line == k, high, jnp.where(line == classes + k, count - high, column))

    column = each(classes, body, jnp.zeros((4 * classes, 128), F32))
    send[send.shape[0] - 1] = column.astype(BF16)
    bundle, width = bundles(pairs, share)

    def rearrange(j):
        packed = 0.0
        for i in range(bundle):
            value = pick(held, j * bundle + i, classes)
            send[j * bundle + i] = value[:, :128].astype(BF16)
            if width:
                packed = packed + (pltpu.roll(value[:, 128:], i * width, 1) if i else value[:, 128:])
        if width:
            send[pairs + j] = packed.astype(BF16)

    loop(pairs // bundle, rearrange, 1)


def bundles(pairs, share):
    if lane_tiles(share) == 1:
        return min(8, pairs), 0
    return min(128 // (share - 128), pairs), share - 128


def spread(held, k, value):
    tiles, lines, width = held.shape
    freqs = value.shape[0] // 2
    for part in range(2):
        for tile in range(tiles):
            held[tile, rows((2 * k + part) * (freqs + SPARE), freqs), :] = value[
                part * freqs : (part + 1) * freqs, tile * width : (tile + 1) * width
            ]


def pick(held, f, classes):
    pitch = held.shape[1] // (2 * classes)
    parts = [
        across(held, pl.ds(2 * f + part, 2 * classes, stride=pitch)) for part in range(2)
    ]
    return jnp.concatenate(parts, 0)


def turn(weights, here, first, second, fwd_hi, fwd_lo, freqs, share, last):
    classes, _, lanes = weights.shape
    bundle, width = bundles(freqs // 2, share)
    entries = freqs // 2 + (freqs // 2 // bundle if width else 0) + 1
    return call(
        functools.partial(turn_kernel, share),
        [weights, here, first, second, fwd_hi, fwd_lo],
        [
            ((classes, ANG, lanes), BF16),
            ((entries, 4 * classes, 128), BF16),
            *([((1, share), F32)] if last else []),
        ],
        [((lanes // 128, 2 * classes * (freqs + SPARE), 128), F32)],
        flops=4 * classes * lanes * ANG * ANG,
    )


def gather_kernel(rounded_ref, fwd_hi, fwd_lo, particles, image, held):
    classes = rounded_ref.shape[0]
    pairs, share, _ = particles.shape
    which = table_rows(ANG // 2, ANG // 2)

    def body(k, carry):
        rounded = rounded_ref[k]
        spread(held, k, dot(fwd_hi[which, :], rounded) + dot(fwd_lo[which, :], rounded))
        return carry

    each(classes, body, 0)

    def accumulate(f):
        left = pick(held, f, classes).astype(BF16)[:, :share]
        take_in(image, f, dot(left, particles[f]), classes)

    loop(pairs, accumulate, 8)


def gather(rounded, fwd_hi, fwd_lo, particles):
    pairs, share, twice = particles.shape
    classes, _, lanes = rounded.shape
    lines = 2 * classes * (2 * pairs + SPARE)
    return call(
        gather_kernel,
        [rounded, fwd_hi, fwd_lo, particles],
        [((lines, twice // 2), F32)],
        [((lanes // 128, lines, 128), F32)],
        flops=4 * classes * lanes * ANG * ANG,
    )[0]


def take_in(image, f, value, classes):
    lines, depth = image.shape
    for part in range(2):
        at = pl.ds(2 * f + part, 2 * classes, stride=lines // (2 * classes))
        image[at, :] = value[
            part * 2 * classes : (part + 1) * 2 * classes, part * depth : (part + 1) * depth
        ]


def finish_kernel(image, mine, spectrum, particles, *refs):
    outs, held = refs[:-1], refs[-1]
    pairs, share, twice = particles.shape
    classes = spectrum.shape[1] // 4
    freqs, depth = 2 * pairs, twice // 2
    radii = depth // 2
    pitch = freqs + SPARE
    bundle, width = bundles(pairs, share)

    def body(j):
        packed = spectrum[pairs + j].astype(F32) if width else None
        for i in range(bundle):
            f = j * bundle + i
            left = spectrum[f]
            if width:
                rest = pltpu.roll(packed, 128 - i * width, 1) if i else packed
                left = jnp.concatenate([left, rest.astype(BF16)], 1)
            take_in(held, f, dot(left[:, :share], particles[f]), classes)

    loop(pairs // bundle, body, 1)
    end = spectrum.shape[0] - 1
    counts = mine[end].astype(F32) + spectrum[end].astype(F32)
    counts = counts[:classes] + counts[classes : 2 * classes]
    lane = lax.broadcasted_iota(jnp.int32, (freqs, depth), 1)
    sign = jnp.where(lane < radii, -1.0, 1.0).astype(F32)
    for k in range(classes):
        plain, turned = [
            image[rows((2 * k + part) * pitch, freqs), :]
            + held[rows((2 * k + part) * pitch, freqs), :]
            for part in range(2)
        ]
        value = plain + sign * pltpu.roll(turned, radii, 1)
        if len(outs) == 1:
            outs[0][pl.ds(k * freqs, freqs), :] = value.astype(BF16)
        else:
            outs[k][pl.ds(0, freqs), :] = value
            outs[k][pl.ds(freqs, SPARE), :] = jnp.broadcast_to(counts[k : k + 1], (SPARE, depth))
    if len(outs) == 1:
        end = outs[0].shape[0] - classes * freqs
        high, low = split(counts)
        spare = [jnp.zeros((end - 2 * classes, depth), F32)] if end > 2 * classes else []
        tail = jnp.concatenate([high.astype(F32), low.astype(F32), *spare], 0)
        outs[0][pl.ds(classes * freqs, end), :] = tail.astype(BF16)


def finish(image, mine, spectrum, particles, last):
    pairs, _, twice = particles.shape
    classes = spectrum.shape[1] // 4
    freqs, depth = 2 * pairs, twice // 2
    if last:
        outs = [((freqs + SPARE, depth), F32)] * classes
    else:
        outs = [((classes * freqs + -(-2 * classes // 16) * 16, depth), BF16)]
    return call(
        finish_kernel,
        [image, mine, spectrum, particles],
        outs,
        [(image.shape, F32)],
        flops=2 * math.prod(spectrum.shape) * twice * 8,
    )


def means_kernel(*refs):
    *parts, evidence_ref, out, last_ref = refs
    last_ref[...] = evidence_ref[...]
    freqs = out.shape[1]
    total = tree(ref[...] for ref in parts)
    out[0] = total[:freqs, :] / (total[freqs : freqs + 1, :] + shrinkage)


def swap(value, axis, size, bit):
    if not bit:
        return value
    return lax.ppermute(value, axis, [(i, i ^ bit) for i in range(size)])


def bits(size):
    assert size > 1 and size & (size - 1) == 0
    return [1 << i for i in range(size.bit_length() - 1)]


def shards(particles, references, noise_inv, prior_rot):
    batch, freqs, depth = particles.shape
    sides = lax.axis_size("cls")
    groups = lax.axis_size("rot")
    blocks = lax.axis_size("blk")
    assert groups == 2 and 2 * groups * freqs == ANG
    share = batch // groups
    inv_hi, inv_lo, fwd_hi, fwd_lo = tables(freqs)
    inverse_noise = noise_inv.reshape(1, depth // 2)
    assert blocks & (blocks - 1) == 0

    (permutation,) = call(permutation_kernel, [], [((256, 256), BF16)], flops=1 << 32)
    first, permutation = lax.optimization_barrier((references, permutation))
    (prior_term,) = call(
        prior_kernel, [prior_rot], [((ANG, lane_tiles(share) * 128), F32)], flops=1 << 26
    )
    sources = [
        swap(first if i else references, "blk", blocks, i ^ (blocks - 1)) for i in range(blocks)
    ][::-1]
    other_images, own_images = prep(particles, permutation, share)
    for step in range(ITERS):
        last = step == ITERS - 1
        message, energy, left = weigh(sources, inverse_noise, other_images, step == 0)
        message = swap(message, "rot", groups, 1)
        own = correlate(left, own_images)
        weights, here = scores(own, message, energy, prior_term, inv_hi, inv_lo, share)
        first = here
        for bit in bits(sides):
            second = swap(first, "cls", sides, bit)
            if 2 * bit < sides:
                (first,) = call(merge_kernel, [first, second], [(here.shape, F32)])
        rounded, send, *evidence = turn(
            weights, here, first, second, fwd_hi, fwd_lo, freqs, share, last
        )
        message = swap(send, "rot", groups, 1)
        image = gather(rounded, fwd_hi, fwd_lo, own_images)
        sums = finish(image, send, message, other_images, last)
        sums = sums if last else sums * blocks
        sources = [swap(sums[i], "blk", blocks, i) for i in reversed(range(blocks))][::-1]
    means, evidence = call(
        means_kernel, [*sources[::-1], *evidence], [((1, freqs, depth), F32), ((1, share), F32)]
    )
    return means, evidence.reshape(share)


def solution(mesh):
    in_specs = (
        P(("grp", "blk"), "rot", None),
        P(("grp", "blk", "cls"), "rot", None),
        P(),
        P(("grp", "blk")),
    )
    out_specs = (P(("grp", "blk", "cls"), "rot", None), P(("grp", "blk", "rot")))
    return jax.shard_map(shards, mesh=mesh, in_specs=in_specs, out_specs=out_specs, check_vma=False)
```

```python
import functools
import math

import jax
import jax.numpy as jnp
import numpy as np
from jax import lax
from jax.experimental import pallas as pl
from jax.experimental.pallas import tpu as pltpu
from jax.sharding import PartitionSpec as P

ANG = 256
ITERS = 2
SIGMA = 32

shrinkage = 1.0

F32 = jnp.float32
BF16 = jnp.bfloat16
SPARE = 8

dot = functools.partial(jnp.dot, preferred_element_type=F32)


def split(x):
    high = x.astype(BF16)
    return high, (x - high.astype(F32)).astype(BF16)


def tables(half_freq):
    turn = np.arange(ANG)
    inverse, forward = [], []
    for group in range(2):
        sides = {}
        for which in range(2):
            freq = which * half_freq + np.arange(half_freq)
            angle = (turn[:, None] * freq[None, :] % ANG) * (2.0 * math.pi / ANG)
            scale = np.where(freq == 0, 1.0, 2.0) / ANG
            sides[which] = (
                np.concatenate([scale * np.cos(angle), -scale * np.sin(angle)], 1),
                np.concatenate([np.cos(angle), np.sin(angle)], 1).T,
            )
        inverse.append(np.concatenate([sides[group][0], sides[1 - group][0]], 1))
        forward.append(np.concatenate([sides[1 - group][1], sides[group][1]], 0))
    result = []
    for table in (inverse, forward):
        table = np.stack(table).astype(np.float32)
        high = table.astype(BF16)
        result += [high, (table - high.astype(np.float32)).astype(BF16)]
    return [jnp.asarray(x.reshape(-1, ANG)) for x in result]


def loop(count, body, unroll):
    while count % unroll:
        unroll -= 1
    if unroll == count:
        for i in range(count):
            body(i)
        return

    def step(outer, carry):
        for inner in range(unroll):
            body(outer * unroll + inner)
        return carry

    lax.fori_loop(0, count // unroll, step, 0)


def each(count, body, init):
    if count <= 8:
        for k in range(count):
            init = body(k, init)
        return init
    return lax.fori_loop(0, count, body, init)


def rows(base, count):
    return pl.ds(pl.multiple_of(base, 8), count)


def call(kernel, ins, outs, scratch=(), flops=0, far=(), room=4 << 20):
    total = 0
    buffers = [(x.shape, x.dtype) for i, x in enumerate(ins) if i not in far]
    for shape, dtype in buffers + list(outs) + [x for x in scratch if isinstance(x, tuple)]:
        dims = [1, 1, *shape]
        lines = -(-dims[-2] // 16) * 16
        lanes = -(-dims[-1] // 128) * 128
        total += math.prod(dims[:-2]) * lines * lanes * jnp.dtype(dtype).itemsize
    kinds = [pltpu.VMEM] * len(ins)
    for i in far:
        kinds[i] = pltpu.MemorySpace.HBM
    return pl.pallas_call(
        kernel,
        out_shape=[jax.ShapeDtypeStruct(*x) for x in outs],
        in_specs=[pl.BlockSpec(memory_space=kind) for kind in kinds],
        out_specs=[pl.BlockSpec(memory_space=pltpu.VMEM)] * len(outs),
        scratch_shapes=[pltpu.VMEM(*x) if isinstance(x, tuple) else x for x in scratch],
        compiler_params=pltpu.CompilerParams(vmem_limit_bytes=min(total + room, 56 << 20)),
        cost_estimate=pl.CostEstimate(flops=flops, bytes_accessed=total, transcendentals=0),
    )(*ins)


def permutation_kernel(out):
    to = lax.broadcasted_iota(jnp.int32, out.shape, 0)
    at = lax.broadcasted_iota(jnp.int32, out.shape, 1)
    out[...] = ((to // 16 == at % 16) & (to % 16 == at // 16)).astype(F32).astype(BF16)


def prior_kernel(prior_ref, prior_term):
    turns = lax.broadcasted_iota(jnp.int32, prior_term.shape, 0)
    lane = lax.broadcasted_iota(jnp.int32, (1, prior_term.shape[1]), 1)
    priors = prior_ref[...].reshape(1, -1)
    half = priors.shape[1] // 2
    first, second = [
        jnp.concatenate([priors[:, i * half : (i + 1) * half], lane[:, half:]], 1)
        for i in range(2)
    ]
    offset = jnp.abs(turns - jnp.where(lax.axis_index("rot") == 0, first, second))
    distance = jnp.minimum(offset, ANG - offset).astype(F32)
    prior_term[...] = -distance * distance / (2.0 * SIGMA * SIGMA)


def prep_kernel(share, particles_ref, permutation_ref, other, own):
    freqs, depth = particles_ref.shape[1:]
    group = lax.axis_index("rot")
    permutation = permutation_ref[...]
    for out, first in ((other, (1 - group) * share), (own, group * share)):
        for p in range(0, share, 16):
            for f in range(0, freqs, 32):
                blocks = [
                    jnp.concatenate(
                        [particles_ref[first + p + j, pl.ds(f + half, 16), :] for j in range(16)],
                        0,
                    )
                    for half in (0, 16)
                ]
                turned = dot(permutation, jnp.concatenate(blocks, 1)).astype(BF16)
                for half in range(2):
                    for j in range(16):
                        pair, part = divmod(f + 16 * half + j, 2)
                        out[pair, pl.ds(p, 16), pl.ds(part * depth, depth)] = turned[
                            16 * j : 16 * j + 16, half * depth : (half + 1) * depth
                        ]


def prep(particles, permutation, share):
    _, freqs, depth = particles.shape
    assert share % 16 == 0 and freqs % 32 == 0
    return call(
        functools.partial(prep_kernel, share),
        [particles, permutation],
        [((freqs // 2, share, 2 * depth), BF16)] * 2,
        flops=1 << 31,
    )


def tree(values):
    values = list(values)
    while len(values) > 1:
        values = [a + b for a, b in zip(values[::2], values[1::2])]
    return values[0]


def weigh_kernel(fresh, count, *refs):
    sources = refs[:count]
    doubled_ref, particles, out, energy_ref, left_ref, image, *rest = refs[count:]
    pairs, share, twice = particles.shape
    freqs, depth = 2 * pairs, twice // 2
    classes, lanes = energy_ref.shape
    pitch = freqs + SPARE
    radii = depth // 2
    lane = lax.broadcasted_iota(jnp.int32, (freqs, depth), 1)
    sign = jnp.where(lane < radii, -1.0, 1.0).astype(F32)
    doubled = jnp.concatenate([doubled_ref[...]] * 2, 1)
    row = lax.broadcasted_iota(jnp.int32, (freqs, depth), 0) + lax.axis_index("rot") * freqs
    scale = jnp.where(row == 0, 1.0 / ANG, 2.0 / ANG).astype(F32) * doubled

    for k in range(classes):
        if fresh:
            plain = sources[k][0].astype(F32)
        else:
            sums, highs, lows = [
                tree(
                    source[pl.ds(base + (k ^ i) * step, step), :].astype(F32)
                    for i, source in enumerate(sources)
                )
                for base, step in ((0, freqs), (classes * freqs, 1), (classes * (freqs + 1), 1))
            ]
            plain = (sums / (highs + lows + shrinkage)).astype(BF16).astype(F32)
        weighted = (plain * doubled).astype(BF16).astype(F32)
        image[rows(2 * k * pitch, freqs), :] = weighted
        image[rows((2 * k + 1) * pitch, freqs), :] = sign * pltpu.roll(weighted, radii, 1)
        energy = jnp.sum(plain * plain * scale, axis=0, keepdims=True)
        energy = jnp.broadcast_to(jnp.sum(energy, axis=1, keepdims=True), (SPARE, lanes))
        energy_ref[pl.ds(k, 1), :] = energy[:1]
        out[rows(2 * k * pitch + freqs, SPARE), :] = energy[:, : out.shape[1]]

    none = jnp.zeros((2 * classes, depth), BF16)

    def correlate(f):
        first, second = [
            image[pl.ds(2 * f + part, 2 * classes, stride=pitch), :].astype(BF16)
            for part in range(2)
        ]
        left = jnp.concatenate(
            [jnp.concatenate([first, none], 1), jnp.concatenate([none, second], 1)], 0
        )
        left_ref[f] = left
        place([out, *rest], f, times(left, particles[f]), classes, pitch)

    loop(pairs, correlate, 32)
    for ref in rest:
        width = share - 128
        for pack in range(-(-2 * classes * width // 128)):
            total = 0.0
            for i in range(min(128 // width, 2 * classes - pack * (128 // width))):
                group = ref[rows((pack * (128 // width) + i) * pitch, pitch), :]
                total = total + (pltpu.roll(group, i * width, 1) if i else group)
            out[rows((2 * classes + pack) * pitch, pitch), :] = total


def times(left, particles):
    return lax.dot_general(left, particles, (((1,), (1,)), ((), ())), preferred_element_type=F32)


def place(outs, f, value, classes, pitch):
    spare = jnp.zeros((value.shape[0], len(outs) * 128 - value.shape[1]), F32)
    value = jnp.concatenate([value, spare], 1) if spare.size else value
    for part in range(2):
        at = pl.ds(2 * f + part, 2 * classes, stride=pitch)
        for tile, out in enumerate(outs):
            out[at, :] = value[
                part * 2 * classes : (part + 1) * 2 * classes, tile * 128 : (tile + 1) * 128
            ]


def lane_tiles(share):
    return -(-share // 128)


def weigh(sources, inverse_noise, particles, fresh):
    pairs, share, twice = particles.shape
    classes = len(sources)
    pitch = 2 * pairs + SPARE
    tiles = lane_tiles(share)
    assert tiles == 1 or tiles == 2 and 128 % (share - 128) == 0
    packs = -(-2 * classes * (share - 128) // 128) if tiles == 2 else 0
    return call(
        functools.partial(weigh_kernel, fresh, classes),
        [*sources, inverse_noise, particles],
        [
            (((2 * classes + packs) * pitch, 128), F32),
            ((classes, tiles * 128), F32),
            ((pairs, 4 * classes, twice), BF16),
        ],
        [((2 * classes * pitch, twice // 2), F32)]
        + [((2 * classes * pitch, 128), F32)] * (tiles - 1),
        flops=8 * classes * share * pairs * twice * 4,
    )


def correlate_kernel(left_ref, particles, out):
    pairs = left_ref.shape[0]
    classes = left_ref.shape[1] // 4

    def body(f):
        outs = [out.at[tile] for tile in range(out.shape[0])]
        place(outs, f, times(left_ref[f], particles[f]), classes, 2 * pairs + SPARE)

    loop(pairs, body, 32)


def correlate(left, particles):
    pairs, share, twice = particles.shape
    lines = left.shape[1] // 2 * (2 * pairs + SPARE)
    return call(
        correlate_kernel,
        [left, particles],
        [((lane_tiles(share), lines, 128), F32)],
        flops=2 * left.shape[1] * share * pairs * twice * 8,
    )[0]


def across(ref, at):
    return jnp.concatenate([ref[tile, at, :] for tile in range(ref.shape[0])], 1)


def table_rows(base, count):
    return pl.ds(pl.multiple_of(lax.axis_index("rot") * ANG + base, 128), count)


def score_kernel(particles, own, other, energy_ref, prior_term, inv_hi, inv_lo, *refs):
    weights, peaks = refs
    classes, share = energy_ref.shape
    tiles, lines, width = own.shape
    pitch = lines // (2 * classes)
    freqs = pitch - SPARE
    which = table_rows(0, ANG)
    def unpacked(group):
        first = other[rows(group * pitch, freqs), :]
        if tiles == 1:
            return first
        width = particles - 128
        bundle = 128 // width
        packed = other[rows((2 * classes + group // bundle) * pitch, freqs), :]
        back = (bundle - group % bundle) % bundle * width
        return jnp.concatenate([first, pltpu.roll(packed, back, 1)], 1)

    def score(k, peak):
        near = [across(own, rows((2 * k + part) * pitch, freqs)) for part in range(2)]
        far = [unpacked(2 * k + part) for part in range(2)]
        value = jnp.concatenate(near + far, 0)
        high, low = split(value)
        inner = dot(inv_hi[which, :], high) + (
            dot(inv_hi[which, :], low) + dot(inv_lo[which, :], high)
        )
        far = other[rows(2 * k * pitch + freqs, SPARE), :][:1]
        energy = energy_ref[pl.ds(k, 1), :] + jnp.concatenate([far] * tiles, 1)
        scores = inner - 0.5 * energy + prior_term[...]
        weights[k] = scores
        return jnp.maximum(peak, jnp.max(scores, axis=0, keepdims=True))

    peak = each(classes, score, jnp.full((1, share), -jnp.inf, F32))

    def weight(k, total):
        value = jnp.exp(weights[k] - peak)
        weights[k] = value
        return total + jnp.sum(value, axis=0, keepdims=True)

    total = each(classes, weight, jnp.zeros((1, share), F32))
    line = lax.broadcasted_iota(jnp.int32, peaks.shape, 0)
    peaks[...] = jnp.where(line == 0, peak, total)


def scores(own, other, energy, prior_term, inv_hi, inv_lo, particles):
    classes, share = energy.shape
    return call(
        functools.partial(score_kernel, particles),
        [own, other, energy, prior_term, inv_hi, inv_lo],
        [((classes, ANG, share), F32), ((8, share), F32)],
        flops=6 * classes * share * ANG * ANG,
    )


def merge(first, second):
    top = jnp.maximum(first[0:1], second[0:1])
    total = first[1:2] * jnp.exp(first[0:1] - top) + second[1:2] * jnp.exp(second[0:1] - top)
    return top, total


def merge_kernel(first, second, out):
    top, total = merge(first[...], second[...])
    line = lax.broadcasted_iota(jnp.int32, out.shape, 0)
    out[...] = jnp.where(line == 0, top, total)


def turn_kernel(share, weights, here, first, second, fwd_hi, fwd_lo, *refs):
    rounded_ref, send, *evidence_ref, held = refs
    classes, _, lanes = weights.shape
    pairs = (held.shape[1] // (2 * classes) - SPARE) // 2
    top, total = merge(first[...], second[...])
    for ref in evidence_ref:
        ref[...] = (top + jnp.log(total))[:, :share]
    factor = jnp.exp(here[0:1, :] - top) / total
    lane = lax.broadcasted_iota(jnp.int32, (1, lanes), 1)
    factor = jnp.where(lane < share, factor, 0.0)
    which = table_rows(0, ANG // 2)
    line = lax.broadcasted_iota(jnp.int32, (4 * classes, share), 0)

    def body(k, column):
        value = weights[k] * factor
        count = jnp.sum(jnp.sum(value, axis=0, keepdims=True), axis=1, keepdims=True)
        rounded = value.astype(BF16)
        rounded_ref[k] = rounded
        spread(held, k, dot(fwd_hi[which, :], rounded) + dot(fwd_lo[which, :], rounded))
        high = count.astype(BF16).astype(F32)
        return jnp.where(line == k, high, jnp.where(line == classes + k, count - high, column))

    column = each(classes, body, jnp.zeros((4 * classes, share), F32))
    send[pairs] = column.astype(BF16)

    def rearrange(f):
        send[f] = pick(held, f, classes, share)

    loop(pairs, rearrange, 32)


def spread(held, k, value):
    tiles, lines, width = held.shape
    freqs = value.shape[0] // 2
    for part in range(2):
        for tile in range(tiles):
            held[tile, rows((2 * k + part) * (freqs + SPARE), freqs), :] = value[
                part * freqs : (part + 1) * freqs, tile * width : (tile + 1) * width
            ]


def pick(held, f, classes, share):
    pitch = held.shape[1] // (2 * classes)
    parts = [
        across(held, pl.ds(2 * f + part, 2 * classes, stride=pitch)).astype(BF16)
        for part in range(2)
    ]
    return jnp.concatenate(parts, 0)[:, :share]


def turn(weights, here, first, second, fwd_hi, fwd_lo, freqs, share, last):
    classes, _, lanes = weights.shape
    return call(
        functools.partial(turn_kernel, share),
        [weights, here, first, second, fwd_hi, fwd_lo],
        [
            ((classes, ANG, lanes), BF16),
            ((freqs // 2 + 1, 4 * classes, share), BF16),
            *([((1, share), F32)] if last else []),
        ],
        [((lanes // 128, 2 * classes * (freqs + SPARE), 128), F32)],
        flops=4 * classes * lanes * ANG * ANG,
    )


def gather_kernel(rounded_ref, fwd_hi, fwd_lo, particles, image, held):
    classes = rounded_ref.shape[0]
    pairs, share, _ = particles.shape
    which = table_rows(ANG // 2, ANG // 2)

    def body(k, carry):
        rounded = rounded_ref[k]
        spread(held, k, dot(fwd_hi[which, :], rounded) + dot(fwd_lo[which, :], rounded))
        return carry

    each(classes, body, 0)

    def accumulate(f):
        take_in(image, f, dot(pick(held, f, classes, share), particles[f]), classes)

    loop(pairs, accumulate, 32)


def gather(rounded, fwd_hi, fwd_lo, particles):
    pairs, share, twice = particles.shape
    classes, _, lanes = rounded.shape
    lines = 2 * classes * (2 * pairs + SPARE)
    return call(
        gather_kernel,
        [rounded, fwd_hi, fwd_lo, particles],
        [((lines, twice // 2), F32)],
        [((lanes // 128, lines, 128), F32)],
        flops=4 * classes * lanes * ANG * ANG,
    )[0]


def take_in(image, f, value, classes):
    lines, depth = image.shape
    for part in range(2):
        at = pl.ds(2 * f + part, 2 * classes, stride=lines // (2 * classes))
        image[at, :] = value[
            part * 2 * classes : (part + 1) * 2 * classes, part * depth : (part + 1) * depth
        ]


def finish_kernel(image, mine, spectrum, particles, *refs):
    outs, held = refs[:-1], refs[-1]
    pairs, _, twice = particles.shape
    classes = spectrum.shape[1] // 4
    freqs, depth = 2 * pairs, twice // 2
    radii = depth // 2
    pitch = freqs + SPARE

    def body(f):
        take_in(held, f, dot(spectrum[f], particles[f]), classes)

    loop(pairs, body, 32)
    counts = (mine[pairs].astype(F32) + spectrum[pairs].astype(F32))[:, :depth]
    counts = counts[:classes] + counts[classes : 2 * classes]
    lane = lax.broadcasted_iota(jnp.int32, (freqs, depth), 1)
    sign = jnp.where(lane < radii, -1.0, 1.0).astype(F32)
    for k in range(classes):
        plain, turned = [
            image[rows((2 * k + part) * pitch, freqs), :]
            + held[rows((2 * k + part) * pitch, freqs), :]
            for part in range(2)
        ]
        value = plain + sign * pltpu.roll(turned, radii, 1)
        if len(outs) == 1:
            outs[0][pl.ds(k * freqs, freqs), :] = value.astype(BF16)
        else:
            outs[k][pl.ds(0, freqs), :] = value
            outs[k][pl.ds(freqs, SPARE), :] = jnp.broadcast_to(counts[k : k + 1], (SPARE, depth))
    if len(outs) == 1:
        end = outs[0].shape[0] - classes * freqs
        high, low = split(counts)
        spare = [jnp.zeros((end - 2 * classes, depth), F32)] if end > 2 * classes else []
        tail = jnp.concatenate([high.astype(F32), low.astype(F32), *spare], 0)
        outs[0][pl.ds(classes * freqs, end), :] = tail.astype(BF16)


def finish(image, mine, spectrum, particles, last):
    pairs, _, twice = particles.shape
    classes = spectrum.shape[1] // 4
    freqs, depth = 2 * pairs, twice // 2
    if last:
        outs = [((freqs + SPARE, depth), F32)] * classes
    else:
        outs = [((classes * freqs + -(-2 * classes // 16) * 16, depth), BF16)]
    return call(
        finish_kernel,
        [image, mine, spectrum, particles],
        outs,
        [(image.shape, F32)],
        flops=2 * math.prod(spectrum.shape) * twice * 8,
    )


def means_kernel(*refs):
    *parts, evidence_ref, out, last_ref = refs
    last_ref[...] = evidence_ref[...]
    freqs = out.shape[1]
    total = tree(ref[...] for ref in parts)
    out[0] = total[:freqs, :] / (total[freqs : freqs + 1, :] + shrinkage)


def swap(value, axis, size, bit):
    if not bit:
        return value
    return lax.ppermute(value, axis, [(i, i ^ bit) for i in range(size)])


def bits(size):
    assert size > 1 and size & (size - 1) == 0
    return [1 << i for i in range(size.bit_length() - 1)]


def shards(particles, references, noise_inv, prior_rot):
    batch, freqs, depth = particles.shape
    sides = lax.axis_size("cls")
    groups = lax.axis_size("rot")
    blocks = lax.axis_size("blk")
    assert groups == 2 and 2 * groups * freqs == ANG
    share = batch // groups
    inv_hi, inv_lo, fwd_hi, fwd_lo = tables(freqs)
    inverse_noise = noise_inv.reshape(1, depth // 2)
    assert blocks & (blocks - 1) == 0

    (permutation,) = call(permutation_kernel, [], [((256, 256), BF16)], flops=1 << 32)
    first, permutation = lax.optimization_barrier((references, permutation))
    (prior_term,) = call(
        prior_kernel, [prior_rot], [((ANG, lane_tiles(share) * 128), F32)], flops=1 << 26
    )
    sources = [
        swap(first if i else references, "blk", blocks, i ^ (blocks - 1)) for i in range(blocks)
    ][::-1]
    other_images, own_images = prep(particles, permutation, share)
    for step in range(ITERS):
        last = step == ITERS - 1
        message, energy, left = weigh(sources, inverse_noise, other_images, step == 0)
        message = swap(message, "rot", groups, 1)
        own = correlate(left, own_images)
        weights, here = scores(own, message, energy, prior_term, inv_hi, inv_lo, share)
        first = here
        for bit in bits(sides):
            second = swap(first, "cls", sides, bit)
            if 2 * bit < sides:
                (first,) = call(merge_kernel, [first, second], [(here.shape, F32)])
        rounded, send, *evidence = turn(
            weights, here, first, second, fwd_hi, fwd_lo, freqs, share, last
        )
        message = swap(send, "rot", groups, 1)
        image = gather(rounded, fwd_hi, fwd_lo, own_images)
        sums = finish(image, send, message, other_images, last)
        sums = sums if last else sums * blocks
        sources = [swap(sums[i], "blk", blocks, i) for i in reversed(range(blocks))][::-1]
    means, evidence = call(
        means_kernel, [*sources[::-1], *evidence], [((1, freqs, depth), F32), ((1, share), F32)]
    )
    return means, evidence.reshape(share)


def solution(mesh):
    in_specs = (
        P(("grp", "blk"), "rot", None),
        P(("grp", "blk", "cls"), "rot", None),
        P(),
        P(("grp", "blk")),
    )
    out_specs = (P(("grp", "blk", "cls"), "rot", None), P(("grp", "blk", "rot")))
    return jax.shard_map(shards, mesh=mesh, in_specs=in_specs, out_specs=out_specs, check_vma=False)
```

```python
import functools
import math

import jax
import jax.numpy as jnp
import numpy as np
from jax import lax
from jax.experimental import pallas as pl
from jax.experimental.pallas import tpu as pltpu
from jax.sharding import PartitionSpec as P

ANG = 256
ITERS = 2
SIGMA = 32

shrinkage = 1.0

F32 = jnp.float32
BF16 = jnp.bfloat16
SPARE = 8

dot = functools.partial(jnp.dot, preferred_element_type=F32)


def split(x):
    high = x.astype(BF16)
    return high, (x - high.astype(F32)).astype(BF16)


def tables(half_freq):
    turn = np.arange(ANG)
    inverse, forward = [], []
    for group in range(2):
        sides = {}
        for which in range(2):
            freq = which * half_freq + np.arange(half_freq)
            angle = (turn[:, None] * freq[None, :] % ANG) * (2.0 * math.pi / ANG)
            scale = np.where(freq == 0, 1.0, 2.0) / ANG
            sides[which] = (
                np.concatenate([scale * np.cos(angle), -scale * np.sin(angle)], 1),
                np.concatenate([np.cos(angle), np.sin(angle)], 1).T,
            )
        inverse.append(np.concatenate([sides[group][0], sides[1 - group][0]], 1))
        forward.append(np.concatenate([sides[1 - group][1], sides[group][1]], 0))
    result = []
    for table in (inverse, forward):
        table = np.stack(table).astype(np.float32)
        high = table.astype(BF16)
        result += [high, (table - high.astype(np.float32)).astype(BF16)]
    return [jnp.asarray(x.reshape(-1, ANG)) for x in result]


def loop(count, body, unroll):
    while count % unroll:
        unroll -= 1
    if unroll == count:
        for i in range(count):
            body(i)
        return

    def step(outer, carry):
        for inner in range(unroll):
            body(outer * unroll + inner)
        return carry

    lax.fori_loop(0, count // unroll, step, 0)


def each(count, body, init):
    if count <= 8:
        for k in range(count):
            init = body(k, init)
        return init
    return lax.fori_loop(0, count, body, init)


def rows(base, count):
    return pl.ds(pl.multiple_of(base, 8), count)


def call(kernel, ins, outs, scratch=(), flops=0, far=(), room=4 << 20):
    total = 0
    buffers = [(x.shape, x.dtype) for i, x in enumerate(ins) if i not in far]
    for shape, dtype in buffers + list(outs) + [x for x in scratch if isinstance(x, tuple)]:
        dims = [1, 1, *shape]
        lines = -(-dims[-2] // 16) * 16
        lanes = -(-dims[-1] // 128) * 128
        total += math.prod(dims[:-2]) * lines * lanes * jnp.dtype(dtype).itemsize
    kinds = [pltpu.VMEM] * len(ins)
    for i in far:
        kinds[i] = pltpu.MemorySpace.HBM
    return pl.pallas_call(
        kernel,
        out_shape=[jax.ShapeDtypeStruct(*x) for x in outs],
        in_specs=[pl.BlockSpec(memory_space=kind) for kind in kinds],
        out_specs=[pl.BlockSpec(memory_space=pltpu.VMEM)] * len(outs),
        scratch_shapes=[pltpu.VMEM(*x) if isinstance(x, tuple) else x for x in scratch],
        compiler_params=pltpu.CompilerParams(vmem_limit_bytes=min(total + room, 56 << 20)),
        cost_estimate=pl.CostEstimate(flops=flops, bytes_accessed=total, transcendentals=0),
    )(*ins)


def permutation_kernel(out):
    to = lax.broadcasted_iota(jnp.int32, out.shape, 0)
    at = lax.broadcasted_iota(jnp.int32, out.shape, 1)
    out[...] = ((to // 16 == at % 16) & (to % 16 == at // 16)).astype(F32).astype(BF16)


def prior_kernel(prior_ref, prior_term):
    turns = lax.broadcasted_iota(jnp.int32, prior_term.shape, 0)
    lane = lax.broadcasted_iota(jnp.int32, (1, prior_term.shape[1]), 1)
    priors = prior_ref[...].reshape(1, -1)
    half = priors.shape[1] // 2
    first, second = [
        jnp.concatenate([priors[:, i * half : (i + 1) * half], lane[:, half:]], 1)
        for i in range(2)
    ]
    offset = jnp.abs(turns - jnp.where(lax.axis_index("rot") == 0, first, second))
    distance = jnp.minimum(offset, ANG - offset).astype(F32)
    prior_term[...] = -distance * distance / (2.0 * SIGMA * SIGMA)


def prep_kernel(share, particles_ref, permutation_ref, other, own):
    freqs, depth = particles_ref.shape[1:]
    group = lax.axis_index("rot")
    permutation = permutation_ref[...]
    for out, first in ((other, (1 - group) * share), (own, group * share)):
        for p in range(0, share, 16):
            for f in range(0, freqs, 32):
                blocks = [
                    jnp.concatenate(
                        [particles_ref[first + p + j, pl.ds(f + half, 16), :] for j in range(16)],
                        0,
                    )
                    for half in (0, 16)
                ]
                turned = dot(permutation, jnp.concatenate(blocks, 1)).astype(BF16)
                for half in range(2):
                    for j in range(16):
                        pair, part = divmod(f + 16 * half + j, 2)
                        out[pair, pl.ds(p, 16), pl.ds(part * depth, depth)] = turned[
                            16 * j : 16 * j + 16, half * depth : (half + 1) * depth
                        ]


def prep(particles, permutation, share):
    _, freqs, depth = particles.shape
    assert share % 16 == 0 and freqs % 32 == 0
    return call(
        functools.partial(prep_kernel, share),
        [particles, permutation],
        [((freqs // 2, share, 2 * depth), BF16)] * 2,
        flops=1 << 31,
    )


def tree(values):
    values = list(values)
    while len(values) > 1:
        values = [a + b for a, b in zip(values[::2], values[1::2])]
    return values[0]


def weigh_kernel(fresh, turns, count, *refs):
    sources = [refs[[0, *turns].index(i)] for i in range(count)]
    doubled_ref, particles, out, energy_ref, left_ref, image, *rest = refs[count:]
    pairs, share, twice = particles.shape
    freqs, depth = 2 * pairs, twice // 2
    classes, lanes = energy_ref.shape
    pitch = freqs + SPARE
    radii = depth // 2
    lane = lax.broadcasted_iota(jnp.int32, (freqs, depth), 1)
    sign = jnp.where(lane < radii, -1.0, 1.0).astype(F32)
    doubled = jnp.concatenate([doubled_ref[...]] * 2, 1)
    row = lax.broadcasted_iota(jnp.int32, (freqs, depth), 0) + lax.axis_index("rot") * freqs
    scale = jnp.where(row == 0, 1.0 / ANG, 2.0 / ANG).astype(F32) * doubled

    for k in range(classes):
        if fresh:
            plain = sources[k][0].astype(F32)
        else:
            sums, highs, lows = [
                tree(
                    source[pl.ds(base + (k ^ i) * step, step), :].astype(F32)
                    for i, source in enumerate(sources)
                )
                for base, step in ((0, freqs), (classes * freqs, 1), (classes * (freqs + 1), 1))
            ]
            plain = (sums / (highs + lows + shrinkage)).astype(BF16).astype(F32)
        weighted = (plain * doubled).astype(BF16).astype(F32)
        image[rows(2 * k * pitch, freqs), :] = weighted
        image[rows((2 * k + 1) * pitch, freqs), :] = sign * pltpu.roll(weighted, radii, 1)
        energy = jnp.sum(plain * plain * scale, axis=0, keepdims=True)
        energy = jnp.broadcast_to(jnp.sum(energy, axis=1, keepdims=True), (SPARE, lanes))
        energy_ref[pl.ds(k, 1), :] = energy[:1]
        out[rows(2 * k * pitch + freqs, SPARE), :] = energy[:, : out.shape[1]]

    none = jnp.zeros((2 * classes, depth), BF16)

    def correlate(f):
        first, second = [
            image[pl.ds(2 * f + part, 2 * classes, stride=pitch), :].astype(BF16)
            for part in range(2)
        ]
        left = jnp.concatenate(
            [jnp.concatenate([first, none], 1), jnp.concatenate([none, second], 1)], 0
        )
        left_ref[f] = left
        place([out, *rest], f, times(left, particles[f]), classes, pitch)

    loop(pairs, correlate, 32)
    for ref in rest:
        width = share - 128
        for pack in range(-(-2 * classes * width // 128)):
            total = 0.0
            for i in range(min(128 // width, 2 * classes - pack * (128 // width))):
                group = ref[rows((pack * (128 // width) + i) * pitch, pitch), :]
                total = total + (pltpu.roll(group, i * width, 1) if i else group)
            out[rows((2 * classes + pack) * pitch, pitch), :] = total


def times(left, particles):
    return lax.dot_general(left, particles, (((1,), (1,)), ((), ())), preferred_element_type=F32)


def place(outs, f, value, classes, pitch):
    spare = jnp.zeros((value.shape[0], len(outs) * 128 - value.shape[1]), F32)
    value = jnp.concatenate([value, spare], 1) if spare.size else value
    for part in range(2):
        at = pl.ds(2 * f + part, 2 * classes, stride=pitch)
        for tile, out in enumerate(outs):
            out[at, :] = value[
                part * 2 * classes : (part + 1) * 2 * classes, tile * 128 : (tile + 1) * 128
            ]


def lane_tiles(share):
    return -(-share // 128)


def weigh(sources, turns, inverse_noise, particles, fresh):
    pairs, share, twice = particles.shape
    classes = len(sources)
    pitch = 2 * pairs + SPARE
    tiles = lane_tiles(share)
    assert tiles == 1 or tiles == 2 and 128 % (share - 128) == 0
    packs = -(-2 * classes * (share - 128) // 128) if tiles == 2 else 0
    return call(
        functools.partial(weigh_kernel, fresh, turns, classes),
        [*[sources[i] for i in (0, *turns)], inverse_noise, particles],
        [
            (((2 * classes + packs) * pitch, 128), F32),
            ((classes, tiles * 128), F32),
            ((pairs, 4 * classes, twice), BF16),
        ],
        [((2 * classes * pitch, twice // 2), F32)]
        + [((2 * classes * pitch, 128), F32)] * (tiles - 1),
        flops=8 * classes * share * pairs * twice * 4,
    )


def correlate_kernel(
    left_ref, particles, energy_ref, prior_term, inv_hi, inv_lo, partial_ref, field
):
    pairs = left_ref.shape[0]
    classes = left_ref.shape[1] // 4
    freqs, pitch = 2 * pairs, 2 * pairs + SPARE
    outs = [field.at[tile] for tile in range(field.shape[0])]

    def body(f):
        place(outs, f, times(left_ref[f], particles[f]), classes, pitch)

    loop(pairs, body, 32)

    def score(k, carry):
        value = [across(field, rows((2 * k + part) * pitch, freqs)) for part in range(2)]
        inner = invert(jnp.concatenate(value, 0), inv_hi, inv_lo, 0)
        partial_ref[k] = inner - 0.5 * energy_ref[pl.ds(k, 1), :] + prior_term[...]
        return carry

    each(classes, score, 0)


def invert(value, inv_hi, inv_lo, half):
    high, low = split(value)
    columns = pl.ds(half * (ANG // 2), ANG // 2)
    at = table_rows(0, ANG)
    return dot(inv_hi[at, columns], high) + (
        dot(inv_hi[at, columns], low) + dot(inv_lo[at, columns], high)
    )


def correlate(left, particles, energy, prior_term, inv_hi, inv_lo):
    pairs, share, twice = particles.shape
    classes, lanes = energy.shape
    lines = 2 * classes * (2 * pairs + SPARE)
    return call(
        correlate_kernel,
        [left, particles, energy, prior_term, inv_hi, inv_lo],
        [((classes, ANG, lanes), F32)],
        [((lanes // 128, lines, 128), F32)],
        flops=2 * left.shape[1] * share * pairs * twice * 8,
    )[0]


def across(ref, at):
    return jnp.concatenate([ref[tile, at, :] for tile in range(ref.shape[0])], 1)


def table_rows(base, count):
    return pl.ds(pl.multiple_of(lax.axis_index("rot") * ANG + base, 128), count)


def score_kernel(particles, partial_ref, other, inv_hi, inv_lo, weights, peaks):
    classes, _, share = partial_ref.shape
    tiles = share // 128
    freqs = ANG // 4
    pitch = freqs + SPARE

    def unpacked(group):
        first = other[rows(group * pitch, freqs), :]
        if tiles == 1:
            return first
        width = particles - 128
        bundle = 128 // width
        packed = other[rows((2 * classes + group // bundle) * pitch, freqs), :]
        back = (bundle - group % bundle) % bundle * width
        return jnp.concatenate([first, pltpu.roll(packed, back, 1)], 1)

    def score(k, peak):
        value = jnp.concatenate([unpacked(2 * k + part) for part in range(2)], 0)
        energy = other[rows(2 * k * pitch + freqs, SPARE), :][:1]
        inner = invert(value, inv_hi, inv_lo, 1)
        scores = partial_ref[k] + inner - 0.5 * jnp.concatenate([energy] * tiles, 1)
        weights[k] = scores
        return jnp.maximum(peak, jnp.max(scores, axis=0, keepdims=True))

    peak = each(classes, score, jnp.full((1, share), -jnp.inf, F32))

    def weight(k, total):
        value = jnp.exp(weights[k] - peak)
        weights[k] = value
        return total + jnp.sum(value, axis=0, keepdims=True)

    total = each(classes, weight, jnp.zeros((1, share), F32))
    line = lax.broadcasted_iota(jnp.int32, peaks.shape, 0)
    peaks[...] = jnp.where(line == 0, peak, total)


def scores(partial, other, inv_hi, inv_lo, particles):
    classes, _, lanes = partial.shape
    return call(
        functools.partial(score_kernel, particles),
        [partial, other, inv_hi, inv_lo],
        [(partial.shape, F32), ((8, lanes), F32)],
        flops=6 * classes * lanes * ANG * ANG,
    )


def merge(first, second):
    top = jnp.maximum(first[0:1], second[0:1])
    total = first[1:2] * jnp.exp(first[0:1] - top) + second[1:2] * jnp.exp(second[0:1] - top)
    return top, total


def merge_kernel(first, second, out):
    top, total = merge(first[...], second[...])
    line = lax.broadcasted_iota(jnp.int32, out.shape, 0)
    out[...] = jnp.where(line == 0, top, total)


def turn_kernel(share, weights, here, first, second, fwd_hi, fwd_lo, *refs):
    rounded_ref, send, *evidence_ref, held = refs
    classes, _, lanes = weights.shape
    pairs = (held.shape[1] // (2 * classes) - SPARE) // 2
    top, total = merge(first[...], second[...])
    for ref in evidence_ref:
        ref[...] = (top + jnp.log(total))[:, :share]
    factor = jnp.exp(here[0:1, :] - top) / total
    lane = lax.broadcasted_iota(jnp.int32, (1, lanes), 1)
    factor = jnp.where(lane < share, factor, 0.0)
    which = table_rows(0, ANG // 2)
    line = lax.broadcasted_iota(jnp.int32, (4 * classes, share), 0)

    def body(k, column):
        value = weights[k] * factor
        count = jnp.sum(jnp.sum(value, axis=0, keepdims=True), axis=1, keepdims=True)
        rounded = value.astype(BF16)
        rounded_ref[k] = rounded
        spread(held, k, dot(fwd_hi[which, :], rounded) + dot(fwd_lo[which, :], rounded))
        high = count.astype(BF16).astype(F32)
        return jnp.where(line == k, high, jnp.where(line == classes + k, count - high, column))

    column = each(classes, body, jnp.zeros((4 * classes, share), F32))
    send[pairs] = column.astype(BF16)

    def rearrange(f):
        send[f] = pick(held, f, classes, share)

    loop(pairs, rearrange, 32)


def spread(held, k, value):
    tiles, lines, width = held.shape
    freqs = value.shape[0] // 2
    for part in range(2):
        for tile in range(tiles):
            held[tile, rows((2 * k + part) * (freqs + SPARE), freqs), :] = value[
                part * freqs : (part + 1) * freqs, tile * width : (tile + 1) * width
            ]


def pick(held, f, classes, share):
    pitch = held.shape[1] // (2 * classes)
    parts = [
        across(held, pl.ds(2 * f + part, 2 * classes, stride=pitch)).astype(BF16)
        for part in range(2)
    ]
    return jnp.concatenate(parts, 0)[:, :share]


def turn(weights, here, first, second, fwd_hi, fwd_lo, freqs, share, last):
    classes, _, lanes = weights.shape
    return call(
        functools.partial(turn_kernel, share),
        [weights, here, first, second, fwd_hi, fwd_lo],
        [
            ((classes, ANG, lanes), BF16),
            ((freqs // 2 + 1, 4 * classes, share), BF16),
            *([((1, share), F32)] if last else []),
        ],
        [((lanes // 128, 2 * classes * (freqs + SPARE), 128), F32)],
        flops=4 * classes * lanes * ANG * ANG,
    )


def gather_kernel(rounded_ref, fwd_hi, fwd_lo, particles, image, held):
    classes = rounded_ref.shape[0]
    pairs, share, _ = particles.shape
    which = table_rows(ANG // 2, ANG // 2)

    def body(k, carry):
        rounded = rounded_ref[k]
        spread(held, k, dot(fwd_hi[which, :], rounded) + dot(fwd_lo[which, :], rounded))
        return carry

    each(classes, body, 0)

    def accumulate(f):
        take_in(image, f, dot(pick(held, f, classes, share), particles[f]), classes)

    loop(pairs, accumulate, 32)


def gather(rounded, fwd_hi, fwd_lo, particles):
    pairs, share, twice = particles.shape
    classes, _, lanes = rounded.shape
    lines = 2 * classes * (2 * pairs + SPARE)
    return call(
        gather_kernel,
        [rounded, fwd_hi, fwd_lo, particles],
        [((lines, twice // 2), F32)],
        [((lanes // 128, lines, 128), F32)],
        flops=4 * classes * lanes * ANG * ANG,
    )[0]


def take_in(image, f, value, classes):
    lines, depth = image.shape
    for part in range(2):
        at = pl.ds(2 * f + part, 2 * classes, stride=lines // (2 * classes))
        image[at, :] = value[
            part * 2 * classes : (part + 1) * 2 * classes, part * depth : (part + 1) * depth
        ]


def finish_kernel(image, mine, spectrum, particles, *refs):
    outs, held = refs[:-1], refs[-1]
    pairs, _, twice = particles.shape
    classes = spectrum.shape[1] // 4
    freqs, depth = 2 * pairs, twice // 2
    radii = depth // 2
    pitch = freqs + SPARE

    def body(f):
        take_in(held, f, dot(spectrum[f], particles[f]), classes)

    loop(pairs, body, 32)
    counts = (mine[pairs].astype(F32) + spectrum[pairs].astype(F32))[:, :depth]
    counts = counts[:classes] + counts[classes : 2 * classes]
    lane = lax.broadcasted_iota(jnp.int32, (freqs, depth), 1)
    sign = jnp.where(lane < radii, -1.0, 1.0).astype(F32)
    for k in range(classes):
        plain, turned = [
            image[rows((2 * k + part) * pitch, freqs), :]
            + held[rows((2 * k + part) * pitch, freqs), :]
            for part in range(2)
        ]
        value = plain + sign * pltpu.roll(turned, radii, 1)
        if len(outs) == 1:
            outs[0][pl.ds(k * freqs, freqs), :] = value.astype(BF16)
        else:
            outs[k][pl.ds(0, freqs), :] = value
            outs[k][pl.ds(freqs, SPARE), :] = jnp.broadcast_to(counts[k : k + 1], (SPARE, depth))
    if len(outs) == 1:
        end = outs[0].shape[0] - classes * freqs
        high, low = split(counts)
        spare = [jnp.zeros((end - 2 * classes, depth), F32)] if end > 2 * classes else []
        tail = jnp.concatenate([high.astype(F32), low.astype(F32), *spare], 0)
        outs[0][pl.ds(classes * freqs, end), :] = tail.astype(BF16)


def finish(image, mine, spectrum, particles, last):
    pairs, _, twice = particles.shape
    classes = spectrum.shape[1] // 4
    freqs, depth = 2 * pairs, twice // 2
    if last:
        outs = [((freqs + SPARE, depth), F32)] * classes
    else:
        outs = [((classes * freqs + -(-2 * classes // 16) * 16, depth), BF16)]
    return call(
        finish_kernel,
        [image, mine, spectrum, particles],
        outs,
        [(image.shape, F32)],
        flops=2 * math.prod(spectrum.shape) * twice * 8,
    )


def means_kernel(*refs):
    *parts, evidence_ref, out, last_ref = refs
    last_ref[...] = evidence_ref[...]
    freqs = out.shape[1]
    total = tree(ref[...] for ref in parts)
    out[0] = total[:freqs, :] / (total[freqs : freqs + 1, :] + shrinkage)


def swap(value, axis, size, bit):
    if not bit:
        return value
    return lax.ppermute(value, axis, [(i, i ^ bit) for i in range(size)])


def bits(size):
    assert size > 1 and size & (size - 1) == 0
    return [1 << i for i in range(size.bit_length() - 1)]


def shards(particles, references, noise_inv, prior_rot):
    batch, freqs, depth = particles.shape
    sides = lax.axis_size("cls")
    groups = lax.axis_size("rot")
    blocks = lax.axis_size("blk")
    assert groups == 2 and 2 * groups * freqs == ANG
    share = batch // groups
    inv_hi, inv_lo, fwd_hi, fwd_lo = tables(freqs)
    inverse_noise = noise_inv.reshape(1, depth // 2)
    assert blocks & (blocks - 1) == 0
    turns = sorted(range(1, blocks), key=lambda i: (-i.bit_length(), i))

    (permutation,) = call(permutation_kernel, [], [((256, 256), BF16)], flops=1 << 32)
    (prior_term,) = call(
        prior_kernel, [prior_rot], [((ANG, lane_tiles(share) * 128), F32)], flops=1 << 26
    )
    sources = {i: swap(references, "blk", blocks, i) for i in (*turns, 0)}
    other_images, own_images = prep(particles, permutation, share)
    for step in range(ITERS):
        last = step == ITERS - 1
        message, energy, left = weigh(sources, turns, inverse_noise, other_images, step == 0)
        message = swap(message, "rot", groups, 1)
        partial = correlate(left, own_images, energy, prior_term, inv_hi, inv_lo)
        weights, here = scores(partial, message, inv_hi, inv_lo, share)
        first = here
        for bit in bits(sides):
            second = swap(first, "cls", sides, bit)
            if 2 * bit < sides:
                (first,) = call(merge_kernel, [first, second], [(here.shape, F32)])
        rounded, send, *evidence = turn(
            weights, here, first, second, fwd_hi, fwd_lo, freqs, share, last
        )
        message = swap(send, "rot", groups, 1)
        image = gather(rounded, fwd_hi, fwd_lo, own_images)
        sums = finish(image, send, message, other_images, last)
        sums = sums if last else sums * blocks
        sources = {i: swap(sums[i], "blk", blocks, i) for i in (*turns, 0)}
    means, evidence = call(
        means_kernel, [*[sources[i] for i in turns], sources[0], *evidence], [((1, freqs, depth), F32), ((1, share), F32)]
    )
    return means, evidence.reshape(share)


def solution(mesh):
    in_specs = (
        P(("grp", "blk"), "rot", None),
        P(("grp", "blk", "cls"), "rot", None),
        P(),
        P(("grp", "blk")),
    )
    out_specs = (P(("grp", "blk", "cls"), "rot", None), P(("grp", "blk", "rot")))
    return jax.shard_map(shards, mesh=mesh, in_specs=in_specs, out_specs=out_specs, check_vma=False)
```

```python
import functools
import math

import jax
import jax.numpy as jnp
import numpy as np
from jax import lax
from jax.experimental import pallas as pl
from jax.experimental.pallas import tpu as pltpu
from jax.sharding import PartitionSpec as P

ANG = 256
ITERS = 2
SIGMA = 32

shrinkage = 1.0

F32 = jnp.float32
BF16 = jnp.bfloat16
SPARE = 8

dot = functools.partial(jnp.dot, preferred_element_type=F32)


def split(x):
    high = x.astype(BF16)
    return high, (x - high.astype(F32)).astype(BF16)


def tables(half_freq):
    turn = np.arange(ANG)
    inverse, forward = [], []
    for group in range(2):
        sides = {}
        for which in range(2):
            freq = which * half_freq + np.arange(half_freq)
            angle = (turn[:, None] * freq[None, :] % ANG) * (2.0 * math.pi / ANG)
            scale = np.where(freq == 0, 1.0, 2.0) / ANG
            sides[which] = (
                np.concatenate([scale * np.cos(angle), -scale * np.sin(angle)], 1),
                np.concatenate([np.cos(angle), np.sin(angle)], 1).T,
            )
        inverse.append(np.concatenate([sides[group][0], sides[1 - group][0]], 1))
        forward.append(np.concatenate([sides[1 - group][1], sides[group][1]], 0))
    result = []
    for table, kinds in ((inverse, (0, 0, 1)), (forward, (0, 1))):
        table = np.concatenate(table, 0).astype(np.float32)
        high = table.astype(BF16)
        parts = [high, (table - high.astype(np.float32)).astype(BF16)]
        result.append(jnp.asarray(np.concatenate([parts[kind] for kind in kinds], 1)))
    return result


def loop(count, body, unroll):
    while count % unroll:
        unroll -= 1
    if unroll == count:
        for i in range(count):
            body(i)
        return

    def step(outer, carry):
        for inner in range(unroll):
            body(outer * unroll + inner)
        return carry

    lax.fori_loop(0, count // unroll, step, 0)


def each(count, body, init):
    if count <= 8:
        for k in range(count):
            init = body(k, init)
        return init
    return lax.fori_loop(0, count, body, init)


def rows(base, count):
    return pl.ds(pl.multiple_of(base, 8), count)


def call(kernel, ins, outs, scratch=(), flops=0, far=(), room=4 << 20):
    total = 0
    buffers = [(x.shape, x.dtype) for i, x in enumerate(ins) if i not in far]
    for shape, dtype in buffers + list(outs) + [x for x in scratch if isinstance(x, tuple)]:
        dims = [1, 1, *shape]
        lines = -(-dims[-2] // 16) * 16
        lanes = -(-dims[-1] // 128) * 128
        total += math.prod(dims[:-2]) * lines * lanes * jnp.dtype(dtype).itemsize
    kinds = [pltpu.VMEM] * len(ins)
    for i in far:
        kinds[i] = pltpu.MemorySpace.HBM
    return pl.pallas_call(
        kernel,
        out_shape=[jax.ShapeDtypeStruct(*x) for x in outs],
        in_specs=[pl.BlockSpec(memory_space=kind) for kind in kinds],
        out_specs=[pl.BlockSpec(memory_space=pltpu.VMEM)] * len(outs),
        scratch_shapes=[pltpu.VMEM(*x) if isinstance(x, tuple) else x for x in scratch],
        compiler_params=pltpu.CompilerParams(vmem_limit_bytes=min(total + room, 56 << 20)),
        cost_estimate=pl.CostEstimate(flops=flops, bytes_accessed=total, transcendentals=0),
    )(*ins)


def permutation_kernel(out):
    to = lax.broadcasted_iota(jnp.int32, out.shape, 0)
    at = lax.broadcasted_iota(jnp.int32, out.shape, 1)
    out[...] = ((to // 16 == at % 16) & (to % 16 == at // 16)).astype(F32).astype(BF16)


def prior_kernel(prior_ref, prior_term):
    turns = lax.broadcasted_iota(jnp.int32, prior_term.shape, 0)
    lane = lax.broadcasted_iota(jnp.int32, (1, prior_term.shape[1]), 1)
    priors = prior_ref[...].reshape(1, -1)
    half = priors.shape[1] // 2
    first, second = [
        jnp.concatenate([priors[:, i * half : (i + 1) * half], lane[:, half:]], 1)
        for i in range(2)
    ]
    offset = jnp.abs(turns - jnp.where(lax.axis_index("rot") == 0, first, second))
    distance = jnp.minimum(offset, ANG - offset).astype(F32)
    prior_term[...] = -distance * distance / (2.0 * SIGMA * SIGMA)


def prep_kernel(share, particles_ref, permutation_ref, other, own):
    freqs, depth = particles_ref.shape[1:]
    group = lax.axis_index("rot")
    permutation = permutation_ref[...]
    for out, first in ((other, (1 - group) * share), (own, group * share)):
        for p in range(0, share, 16):
            for f in range(0, freqs, 32):
                blocks = [
                    jnp.concatenate(
                        [particles_ref[first + p + j, pl.ds(f + half, 16), :] for j in range(16)],
                        0,
                    )
                    for half in (0, 16)
                ]
                turned = dot(permutation, jnp.concatenate(blocks, 1)).astype(BF16)
                for half in range(2):
                    for j in range(16):
                        pair, part = divmod(f + 16 * half + j, 2)
                        out[pair, pl.ds(p, 16), pl.ds(part * depth, depth)] = turned[
                            16 * j : 16 * j + 16, half * depth : (half + 1) * depth
                        ]


def prep(particles, permutation, share):
    _, freqs, depth = particles.shape
    assert share % 16 == 0 and freqs % 32 == 0
    return call(
        functools.partial(prep_kernel, share),
        [particles, permutation],
        [((freqs // 2, share, 2 * depth), BF16)] * 2,
        flops=1 << 31,
    )


def tree(values):
    values = list(values)
    while len(values) > 1:
        values = [a + b for a, b in zip(values[::2], values[1::2])]
    return values[0]


def weigh_kernel(fresh, order, count, *refs):
    sources = [refs[order.index(i)] for i in range(count)]
    doubled_ref, particles, out, energy_ref, left_ref, image, *rest = refs[count:]
    pairs, share, twice = particles.shape
    freqs, depth = 2 * pairs, twice // 2
    classes, lanes = energy_ref.shape
    pitch = freqs + SPARE
    radii = depth // 2
    lane = lax.broadcasted_iota(jnp.int32, (freqs, depth), 1)
    sign = jnp.where(lane < radii, -1.0, 1.0).astype(F32)
    doubled = jnp.concatenate([doubled_ref[...]] * 2, 1)
    row = lax.broadcasted_iota(jnp.int32, (freqs, depth), 0) + lax.axis_index("rot") * freqs
    scale = jnp.where(row == 0, 1.0 / ANG, 2.0 / ANG).astype(F32) * doubled

    for k in range(classes):
        if fresh:
            plain = sources[k][0].astype(F32)
        else:
            sums, highs, lows = [
                tree(
                    source[pl.ds(base + (k ^ i) * step, step), :].astype(F32)
                    for i, source in enumerate(sources)
                )
                for base, step in ((0, freqs), (classes * freqs, 1), (classes * (freqs + 1), 1))
            ]
            plain = (sums / (highs + lows + shrinkage)).astype(BF16).astype(F32)
        weighted = (plain * doubled).astype(BF16).astype(F32)
        image[rows(2 * k * pitch, freqs), :] = weighted
        image[rows((2 * k + 1) * pitch, freqs), :] = sign * pltpu.roll(weighted, radii, 1)
        energy = jnp.sum(plain * plain * scale, axis=0, keepdims=True)
        energy = jnp.broadcast_to(jnp.sum(energy, axis=1, keepdims=True), (SPARE, lanes))
        energy_ref[pl.ds(k, 1), :] = energy[:1]
        out[rows(2 * k * pitch + freqs, SPARE), :] = energy[:, : out.shape[1]]

    none = jnp.zeros((2 * classes, depth), BF16)

    def correlate(f):
        first, second = [
            image[pl.ds(2 * f + part, 2 * classes, stride=pitch), :].astype(BF16)
            for part in range(2)
        ]
        left = jnp.concatenate(
            [jnp.concatenate([first, none], 1), jnp.concatenate([none, second], 1)], 0
        )
        left_ref[f] = left
        place([out, *rest], f, times(left, particles[f]), classes, pitch)

    loop(pairs, correlate, 32)
    for ref in rest:
        width = share - 128
        for pack in range(-(-2 * classes * width // 128)):
            total = 0.0
            for i in range(min(128 // width, 2 * classes - pack * (128 // width))):
                group = ref[rows((pack * (128 // width) + i) * pitch, pitch), :]
                total = total + (pltpu.roll(group, i * width, 1) if i else group)
            out[rows((2 * classes + pack) * pitch, pitch), :] = total


def times(left, particles):
    return lax.dot_general(left, particles, (((1,), (1,)), ((), ())), preferred_element_type=F32)


def place(outs, f, value, classes, pitch):
    spare = jnp.zeros((value.shape[0], len(outs) * 128 - value.shape[1]), F32)
    value = jnp.concatenate([value, spare], 1) if spare.size else value
    for part in range(2):
        at = pl.ds(2 * f + part, 2 * classes, stride=pitch)
        for tile, out in enumerate(outs):
            out[at, :] = value[
                part * 2 * classes : (part + 1) * 2 * classes, tile * 128 : (tile + 1) * 128
            ]


def lane_tiles(share):
    return -(-share // 128)


def weigh(sources, order, inverse_noise, particles, fresh):
    pairs, share, twice = particles.shape
    classes = len(sources)
    pitch = 2 * pairs + SPARE
    tiles = lane_tiles(share)
    assert tiles == 1 or tiles == 2 and 128 % (share - 128) == 0
    packs = -(-2 * classes * (share - 128) // 128) if tiles == 2 else 0
    return call(
        functools.partial(weigh_kernel, fresh, order, classes),
        [*[sources[i] for i in order], inverse_noise, particles],
        [
            (((2 * classes + packs) * pitch, 128), F32),
            ((classes, tiles * 128), F32),
            ((pairs, 4 * classes, twice), BF16),
        ],
        [((2 * classes * pitch, twice // 2), F32)]
        + [((2 * classes * pitch, 128), F32)] * (tiles - 1),
        flops=8 * classes * share * pairs * twice * 4,
    )


def correlate_kernel(left_ref, particles, out):
    pairs = left_ref.shape[0]
    classes = left_ref.shape[1] // 4

    def body(f):
        outs = [out.at[tile] for tile in range(out.shape[0])]
        place(outs, f, times(left_ref[f], particles[f]), classes, 2 * pairs + SPARE)

    loop(pairs, body, 32)


def correlate(left, particles):
    pairs, share, twice = particles.shape
    lines = left.shape[1] // 2 * (2 * pairs + SPARE)
    return call(
        correlate_kernel,
        [left, particles],
        [((lane_tiles(share), lines, 128), F32)],
        flops=2 * left.shape[1] * share * pairs * twice * 8,
    )[0]


def across(ref, at):
    return jnp.concatenate([ref[tile, at, :] for tile in range(ref.shape[0])], 1)


def table_rows(base, count):
    return pl.ds(pl.multiple_of(lax.axis_index("rot") * ANG + base, 128), count)


def score_kernel(particles, own, other, energy_ref, prior_term, inverse, *refs):
    weights, tops, peaks = refs
    classes, share = energy_ref.shape
    tiles, lines, width = own.shape
    pitch = lines // (2 * classes)
    freqs = pitch - SPARE
    which = table_rows(0, ANG)

    def unpacked(group):
        first = other[rows(group * pitch, freqs), :]
        if tiles == 1:
            return first
        width = particles - 128
        bundle = 128 // width
        packed = other[rows((2 * classes + group // bundle) * pitch, freqs), :]
        back = (bundle - group % bundle) % bundle * width
        return jnp.concatenate([first, pltpu.roll(packed, back, 1)], 1)

    def score(k, carry):
        near = [across(own, rows((2 * k + part) * pitch, freqs)) for part in range(2)]
        far = [unpacked(2 * k + part) for part in range(2)]
        high, low = split(jnp.concatenate(near + far, 0))
        inner = dot(inverse[which, :], jnp.concatenate([high, low, high], 0))
        far = other[rows(2 * k * pitch + freqs, SPARE), :][:1]
        energy = energy_ref[pl.ds(k, 1), :] + jnp.concatenate([far] * tiles, 1)
        scores = inner - 0.5 * energy + prior_term[...]
        top = jnp.max(scores, axis=0, keepdims=True)
        value = jnp.exp(scores - top)
        weights[k] = value
        total = jnp.sum(value, axis=0, keepdims=True)
        tops[pl.ds(k, 1), :] = top
        return merge(carry, (top, total))

    first = (jnp.full((1, share), -jnp.inf, F32), jnp.zeros((1, share), F32))
    top, total = each(classes, score, first)
    line = lax.broadcasted_iota(jnp.int32, peaks.shape, 0)
    peaks[...] = jnp.where(line == 0, top, total)


def scores(own, other, energy, prior_term, inverse, particles):
    classes, lanes = energy.shape
    return call(
        functools.partial(score_kernel, particles),
        [own, other, energy, prior_term, inverse],
        [((classes, ANG, lanes), F32), ((classes, lanes), F32), ((8, lanes), F32)],
        flops=6 * classes * lanes * ANG * ANG,
    )


def merge(first, second):
    top = jnp.maximum(first[0], second[0])
    return top, first[1] * jnp.exp(first[0] - top) + second[1] * jnp.exp(second[0] - top)


def two_lines(ref):
    return ref[0:1, :], ref[1:2, :]


def merge_kernel(first, second, out):
    top, total = merge(two_lines(first), two_lines(second))
    line = lax.broadcasted_iota(jnp.int32, out.shape, 0)
    out[...] = jnp.where(line == 0, top, total)


def turn_kernel(share, weights, tops, first, second, forward, *refs):
    rounded_ref, send, *evidence_ref, held = refs
    classes, _, lanes = weights.shape
    pairs = (held.shape[1] // (2 * classes) - SPARE) // 2
    top, total = merge(two_lines(first), two_lines(second))
    for ref in evidence_ref:
        ref[...] = (top + jnp.log(total))[:, :share]
    lane = lax.broadcasted_iota(jnp.int32, (1, lanes), 1)
    inverse_total = jnp.where(lane < share, 1.0 / total, 0.0)
    which = table_rows(0, ANG // 2)
    line = lax.broadcasted_iota(jnp.int32, (4 * classes, share), 0)

    def body(k, column):
        value = weights[k] * (jnp.exp(tops[pl.ds(k, 1), :] - top) * inverse_total)
        count = jnp.sum(jnp.sum(value, axis=0, keepdims=True), axis=1, keepdims=True)
        rounded = value.astype(BF16)
        rounded_ref[k] = rounded
        spread(held, k, dot(forward[which, :], jnp.concatenate([rounded, rounded], 0)))
        high = count.astype(BF16).astype(F32)
        return jnp.where(line == k, high, jnp.where(line == classes + k, count - high, column))

    column = each(classes, body, jnp.zeros((4 * classes, share), F32))
    send[pairs] = column.astype(BF16)

    def rearrange(f):
        send[f] = pick(held, f, classes, share)

    loop(pairs, rearrange, 32)


def spread(held, k, value):
    tiles, lines, width = held.shape
    freqs = value.shape[0] // 2
    for part in range(2):
        for tile in range(tiles):
            held[tile, rows((2 * k + part) * (freqs + SPARE), freqs), :] = value[
                part * freqs : (part + 1) * freqs, tile * width : (tile + 1) * width
            ]


def pick(held, f, classes, share):
    pitch = held.shape[1] // (2 * classes)
    parts = [
        across(held, pl.ds(2 * f + part, 2 * classes, stride=pitch)).astype(BF16)
        for part in range(2)
    ]
    return jnp.concatenate(parts, 0)[:, :share]


def turn(weights, tops, first, second, forward, freqs, share, last):
    classes, _, lanes = weights.shape
    return call(
        functools.partial(turn_kernel, share),
        [weights, tops, first, second, forward],
        [
            ((classes, ANG, lanes), BF16),
            ((freqs // 2 + 1, 4 * classes, share), BF16),
            *([((1, share), F32)] if last else []),
        ],
        [((lanes // 128, 2 * classes * (freqs + SPARE), 128), F32)],
        flops=4 * classes * lanes * ANG * ANG,
    )


def gather_kernel(rounded_ref, forward, particles, image, held):
    classes = rounded_ref.shape[0]
    pairs, share, _ = particles.shape
    which = table_rows(ANG // 2, ANG // 2)

    def body(k, carry):
        rounded = rounded_ref[k]
        spread(held, k, dot(forward[which, :], jnp.concatenate([rounded, rounded], 0)))
        return carry

    each(classes, body, 0)

    def accumulate(f):
        take_in(image, f, dot(pick(held, f, classes, share), particles[f]), classes)

    loop(pairs, accumulate, 32)


def gather(rounded, forward, particles):
    pairs, share, twice = particles.shape
    classes, _, lanes = rounded.shape
    lines = 2 * classes * (2 * pairs + SPARE)
    return call(
        gather_kernel,
        [rounded, forward, particles],
        [((lines, twice // 2), F32)],
        [((lanes // 128, lines, 128), F32)],
        flops=4 * classes * lanes * ANG * ANG,
    )[0]


def take_in(image, f, value, classes):
    lines, depth = image.shape
    for part in range(2):
        at = pl.ds(2 * f + part, 2 * classes, stride=lines // (2 * classes))
        image[at, :] = value[
            part * 2 * classes : (part + 1) * 2 * classes, part * depth : (part + 1) * depth
        ]


def finish_kernel(image, mine, spectrum, particles, *refs):
    outs, held = refs[:-1], refs[-1]
    pairs, _, twice = particles.shape
    classes = spectrum.shape[1] // 4
    freqs, depth = 2 * pairs, twice // 2
    radii = depth // 2
    pitch = freqs + SPARE

    def body(f):
        take_in(held, f, dot(spectrum[f], particles[f]), classes)

    loop(pairs, body, 32)
    counts = (mine[pairs].astype(F32) + spectrum[pairs].astype(F32))[:, :depth]
    counts = counts[:classes] + counts[classes : 2 * classes]
    lane = lax.broadcasted_iota(jnp.int32, (freqs, depth), 1)
    sign = jnp.where(lane < radii, -1.0, 1.0).astype(F32)
    for k in range(classes):
        plain, turned = [
            image[rows((2 * k + part) * pitch, freqs), :]
            + held[rows((2 * k + part) * pitch, freqs), :]
            for part in range(2)
        ]
        value = plain + sign * pltpu.roll(turned, radii, 1)
        if len(outs) == 1:
            outs[0][pl.ds(k * freqs, freqs), :] = value.astype(BF16)
        else:
            outs[k][pl.ds(0, freqs), :] = value
            outs[k][pl.ds(freqs, SPARE), :] = jnp.broadcast_to(counts[k : k + 1], (SPARE, depth))
    if len(outs) == 1:
        end = outs[0].shape[0] - classes * freqs
        high, low = split(counts)
        spare = [jnp.zeros((end - 2 * classes, depth), F32)] if end > 2 * classes else []
        tail = jnp.concatenate([high.astype(F32), low.astype(F32), *spare], 0)
        outs[0][pl.ds(classes * freqs, end), :] = tail.astype(BF16)


def finish(image, mine, spectrum, particles, last):
    pairs, _, twice = particles.shape
    classes = spectrum.shape[1] // 4
    freqs, depth = 2 * pairs, twice // 2
    if last:
        outs = [((freqs + SPARE, depth), F32)] * classes
    else:
        outs = [((classes * freqs + -(-2 * classes // 16) * 16, depth), BF16)]
    return call(
        finish_kernel,
        [image, mine, spectrum, particles],
        outs,
        [(image.shape, F32)],
        flops=2 * math.prod(spectrum.shape) * twice * 8,
    )


def means_kernel(*refs):
    *parts, evidence_ref, out, last_ref = refs
    last_ref[...] = evidence_ref[...]
    freqs = out.shape[1]
    total = tree(ref[...] for ref in parts)
    out[0] = total[:freqs, :] / (total[freqs : freqs + 1, :] + shrinkage)


def swap(value, axis, size, bit):
    if not bit:
        return value
    return lax.ppermute(value, axis, [(i, i ^ bit) for i in range(size)])


def bits(size):
    assert size > 1 and size & (size - 1) == 0
    return [1 << i for i in range(size.bit_length() - 1)]


def shards(particles, references, noise_inv, prior_rot):
    batch, freqs, depth = particles.shape
    sides = lax.axis_size("cls")
    groups = lax.axis_size("rot")
    blocks = lax.axis_size("blk")
    assert groups == 2 and 2 * groups * freqs == ANG
    share = batch // groups
    inverse, forward = tables(freqs)
    inverse_noise = noise_inv.reshape(1, depth // 2)
    assert blocks & (blocks - 1) == 0
    turns = sorted(range(1, blocks), key=lambda i: (-i.bit_length(), i))

    (permutation,) = call(permutation_kernel, [], [((256, 256), BF16)], flops=1 << 32)
    (prior_term,) = call(
        prior_kernel, [prior_rot], [((ANG, lane_tiles(share) * 128), F32)], flops=1 << 26
    )
    sources = {i: swap(references, "blk", blocks, i) for i in (*turns, 0)}
    other_images, own_images = prep(particles, permutation, share)
    for step in range(ITERS):
        last = step == ITERS - 1
        order = [0, *(reversed(turns) if step else reversed(range(1, blocks)))]
        message, energy, left = weigh(sources, order, inverse_noise, other_images, step == 0)
        message = swap(message, "rot", groups, 1)
        own = correlate(left, own_images)
        weights, tops, here = scores(own, message, energy, prior_term, inverse, share)
        first = here
        for bit in bits(sides):
            second = swap(first, "cls", sides, bit)
            if 2 * bit < sides:
                (first,) = call(merge_kernel, [first, second], [(here.shape, F32)])
        rounded, send, *evidence = turn(
            weights, tops, first, second, forward, freqs, share, last
        )
        message = swap(send, "rot", groups, 1)
        image = gather(rounded, forward, own_images)
        sums = finish(image, send, message, other_images, last)
        sums = sums if last else sums * blocks
        sources = {i: swap(sums[i], "blk", blocks, i) for i in (*turns, 0)}
    means, evidence = call(
        means_kernel, [*[sources[i] for i in turns], sources[0], *evidence], [((1, freqs, depth), F32), ((1, share), F32)]
    )
    return means, evidence.reshape(share)


def solution(mesh):
    in_specs = (
        P(("grp", "blk"), "rot", None),
        P(("grp", "blk", "cls"), "rot", None),
        P(),
        P(("grp", "blk")),
    )
    out_specs = (P(("grp", "blk", "cls"), "rot", None), P(("grp", "blk", "rot")))
    return jax.shard_map(shards, mesh=mesh, in_specs=in_specs, out_specs=out_specs, check_vma=False)
```

```python
import functools
import math

import jax
import jax.numpy as jnp
import numpy as np
from jax import lax
from jax.experimental import pallas as pl
from jax.experimental.pallas import tpu as pltpu
from jax.sharding import PartitionSpec as P

ANG = 256
ITERS = 2
SIGMA = 32

shrinkage = 1.0

F32 = jnp.float32
BF16 = jnp.bfloat16
SPARE = 8

dot = functools.partial(jnp.dot, preferred_element_type=F32)


def split(x):
    high = x.astype(BF16)
    return high, (x - high.astype(F32)).astype(BF16)


def tables(half_freq):
    turn = np.arange(ANG)
    inverse, forward = [], []
    for group in range(2):
        sides = {}
        for which in range(2):
            freq = which * half_freq + np.arange(half_freq)
            angle = (turn[:, None] * freq[None, :] % ANG) * (2.0 * math.pi / ANG)
            scale = np.where(freq == 0, 1.0, 2.0) / ANG
            sides[which] = (
                np.concatenate([scale * np.cos(angle), -scale * np.sin(angle)], 1),
                np.concatenate([np.cos(angle), np.sin(angle)], 1).T,
            )
        inverse.append(np.concatenate([sides[group][0], sides[1 - group][0]], 1))
        forward.append(np.concatenate([sides[1 - group][1], sides[group][1]], 0))
    result = []
    for table, kinds in ((inverse, (0, 0, 1)), (forward, (0, 1))):
        table = np.concatenate(table, 0).astype(np.float32)
        high = table.astype(BF16)
        parts = [high, (table - high.astype(np.float32)).astype(BF16)]
        result.append(jnp.asarray(np.concatenate([parts[kind] for kind in kinds], 1)))
    return result


def loop(count, body, unroll):
    while count % unroll:
        unroll -= 1
    if unroll == count:
        for i in range(count):
            body(i)
        return

    def step(outer, carry):
        for inner in range(unroll):
            body(outer * unroll + inner)
        return carry

    lax.fori_loop(0, count // unroll, step, 0)


def each(count, body, init):
    if count <= 8:
        for k in range(count):
            init = body(k, init)
        return init
    return lax.fori_loop(0, count, body, init)


def rows(base, count):
    return pl.ds(pl.multiple_of(base, 8), count)


def call(kernel, ins, outs, scratch=(), flops=0, far=(), room=4 << 20):
    total = 0
    buffers = [(x.shape, x.dtype) for i, x in enumerate(ins) if i not in far]
    for shape, dtype in buffers + list(outs) + [x for x in scratch if isinstance(x, tuple)]:
        dims = [1, 1, *shape]
        lines = -(-dims[-2] // 16) * 16
        lanes = -(-dims[-1] // 128) * 128
        total += math.prod(dims[:-2]) * lines * lanes * jnp.dtype(dtype).itemsize
    kinds = [pltpu.VMEM] * len(ins)
    for i in far:
        kinds[i] = pltpu.MemorySpace.HBM
    return pl.pallas_call(
        kernel,
        out_shape=[jax.ShapeDtypeStruct(*x) for x in outs],
        in_specs=[pl.BlockSpec(memory_space=kind) for kind in kinds],
        out_specs=[pl.BlockSpec(memory_space=pltpu.VMEM)] * len(outs),
        scratch_shapes=[pltpu.VMEM(*x) if isinstance(x, tuple) else x for x in scratch],
        compiler_params=pltpu.CompilerParams(vmem_limit_bytes=min(total + room, 56 << 20)),
        cost_estimate=pl.CostEstimate(flops=flops, bytes_accessed=total, transcendentals=0),
    )(*ins)


def permutation_kernel(out):
    to = lax.broadcasted_iota(jnp.int32, out.shape, 0)
    at = lax.broadcasted_iota(jnp.int32, out.shape, 1)
    out[...] = ((to // 16 == at % 16) & (to % 16 == at // 16)).astype(F32).astype(BF16)


def prior_kernel(share, prior_ref, prior_term):
    turns = lax.broadcasted_iota(jnp.int32, (ANG, 256), 0)
    lane = lax.broadcasted_iota(jnp.int32, (1, 256), 1)
    priors = prior_ref[...].reshape(1, -1)
    first, second = [
        jnp.concatenate([priors[:, i * share : (i + 1) * share], lane[:, share:]], 1)
        for i in range(2)
    ]
    offset = jnp.abs(turns - jnp.where(lax.axis_index("rot") == 0, first, second))
    distance = jnp.minimum(offset, ANG - offset).astype(F32)
    term = -distance * distance / (2.0 * SIGMA * SIGMA)
    prior_term[:, :128] = term[:, :128]
    prior_term[:, 128:] = repeat(term[:, 128:], share - 128, 128 // (share - 128))


def turned(value, lanes):
    return pltpu.roll(value, lanes % 128, 1) if lanes % 128 else value


def repeat(value, width, times):
    lane = lax.broadcasted_iota(jnp.int32, value.shape, 1)
    value = jnp.where(lane < width, value, 0.0)
    return sum(turned(value, i * width) for i in range(times))


def layout(classes, share):
    width = share - 128
    assert 0 < width < 128 and 128 % width == 0 and classes % 2 == 0
    bundle = min(128 // width, classes)
    assert classes % bundle == 0
    return width, bundle, classes // bundle


def prep_kernel(share, particles_ref, permutation_ref, other, own):
    freqs, depth = particles_ref.shape[1:]
    group = lax.axis_index("rot")
    permutation = permutation_ref[...]
    for out, first in ((other, (1 - group) * share), (own, group * share)):
        for p in range(0, share, 16):
            for f in range(0, freqs, 32):
                blocks = [
                    jnp.concatenate(
                        [particles_ref[first + p + j, pl.ds(f + half, 16), :] for j in range(16)],
                        0,
                    )
                    for half in (0, 16)
                ]
                turned = dot(permutation, jnp.concatenate(blocks, 1)).astype(BF16)
                for half in range(2):
                    for j in range(16):
                        pair, part = divmod(f + 16 * half + j, 2)
                        out[pair, pl.ds(p, 16), pl.ds(part * depth, depth)] = turned[
                            16 * j : 16 * j + 16, half * depth : (half + 1) * depth
                        ]


def prep(particles, permutation, share):
    _, freqs, depth = particles.shape
    assert share % 16 == 0 and freqs % 32 == 0
    return call(
        functools.partial(prep_kernel, share),
        [particles, permutation],
        [((freqs // 2, share, 2 * depth), BF16)] * 2,
        flops=1 << 31,
    )


def tree(values):
    values = list(values)
    while len(values) > 1:
        values = [a + b for a, b in zip(values[::2], values[1::2])]
    return values[0]


def weigh_kernel(fresh, order, count, *refs):
    sources = [refs[order.index(i)] for i in range(count)]
    doubled_ref, particles, out, energy_ref, left_ref, image, rest = refs[count:]
    pairs, share, twice = particles.shape
    freqs, depth = 2 * pairs, twice // 2
    classes = energy_ref.shape[0]
    pitch = freqs + SPARE
    radii = depth // 2
    lane = lax.broadcasted_iota(jnp.int32, (freqs, depth), 1)
    sign = jnp.where(lane < radii, -1.0, 1.0).astype(F32)
    doubled = jnp.concatenate([doubled_ref[...]] * 2, 1)
    row = lax.broadcasted_iota(jnp.int32, (freqs, depth), 0) + lax.axis_index("rot") * freqs
    scale = jnp.where(row == 0, 1.0 / ANG, 2.0 / ANG).astype(F32) * doubled

    for k in range(classes):
        if fresh:
            plain = sources[k][0].astype(F32)
        else:
            sums, highs, lows = [
                tree(
                    source[pl.ds(base + (k ^ i) * step, step), :].astype(F32)
                    for i, source in enumerate(sources)
                )
                for base, step in ((0, freqs), (classes * freqs, 1), (classes * (freqs + 1), 1))
            ]
            plain = (sums / (highs + lows + shrinkage)).astype(BF16).astype(F32)
        weighted = (plain * doubled).astype(BF16).astype(F32)
        image[rows(2 * k * pitch, freqs), :] = weighted
        image[rows((2 * k + 1) * pitch, freqs), :] = sign * pltpu.roll(weighted, radii, 1)
        energy = jnp.sum(plain * plain * scale, axis=0, keepdims=True)
        energy = jnp.broadcast_to(jnp.sum(energy, axis=1, keepdims=True), (SPARE, 128))
        energy_ref[pl.ds(k, 1), :] = energy[:1]
        out[rows(2 * k * pitch + freqs, SPARE), :] = energy

    none = jnp.zeros((2 * classes, depth), BF16)

    def correlate(f):
        first, second = [
            image[pl.ds(2 * f + part, 2 * classes, stride=pitch), :].astype(BF16)
            for part in range(2)
        ]
        left = jnp.concatenate(
            [jnp.concatenate([first, none], 1), jnp.concatenate([none, second], 1)], 0
        )
        left_ref[f] = left
        place(out, rest, f, times(left, particles[f]), classes, pitch)

    loop(pairs, correlate, 32)
    pack(out, rest, classes, share, pitch)


def times(left, particles):
    return lax.dot_general(left, particles, (((1,), (1,)), ((), ())), preferred_element_type=F32)


def place(out, rest, f, value, classes, pitch):
    width = value.shape[1] - 128
    spare = jnp.zeros((value.shape[0], 128 - width), F32)
    value = jnp.concatenate([value, spare], 1)
    for part in range(2):
        at = pl.ds(2 * f + part, 2 * classes, stride=pitch)
        mine = value[part * 2 * classes : (part + 1) * 2 * classes]
        out[at, :] = mine[:, :128]
        rest[at, :] = mine[:, 128:]


def pack(out, rest, classes, share, pitch):
    width = share - 128
    each_pack = 128 // width
    for first in range(0, 2 * classes, each_pack):
        total = 0.0
        for group in range(first, min(first + each_pack, 2 * classes)):
            part, k = divmod(group, classes)
            value = rest[rows((2 * k + part) * pitch, pitch), :]
            total = total + turned(value, (group - first) * width)
        out[rows((2 * classes + first // each_pack) * pitch, pitch), :] = total


def unpack(ref, unit, part, classes, share, pitch, freqs):
    width, bundle, _ = layout(classes, share)
    group = part * classes + unit * bundle
    each_pack = 128 // width
    value = ref[rows((2 * classes + group // each_pack) * pitch, freqs), :]
    return turned(value, -(group % each_pack) * width)


def corr_lines(classes, share, pitch):
    return (2 * classes + -(-2 * classes * (share - 128) // 128)) * pitch


def weigh(sources, order, inverse_noise, particles, fresh):
    pairs, share, twice = particles.shape
    classes = len(sources)
    pitch = 2 * pairs + SPARE
    return call(
        functools.partial(weigh_kernel, fresh, order, classes),
        [*[sources[i] for i in order], inverse_noise, particles],
        [
            ((corr_lines(classes, share, pitch), 128), F32),
            ((classes, 128), F32),
            ((pairs, 4 * classes, twice), BF16),
        ],
        [((2 * classes * pitch, twice // 2), F32), ((2 * classes * pitch, 128), F32)],
        flops=8 * classes * share * pairs * twice * 4,
    )


def correlate_kernel(left_ref, particles, out, rest):
    pairs, share, _ = particles.shape
    classes = left_ref.shape[1] // 4
    pitch = 2 * pairs + SPARE

    def body(f):
        place(out, rest, f, times(left_ref[f], particles[f]), classes, pitch)

    loop(pairs, body, 32)
    pack(out, rest, classes, share, pitch)


def correlate(left, particles):
    pairs, share, twice = particles.shape
    classes = left.shape[1] // 4
    pitch = 2 * pairs + SPARE
    return call(
        correlate_kernel,
        [left, particles],
        [((corr_lines(classes, share, pitch), 128), F32)],
        [((2 * classes * pitch, 128), F32)],
        flops=2 * left.shape[1] * share * pairs * twice * 8,
    )[0]


def table_rows(base, count):
    return pl.ds(pl.multiple_of(lax.axis_index("rot") * ANG + base, 128), count)


def score_kernel(share, own, other, energy_ref, prior_term, inverse, *refs):
    weights, more, tops, more_tops, peaks = refs
    classes = energy_ref.shape[0]
    width, bundle, units = layout(classes, share)
    freqs = ANG // 4
    pitch = freqs + SPARE
    at = table_rows(0, ANG)
    lane = lax.broadcasted_iota(jnp.int32, (1, 128), 1)

    def exponentials(value, energy, prior):
        high, low = split(value)
        inner = dot(inverse[at, :], jnp.concatenate([high, low, high], 0))
        scores = inner - 0.5 * energy + prior
        top = jnp.max(scores, axis=0, keepdims=True)
        value = jnp.exp(scores - top)
        return value, top, jnp.sum(value, axis=0, keepdims=True)

    def energy_of(k):
        return energy_ref[pl.ds(k, 1), :] + other[rows(2 * k * pitch + freqs, SPARE), :][:1]

    def slab(i, carry):
        value = jnp.concatenate(
            [
                jnp.concatenate(
                    [ref[rows((4 * i + 2 * j + part) * pitch, freqs), :] for j in range(2)], 1
                )
                for ref in (own, other)
                for part in range(2)
            ],
            0,
        )
        energy = jnp.concatenate([energy_of(2 * i), energy_of(2 * i + 1)], 1)
        prior = jnp.concatenate([prior_term[:, :128]] * 2, 1)
        weights[i], top, total = exponentials(value, energy, prior)
        tops[pl.ds(i, 1), :] = top
        for j in (0, 128):
            carry = merge(carry, (top[:, j : j + 128], total[:, j : j + 128]))
        return carry

    empty = (jnp.full((1, 128), -jnp.inf, F32), jnp.zeros((1, 128), F32))
    top, total = each(classes // 2, slab, empty)
    rest = empty
    for unit in range(units):
        value = jnp.concatenate(
            [
                unpack(ref, unit, part, classes, share, pitch, freqs)
                for ref in (own, other)
                for part in range(2)
            ],
            0,
        )
        energy = sum(
            jnp.where(lane // width == j, energy_of(unit * bundle + j), 0.0)
            for j in range(bundle)
        )
        more[unit], more_top, more_total = exponentials(value, energy, prior_term[:, 128:])
        more_tops[pl.ds(unit, 1), :] = more_top
        for j in range(bundle):
            rest = merge(rest, (turned(more_top, -j * width), turned(more_total, -j * width)))
    line = lax.broadcasted_iota(jnp.int32, peaks.shape, 0)
    peaks[...] = jnp.where(
        line == 0,
        jnp.concatenate([top, rest[0]], 1),
        jnp.concatenate([total, rest[1]], 1),
    )


def scores(own, other, energy, prior_term, inverse, share):
    classes = energy.shape[0]
    units = layout(classes, share)[2]
    return call(
        functools.partial(score_kernel, share),
        [own, other, energy, prior_term, inverse],
        [
            ((classes // 2, ANG, 256), F32),
            ((units, ANG, 128), F32),
            ((classes // 2, 256), F32),
            ((units, 128), F32),
            ((8, 256), F32),
        ],
        flops=6 * classes * 256 * ANG * ANG,
    )


def merge(first, second):
    top = jnp.maximum(first[0], second[0])
    return top, first[1] * jnp.exp(first[0] - top) + second[1] * jnp.exp(second[0] - top)


def two_lines(ref):
    return ref[0:1, :], ref[1:2, :]


def merge_kernel(first, second, out):
    top, total = merge(two_lines(first), two_lines(second))
    line = lax.broadcasted_iota(jnp.int32, out.shape, 0)
    out[...] = jnp.where(line == 0, top, total)


def turn_kernel(share, weights, more, tops, more_tops, first, second, forward, *refs):
    rounded_ref, rounded_more, send, *evidence_ref, held = refs
    classes = 2 * weights.shape[0]
    width, bundle, units = layout(classes, share)
    pairs = (held.shape[0] // (2 * classes) - SPARE) // 2
    top, total = merge(two_lines(first), two_lines(second))
    for ref in evidence_ref:
        ref[...] = (top + jnp.log(total))[:, :share]
    scale = 1.0 / total
    at = table_rows(0, ANG // 2)
    lane = lax.broadcasted_iota(jnp.int32, (1, 128), 1)
    line = lax.broadcasted_iota(jnp.int32, (4 * classes, 128), 0)

    def put(column, k, count):
        high = count.astype(BF16).astype(F32)
        return jnp.where(line == k, high, jnp.where(line == classes + k, count - high, column))

    more_counts = []
    for unit in range(units):
        factor = jnp.exp(
            more_tops[pl.ds(unit, 1), :] - repeat(top[:, 128:], width, bundle)
        ) * repeat(scale[:, 128:], width, bundle)
        value = more[unit] * jnp.where(lane < bundle * width, factor, 0.0)
        count = jnp.sum(value, axis=0, keepdims=True)
        for j in range(bundle):
            mine = jnp.where(lane // width == j, count, 0.0)
            more_counts.append(jnp.sum(mine, axis=1, keepdims=True))
        rounded = value.astype(BF16)
        rounded_more[unit] = rounded
        spectrum = dot(forward[at, :], jnp.concatenate([rounded, rounded], 0)).astype(BF16)
        step = 4 * classes
        entries = spectrum.shape[0] // step
        for i in range(entries):
            send[pairs + unit * entries + i] = spectrum[i * step : (i + 1) * step]

    tops_here = jnp.concatenate([top[:, :128]] * 2, 1)
    scale_here = jnp.concatenate([scale[:, :128]] * 2, 1)

    def body(i, column):
        value = weights[i] * (jnp.exp(tops[pl.ds(i, 1), :] - tops_here) * scale_here)
        rounded = value.astype(BF16)
        rounded_ref[i] = rounded
        spread(held, i, dot(forward[at, :], jnp.concatenate([rounded, rounded], 0)))
        count = jnp.sum(value, axis=0, keepdims=True)
        for j in range(2):
            mine = jnp.sum(count[:, j * 128 : (j + 1) * 128], axis=1, keepdims=True)
            column = put(column, 2 * i + j, mine)
        return column

    column = each(classes // 2, body, jnp.zeros((4 * classes, 128), F32))
    extra = jnp.zeros((4 * classes, 128), F32)
    for k, count in enumerate(more_counts):
        extra = put(extra, k, count)
    send[send.shape[0] - 2] = column.astype(BF16)
    send[send.shape[0] - 1] = extra.astype(BF16)

    def rearrange(f):
        send[f] = pick(held, f, classes).astype(BF16)

    loop(pairs, rearrange, 32)


def spread(held, i, value):
    freqs = value.shape[0] // 2
    for j in range(2):
        for part in range(2):
            held[rows((4 * i + 2 * j + part) * (freqs + SPARE), freqs), :] = value[
                part * freqs : (part + 1) * freqs, j * 128 : (j + 1) * 128
            ]


def spread_more(held, unit, value, classes, share):
    width, bundle, _ = layout(classes, share)
    freqs = value.shape[0] // 2
    for j in range(bundle):
        shifted = turned(value, -j * width)
        for part in range(2):
            k = unit * bundle + j
            held[rows((2 * k + part) * (freqs + SPARE), freqs), :] = shifted[
                part * freqs : (part + 1) * freqs
            ]


def pick(held, f, classes):
    pitch = held.shape[0] // (2 * classes)
    return jnp.concatenate(
        [held[pl.ds(2 * f + part, 2 * classes, stride=pitch), :] for part in range(2)], 0
    )


def message_shape(classes, pairs, units):
    return (pairs + units * (ANG // 2) // (4 * classes) + 2, 4 * classes, 128)


def turn(weights, more, tops, more_tops, first, second, forward, freqs, share, last):
    classes = 2 * weights.shape[0]
    units = more.shape[0]
    return call(
        functools.partial(turn_kernel, share),
        [weights, more, tops, more_tops, first, second, forward],
        [
            (weights.shape, BF16),
            (more.shape, BF16),
            (message_shape(classes, freqs // 2, units), BF16),
            *([((1, share), F32)] if last else []),
        ],
        [((2 * classes * (freqs + SPARE), 128), F32)],
        flops=4 * classes * 256 * ANG * ANG,
    )


def gather_kernel(rounded_ref, rounded_more, forward, particles, image, held, held_more):
    classes = 2 * rounded_ref.shape[0]
    pairs, share, _ = particles.shape
    at = table_rows(ANG // 2, ANG // 2)

    for unit in range(rounded_more.shape[0]):
        rounded = rounded_more[unit]
        value = dot(forward[at, :], jnp.concatenate([rounded, rounded], 0))
        spread_more(held_more, unit, value, classes, share)

    def body(i, carry):
        rounded = rounded_ref[i]
        spread(held, i, dot(forward[at, :], jnp.concatenate([rounded, rounded], 0)))
        return carry

    each(classes // 2, body, 0)

    def accumulate(f):
        left = [pick(ref, f, classes).astype(BF16) for ref in (held, held_more)]
        left = jnp.concatenate(left, 1)[:, :share]
        take_in(image, f, dot(left, particles[f]), classes)

    loop(pairs, accumulate, 32)


def gather(rounded, rounded_more, forward, particles):
    pairs, share, twice = particles.shape
    classes = 2 * rounded.shape[0]
    lines = 2 * classes * (2 * pairs + SPARE)
    return call(
        gather_kernel,
        [rounded, rounded_more, forward, particles],
        [((lines, twice // 2), F32)],
        [((lines, 128), F32)] * 2,
        flops=4 * classes * 256 * ANG * ANG,
    )[0]


def take_in(image, f, value, classes):
    lines, depth = image.shape
    for part in range(2):
        at = pl.ds(2 * f + part, 2 * classes, stride=lines // (2 * classes))
        image[at, :] = value[
            part * 2 * classes : (part + 1) * 2 * classes, part * depth : (part + 1) * depth
        ]


def finish_kernel(image, mine, spectrum, particles, *refs):
    *outs, held, held_more = refs
    pairs, share, twice = particles.shape
    classes = spectrum.shape[1] // 4
    freqs, depth = 2 * pairs, twice // 2
    radii = depth // 2
    pitch = freqs + SPARE

    units = layout(classes, share)[2]
    entries = ANG // 2 // (4 * classes)
    for unit in range(units):
        first = pairs + unit * entries
        value = jnp.concatenate([spectrum[first + i] for i in range(entries)], 0)
        spread_more(held_more, unit, value.astype(F32), classes, share)

    def body(f):
        left = jnp.concatenate([spectrum[f], pick(held_more, f, classes).astype(BF16)], 1)
        take_in(held, f, dot(left[:, :share], particles[f]), classes)

    loop(pairs, body, 32)
    end = spectrum.shape[0]
    counts = sum(ref[i].astype(F32) for ref in (mine, spectrum) for i in (end - 2, end - 1))
    counts = counts[:classes] + counts[classes : 2 * classes]
    lane = lax.broadcasted_iota(jnp.int32, (freqs, depth), 1)
    sign = jnp.where(lane < radii, -1.0, 1.0).astype(F32)
    for k in range(classes):
        plain, turned = [
            image[rows((2 * k + part) * pitch, freqs), :]
            + held[rows((2 * k + part) * pitch, freqs), :]
            for part in range(2)
        ]
        value = plain + sign * pltpu.roll(turned, radii, 1)
        if len(outs) == 1:
            outs[0][pl.ds(k * freqs, freqs), :] = value.astype(BF16)
        else:
            outs[k][pl.ds(0, freqs), :] = value
            outs[k][pl.ds(freqs, SPARE), :] = jnp.broadcast_to(counts[k : k + 1], (SPARE, depth))
    if len(outs) == 1:
        end = outs[0].shape[0] - classes * freqs
        high, low = split(counts)
        spare = [jnp.zeros((end - 2 * classes, depth), F32)] if end > 2 * classes else []
        tail = jnp.concatenate([high.astype(F32), low.astype(F32), *spare], 0)
        outs[0][pl.ds(classes * freqs, end), :] = tail.astype(BF16)


def finish(image, mine, spectrum, particles, last):
    pairs, _, twice = particles.shape
    classes = spectrum.shape[1] // 4
    freqs, depth = 2 * pairs, twice // 2
    if last:
        outs = [((freqs + SPARE, depth), F32)] * classes
    else:
        outs = [((classes * freqs + -(-2 * classes // 16) * 16, depth), BF16)]
    return call(
        finish_kernel,
        [image, mine, spectrum, particles],
        outs,
        [(image.shape, F32)] * 2,
        flops=2 * math.prod(spectrum.shape) * twice * 8,
    )


def means_kernel(*refs):
    *parts, evidence_ref, out, last_ref = refs
    last_ref[...] = evidence_ref[...]
    freqs = out.shape[1]
    total = tree(ref[...] for ref in parts)
    out[0] = total[:freqs, :] / (total[freqs : freqs + 1, :] + shrinkage)


def swap(value, axis, size, bit):
    if not bit:
        return value
    return lax.ppermute(value, axis, [(i, i ^ bit) for i in range(size)])


def bits(size):
    assert size > 1 and size & (size - 1) == 0
    return [1 << i for i in range(size.bit_length() - 1)]


def shards(particles, references, noise_inv, prior_rot):
    batch, freqs, depth = particles.shape
    sides = lax.axis_size("cls")
    groups = lax.axis_size("rot")
    blocks = lax.axis_size("blk")
    assert groups == 2 and 2 * groups * freqs == ANG
    share = batch // groups
    inverse, forward = tables(freqs)
    inverse_noise = noise_inv.reshape(1, depth // 2)
    assert blocks & (blocks - 1) == 0
    turns = sorted(range(1, blocks), key=lambda i: (-i.bit_length(), i))

    (permutation,) = call(permutation_kernel, [], [((256, 256), BF16)], flops=1 << 32)
    (prior_term,) = call(
        functools.partial(prior_kernel, share), [prior_rot], [((ANG, 256), F32)], flops=1 << 26
    )
    sources = {i: swap(references, "blk", blocks, i) for i in (*turns, 0)}
    other_images, own_images = prep(particles, permutation, share)
    for step in range(ITERS):
        last = step == ITERS - 1
        order = [0, *(reversed(turns) if step else reversed(range(1, blocks)))]
        message, energy, left = weigh(sources, order, inverse_noise, other_images, step == 0)
        message = swap(message, "rot", groups, 1)
        own = correlate(left, own_images)
        *weights, here = scores(own, message, energy, prior_term, inverse, share)
        first = here
        for bit in bits(sides):
            second = swap(first, "cls", sides, bit)
            if 2 * bit < sides:
                (first,) = call(merge_kernel, [first, second], [(here.shape, F32)])
        rounded, more, send, *evidence = turn(
            *weights, first, second, forward, freqs, share, last
        )
        message = swap(send, "rot", groups, 1)
        image = gather(rounded, more, forward, own_images)
        sums = finish(image, send, message, other_images, last)
        sums = sums if last else sums * blocks
        sources = {i: swap(sums[i], "blk", blocks, i) for i in (*turns, 0)}
    means, evidence = call(
        means_kernel, [*[sources[i] for i in turns], sources[0], *evidence], [((1, freqs, depth), F32), ((1, share), F32)]
    )
    return means, evidence.reshape(share)


def solution(mesh):
    in_specs = (
        P(("grp", "blk"), "rot", None),
        P(("grp", "blk", "cls"), "rot", None),
        P(),
        P(("grp", "blk")),
    )
    out_specs = (P(("grp", "blk", "cls"), "rot", None), P(("grp", "blk", "rot")))
    return jax.shard_map(shards, mesh=mesh, in_specs=in_specs, out_specs=out_specs, check_vma=False)
```

```python
import functools
import math

import jax
import jax.numpy as jnp
import numpy as np
from jax import lax
from jax.experimental import pallas as pl
from jax.experimental.pallas import tpu as pltpu
from jax.sharding import PartitionSpec as P

ANG = 256
ITERS = 2
SIGMA = 32

shrinkage = 1.0

F32 = jnp.float32
BF16 = jnp.bfloat16
SPARE = 8

dot = functools.partial(jnp.dot, preferred_element_type=F32)


def split(x):
    high = x.astype(BF16)
    return high, (x - high.astype(F32)).astype(BF16)


def tables(half_freq):
    turn = np.arange(ANG)
    inverse, forward = [], []
    for group in range(2):
        sides = {}
        for which in range(2):
            freq = which * half_freq + np.arange(half_freq)
            angle = (turn[:, None] * freq[None, :] % ANG) * (2.0 * math.pi / ANG)
            scale = np.where(freq == 0, 1.0, 2.0) / ANG
            sides[which] = (
                np.concatenate([scale * np.cos(angle), -scale * np.sin(angle)], 1),
                np.concatenate([np.cos(angle), np.sin(angle)], 1).T,
            )
        inverse.append(np.concatenate([sides[group][0], sides[1 - group][0]], 1))
        forward.append(np.concatenate([sides[1 - group][1], sides[group][1]], 0))
    result = []
    for table, kinds in ((inverse, (0, 0, 1)), (forward, (0, 1))):
        table = np.concatenate(table, 0).astype(np.float32)
        high = table.astype(BF16)
        parts = [high, (table - high.astype(np.float32)).astype(BF16)]
        result.append(jnp.asarray(np.concatenate([parts[kind] for kind in kinds], 1)))
    return result


def loop(count, body, unroll):
    while count % unroll:
        unroll -= 1
    if unroll == count:
        for i in range(count):
            body(i)
        return

    def step(outer, carry):
        for inner in range(unroll):
            body(outer * unroll + inner)
        return carry

    lax.fori_loop(0, count // unroll, step, 0)


def each(count, body, init):
    if count <= 8:
        for k in range(count):
            init = body(k, init)
        return init
    return lax.fori_loop(0, count, body, init)


def rows(base, count):
    return pl.ds(pl.multiple_of(base, 8), count)


def call(kernel, ins, outs, scratch=(), flops=0, far=(), room=4 << 20):
    total = 0
    buffers = [(x.shape, x.dtype) for i, x in enumerate(ins) if i not in far]
    for shape, dtype in buffers + list(outs) + [x for x in scratch if isinstance(x, tuple)]:
        dims = [1, 1, *shape]
        lines = -(-dims[-2] // 16) * 16
        lanes = -(-dims[-1] // 128) * 128
        total += math.prod(dims[:-2]) * lines * lanes * jnp.dtype(dtype).itemsize
    kinds = [pltpu.VMEM] * len(ins)
    for i in far:
        kinds[i] = pltpu.MemorySpace.HBM
    return pl.pallas_call(
        kernel,
        out_shape=[jax.ShapeDtypeStruct(*x) for x in outs],
        in_specs=[pl.BlockSpec(memory_space=kind) for kind in kinds],
        out_specs=[pl.BlockSpec(memory_space=pltpu.VMEM)] * len(outs),
        scratch_shapes=[pltpu.VMEM(*x) if isinstance(x, tuple) else x for x in scratch],
        compiler_params=pltpu.CompilerParams(vmem_limit_bytes=min(total + room, 56 << 20)),
        cost_estimate=pl.CostEstimate(flops=flops, bytes_accessed=total, transcendentals=0),
    )(*ins)


def permutation_kernel(out):
    to = lax.broadcasted_iota(jnp.int32, out.shape, 0)
    at = lax.broadcasted_iota(jnp.int32, out.shape, 1)
    out[...] = ((to // 16 == at % 16) & (to % 16 == at // 16)).astype(F32).astype(BF16)


def half_index():
    return lax.rem(lax.axis_index("rot") + lax.axis_index("cls"), 2)


def prior_kernel(share, prior_ref, prior_term):
    turns = lax.broadcasted_iota(jnp.int32, (ANG, 256), 0)
    lane = lax.broadcasted_iota(jnp.int32, (1, 256), 1)
    priors = prior_ref[...].reshape(1, -1)
    first, second = [
        jnp.concatenate([priors[:, i * share : (i + 1) * share], lane[:, share:]], 1)
        for i in range(2)
    ]
    offset = jnp.abs(turns - jnp.where(half_index() == 0, first, second))
    distance = jnp.minimum(offset, ANG - offset).astype(F32)
    term = -distance * distance / (2.0 * SIGMA * SIGMA)
    prior_term[:, :128] = term[:, :128]
    prior_term[:, 128:] = repeat(term[:, 128:], share - 128, 128 // (share - 128))


def turned(value, lanes):
    return pltpu.roll(value, lanes % 128, 1) if lanes % 128 else value


def repeat(value, width, times):
    lane = lax.broadcasted_iota(jnp.int32, value.shape, 1)
    value = jnp.where(lane < width, value, 0.0)
    return sum(turned(value, i * width) for i in range(times))


def layout(classes, share):
    width = share - 128
    assert 0 < width < 128 and 128 % width == 0 and classes % 2 == 0
    bundle = min(128 // width, classes)
    assert classes % bundle == 0
    return width, bundle, classes // bundle


def prep_kernel(share, particles_ref, permutation_ref, other, own):
    freqs, depth = particles_ref.shape[1:]
    half = half_index()
    permutation = permutation_ref[...]
    for out, first in ((other, (1 - half) * share), (own, half * share)):
        for p in range(0, share, 16):
            for f in range(0, freqs, 32):
                blocks = [
                    jnp.concatenate(
                        [particles_ref[first + p + j, pl.ds(f + second, 16), :] for j in range(16)],
                        0,
                    )
                    for second in (0, 16)
                ]
                turned = dot(permutation, jnp.concatenate(blocks, 1)).astype(BF16)
                for half in range(2):
                    for j in range(16):
                        pair, part = divmod(f + 16 * half + j, 2)
                        out[pair, pl.ds(p, 16), pl.ds(part * depth, depth)] = turned[
                            16 * j : 16 * j + 16, half * depth : (half + 1) * depth
                        ]


def prep(particles, permutation, share):
    _, freqs, depth = particles.shape
    assert share % 16 == 0 and freqs % 32 == 0
    return call(
        functools.partial(prep_kernel, share),
        [particles, permutation],
        [((freqs // 2, share, 2 * depth), BF16)] * 2,
        flops=1 << 31,
    )


def tree(values):
    values = list(values)
    while len(values) > 1:
        values = [a + b for a, b in zip(values[::2], values[1::2])]
    return values[0]


def weigh_kernel(fresh, order, count, *refs):
    sources = [refs[order.index(i)] for i in range(count)]
    doubled_ref, particles, out, energy_ref, left_ref, image, rest = refs[count:]
    pairs, share, twice = particles.shape
    freqs, depth = 2 * pairs, twice // 2
    classes = energy_ref.shape[0]
    pitch = freqs + SPARE
    radii = depth // 2
    lane = lax.broadcasted_iota(jnp.int32, (freqs, depth), 1)
    sign = jnp.where(lane < radii, -1.0, 1.0).astype(F32)
    doubled = jnp.concatenate([doubled_ref[...]] * 2, 1)
    row = lax.broadcasted_iota(jnp.int32, (freqs, depth), 0) + lax.axis_index("rot") * freqs
    scale = jnp.where(row == 0, 1.0 / ANG, 2.0 / ANG).astype(F32) * doubled

    for k in range(classes):
        if fresh:
            plain = sources[k][0].astype(F32)
        else:
            sums, highs, lows = [
                tree(
                    source[pl.ds(base + (k ^ i) * step, step), :].astype(F32)
                    for i, source in enumerate(sources)
                )
                for base, step in ((0, freqs), (classes * freqs, 1), (classes * (freqs + 1), 1))
            ]
            plain = (sums / (highs + lows + shrinkage)).astype(BF16).astype(F32)
        weighted = (plain * doubled).astype(BF16).astype(F32)
        image[rows(2 * k * pitch, freqs), :] = weighted
        image[rows((2 * k + 1) * pitch, freqs), :] = sign * pltpu.roll(weighted, radii, 1)
        energy = jnp.sum(plain * plain * scale, axis=0, keepdims=True)
        energy = jnp.broadcast_to(jnp.sum(energy, axis=1, keepdims=True), (SPARE, 128))
        energy_ref[pl.ds(k, 1), :] = energy[:1]
        out[rows(2 * k * pitch + freqs, SPARE), :] = energy

    none = jnp.zeros((2 * classes, depth), BF16)

    def correlate(f):
        first, second = [
            image[pl.ds(2 * f + part, 2 * classes, stride=pitch), :].astype(BF16)
            for part in range(2)
        ]
        left = jnp.concatenate(
            [jnp.concatenate([first, none], 1), jnp.concatenate([none, second], 1)], 0
        )
        left_ref[f] = left
        place(out, rest, f, times(left, particles[f]), classes, pitch)

    loop(pairs, correlate, 32)
    pack(out, rest, classes, share, pitch)


def times(left, particles):
    return lax.dot_general(left, particles, (((1,), (1,)), ((), ())), preferred_element_type=F32)


def place(out, rest, f, value, classes, pitch):
    width = value.shape[1] - 128
    spare = jnp.zeros((value.shape[0], 128 - width), F32)
    value = jnp.concatenate([value, spare], 1)
    for part in range(2):
        at = pl.ds(2 * f + part, 2 * classes, stride=pitch)
        mine = value[part * 2 * classes : (part + 1) * 2 * classes]
        out[at, :] = mine[:, :128]
        rest[at, :] = mine[:, 128:]


def pack(out, rest, classes, share, pitch):
    width = share - 128
    each_pack = 128 // width
    for first in range(0, 2 * classes, each_pack):
        total = 0.0
        for group in range(first, min(first + each_pack, 2 * classes)):
            part, k = divmod(group, classes)
            value = rest[rows((2 * k + part) * pitch, pitch), :]
            total = total + turned(value, (group - first) * width)
        out[rows((2 * classes + first // each_pack) * pitch, pitch), :] = total


def unpack(ref, unit, part, classes, share, pitch, freqs):
    width, bundle, _ = layout(classes, share)
    group = part * classes + unit * bundle
    each_pack = 128 // width
    value = ref[rows((2 * classes + group // each_pack) * pitch, freqs), :]
    return turned(value, -(group % each_pack) * width)


def corr_lines(classes, share, pitch):
    return (2 * classes + -(-2 * classes * (share - 128) // 128)) * pitch


def weigh(sources, order, inverse_noise, particles, fresh):
    pairs, share, twice = particles.shape
    classes = len(sources)
    pitch = 2 * pairs + SPARE
    return call(
        functools.partial(weigh_kernel, fresh, order, classes),
        [*[sources[i] for i in order], inverse_noise, particles],
        [
            ((corr_lines(classes, share, pitch), 128), F32),
            ((classes, 128), F32),
            ((pairs, 4 * classes, twice), BF16),
        ],
        [((2 * classes * pitch, twice // 2), F32), ((2 * classes * pitch, 128), F32)],
        flops=8 * classes * share * pairs * twice * 4,
    )


def correlate_kernel(left_ref, particles, out, rest):
    pairs, share, _ = particles.shape
    classes = left_ref.shape[1] // 4
    pitch = 2 * pairs + SPARE

    def body(f):
        place(out, rest, f, times(left_ref[f], particles[f]), classes, pitch)

    loop(pairs, body, 32)
    pack(out, rest, classes, share, pitch)


def correlate(left, particles):
    pairs, share, twice = particles.shape
    classes = left.shape[1] // 4
    pitch = 2 * pairs + SPARE
    return call(
        correlate_kernel,
        [left, particles],
        [((corr_lines(classes, share, pitch), 128), F32)],
        [((2 * classes * pitch, 128), F32)],
        flops=2 * left.shape[1] * share * pairs * twice * 8,
    )[0]


def table_rows(base, count):
    return pl.ds(pl.multiple_of(lax.axis_index("rot") * ANG + base, 128), count)


def score_kernel(share, own, other, energy_ref, prior_term, inverse, *refs):
    weights, more, tops, more_tops, peaks = refs
    classes = energy_ref.shape[0]
    width, bundle, units = layout(classes, share)
    freqs = ANG // 4
    pitch = freqs + SPARE
    at = table_rows(0, ANG)
    lane = lax.broadcasted_iota(jnp.int32, (1, 128), 1)

    def exponentials(value, energy, prior):
        high, low = split(value)
        inner = dot(inverse[at, :], jnp.concatenate([high, low, high], 0))
        scores = inner - 0.5 * energy + prior
        top = jnp.max(scores, axis=0, keepdims=True)
        value = jnp.exp(scores - top)
        return value, top, jnp.sum(value, axis=0, keepdims=True)

    def energy_of(k):
        return energy_ref[pl.ds(k, 1), :] + other[rows(2 * k * pitch + freqs, SPARE), :][:1]

    def slab(i, carry):
        value = jnp.concatenate(
            [
                jnp.concatenate(
                    [ref[rows((4 * i + 2 * j + part) * pitch, freqs), :] for j in range(2)], 1
                )
                for ref in (own, other)
                for part in range(2)
            ],
            0,
        )
        energy = jnp.concatenate([energy_of(2 * i), energy_of(2 * i + 1)], 1)
        prior = jnp.concatenate([prior_term[:, :128]] * 2, 1)
        weights[i], top, total = exponentials(value, energy, prior)
        tops[pl.ds(i, 1), :] = top
        for j in (0, 128):
            carry = merge(carry, (top[:, j : j + 128], total[:, j : j + 128]))
        return carry

    empty = (jnp.full((1, 128), -jnp.inf, F32), jnp.zeros((1, 128), F32))
    top, total = each(classes // 2, slab, empty)
    rest = empty
    for unit in range(units):
        value = jnp.concatenate(
            [
                unpack(ref, unit, part, classes, share, pitch, freqs)
                for ref in (own, other)
                for part in range(2)
            ],
            0,
        )
        energy = sum(
            jnp.where(lane // width == j, energy_of(unit * bundle + j), 0.0)
            for j in range(bundle)
        )
        more[unit], more_top, more_total = exponentials(value, energy, prior_term[:, 128:])
        more_tops[pl.ds(unit, 1), :] = more_top
        for j in range(bundle):
            rest = merge(rest, (turned(more_top, -j * width), turned(more_total, -j * width)))
    line = lax.broadcasted_iota(jnp.int32, peaks.shape, 0)
    peaks[...] = jnp.where(
        line == 0,
        jnp.concatenate([top, rest[0]], 1),
        jnp.concatenate([total, rest[1]], 1),
    )


def scores(own, other, energy, prior_term, inverse, share):
    classes = energy.shape[0]
    units = layout(classes, share)[2]
    return call(
        functools.partial(score_kernel, share),
        [own, other, energy, prior_term, inverse],
        [
            ((classes // 2, ANG, 256), F32),
            ((units, ANG, 128), F32),
            ((classes // 2, 256), F32),
            ((units, 128), F32),
            ((8, 256), F32),
        ],
        flops=6 * classes * 256 * ANG * ANG,
    )


def merge(first, second):
    top = jnp.maximum(first[0], second[0])
    return top, first[1] * jnp.exp(first[0] - top) + second[1] * jnp.exp(second[0] - top)


def two_lines(ref):
    return ref[0:1, :], ref[1:2, :]


def merge_kernel(first, second, out):
    top, total = merge(two_lines(first), two_lines(second))
    line = lax.broadcasted_iota(jnp.int32, out.shape, 0)
    out[...] = jnp.where(line == 0, top, total)


def turn_kernel(share, weights, more, tops, more_tops, first, second, forward, *refs):
    rounded_ref, rounded_more, send, *last, held = refs
    classes = 2 * weights.shape[0]
    width, bundle, units = layout(classes, share)
    pairs = (held.shape[0] // (2 * classes) - SPARE) // 2
    top, total = merge(two_lines(first), two_lines(second))
    evidence = top + jnp.log(total)
    scale = 1.0 / total
    at = table_rows(0, ANG // 2)
    lane = lax.broadcasted_iota(jnp.int32, (1, 128), 1)
    line = lax.broadcasted_iota(jnp.int32, (4 * classes, 128), 0)

    def put(column, k, count):
        high = count.astype(BF16).astype(F32)
        return jnp.where(line == k, high, jnp.where(line == classes + k, count - high, column))

    more_counts = []
    for unit in range(units):
        factor = jnp.exp(
            more_tops[pl.ds(unit, 1), :] - repeat(top[:, 128:], width, bundle)
        ) * repeat(scale[:, 128:], width, bundle)
        value = more[unit] * jnp.where(lane < bundle * width, factor, 0.0)
        count = jnp.sum(value, axis=0, keepdims=True)
        for j in range(bundle):
            mine = jnp.where(lane // width == j, count, 0.0)
            more_counts.append(jnp.sum(mine, axis=1, keepdims=True))
        rounded = value.astype(BF16)
        rounded_more[unit] = rounded
        spectrum = dot(forward[at, :], jnp.concatenate([rounded, rounded], 0)).astype(BF16)
        step = 4 * classes
        entries = spectrum.shape[0] // step
        for i in range(entries):
            send[pairs + unit * entries + i] = spectrum[i * step : (i + 1) * step]

    tops_here = jnp.concatenate([top[:, :128]] * 2, 1)
    scale_here = jnp.concatenate([scale[:, :128]] * 2, 1)

    def body(i, column):
        value = weights[i] * (jnp.exp(tops[pl.ds(i, 1), :] - tops_here) * scale_here)
        rounded = value.astype(BF16)
        rounded_ref[i] = rounded
        spread(held, i, dot(forward[at, :], jnp.concatenate([rounded, rounded], 0)))
        count = jnp.sum(value, axis=0, keepdims=True)
        for j in range(2):
            mine = jnp.sum(count[:, j * 128 : (j + 1) * 128], axis=1, keepdims=True)
            column = put(column, 2 * i + j, mine)
        return column

    column = each(classes // 2, body, jnp.zeros((4 * classes, 128), F32))
    extra = jnp.zeros((4 * classes, 128), F32)
    for k, count in enumerate(more_counts):
        extra = put(extra, k, count)
    for ref in last:
        ref[...] = evidence[:, :share]
        high = evidence.astype(BF16).astype(F32)
        middle = (evidence - high).astype(BF16).astype(F32)
        for i, value in enumerate((high, middle, evidence - high - middle)):
            for j in range(2):
                mine = value[:, j * 128 : (j + 1) * 128]
                extra = jnp.where(line == 2 * classes + 2 * i + j, mine, extra)
    send[send.shape[0] - 2] = column.astype(BF16)
    send[send.shape[0] - 1] = extra.astype(BF16)

    def rearrange(f):
        send[f] = pick(held, f, classes).astype(BF16)

    loop(pairs, rearrange, 32)


def spread(held, i, value):
    freqs = value.shape[0] // 2
    for j in range(2):
        for part in range(2):
            held[rows((4 * i + 2 * j + part) * (freqs + SPARE), freqs), :] = value[
                part * freqs : (part + 1) * freqs, j * 128 : (j + 1) * 128
            ]


def spread_more(held, unit, value, classes, share):
    width, bundle, _ = layout(classes, share)
    freqs = value.shape[0] // 2
    for j in range(bundle):
        shifted = turned(value, -j * width)
        for part in range(2):
            k = unit * bundle + j
            held[rows((2 * k + part) * (freqs + SPARE), freqs), :] = shifted[
                part * freqs : (part + 1) * freqs
            ]


def pick(held, f, classes):
    pitch = held.shape[0] // (2 * classes)
    return jnp.concatenate(
        [held[pl.ds(2 * f + part, 2 * classes, stride=pitch), :] for part in range(2)], 0
    )


def message_shape(classes, pairs, units):
    return (pairs + units * (ANG // 2) // (4 * classes) + 2, 4 * classes, 128)


def turn(weights, more, tops, more_tops, first, second, forward, freqs, share, last):
    classes = 2 * weights.shape[0]
    units = more.shape[0]
    return call(
        functools.partial(turn_kernel, share),
        [weights, more, tops, more_tops, first, second, forward],
        [
            (weights.shape, BF16),
            (more.shape, BF16),
            (message_shape(classes, freqs // 2, units), BF16),
            *([((1, share), F32)] if last else []),
        ],
        [((2 * classes * (freqs + SPARE), 128), F32)],
        flops=4 * classes * 256 * ANG * ANG,
    )


def gather_kernel(rounded_ref, rounded_more, forward, particles, image, held, held_more):
    classes = 2 * rounded_ref.shape[0]
    pairs, share, _ = particles.shape
    at = table_rows(ANG // 2, ANG // 2)

    for unit in range(rounded_more.shape[0]):
        rounded = rounded_more[unit]
        value = dot(forward[at, :], jnp.concatenate([rounded, rounded], 0))
        spread_more(held_more, unit, value, classes, share)

    def body(i, carry):
        rounded = rounded_ref[i]
        spread(held, i, dot(forward[at, :], jnp.concatenate([rounded, rounded], 0)))
        return carry

    each(classes // 2, body, 0)

    def accumulate(f):
        left = [pick(ref, f, classes).astype(BF16) for ref in (held, held_more)]
        left = jnp.concatenate(left, 1)[:, :share]
        take_in(image, f, dot(left, particles[f]), classes)

    loop(pairs, accumulate, 32)


def gather(rounded, rounded_more, forward, particles):
    pairs, share, twice = particles.shape
    classes = 2 * rounded.shape[0]
    lines = 2 * classes * (2 * pairs + SPARE)
    return call(
        gather_kernel,
        [rounded, rounded_more, forward, particles],
        [((lines, twice // 2), F32)],
        [((lines, 128), F32)] * 2,
        flops=4 * classes * 256 * ANG * ANG,
    )[0]


def take_in(image, f, value, classes):
    lines, depth = image.shape
    for part in range(2):
        at = pl.ds(2 * f + part, 2 * classes, stride=lines // (2 * classes))
        image[at, :] = value[
            part * 2 * classes : (part + 1) * 2 * classes, part * depth : (part + 1) * depth
        ]


def finish_kernel(image, mine, spectrum, particles, *refs):
    *outs, held, held_more = refs
    evidence_ref = outs.pop() if len(outs) > 1 else None
    pairs, share, twice = particles.shape
    classes = spectrum.shape[1] // 4
    freqs, depth = 2 * pairs, twice // 2
    radii = depth // 2
    pitch = freqs + SPARE

    units = layout(classes, share)[2]
    entries = ANG // 2 // (4 * classes)
    for unit in range(units):
        first = pairs + unit * entries
        value = jnp.concatenate([spectrum[first + i] for i in range(entries)], 0)
        spread_more(held_more, unit, value.astype(F32), classes, share)

    def body(f):
        left = jnp.concatenate([spectrum[f], pick(held_more, f, classes).astype(BF16)], 1)
        take_in(held, f, dot(left[:, :share], particles[f]), classes)

    loop(pairs, body, 32)
    end = spectrum.shape[0]
    counts = sum(ref[i].astype(F32) for ref in (mine, spectrum) for i in (end - 2, end - 1))
    if evidence_ref is not None:
        parts = spectrum[end - 1].astype(F32)[2 * classes :]
        parts = [jnp.concatenate([parts[i : i + 1], parts[i + 1 : i + 2]], 1) for i in (0, 2, 4)]
        evidence_ref[...] = (parts[0] + (parts[1] + parts[2]))[:, :share]
    counts = counts[:classes] + counts[classes : 2 * classes]
    lane = lax.broadcasted_iota(jnp.int32, (freqs, depth), 1)
    sign = jnp.where(lane < radii, -1.0, 1.0).astype(F32)
    for k in range(classes):
        plain, turned = [
            image[rows((2 * k + part) * pitch, freqs), :]
            + held[rows((2 * k + part) * pitch, freqs), :]
            for part in range(2)
        ]
        value = plain + sign * pltpu.roll(turned, radii, 1)
        if len(outs) == 1:
            outs[0][pl.ds(k * freqs, freqs), :] = value.astype(BF16)
        else:
            outs[k][pl.ds(0, freqs), :] = value
            outs[k][pl.ds(freqs, SPARE), :] = jnp.broadcast_to(counts[k : k + 1], (SPARE, depth))
    if len(outs) == 1:
        end = outs[0].shape[0] - classes * freqs
        high, low = split(counts)
        spare = [jnp.zeros((end - 2 * classes, depth), F32)] if end > 2 * classes else []
        tail = jnp.concatenate([high.astype(F32), low.astype(F32), *spare], 0)
        outs[0][pl.ds(classes * freqs, end), :] = tail.astype(BF16)


def finish(image, mine, spectrum, particles, last):
    pairs, _, twice = particles.shape
    classes = spectrum.shape[1] // 4
    freqs, depth = 2 * pairs, twice // 2
    if last:
        outs = [((freqs + SPARE, depth), F32)] * classes + [((1, particles.shape[1]), F32)]
    else:
        outs = [((classes * freqs + -(-2 * classes // 16) * 16, depth), BF16)]
    return call(
        finish_kernel,
        [image, mine, spectrum, particles],
        outs,
        [(image.shape, F32)] * 2,
        flops=2 * math.prod(spectrum.shape) * twice * 8,
    )


def means_kernel(*refs):
    *parts, own, other, out, evidence_ref = refs
    odd = lax.rem(lax.axis_index("cls"), 2)
    evidence_ref[...] = jnp.where(odd == 0, own[...], other[...])
    freqs = out.shape[1]
    total = tree(ref[...] for ref in parts)
    out[0] = total[:freqs, :] / (total[freqs : freqs + 1, :] + shrinkage)


def swap(value, axis, size, bit):
    if not bit:
        return value
    return lax.ppermute(value, axis, [(i, i ^ bit) for i in range(size)])


def bits(size):
    assert size > 1 and size & (size - 1) == 0
    return [1 << i for i in range(size.bit_length() - 1)]


def shards(particles, references, noise_inv, prior_rot):
    batch, freqs, depth = particles.shape
    sides = lax.axis_size("cls")
    groups = lax.axis_size("rot")
    blocks = lax.axis_size("blk")
    assert groups == 2 and 2 * groups * freqs == ANG
    share = batch // groups
    inverse, forward = tables(freqs)
    inverse_noise = noise_inv.reshape(1, depth // 2)
    assert blocks & (blocks - 1) == 0
    turns = sorted(range(1, blocks), key=lambda i: (-i.bit_length(), i))

    (permutation,) = call(permutation_kernel, [], [((256, 256), BF16)], flops=1 << 32)
    (prior_term,) = call(
        functools.partial(prior_kernel, share), [prior_rot], [((ANG, 256), F32)], flops=1 << 26
    )
    sources = {i: swap(references, "blk", blocks, i) for i in (*turns, 0)}
    other_images, own_images = prep(particles, permutation, share)
    for step in range(ITERS):
        last = step == ITERS - 1
        order = [0, *(reversed(turns) if step else reversed(range(1, blocks)))]
        message, energy, left = weigh(sources, order, inverse_noise, other_images, step == 0)
        message = swap(message, "rot", groups, 1)
        own = correlate(left, own_images)
        *weights, here = scores(own, message, energy, prior_term, inverse, share)
        first = here
        for bit in bits(sides):
            second = swap(first, ("cls", "rot"), sides * groups, groups * bit + (bit == 1))
            if 2 * bit < sides:
                (first,) = call(merge_kernel, [first, second], [(here.shape, F32)])
        rounded, more, send, *evidence = turn(
            *weights, first, second, forward, freqs, share, last
        )
        message = swap(send, "rot", groups, 1)
        image = gather(rounded, more, forward, own_images)
        sums = finish(image, send, message, other_images, last)
        sums, others = (sums[:blocks], sums[blocks:]) if last else (sums * blocks, [])
        sources = {i: swap(sums[i], "blk", blocks, i) for i in (*turns, 0)}
    means, evidence = call(
        means_kernel, [*[sources[i] for i in turns], sources[0], *evidence, *others], [((1, freqs, depth), F32), ((1, share), F32)]
    )
    return means, evidence.reshape(share)


def solution(mesh):
    in_specs = (
        P(("grp", "blk"), "rot", None),
        P(("grp", "blk", "cls"), "rot", None),
        P(),
        P(("grp", "blk")),
    )
    out_specs = (P(("grp", "blk", "cls"), "rot", None), P(("grp", "blk", "rot")))
    return jax.shard_map(shards, mesh=mesh, in_specs=in_specs, out_specs=out_specs, check_vma=False)
```

```python
import functools
import math

import jax
import jax.numpy as jnp
import numpy as np
from jax import lax
from jax.experimental import pallas as pl
from jax.experimental.pallas import tpu as pltpu
from jax.sharding import PartitionSpec as P

ANG = 256
ITERS = 2
SIGMA = 32

shrinkage = 1.0

F32 = jnp.float32
BF16 = jnp.bfloat16
SPARE = 8

dot = functools.partial(jnp.dot, preferred_element_type=F32)


def split(x):
    high = x.astype(BF16)
    return high, (x - high.astype(F32)).astype(BF16)


def tables(half_freq):
    turn = np.arange(ANG)
    inverse, forward = [], []
    for group in range(2):
        sides = {}
        for which in range(2):
            freq = which * half_freq + np.arange(half_freq)
            angle = (turn[:, None] * freq[None, :] % ANG) * (2.0 * math.pi / ANG)
            scale = np.where(freq == 0, 1.0, 2.0) / ANG
            sides[which] = (
                np.concatenate([scale * np.cos(angle), -scale * np.sin(angle)], 1),
                np.concatenate([np.cos(angle), np.sin(angle)], 1).T,
            )
        inverse.append(np.concatenate([sides[group][0], sides[1 - group][0]], 1))
        forward.append(np.concatenate([sides[1 - group][1], sides[group][1]], 0))
    result = []
    for table, kinds in ((inverse, (0, 0, 1)), (forward, (0, 1))):
        table = np.concatenate(table, 0).astype(np.float32)
        high = table.astype(BF16)
        parts = [high, (table - high.astype(np.float32)).astype(BF16)]
        result.append(jnp.asarray(np.concatenate([parts[kind] for kind in kinds], 1)))
    return result


def loop(count, body, unroll):
    while count % unroll:
        unroll -= 1
    if unroll == count:
        for i in range(count):
            body(i)
        return

    def step(outer, carry):
        for inner in range(unroll):
            body(outer * unroll + inner)
        return carry

    lax.fori_loop(0, count // unroll, step, 0)


def each(count, body, init):
    if count <= 8:
        for k in range(count):
            init = body(k, init)
        return init
    return lax.fori_loop(0, count, body, init)


def rows(base, count):
    return pl.ds(pl.multiple_of(base, 8), count)


def call(kernel, ins, outs, scratch=(), flops=0, far=(), room=4 << 20):
    total = 0
    buffers = [(x.shape, x.dtype) for i, x in enumerate(ins) if i not in far]
    for shape, dtype in buffers + list(outs) + [x for x in scratch if isinstance(x, tuple)]:
        dims = [1, 1, *shape]
        lines = -(-dims[-2] // 16) * 16
        lanes = -(-dims[-1] // 128) * 128
        total += math.prod(dims[:-2]) * lines * lanes * jnp.dtype(dtype).itemsize
    kinds = [pltpu.VMEM] * len(ins)
    for i in far:
        kinds[i] = pltpu.MemorySpace.HBM
    return pl.pallas_call(
        kernel,
        out_shape=[jax.ShapeDtypeStruct(*x) for x in outs],
        in_specs=[pl.BlockSpec(memory_space=kind) for kind in kinds],
        out_specs=[pl.BlockSpec(memory_space=pltpu.VMEM)] * len(outs),
        scratch_shapes=[pltpu.VMEM(*x) if isinstance(x, tuple) else x for x in scratch],
        compiler_params=pltpu.CompilerParams(vmem_limit_bytes=min(total + room, 56 << 20)),
        cost_estimate=pl.CostEstimate(flops=flops, bytes_accessed=total, transcendentals=0),
    )(*ins)


def permutation_kernel(out):
    to = lax.broadcasted_iota(jnp.int32, out.shape, 0)
    at = lax.broadcasted_iota(jnp.int32, out.shape, 1)
    out[...] = ((to // 16 == at % 16) & (to % 16 == at // 16)).astype(F32).astype(BF16)


def half_index():
    return lax.rem(lax.axis_index("rot") + lax.axis_index("cls"), 2)


def prior_kernel(share, prior_ref, prior_term):
    turns = lax.broadcasted_iota(jnp.int32, (ANG, 256), 0)
    lane = lax.broadcasted_iota(jnp.int32, (1, 256), 1)
    priors = prior_ref[...].reshape(1, -1)
    first, second = [
        jnp.concatenate([priors[:, i * share : (i + 1) * share], lane[:, share:]], 1)
        for i in range(2)
    ]
    offset = jnp.abs(turns - jnp.where(half_index() == 0, first, second))
    distance = jnp.minimum(offset, ANG - offset).astype(F32)
    term = -distance * distance / (2.0 * SIGMA * SIGMA)
    prior_term[:, :128] = term[:, :128]
    prior_term[:, 128:] = repeat(term[:, 128:], share - 128, 128 // (share - 128))


def turned(value, lanes):
    return pltpu.roll(value, lanes % 128, 1) if lanes % 128 else value


def repeat(value, width, times):
    lane = lax.broadcasted_iota(jnp.int32, value.shape, 1)
    value = jnp.where(lane < width, value, 0.0)
    return sum(turned(value, i * width) for i in range(times))


def layout(classes, share):
    width = share - 128
    assert 0 < width < 128 and 128 % width == 0 and classes % 2 == 0
    bundle = min(128 // width, classes)
    assert classes % bundle == 0
    return width, bundle, classes // bundle


def prep_kernel(share, particles_ref, permutation_ref, other, own):
    freqs, depth = particles_ref.shape[1:]
    half = half_index()
    permutation = permutation_ref[...]
    for out, first in ((other, (1 - half) * share), (own, half * share)):
        for p in range(0, share, 16):
            for f in range(0, freqs, 32):
                blocks = [
                    jnp.concatenate(
                        [particles_ref[first + p + j, pl.ds(f + second, 16), :] for j in range(16)],
                        0,
                    )
                    for second in (0, 16)
                ]
                turned = dot(permutation, jnp.concatenate(blocks, 1)).astype(BF16)
                for half in range(2):
                    for j in range(16):
                        pair, part = divmod(f + 16 * half + j, 2)
                        out[pair, pl.ds(p, 16), pl.ds(part * depth, depth)] = turned[
                            16 * j : 16 * j + 16, half * depth : (half + 1) * depth
                        ]


def prep(particles, permutation, share):
    _, freqs, depth = particles.shape
    assert share % 16 == 0 and freqs % 32 == 0
    return call(
        functools.partial(prep_kernel, share),
        [particles, permutation],
        [((freqs // 2, share, 2 * depth), BF16)] * 2,
        flops=1 << 31,
    )


def tree(values):
    values = list(values)
    while len(values) > 1:
        values = [a + b for a, b in zip(values[::2], values[1::2])]
    return values[0]


def weigh_kernel(fresh, order, count, *refs):
    sources = [refs[order.index(i)] for i in range(count)]
    doubled_ref, particles, out, energy_ref, left_ref, image, rest = refs[count:]
    pairs, share, twice = particles.shape
    freqs, depth = 2 * pairs, twice // 2
    classes = energy_ref.shape[0]
    pitch = freqs + SPARE
    radii = depth // 2
    lane = lax.broadcasted_iota(jnp.int32, (freqs, depth), 1)
    sign = jnp.where(lane < radii, -1.0, 1.0).astype(F32)
    doubled = jnp.concatenate([doubled_ref[...]] * 2, 1)
    row = lax.broadcasted_iota(jnp.int32, (freqs, depth), 0) + lax.axis_index("rot") * freqs
    scale = jnp.where(row == 0, 1.0 / ANG, 2.0 / ANG).astype(F32) * doubled

    for k in range(classes):
        if fresh:
            plain = sources[k][0].astype(F32)
        else:
            sums, highs, lows = [
                tree(
                    source[pl.ds(base + (k ^ i) * step, step), :].astype(F32)
                    for i, source in enumerate(sources)
                )
                for base, step in ((0, freqs), (classes * freqs, 1), (classes * (freqs + 1), 1))
            ]
            plain = (sums / (highs + lows + shrinkage)).astype(BF16).astype(F32)
        weighted = (plain * doubled).astype(BF16).astype(F32)
        image[rows(2 * k * pitch, freqs), :] = weighted
        image[rows((2 * k + 1) * pitch, freqs), :] = sign * pltpu.roll(weighted, radii, 1)
        energy = jnp.sum(plain * plain * scale, axis=0, keepdims=True)
        energy = jnp.broadcast_to(jnp.sum(energy, axis=1, keepdims=True), (SPARE, 128))
        energy_ref[pl.ds(k, 1), :] = energy[:1]
        out[rows(2 * k * pitch + freqs, SPARE), :] = energy

    none = jnp.zeros((2 * classes, depth), BF16)

    def correlate(f):
        first, second = [
            image[pl.ds(2 * f + part, 2 * classes, stride=pitch), :].astype(BF16)
            for part in range(2)
        ]
        left = jnp.concatenate(
            [jnp.concatenate([first, none], 1), jnp.concatenate([none, second], 1)], 0
        )
        left_ref[f] = left
        place(out, rest, f, times(left, particles[f]), classes, pitch)

    loop(pairs, correlate, 32)
    pack(out, rest, classes, share, pitch)


def times(left, particles):
    return lax.dot_general(left, particles, (((1,), (1,)), ((), ())), preferred_element_type=F32)


def place(out, rest, f, value, classes, pitch):
    width = value.shape[1] - 128
    spare = jnp.zeros((value.shape[0], 128 - width), F32)
    value = jnp.concatenate([value, spare], 1)
    for part in range(2):
        at = pl.ds(2 * f + part, 2 * classes, stride=pitch)
        mine = value[part * 2 * classes : (part + 1) * 2 * classes]
        out[at, :] = mine[:, :128]
        rest[at, :] = mine[:, 128:]


def pack(out, rest, classes, share, pitch):
    width = share - 128
    each_pack = 128 // width
    for first in range(0, 2 * classes, each_pack):
        total = 0.0
        for group in range(first, min(first + each_pack, 2 * classes)):
            part, k = divmod(group, classes)
            value = rest[rows((2 * k + part) * pitch, pitch), :]
            total = total + turned(value, (group - first) * width)
        out[rows((2 * classes + first // each_pack) * pitch, pitch), :] = total


def unpack(ref, unit, part, classes, share, pitch, freqs):
    width, bundle, _ = layout(classes, share)
    group = part * classes + unit * bundle
    each_pack = 128 // width
    value = ref[rows((2 * classes + group // each_pack) * pitch, freqs), :]
    return turned(value, -(group % each_pack) * width)


def corr_lines(classes, share, pitch):
    return (2 * classes + -(-2 * classes * (share - 128) // 128)) * pitch


def weigh(sources, order, inverse_noise, particles, fresh):
    pairs, share, twice = particles.shape
    classes = len(sources)
    pitch = 2 * pairs + SPARE
    return call(
        functools.partial(weigh_kernel, fresh, order, classes),
        [*[sources[i] for i in order], inverse_noise, particles],
        [
            ((corr_lines(classes, share, pitch), 128), F32),
            ((classes, 128), F32),
            ((pairs, 4 * classes, twice), BF16),
        ],
        [((2 * classes * pitch, twice // 2), F32), ((2 * classes * pitch, 128), F32)],
        flops=8 * classes * share * pairs * twice * 4,
    )


def correlate_kernel(left_ref, particles, out, rest):
    pairs, share, _ = particles.shape
    classes = left_ref.shape[1] // 4
    pitch = 2 * pairs + SPARE

    def body(f):
        place(out, rest, f, times(left_ref[f], particles[f]), classes, pitch)

    loop(pairs, body, 32)
    pack(out, rest, classes, share, pitch)


def correlate(left, particles):
    pairs, share, twice = particles.shape
    classes = left.shape[1] // 4
    pitch = 2 * pairs + SPARE
    return call(
        correlate_kernel,
        [left, particles],
        [((corr_lines(classes, share, pitch), 128), F32)],
        [((2 * classes * pitch, 128), F32)],
        flops=2 * left.shape[1] * share * pairs * twice * 8,
    )[0]


def table_rows(base, count):
    return pl.ds(pl.multiple_of(lax.axis_index("rot") * ANG + base, 128), count)


def score_kernel(share, own, other, energy_ref, prior_term, inverse, *refs):
    weights, more, tops, more_tops, peaks = refs
    classes = energy_ref.shape[0]
    width, bundle, units = layout(classes, share)
    freqs = ANG // 4
    pitch = freqs + SPARE
    at = table_rows(0, ANG)
    lane = lax.broadcasted_iota(jnp.int32, (1, 128), 1)

    def exponentials(value, energy, prior):
        high, low = split(value)
        inner = dot(inverse[at, :], jnp.concatenate([high, low, high], 0))
        scores = inner - 0.5 * energy + prior
        top = jnp.max(scores, axis=0, keepdims=True)
        value = jnp.exp(scores - top)
        return value, top, jnp.sum(value, axis=0, keepdims=True)

    def energy_of(k):
        return energy_ref[pl.ds(k, 1), :] + other[rows(2 * k * pitch + freqs, SPARE), :][:1]

    def slab(i, carry):
        value = jnp.concatenate(
            [
                jnp.concatenate(
                    [ref[rows((4 * i + 2 * j + part) * pitch, freqs), :] for j in range(2)], 1
                )
                for ref in (own, other)
                for part in range(2)
            ],
            0,
        )
        energy = jnp.concatenate([energy_of(2 * i), energy_of(2 * i + 1)], 1)
        prior = jnp.concatenate([prior_term[:, :128]] * 2, 1)
        weights[i], top, total = exponentials(value, energy, prior)
        tops[pl.ds(i, 1), :] = top
        for j in (0, 128):
            carry = merge(carry, (top[:, j : j + 128], total[:, j : j + 128]))
        return carry

    empty = (jnp.full((1, 128), -jnp.inf, F32), jnp.zeros((1, 128), F32))
    top, total = each(classes // 2, slab, empty)
    rest = empty
    for unit in range(units):
        value = jnp.concatenate(
            [
                unpack(ref, unit, part, classes, share, pitch, freqs)
                for ref in (own, other)
                for part in range(2)
            ],
            0,
        )
        energy = sum(
            jnp.where(lane // width == j, energy_of(unit * bundle + j), 0.0)
            for j in range(bundle)
        )
        more[unit], more_top, more_total = exponentials(value, energy, prior_term[:, 128:])
        more_tops[pl.ds(unit, 1), :] = more_top
        for j in range(bundle):
            rest = merge(rest, (turned(more_top, -j * width), turned(more_total, -j * width)))
    line = lax.broadcasted_iota(jnp.int32, peaks.shape, 0)
    peaks[...] = jnp.where(
        line == 0,
        jnp.concatenate([top, rest[0]], 1),
        jnp.concatenate([total, rest[1]], 1),
    )


def scores(own, other, energy, prior_term, inverse, share):
    classes = energy.shape[0]
    units = layout(classes, share)[2]
    return call(
        functools.partial(score_kernel, share),
        [own, other, energy, prior_term, inverse],
        [
            ((classes // 2, ANG, 256), F32),
            ((units, ANG, 128), F32),
            ((classes // 2, 256), F32),
            ((units, 128), F32),
            ((8, 256), F32),
        ],
        flops=6 * classes * 256 * ANG * ANG,
    )


def merge(first, second):
    top = jnp.maximum(first[0], second[0])
    return top, first[1] * jnp.exp(first[0] - top) + second[1] * jnp.exp(second[0] - top)


def two_lines(ref):
    return ref[0:1, :], ref[1:2, :]


def merge_kernel(first, second, out):
    top, total = merge(two_lines(first), two_lines(second))
    line = lax.broadcasted_iota(jnp.int32, out.shape, 0)
    out[...] = jnp.where(line == 0, top, total)


def turn_kernel(share, weights, more, tops, more_tops, first, second, forward, *refs):
    rounded_ref, rounded_more, send, *last, held = refs
    classes = 2 * weights.shape[0]
    width, bundle, units = layout(classes, share)
    pairs = (held.shape[0] // (2 * classes) - SPARE) // 2
    top, total = merge(two_lines(first), two_lines(second))
    evidence = top + jnp.log(total)
    scale = 1.0 / total
    at = table_rows(0, ANG // 2)
    lane = lax.broadcasted_iota(jnp.int32, (1, 128), 1)
    line = lax.broadcasted_iota(jnp.int32, (4 * classes, 128), 0)

    def put(column, k, count):
        high = count.astype(BF16).astype(F32)
        return jnp.where(line == k, high, jnp.where(line == classes + k, count - high, column))

    more_counts = []
    for unit in range(units):
        factor = jnp.exp(
            more_tops[pl.ds(unit, 1), :] - repeat(top[:, 128:], width, bundle)
        ) * repeat(scale[:, 128:], width, bundle)
        value = more[unit] * jnp.where(lane < bundle * width, factor, 0.0)
        count = jnp.sum(value, axis=0, keepdims=True)
        for j in range(bundle):
            mine = jnp.where(lane // width == j, count, 0.0)
            more_counts.append(jnp.sum(mine, axis=1, keepdims=True))
        rounded = value.astype(BF16)
        rounded_more[unit] = rounded
        spectrum = dot(forward[at, :], jnp.concatenate([rounded, rounded], 0)).astype(BF16)
        step = 4 * classes
        entries = spectrum.shape[0] // step
        for i in range(entries):
            send[pairs + unit * entries + i] = spectrum[i * step : (i + 1) * step]

    tops_here = jnp.concatenate([top[:, :128]] * 2, 1)
    scale_here = jnp.concatenate([scale[:, :128]] * 2, 1)

    def body(i, column):
        value = weights[i] * (jnp.exp(tops[pl.ds(i, 1), :] - tops_here) * scale_here)
        rounded = value.astype(BF16)
        rounded_ref[i] = rounded
        spread(held, i, dot(forward[at, :], jnp.concatenate([rounded, rounded], 0)))
        count = jnp.sum(value, axis=0, keepdims=True)
        for j in range(2):
            mine = jnp.sum(count[:, j * 128 : (j + 1) * 128], axis=1, keepdims=True)
            column = put(column, 2 * i + j, mine)
        return column

    column = each(classes // 2, body, jnp.zeros((4 * classes, 128), F32))
    extra = jnp.zeros((4 * classes, 128), F32)
    for k, count in enumerate(more_counts):
        extra = put(extra, k, count)
    for ref in last:
        ref[...] = evidence[:, :share]
        high = evidence.astype(BF16).astype(F32)
        middle = (evidence - high).astype(BF16).astype(F32)
        for i, value in enumerate((high, middle, evidence - high - middle)):
            for j in range(2):
                mine = value[:, j * 128 : (j + 1) * 128]
                extra = jnp.where(line == 2 * classes + 2 * i + j, mine, extra)
    send[send.shape[0] - 2] = column.astype(BF16)
    send[send.shape[0] - 1] = extra.astype(BF16)

    def rearrange(f):
        send[f] = pick(held, f, classes).astype(BF16)

    loop(pairs, rearrange, 32)


def spread(held, i, value):
    freqs = value.shape[0] // 2
    for j in range(2):
        for part in range(2):
            held[rows((4 * i + 2 * j + part) * (freqs + SPARE), freqs), :] = value[
                part * freqs : (part + 1) * freqs, j * 128 : (j + 1) * 128
            ]


def spread_more(held, unit, value, classes, share):
    width, bundle, _ = layout(classes, share)
    freqs = value.shape[0] // 2
    for j in range(bundle):
        shifted = turned(value, -j * width)
        for part in range(2):
            k = unit * bundle + j
            held[rows((2 * k + part) * (freqs + SPARE), freqs), :] = shifted[
                part * freqs : (part + 1) * freqs
            ]


def pick(held, f, classes):
    pitch = held.shape[0] // (2 * classes)
    return jnp.concatenate(
        [held[pl.ds(2 * f + part, 2 * classes, stride=pitch), :] for part in range(2)], 0
    )


def message_shape(classes, pairs, units):
    return (pairs + units * (ANG // 2) // (4 * classes) + 2, 4 * classes, 128)


def turn(weights, more, tops, more_tops, first, second, forward, freqs, share, last):
    classes = 2 * weights.shape[0]
    units = more.shape[0]
    return call(
        functools.partial(turn_kernel, share),
        [weights, more, tops, more_tops, first, second, forward],
        [
            (weights.shape, BF16),
            (more.shape, BF16),
            (message_shape(classes, freqs // 2, units), BF16),
            *([((1, share), F32)] if last else []),
        ],
        [((2 * classes * (freqs + SPARE), 128), F32)],
        flops=4 * classes * 256 * ANG * ANG,
    )


def gather_kernel(rounded_ref, rounded_more, forward, particles, image, held, held_more):
    classes = 2 * rounded_ref.shape[0]
    pairs, share, _ = particles.shape
    at = table_rows(ANG // 2, ANG // 2)

    for unit in range(rounded_more.shape[0]):
        rounded = rounded_more[unit]
        value = dot(forward[at, :], jnp.concatenate([rounded, rounded], 0))
        spread_more(held_more, unit, value, classes, share)

    def body(i, carry):
        rounded = rounded_ref[i]
        spread(held, i, dot(forward[at, :], jnp.concatenate([rounded, rounded], 0)))
        return carry

    each(classes // 2, body, 0)

    def accumulate(f):
        left = [pick(ref, f, classes).astype(BF16) for ref in (held, held_more)]
        left = jnp.concatenate(left, 1)[:, :share]
        take_in(image, f, dot(left, particles[f]), classes)

    loop(pairs, accumulate, 32)


def gather(rounded, rounded_more, forward, particles):
    pairs, share, twice = particles.shape
    classes = 2 * rounded.shape[0]
    lines = 2 * classes * (2 * pairs + SPARE)
    return call(
        gather_kernel,
        [rounded, rounded_more, forward, particles],
        [((lines, twice // 2), F32)],
        [((lines, 128), F32)] * 2,
        flops=4 * classes * 256 * ANG * ANG,
    )[0]


def take_in(image, f, value, classes):
    lines, depth = image.shape
    for part in range(2):
        at = pl.ds(2 * f + part, 2 * classes, stride=lines // (2 * classes))
        image[at, :] = value[
            part * 2 * classes : (part + 1) * 2 * classes, part * depth : (part + 1) * depth
        ]


def finish_kernel(image, mine, spectrum, particles, *refs):
    *outs, held, held_more = refs
    evidence_ref = outs.pop() if len(outs) > 1 else None
    pairs, share, twice = particles.shape
    classes = spectrum.shape[1] // 4
    freqs, depth = 2 * pairs, twice // 2
    radii = depth // 2
    pitch = freqs + SPARE

    units = layout(classes, share)[2]
    entries = ANG // 2 // (4 * classes)
    for unit in range(units):
        first = pairs + unit * entries
        value = jnp.concatenate([spectrum[first + i] for i in range(entries)], 0)
        spread_more(held_more, unit, value.astype(F32), classes, share)

    def body(f):
        left = jnp.concatenate([spectrum[f], pick(held_more, f, classes).astype(BF16)], 1)
        take_in(held, f, dot(left[:, :share], particles[f]), classes)

    loop(pairs, body, 32)
    end = spectrum.shape[0]
    counts = sum(ref[i].astype(F32) for ref in (mine, spectrum) for i in (end - 2, end - 1))
    if evidence_ref is not None:
        parts = spectrum[end - 1].astype(F32)[2 * classes :]
        parts = [jnp.concatenate([parts[i : i + 1], parts[i + 1 : i + 2]], 1) for i in (0, 2, 4)]
        evidence_ref[...] = (parts[0] + (parts[1] + parts[2]))[:, :share]
    counts = counts[:classes] + counts[classes : 2 * classes]
    lane = lax.broadcasted_iota(jnp.int32, (freqs, depth), 1)
    sign = jnp.where(lane < radii, -1.0, 1.0).astype(F32)
    for k in range(classes):
        plain, turned = [
            image[rows((2 * k + part) * pitch, freqs), :]
            + held[rows((2 * k + part) * pitch, freqs), :]
            for part in range(2)
        ]
        value = plain + sign * pltpu.roll(turned, radii, 1)
        if len(outs) == 1:
            outs[0][pl.ds(k * freqs, freqs), :] = value.astype(BF16)
        else:
            high = counts[k : k + 1].astype(BF16).astype(F32)
            line = lax.broadcasted_iota(jnp.int32, (outs[k].shape[0] - freqs, depth), 0)
            tail = jnp.where(line == 0, high, jnp.where(line == 1, counts[k : k + 1] - high, 0.0))
            outs[k][pl.ds(0, freqs), :] = value.astype(outs[k].dtype)
            outs[k][pl.ds(freqs, tail.shape[0]), :] = tail.astype(outs[k].dtype)
    if len(outs) == 1:
        end = outs[0].shape[0] - classes * freqs
        high, low = split(counts)
        spare = [jnp.zeros((end - 2 * classes, depth), F32)] if end > 2 * classes else []
        tail = jnp.concatenate([high.astype(F32), low.astype(F32), *spare], 0)
        outs[0][pl.ds(classes * freqs, end), :] = tail.astype(BF16)


def finish(image, mine, spectrum, particles, last):
    pairs, _, twice = particles.shape
    classes = spectrum.shape[1] // 4
    freqs, depth = 2 * pairs, twice // 2
    if last:
        near, far = ((freqs + SPARE, depth), F32), ((freqs + 16, depth), BF16)
        outs = [near if k < 2 else far for k in range(classes)]
        outs.append(((1, particles.shape[1]), F32))
    else:
        outs = [((classes * freqs + -(-2 * classes // 16) * 16, depth), BF16)]
    return call(
        finish_kernel,
        [image, mine, spectrum, particles],
        outs,
        [(image.shape, F32)] * 2,
        flops=2 * math.prod(spectrum.shape) * twice * 8,
    )


def means_kernel(*refs):
    *parts, own, other, out, evidence_ref = refs
    odd = lax.rem(lax.axis_index("cls"), 2)
    evidence_ref[...] = jnp.where(odd == 0, own[...], other[...])
    freqs = out.shape[1]
    total = tree(ref[...].astype(F32)[: freqs + 2] for ref in parts)
    counts = total[freqs : freqs + 1, :] + total[freqs + 1 : freqs + 2, :]
    out[0] = total[:freqs, :] / (counts + shrinkage)


def swap(value, axis, size, bit):
    if not bit:
        return value
    return lax.ppermute(value, axis, [(i, i ^ bit) for i in range(size)])


def bits(size):
    assert size > 1 and size & (size - 1) == 0
    return [1 << i for i in range(size.bit_length() - 1)]


def shards(particles, references, noise_inv, prior_rot):
    batch, freqs, depth = particles.shape
    sides = lax.axis_size("cls")
    groups = lax.axis_size("rot")
    blocks = lax.axis_size("blk")
    assert groups == 2 and 2 * groups * freqs == ANG
    share = batch // groups
    inverse, forward = tables(freqs)
    inverse_noise = noise_inv.reshape(1, depth // 2)
    assert blocks & (blocks - 1) == 0
    turns = sorted(range(1, blocks), key=lambda i: (-i.bit_length(), i))

    (permutation,) = call(permutation_kernel, [], [((256, 256), BF16)], flops=1 << 32)
    (prior_term,) = call(
        functools.partial(prior_kernel, share), [prior_rot], [((ANG, 256), F32)], flops=1 << 26
    )
    sources = {i: swap(references, "blk", blocks, i) for i in (*turns, 0)}
    other_images, own_images = prep(particles, permutation, share)
    for step in range(ITERS):
        last = step == ITERS - 1
        order = [0, *(reversed(turns) if step else reversed(range(1, blocks)))]
        message, energy, left = weigh(sources, order, inverse_noise, other_images, step == 0)
        message = swap(message, "rot", groups, 1)
        own = correlate(left, own_images)
        *weights, here = scores(own, message, energy, prior_term, inverse, share)
        first = here
        for bit in bits(sides):
            second = swap(first, ("cls", "rot"), sides * groups, groups * bit + (bit == 1))
            if 2 * bit < sides:
                (first,) = call(merge_kernel, [first, second], [(here.shape, F32)])
        rounded, more, send, *evidence = turn(
            *weights, first, second, forward, freqs, share, last
        )
        message = swap(send, "rot", groups, 1)
        image = gather(rounded, more, forward, own_images)
        sums = finish(image, send, message, other_images, last)
        sums, others = (sums[:blocks], sums[blocks:]) if last else (sums * blocks, [])
        sources = {i: swap(sums[i], "blk", blocks, i) for i in (*turns, 0)}
    means, evidence = call(
        means_kernel, [*[sources[i] for i in turns], sources[0], *evidence, *others], [((1, freqs, depth), F32), ((1, share), F32)]
    )
    return means, evidence.reshape(share)


def solution(mesh):
    in_specs = (
        P(("grp", "blk"), "rot", None),
        P(("grp", "blk", "cls"), "rot", None),
        P(),
        P(("grp", "blk")),
    )
    out_specs = (P(("grp", "blk", "cls"), "rot", None), P(("grp", "blk", "rot")))
    return jax.shard_map(shards, mesh=mesh, in_specs=in_specs, out_specs=out_specs, check_vma=False)
```

```python
import functools
import math

import jax
import jax.numpy as jnp
import numpy as np
from jax import lax
from jax.experimental import pallas as pl
from jax.experimental.pallas import tpu as pltpu
from jax.sharding import PartitionSpec as P

ANG = 256
ITERS = 2
SIGMA = 32

shrinkage = 1.0

F32 = jnp.float32
BF16 = jnp.bfloat16
SPARE = 8

dot = functools.partial(jnp.dot, preferred_element_type=F32)


def split(x):
    high = x.astype(BF16)
    return high, (x - high.astype(F32)).astype(BF16)


def tables(half_freq):
    turn = np.arange(ANG)
    inverse, forward = [], []
    for group in range(2):
        sides = {}
        for which in range(2):
            freq = which * half_freq + np.arange(half_freq)
            angle = (turn[:, None] * freq[None, :] % ANG) * (2.0 * math.pi / ANG)
            scale = np.where(freq == 0, 1.0, 2.0) / ANG
            sides[which] = (
                np.concatenate([scale * np.cos(angle), -scale * np.sin(angle)], 1),
                np.concatenate([np.cos(angle), np.sin(angle)], 1).T,
            )
        inverse.append(np.concatenate([sides[group][0], sides[1 - group][0]], 1))
        forward.append(np.concatenate([sides[1 - group][1], sides[group][1]], 0))
    result = []
    for table, kinds in ((inverse, (0, 0, 1)), (forward, (0, 1))):
        table = np.concatenate(table, 0).astype(np.float32)
        high = table.astype(BF16)
        parts = [high, (table - high.astype(np.float32)).astype(BF16)]
        result.append(jnp.asarray(np.concatenate([parts[kind] for kind in kinds], 1)))
    return result


def loop(count, body, unroll):
    while count % unroll:
        unroll -= 1
    if unroll == count:
        for i in range(count):
            body(i)
        return

    def step(outer, carry):
        for inner in range(unroll):
            body(outer * unroll + inner)
        return carry

    lax.fori_loop(0, count // unroll, step, 0)


def each(count, body, init):
    if count <= 8:
        for k in range(count):
            init = body(k, init)
        return init
    return lax.fori_loop(0, count, body, init)


def rows(base, count):
    return pl.ds(pl.multiple_of(base, 8), count)


def call(kernel, ins, outs, scratch=(), flops=0, far=(), room=4 << 20):
    total = 0
    buffers = [(x.shape, x.dtype) for i, x in enumerate(ins) if i not in far]
    for shape, dtype in buffers + list(outs) + [x for x in scratch if isinstance(x, tuple)]:
        dims = [1, 1, *shape]
        lines = -(-dims[-2] // 16) * 16
        lanes = -(-dims[-1] // 128) * 128
        total += math.prod(dims[:-2]) * lines * lanes * jnp.dtype(dtype).itemsize
    kinds = [pltpu.VMEM] * len(ins)
    for i in far:
        kinds[i] = pltpu.MemorySpace.HBM
    return pl.pallas_call(
        kernel,
        out_shape=[jax.ShapeDtypeStruct(*x) for x in outs],
        in_specs=[pl.BlockSpec(memory_space=kind) for kind in kinds],
        out_specs=[pl.BlockSpec(memory_space=pltpu.VMEM)] * len(outs),
        scratch_shapes=[pltpu.VMEM(*x) if isinstance(x, tuple) else x for x in scratch],
        compiler_params=pltpu.CompilerParams(vmem_limit_bytes=min(total + room, 56 << 20)),
        cost_estimate=pl.CostEstimate(flops=flops, bytes_accessed=total, transcendentals=0),
    )(*ins)


def permutation_kernel(out):
    to = lax.broadcasted_iota(jnp.int32, out.shape, 0)
    at = lax.broadcasted_iota(jnp.int32, out.shape, 1)
    out[...] = ((to // 16 == at % 16) & (to % 16 == at // 16)).astype(F32).astype(BF16)


def half_index():
    return lax.rem(lax.axis_index("rot") + lax.axis_index("cls"), 2)


def prior_kernel(share, prior_ref, prior_term):
    turns = lax.broadcasted_iota(jnp.int32, (ANG, 256), 0)
    lane = lax.broadcasted_iota(jnp.int32, (1, 256), 1)
    priors = prior_ref[...].reshape(1, -1)
    first, second = [
        jnp.concatenate([priors[:, i * share : (i + 1) * share], lane[:, share:]], 1)
        for i in range(2)
    ]
    offset = jnp.abs(turns - jnp.where(half_index() == 0, first, second))
    distance = jnp.minimum(offset, ANG - offset).astype(F32)
    term = -distance * distance / (2.0 * SIGMA * SIGMA)
    prior_term[:, :128] = term[:, :128]
    prior_term[:, 128:] = repeat(term[:, 128:], share - 128, 128 // (share - 128))


def turned(value, lanes):
    return pltpu.roll(value, lanes % 128, 1) if lanes % 128 else value


def repeat(value, width, times):
    lane = lax.broadcasted_iota(jnp.int32, value.shape, 1)
    value = jnp.where(lane < width, value, 0.0)
    return sum(turned(value, i * width) for i in range(times))


def layout(classes, share):
    width = share - 128
    assert 0 < width < 128 and 128 % width == 0 and classes % 2 == 0
    bundle = min(128 // width, classes)
    assert classes % bundle == 0
    return width, bundle, classes // bundle


def prep_kernel(share, particles_ref, permutation_ref, other, own):
    freqs, depth = particles_ref.shape[1:]
    half = half_index()
    permutation = permutation_ref[...]
    for out, first in ((other, (1 - half) * share), (own, half * share)):
        for p in range(0, share, 16):
            for f in range(0, freqs, 32):
                blocks = [
                    jnp.concatenate(
                        [particles_ref[first + p + j, pl.ds(f + second, 16), :] for j in range(16)],
                        0,
                    )
                    for second in (0, 16)
                ]
                turned = dot(permutation, jnp.concatenate(blocks, 1)).astype(BF16)
                for half in range(2):
                    for j in range(16):
                        pair, part = divmod(f + 16 * half + j, 2)
                        out[pair, pl.ds(p, 16), pl.ds(part * depth, depth)] = turned[
                            16 * j : 16 * j + 16, half * depth : (half + 1) * depth
                        ]


def prep(particles, permutation, share):
    _, freqs, depth = particles.shape
    assert share % 16 == 0 and freqs % 32 == 0
    return call(
        functools.partial(prep_kernel, share),
        [particles, permutation],
        [((freqs // 2, share, 2 * depth), BF16)] * 2,
        flops=1 << 31,
    )


def tree(values):
    values = list(values)
    while len(values) > 1:
        values = [a + b for a, b in zip(values[::2], values[1::2])]
    return values[0]


def weigh_kernel(fresh, order, count, *refs):
    sources = [[ref for ref, at in zip(refs, order) if at == i] for i in range(count)]
    doubled_ref, particles, out, energy_ref, left_ref, image, rest = refs[len(order) :]
    pairs, share, twice = particles.shape
    freqs, depth = 2 * pairs, twice // 2
    classes = energy_ref.shape[0]
    pitch = freqs + SPARE
    radii = depth // 2
    lane = lax.broadcasted_iota(jnp.int32, (freqs, depth), 1)
    sign = jnp.where(lane < radii, -1.0, 1.0).astype(F32)
    doubled = jnp.concatenate([doubled_ref[...]] * 2, 1)
    row = lax.broadcasted_iota(jnp.int32, (freqs, depth), 0) + lax.axis_index("rot") * freqs
    scale = jnp.where(row == 0, 1.0 / ANG, 2.0 / ANG).astype(F32) * doubled

    for k in range(classes):
        if fresh:
            plain = sum(source[0].astype(F32) for source in sources[k])
        else:
            sums, highs, lows = [
                tree(
                    source[pl.ds(base + (k ^ i) * step, step), :].astype(F32)
                    for i, (source,) in enumerate(sources)
                )
                for base, step in ((0, freqs), (classes * freqs, 1), (classes * (freqs + 1), 1))
            ]
            plain = (sums / (highs + lows + shrinkage)).astype(BF16).astype(F32)
        weighted = (plain * doubled).astype(BF16).astype(F32)
        image[rows(2 * k * pitch, freqs), :] = weighted
        image[rows((2 * k + 1) * pitch, freqs), :] = sign * pltpu.roll(weighted, radii, 1)
        energy = jnp.sum(plain * plain * scale, axis=0, keepdims=True)
        energy = jnp.broadcast_to(jnp.sum(energy, axis=1, keepdims=True), (SPARE, 128))
        energy_ref[pl.ds(k, 1), :] = energy[:1]
        out[rows(2 * k * pitch + freqs, SPARE), :] = energy

    none = jnp.zeros((2 * classes, depth), BF16)

    def correlate(f):
        first, second = [
            image[pl.ds(2 * f + part, 2 * classes, stride=pitch), :].astype(BF16)
            for part in range(2)
        ]
        left = jnp.concatenate(
            [jnp.concatenate([first, none], 1), jnp.concatenate([none, second], 1)], 0
        )
        left_ref[f] = left
        place(out, rest, f, times(left, particles[f]), classes, pitch)

    loop(pairs, correlate, 32)
    pack(out, rest, classes, share, pitch)


def times(left, particles):
    return lax.dot_general(left, particles, (((1,), (1,)), ((), ())), preferred_element_type=F32)


def place(out, rest, f, value, classes, pitch):
    width = value.shape[1] - 128
    spare = jnp.zeros((value.shape[0], 128 - width), F32)
    value = jnp.concatenate([value, spare], 1)
    for part in range(2):
        at = pl.ds(2 * f + part, 2 * classes, stride=pitch)
        mine = value[part * 2 * classes : (part + 1) * 2 * classes]
        out[at, :] = mine[:, :128]
        rest[at, :] = mine[:, 128:]


def pack(out, rest, classes, share, pitch):
    width = share - 128
    each_pack = 128 // width
    for first in range(0, 2 * classes, each_pack):
        total = 0.0
        for group in range(first, min(first + each_pack, 2 * classes)):
            part, k = divmod(group, classes)
            value = rest[rows((2 * k + part) * pitch, pitch), :]
            total = total + turned(value, (group - first) * width)
        out[rows((2 * classes + first // each_pack) * pitch, pitch), :] = total


def unpack(ref, unit, part, classes, share, pitch, freqs):
    width, bundle, _ = layout(classes, share)
    group = part * classes + unit * bundle
    each_pack = 128 // width
    value = ref[rows((2 * classes + group // each_pack) * pitch, freqs), :]
    return turned(value, -(group % each_pack) * width)


def corr_lines(classes, share, pitch):
    return (2 * classes + -(-2 * classes * (share - 128) // 128)) * pitch


def weigh(sources, order, inverse_noise, particles, fresh):
    pairs, share, twice = particles.shape
    classes = len(sources)
    operands = [sources[i][order[:at].count(i)] for at, i in enumerate(order)]
    pitch = 2 * pairs + SPARE
    return call(
        functools.partial(weigh_kernel, fresh, order, classes),
        [*operands, inverse_noise, particles],
        [
            ((corr_lines(classes, share, pitch), 128), F32),
            ((classes, 128), F32),
            ((pairs, 4 * classes, twice), BF16),
        ],
        [((2 * classes * pitch, twice // 2), F32), ((2 * classes * pitch, 128), F32)],
        flops=8 * classes * share * pairs * twice * 4,
    )


def correlate_kernel(left_ref, particles, out, rest):
    pairs, share, _ = particles.shape
    classes = left_ref.shape[1] // 4
    pitch = 2 * pairs + SPARE

    def body(f):
        place(out, rest, f, times(left_ref[f], particles[f]), classes, pitch)

    loop(pairs, body, 32)
    pack(out, rest, classes, share, pitch)


def correlate(left, particles):
    pairs, share, twice = particles.shape
    classes = left.shape[1] // 4
    pitch = 2 * pairs + SPARE
    return call(
        correlate_kernel,
        [left, particles],
        [((corr_lines(classes, share, pitch), 128), F32)],
        [((2 * classes * pitch, 128), F32)],
        flops=2 * left.shape[1] * share * pairs * twice * 8,
    )[0]


def table_rows(base, count):
    return pl.ds(pl.multiple_of(lax.axis_index("rot") * ANG + base, 128), count)


def score_kernel(share, own, other, energy_ref, prior_term, inverse, *refs):
    weights, more, tops, more_tops, peaks = refs
    classes = energy_ref.shape[0]
    width, bundle, units = layout(classes, share)
    freqs = ANG // 4
    pitch = freqs + SPARE
    at = table_rows(0, ANG)
    lane = lax.broadcasted_iota(jnp.int32, (1, 128), 1)

    def exponentials(value, energy, prior):
        high, low = split(value)
        inner = dot(inverse[at, :], jnp.concatenate([high, low, high], 0))
        scores = inner - 0.5 * energy + prior
        top = jnp.max(scores, axis=0, keepdims=True)
        value = jnp.exp(scores - top)
        return value, top, jnp.sum(value, axis=0, keepdims=True)

    def energy_of(k):
        return energy_ref[pl.ds(k, 1), :] + other[rows(2 * k * pitch + freqs, SPARE), :][:1]

    def slab(i, carry):
        value = jnp.concatenate(
            [
                jnp.concatenate(
                    [ref[rows((4 * i + 2 * j + part) * pitch, freqs), :] for j in range(2)], 1
                )
                for ref in (own, other)
                for part in range(2)
            ],
            0,
        )
        energy = jnp.concatenate([energy_of(2 * i), energy_of(2 * i + 1)], 1)
        prior = jnp.concatenate([prior_term[:, :128]] * 2, 1)
        weights[i], top, total = exponentials(value, energy, prior)
        tops[pl.ds(i, 1), :] = top
        for j in (0, 128):
            carry = merge(carry, (top[:, j : j + 128], total[:, j : j + 128]))
        return carry

    empty = (jnp.full((1, 128), -jnp.inf, F32), jnp.zeros((1, 128), F32))
    top, total = each(classes // 2, slab, empty)
    rest = empty
    for unit in range(units):
        value = jnp.concatenate(
            [
                unpack(ref, unit, part, classes, share, pitch, freqs)
                for ref in (own, other)
                for part in range(2)
            ],
            0,
        )
        energy = sum(
            jnp.where(lane // width == j, energy_of(unit * bundle + j), 0.0)
            for j in range(bundle)
        )
        more[unit], more_top, more_total = exponentials(value, energy, prior_term[:, 128:])
        more_tops[pl.ds(unit, 1), :] = more_top
        for j in range(bundle):
            rest = merge(rest, (turned(more_top, -j * width), turned(more_total, -j * width)))
    line = lax.broadcasted_iota(jnp.int32, peaks.shape, 0)
    peaks[...] = jnp.where(
        line == 0,
        jnp.concatenate([top, rest[0]], 1),
        jnp.concatenate([total, rest[1]], 1),
    )


def scores(own, other, energy, prior_term, inverse, share):
    classes = energy.shape[0]
    units = layout(classes, share)[2]
    return call(
        functools.partial(score_kernel, share),
        [own, other, energy, prior_term, inverse],
        [
            ((classes // 2, ANG, 256), F32),
            ((units, ANG, 128), F32),
            ((classes // 2, 256), F32),
            ((units, 128), F32),
            ((8, 256), F32),
        ],
        flops=6 * classes * 256 * ANG * ANG,
    )


def merge(first, second):
    top = jnp.maximum(first[0], second[0])
    return top, first[1] * jnp.exp(first[0] - top) + second[1] * jnp.exp(second[0] - top)


def two_lines(ref):
    return ref[0:1, :], ref[1:2, :]


def merge_kernel(first, second, out):
    top, total = merge(two_lines(first), two_lines(second))
    line = lax.broadcasted_iota(jnp.int32, out.shape, 0)
    out[...] = jnp.where(line == 0, top, total)


def turn_kernel(share, weights, more, tops, more_tops, first, second, forward, *refs):
    rounded_ref, rounded_more, send, *last, held = refs
    classes = 2 * weights.shape[0]
    width, bundle, units = layout(classes, share)
    pairs = (held.shape[0] // (2 * classes) - SPARE) // 2
    top, total = merge(two_lines(first), two_lines(second))
    evidence = top + jnp.log(total)
    scale = 1.0 / total
    at = table_rows(0, ANG // 2)
    lane = lax.broadcasted_iota(jnp.int32, (1, 128), 1)
    line = lax.broadcasted_iota(jnp.int32, (4 * classes, 128), 0)

    def put(column, k, count):
        high = count.astype(BF16).astype(F32)
        return jnp.where(line == k, high, jnp.where(line == classes + k, count - high, column))

    more_counts = []
    for unit in range(units):
        factor = jnp.exp(
            more_tops[pl.ds(unit, 1), :] - repeat(top[:, 128:], width, bundle)
        ) * repeat(scale[:, 128:], width, bundle)
        value = more[unit] * jnp.where(lane < bundle * width, factor, 0.0)
        count = jnp.sum(value, axis=0, keepdims=True)
        for j in range(bundle):
            mine = jnp.where(lane // width == j, count, 0.0)
            more_counts.append(jnp.sum(mine, axis=1, keepdims=True))
        rounded = value.astype(BF16)
        rounded_more[unit] = rounded
        spectrum = dot(forward[at, :], jnp.concatenate([rounded, rounded], 0)).astype(BF16)
        step = 4 * classes
        entries = spectrum.shape[0] // step
        for i in range(entries):
            send[pairs + unit * entries + i] = spectrum[i * step : (i + 1) * step]

    tops_here = jnp.concatenate([top[:, :128]] * 2, 1)
    scale_here = jnp.concatenate([scale[:, :128]] * 2, 1)

    def body(i, column):
        value = weights[i] * (jnp.exp(tops[pl.ds(i, 1), :] - tops_here) * scale_here)
        rounded = value.astype(BF16)
        rounded_ref[i] = rounded
        spread(held, i, dot(forward[at, :], jnp.concatenate([rounded, rounded], 0)))
        count = jnp.sum(value, axis=0, keepdims=True)
        for j in range(2):
            mine = jnp.sum(count[:, j * 128 : (j + 1) * 128], axis=1, keepdims=True)
            column = put(column, 2 * i + j, mine)
        return column

    column = each(classes // 2, body, jnp.zeros((4 * classes, 128), F32))
    extra = jnp.zeros((4 * classes, 128), F32)
    for k, count in enumerate(more_counts):
        extra = put(extra, k, count)
    for ref in last:
        ref[...] = evidence[:, :share]
        high = evidence.astype(BF16).astype(F32)
        middle = (evidence - high).astype(BF16).astype(F32)
        for i, value in enumerate((high, middle, evidence - high - middle)):
            for j in range(2):
                mine = value[:, j * 128 : (j + 1) * 128]
                extra = jnp.where(line == 2 * classes + 2 * i + j, mine, extra)
    send[send.shape[0] - 2] = column.astype(BF16)
    send[send.shape[0] - 1] = extra.astype(BF16)

    def rearrange(f):
        send[f] = pick(held, f, classes).astype(BF16)

    loop(pairs, rearrange, 32)


def spread(held, i, value):
    freqs = value.shape[0] // 2
    for j in range(2):
        for part in range(2):
            held[rows((4 * i + 2 * j + part) * (freqs + SPARE), freqs), :] = value[
                part * freqs : (part + 1) * freqs, j * 128 : (j + 1) * 128
            ]


def spread_more(held, unit, value, classes, share):
    width, bundle, _ = layout(classes, share)
    freqs = value.shape[0] // 2
    for j in range(bundle):
        shifted = turned(value, -j * width)
        for part in range(2):
            k = unit * bundle + j
            held[rows((2 * k + part) * (freqs + SPARE), freqs), :] = shifted[
                part * freqs : (part + 1) * freqs
            ]


def pick(held, f, classes):
    pitch = held.shape[0] // (2 * classes)
    return jnp.concatenate(
        [held[pl.ds(2 * f + part, 2 * classes, stride=pitch), :] for part in range(2)], 0
    )


def message_shape(classes, pairs, units):
    return (pairs + units * (ANG // 2) // (4 * classes) + 2, 4 * classes, 128)


def turn(weights, more, tops, more_tops, first, second, forward, freqs, share, last):
    classes = 2 * weights.shape[0]
    units = more.shape[0]
    return call(
        functools.partial(turn_kernel, share),
        [weights, more, tops, more_tops, first, second, forward],
        [
            (weights.shape, BF16),
            (more.shape, BF16),
            (message_shape(classes, freqs // 2, units), BF16),
            *([((1, share), F32)] if last else []),
        ],
        [((2 * classes * (freqs + SPARE), 128), F32)],
        flops=4 * classes * 256 * ANG * ANG,
    )


def gather_kernel(rounded_ref, rounded_more, forward, particles, image, held, held_more):
    classes = 2 * rounded_ref.shape[0]
    pairs, share, _ = particles.shape
    at = table_rows(ANG // 2, ANG // 2)

    for unit in range(rounded_more.shape[0]):
        rounded = rounded_more[unit]
        value = dot(forward[at, :], jnp.concatenate([rounded, rounded], 0))
        spread_more(held_more, unit, value, classes, share)

    def body(i, carry):
        rounded = rounded_ref[i]
        spread(held, i, dot(forward[at, :], jnp.concatenate([rounded, rounded], 0)))
        return carry

    each(classes // 2, body, 0)

    def accumulate(f):
        left = [pick(ref, f, classes).astype(BF16) for ref in (held, held_more)]
        left = jnp.concatenate(left, 1)[:, :share]
        take_in(image, f, dot(left, particles[f]), classes)

    loop(pairs, accumulate, 32)


def gather(rounded, rounded_more, forward, particles):
    pairs, share, twice = particles.shape
    classes = 2 * rounded.shape[0]
    lines = 2 * classes * (2 * pairs + SPARE)
    return call(
        gather_kernel,
        [rounded, rounded_more, forward, particles],
        [((lines, twice // 2), F32)],
        [((lines, 128), F32)] * 2,
        flops=4 * classes * 256 * ANG * ANG,
    )[0]


def take_in(image, f, value, classes):
    lines, depth = image.shape
    for part in range(2):
        at = pl.ds(2 * f + part, 2 * classes, stride=lines // (2 * classes))
        image[at, :] = value[
            part * 2 * classes : (part + 1) * 2 * classes, part * depth : (part + 1) * depth
        ]


def finish_kernel(image, mine, spectrum, particles, *refs):
    *outs, held, held_more = refs
    evidence_ref = outs.pop() if len(outs) > 1 else None
    pairs, share, twice = particles.shape
    classes = spectrum.shape[1] // 4
    freqs, depth = 2 * pairs, twice // 2
    radii = depth // 2
    pitch = freqs + SPARE

    units = layout(classes, share)[2]
    entries = ANG // 2 // (4 * classes)
    for unit in range(units):
        first = pairs + unit * entries
        value = jnp.concatenate([spectrum[first + i] for i in range(entries)], 0)
        spread_more(held_more, unit, value.astype(F32), classes, share)

    def body(f):
        left = jnp.concatenate([spectrum[f], pick(held_more, f, classes).astype(BF16)], 1)
        take_in(held, f, dot(left[:, :share], particles[f]), classes)

    loop(pairs, body, 32)
    end = spectrum.shape[0]
    counts = sum(ref[i].astype(F32) for ref in (mine, spectrum) for i in (end - 2, end - 1))
    if evidence_ref is not None:
        parts = spectrum[end - 1].astype(F32)[2 * classes :]
        parts = [jnp.concatenate([parts[i : i + 1], parts[i + 1 : i + 2]], 1) for i in (0, 2, 4)]
        evidence_ref[...] = (parts[0] + (parts[1] + parts[2]))[:, :share]
    counts = counts[:classes] + counts[classes : 2 * classes]
    lane = lax.broadcasted_iota(jnp.int32, (freqs, depth), 1)
    sign = jnp.where(lane < radii, -1.0, 1.0).astype(F32)
    for k in range(classes):
        plain, turned = [
            image[rows((2 * k + part) * pitch, freqs), :]
            + held[rows((2 * k + part) * pitch, freqs), :]
            for part in range(2)
        ]
        value = plain + sign * pltpu.roll(turned, radii, 1)
        if len(outs) == 1:
            outs[0][pl.ds(k * freqs, freqs), :] = value.astype(BF16)
        else:
            outs[k][pl.ds(0, freqs), :] = value
            outs[k][pl.ds(freqs, SPARE), :] = jnp.broadcast_to(counts[k : k + 1], (SPARE, depth))
    if len(outs) == 1:
        end = outs[0].shape[0] - classes * freqs
        high, low = split(counts)
        spare = [jnp.zeros((end - 2 * classes, depth), F32)] if end > 2 * classes else []
        tail = jnp.concatenate([high.astype(F32), low.astype(F32), *spare], 0)
        outs[0][pl.ds(classes * freqs, end), :] = tail.astype(BF16)


def finish(image, mine, spectrum, particles, last):
    pairs, _, twice = particles.shape
    classes = spectrum.shape[1] // 4
    freqs, depth = 2 * pairs, twice // 2
    if last:
        outs = [((freqs + SPARE, depth), F32)] * classes + [((1, particles.shape[1]), F32)]
    else:
        outs = [((classes * freqs + -(-2 * classes // 16) * 16, depth), BF16)]
    return call(
        finish_kernel,
        [image, mine, spectrum, particles],
        outs,
        [(image.shape, F32)] * 2,
        flops=2 * math.prod(spectrum.shape) * twice * 8,
    )


def means_kernel(*refs):
    *parts, own, other, out, evidence_ref = refs
    odd = lax.rem(lax.axis_index("cls"), 2)
    evidence_ref[...] = jnp.where(odd == 0, own[...], other[...])
    freqs = out.shape[1]
    total = tree(ref[...] for ref in parts)
    out[0] = total[:freqs, :] / (total[freqs : freqs + 1, :] + shrinkage)


def swap(value, axis, size, bit):
    if not bit:
        return value
    return lax.ppermute(value, axis, [(i, i ^ bit) for i in range(size)])


def bits(size):
    assert size > 1 and size & (size - 1) == 0
    return [1 << i for i in range(size.bit_length() - 1)]


def shards(particles, references, noise_inv, prior_rot):
    batch, freqs, depth = particles.shape
    sides = lax.axis_size("cls")
    groups = lax.axis_size("rot")
    blocks = lax.axis_size("blk")
    assert groups == 2 and 2 * groups * freqs == ANG
    share = batch // groups
    inverse, forward = tables(freqs)
    inverse_noise = noise_inv.reshape(1, depth // 2)
    assert blocks & (blocks - 1) == 0
    turns = sorted(range(1, blocks), key=lambda i: (-i.bit_length(), i))

    (permutation,) = call(permutation_kernel, [], [((256, 256), BF16)], flops=1 << 32)
    (prior_term,) = call(
        functools.partial(prior_kernel, share), [prior_rot], [((ANG, 256), F32)], flops=1 << 26
    )
    sources = {i: [swap(references, "blk", blocks, i)] for i in (*turns[1:], 0)}
    ways = [(i, i ^ turns[0]) for i in range(blocks)]
    sources[turns[0]] = [
        lax.ppermute(references, "blk", [(i, j) for i, j in ways if (i < j) == up])
        for up in (True, False)
    ]
    other_images, own_images = prep(particles, permutation, share)
    for step in range(ITERS):
        last = step == ITERS - 1
        order = [0, *reversed(turns)]
        if not step:
            order = [0, turns[0], *turns[1:-1], turns[0], turns[-1]]
        message, energy, left = weigh(sources, order, inverse_noise, other_images, step == 0)
        message = swap(message, "rot", groups, 1)
        own = correlate(left, own_images)
        *weights, here = scores(own, message, energy, prior_term, inverse, share)
        first = here
        for bit in bits(sides):
            second = swap(first, ("cls", "rot"), sides * groups, groups * bit + (bit == 1))
            if 2 * bit < sides:
                (first,) = call(merge_kernel, [first, second], [(here.shape, F32)])
        rounded, more, send, *evidence = turn(
            *weights, first, second, forward, freqs, share, last
        )
        message = swap(send, "rot", groups, 1)
        image = gather(rounded, more, forward, own_images)
        sums = finish(image, send, message, other_images, last)
        sums, others = (sums[:blocks], sums[blocks:]) if last else (sums * blocks, [])
        sources = {i: [swap(sums[i], "blk", blocks, i)] for i in (*turns, 0)}
    means, evidence = call(
        means_kernel, [*[sources[i][0] for i in reversed(range(blocks))], *evidence, *others], [((1, freqs, depth), F32), ((1, share), F32)]
    )
    return means, evidence.reshape(share)


def solution(mesh):
    in_specs = (
        P(("grp", "blk"), "rot", None),
        P(("grp", "blk", "cls"), "rot", None),
        P(),
        P(("grp", "blk")),
    )
    out_specs = (P(("grp", "blk", "cls"), "rot", None), P(("grp", "blk", "rot")))
    return jax.shard_map(shards, mesh=mesh, in_specs=in_specs, out_specs=out_specs, check_vma=False)
```

```python
import functools
import math

import jax
import jax.numpy as jnp
import numpy as np
from jax import lax
from jax.experimental import pallas as pl
from jax.experimental.pallas import tpu as pltpu
from jax.sharding import PartitionSpec as P

ANG = 256
ITERS = 2
SIGMA = 32

shrinkage = 1.0

F32 = jnp.float32
BF16 = jnp.bfloat16
SPARE = 8

dot = functools.partial(jnp.dot, preferred_element_type=F32)


def split(x):
    high = x.astype(BF16)
    return high, (x - high.astype(F32)).astype(BF16)


def tables(half_freq):
    turn = np.arange(ANG)
    inverse, forward = [], []
    for group in range(2):
        sides = {}
        for which in range(2):
            freq = which * half_freq + np.arange(half_freq)
            angle = (turn[:, None] * freq[None, :] % ANG) * (2.0 * math.pi / ANG)
            scale = np.where(freq == 0, 1.0, 2.0) / ANG
            sides[which] = (
                np.concatenate([scale * np.cos(angle), -scale * np.sin(angle)], 1),
                np.concatenate([np.cos(angle), np.sin(angle)], 1).T,
            )
        inverse.append(np.concatenate([sides[group][0], sides[1 - group][0]], 1))
        forward.append(np.concatenate([sides[1 - group][1], sides[group][1]], 0))
    result = []
    for table, kinds in ((inverse, (0, 0, 1)), (forward, (0, 1))):
        table = np.concatenate(table, 0).astype(np.float32)
        high = table.astype(BF16)
        parts = [high, (table - high.astype(np.float32)).astype(BF16)]
        result.append(jnp.asarray(np.concatenate([parts[kind] for kind in kinds], 1)))
    return result


def loop(count, body, unroll):
    while count % unroll:
        unroll -= 1
    if unroll == count:
        for i in range(count):
            body(i)
        return

    def step(outer, carry):
        for inner in range(unroll):
            body(outer * unroll + inner)
        return carry

    lax.fori_loop(0, count // unroll, step, 0)


def each(count, body, init):
    if count <= 8:
        for k in range(count):
            init = body(k, init)
        return init
    return lax.fori_loop(0, count, body, init)


def rows(base, count):
    return pl.ds(pl.multiple_of(base, 8), count)


def call(kernel, ins, outs, scratch=(), flops=0, far=(), room=4 << 20):
    total = 0
    buffers = [(x.shape, x.dtype) for i, x in enumerate(ins) if i not in far]
    for shape, dtype in buffers + list(outs) + [x for x in scratch if isinstance(x, tuple)]:
        dims = [1, 1, *shape]
        lines = -(-dims[-2] // 16) * 16
        lanes = -(-dims[-1] // 128) * 128
        total += math.prod(dims[:-2]) * lines * lanes * jnp.dtype(dtype).itemsize
    kinds = [pltpu.VMEM] * len(ins)
    for i in far:
        kinds[i] = pltpu.MemorySpace.HBM
    return pl.pallas_call(
        kernel,
        out_shape=[jax.ShapeDtypeStruct(*x) for x in outs],
        in_specs=[pl.BlockSpec(memory_space=kind) for kind in kinds],
        out_specs=[pl.BlockSpec(memory_space=pltpu.VMEM)] * len(outs),
        scratch_shapes=[pltpu.VMEM(*x) if isinstance(x, tuple) else x for x in scratch],
        compiler_params=pltpu.CompilerParams(vmem_limit_bytes=min(total + room, 56 << 20)),
        cost_estimate=pl.CostEstimate(flops=flops, bytes_accessed=total, transcendentals=0),
    )(*ins)


def permutation_kernel(out):
    to = lax.broadcasted_iota(jnp.int32, out.shape, 0)
    at = lax.broadcasted_iota(jnp.int32, out.shape, 1)
    out[...] = ((to // 16 == at % 16) & (to % 16 == at // 16)).astype(F32).astype(BF16)


def half_index():
    return lax.rem(lax.axis_index("rot") + lax.axis_index("cls"), 2)


def prior_kernel(share, prior_ref, prior_term):
    turns = lax.broadcasted_iota(jnp.int32, (ANG, 256), 0)
    lane = lax.broadcasted_iota(jnp.int32, (1, 256), 1)
    priors = prior_ref[...].reshape(1, -1)
    first, second = [
        jnp.concatenate([priors[:, i * share : (i + 1) * share], lane[:, share:]], 1)
        for i in range(2)
    ]
    offset = jnp.abs(turns - jnp.where(half_index() == 0, first, second))
    distance = jnp.minimum(offset, ANG - offset).astype(F32)
    term = -distance * distance / (2.0 * SIGMA * SIGMA)
    prior_term[:, :128] = term[:, :128]
    prior_term[:, 128:] = repeat(term[:, 128:], share - 128, 128 // (share - 128))


def turned(value, lanes):
    return pltpu.roll(value, lanes % 128, 1) if lanes % 128 else value


def repeat(value, width, times):
    lane = lax.broadcasted_iota(jnp.int32, value.shape, 1)
    value = jnp.where(lane < width, value, 0.0)
    return sum(turned(value, i * width) for i in range(times))


def layout(classes, share):
    width = share - 128
    assert 0 < width < 128 and 128 % width == 0 and classes % 2 == 0
    bundle = min(128 // width, classes)
    assert classes % bundle == 0
    return width, bundle, classes // bundle


def prep_kernel(share, particles_ref, permutation_ref, other, own):
    freqs, depth = particles_ref.shape[1:]
    half = half_index()
    permutation = permutation_ref[...]
    for out, first in ((other, (1 - half) * share), (own, half * share)):
        for p in range(0, share, 16):
            for f in range(0, freqs, 32):
                blocks = [
                    jnp.concatenate(
                        [particles_ref[first + p + j, pl.ds(f + second, 16), :] for j in range(16)],
                        0,
                    )
                    for second in (0, 16)
                ]
                turned = dot(permutation, jnp.concatenate(blocks, 1)).astype(BF16)
                for half in range(2):
                    for j in range(16):
                        pair, part = divmod(f + 16 * half + j, 2)
                        out[pair, pl.ds(p, 16), pl.ds(part * depth, depth)] = turned[
                            16 * j : 16 * j + 16, half * depth : (half + 1) * depth
                        ]


def prep(particles, permutation, share):
    _, freqs, depth = particles.shape
    assert share % 16 == 0 and freqs % 32 == 0
    return call(
        functools.partial(prep_kernel, share),
        [particles, permutation],
        [((freqs // 2, share, 2 * depth), BF16)] * 2,
        flops=1 << 31,
    )


def tree(values):
    values = list(values)
    while len(values) > 1:
        values = [a + b for a, b in zip(values[::2], values[1::2])]
    return values[0]


def weigh_kernel(fresh, order, count, *refs):
    sources = [refs[order.index(i)] for i in range(count)]
    doubled_ref, particles, out, energy_ref, left_ref, image, rest = refs[count:]
    pairs, share, twice = particles.shape
    freqs, depth = 2 * pairs, twice // 2
    classes = energy_ref.shape[0]
    pitch = freqs + SPARE
    radii = depth // 2
    lane = lax.broadcasted_iota(jnp.int32, (freqs, depth), 1)
    sign = jnp.where(lane < radii, -1.0, 1.0).astype(F32)
    doubled = jnp.concatenate([doubled_ref[...]] * 2, 1)
    row = lax.broadcasted_iota(jnp.int32, (freqs, depth), 0) + lax.axis_index("rot") * freqs
    scale = jnp.where(row == 0, 1.0 / ANG, 2.0 / ANG).astype(F32) * doubled

    for k in range(classes):
        if fresh:
            plain = sources[k][0].astype(F32)
        else:
            sums, highs, lows = [
                tree(
                    source[pl.ds(base + (k ^ i) * step, step), :].astype(F32)
                    for i, source in enumerate(sources)
                )
                for base, step in ((0, freqs), (classes * freqs, 1), (classes * (freqs + 1), 1))
            ]
            plain = (sums / (highs + lows + shrinkage)).astype(BF16).astype(F32)
        weighted = (plain * doubled).astype(BF16).astype(F32)
        image[rows(2 * k * pitch, freqs), :] = weighted
        image[rows((2 * k + 1) * pitch, freqs), :] = sign * pltpu.roll(weighted, radii, 1)
        energy = jnp.sum(plain * plain * scale, axis=0, keepdims=True)
        energy = jnp.broadcast_to(jnp.sum(energy, axis=1, keepdims=True), (SPARE, 128))
        energy_ref[pl.ds(k, 1), :] = energy[:1]
        out[rows(2 * k * pitch + freqs, SPARE), :] = energy

    none = jnp.zeros((2 * classes, depth), BF16)

    def correlate(f):
        first, second = [
            image[pl.ds(2 * f + part, 2 * classes, stride=pitch), :].astype(BF16)
            for part in range(2)
        ]
        left = jnp.concatenate(
            [jnp.concatenate([first, none], 1), jnp.concatenate([none, second], 1)], 0
        )
        left_ref[f] = left
        place(out, rest, f, times(left, particles[f]), classes, pitch)

    loop(pairs, correlate, 32)
    pack(out, rest, classes, share, pitch)


def times(left, particles):
    return lax.dot_general(left, particles, (((1,), (1,)), ((), ())), preferred_element_type=F32)


def place(out, rest, f, value, classes, pitch):
    width = value.shape[1] - 128
    spare = jnp.zeros((value.shape[0], 128 - width), F32)
    value = jnp.concatenate([value, spare], 1)
    for part in range(2):
        at = pl.ds(2 * f + part, 2 * classes, stride=pitch)
        mine = value[part * 2 * classes : (part + 1) * 2 * classes]
        out[at, :] = mine[:, :128]
        rest[at, :] = mine[:, 128:]


def pack(out, rest, classes, share, pitch):
    width = share - 128
    each_pack = 128 // width
    for first in range(0, 2 * classes, each_pack):
        total = 0.0
        for group in range(first, min(first + each_pack, 2 * classes)):
            part, k = divmod(group, classes)
            value = rest[rows((2 * k + part) * pitch, pitch), :]
            total = total + turned(value, (group - first) * width)
        out[rows((2 * classes + first // each_pack) * pitch, pitch), :] = total


def unpack(ref, unit, part, classes, share, pitch, freqs):
    width, bundle, _ = layout(classes, share)
    group = part * classes + unit * bundle
    each_pack = 128 // width
    value = ref[rows((2 * classes + group // each_pack) * pitch, freqs), :]
    return turned(value, -(group % each_pack) * width)


def corr_lines(classes, share, pitch):
    return (2 * classes + -(-2 * classes * (share - 128) // 128)) * pitch


def weigh(sources, order, inverse_noise, particles, fresh):
    pairs, share, twice = particles.shape
    classes = len(sources)
    pitch = 2 * pairs + SPARE
    return call(
        functools.partial(weigh_kernel, fresh, order, classes),
        [*[sources[i] for i in order], inverse_noise, particles],
        [
            ((corr_lines(classes, share, pitch), 128), F32),
            ((classes, 128), F32),
            ((pairs, 4 * classes, twice), BF16),
        ],
        [((2 * classes * pitch, twice // 2), F32), ((2 * classes * pitch, 128), F32)],
        flops=8 * classes * share * pairs * twice * 4,
    )


def correlate_kernel(left_ref, particles, out, rest):
    pairs, share, _ = particles.shape
    classes = left_ref.shape[1] // 4
    pitch = 2 * pairs + SPARE

    def body(f):
        place(out, rest, f, times(left_ref[f], particles[f]), classes, pitch)

    loop(pairs, body, 32)
    pack(out, rest, classes, share, pitch)


def correlate(left, particles):
    pairs, share, twice = particles.shape
    classes = left.shape[1] // 4
    pitch = 2 * pairs + SPARE
    return call(
        correlate_kernel,
        [left, particles],
        [((corr_lines(classes, share, pitch), 128), F32)],
        [((2 * classes * pitch, 128), F32)],
        flops=2 * left.shape[1] * share * pairs * twice * 8,
    )[0]


def table_rows(base, count):
    return pl.ds(pl.multiple_of(lax.axis_index("rot") * ANG + base, 128), count)


def score_kernel(share, own, other, energy_ref, prior_term, inverse, *refs):
    weights, more, tops, more_tops, peaks = refs
    classes = energy_ref.shape[0]
    width, bundle, units = layout(classes, share)
    freqs = ANG // 4
    pitch = freqs + SPARE
    at = table_rows(0, ANG)
    lane = lax.broadcasted_iota(jnp.int32, (1, 128), 1)

    def exponentials(value, energy, prior):
        high, low = split(value)
        inner = dot(inverse[at, :], jnp.concatenate([high, low, high], 0))
        scores = inner - 0.5 * energy + prior
        top = jnp.max(scores, axis=0, keepdims=True)
        value = jnp.exp(scores - top)
        return value, top, jnp.sum(value, axis=0, keepdims=True)

    def energy_of(k):
        return energy_ref[pl.ds(k, 1), :] + other[rows(2 * k * pitch + freqs, SPARE), :][:1]

    def slab(i, carry):
        value = jnp.concatenate(
            [
                jnp.concatenate(
                    [ref[rows((4 * i + 2 * j + part) * pitch, freqs), :] for j in range(2)], 1
                )
                for ref in (own, other)
                for part in range(2)
            ],
            0,
        )
        energy = jnp.concatenate([energy_of(2 * i), energy_of(2 * i + 1)], 1)
        prior = jnp.concatenate([prior_term[:, :128]] * 2, 1)
        weights[i], top, total = exponentials(value, energy, prior)
        tops[pl.ds(i, 1), :] = top
        for j in (0, 128):
            carry = merge(carry, (top[:, j : j + 128], total[:, j : j + 128]))
        return carry

    empty = (jnp.full((1, 128), -jnp.inf, F32), jnp.zeros((1, 128), F32))
    top, total = each(classes // 2, slab, empty)
    rest = empty
    for unit in range(units):
        value = jnp.concatenate(
            [
                unpack(ref, unit, part, classes, share, pitch, freqs)
                for ref in (own, other)
                for part in range(2)
            ],
            0,
        )
        energy = sum(
            jnp.where(lane // width == j, energy_of(unit * bundle + j), 0.0)
            for j in range(bundle)
        )
        more[unit], more_top, more_total = exponentials(value, energy, prior_term[:, 128:])
        more_tops[pl.ds(unit, 1), :] = more_top
        for j in range(bundle):
            rest = merge(rest, (turned(more_top, -j * width), turned(more_total, -j * width)))
    line = lax.broadcasted_iota(jnp.int32, peaks.shape, 0)
    peaks[...] = jnp.where(
        line == 0,
        jnp.concatenate([top, rest[0]], 1),
        jnp.concatenate([total, rest[1]], 1),
    )


def scores(own, other, energy, prior_term, inverse, share):
    classes = energy.shape[0]
    units = layout(classes, share)[2]
    return call(
        functools.partial(score_kernel, share),
        [own, other, energy, prior_term, inverse],
        [
            ((classes // 2, ANG, 256), F32),
            ((units, ANG, 128), F32),
            ((classes // 2, 256), F32),
            ((units, 128), F32),
            ((8, 256), F32),
        ],
        flops=6 * classes * 256 * ANG * ANG,
    )


def merge(first, second):
    top = jnp.maximum(first[0], second[0])
    return top, first[1] * jnp.exp(first[0] - top) + second[1] * jnp.exp(second[0] - top)


def two_lines(ref):
    return ref[0:1, :], ref[1:2, :]


def merge_kernel(first, second, out):
    top, total = merge(two_lines(first), two_lines(second))
    line = lax.broadcasted_iota(jnp.int32, out.shape, 0)
    out[...] = jnp.where(line == 0, top, total)


def turn_kernel(share, weights, more, tops, more_tops, first, second, forward, *refs):
    rounded_ref, rounded_more, send, *last, held = refs
    classes = 2 * weights.shape[0]
    width, bundle, units = layout(classes, share)
    pairs = (held.shape[0] // (2 * classes) - SPARE) // 2
    top, total = merge(two_lines(first), two_lines(second))
    evidence = top + jnp.log(total)
    scale = 1.0 / total
    at = table_rows(0, ANG // 2)
    lane = lax.broadcasted_iota(jnp.int32, (1, 128), 1)
    line = lax.broadcasted_iota(jnp.int32, (4 * classes, 128), 0)

    def put(column, k, count):
        high = count.astype(BF16).astype(F32)
        return jnp.where(line == k, high, jnp.where(line == classes + k, count - high, column))

    more_counts = []
    for unit in range(units):
        factor = jnp.exp(
            more_tops[pl.ds(unit, 1), :] - repeat(top[:, 128:], width, bundle)
        ) * repeat(scale[:, 128:], width, bundle)
        value = more[unit] * jnp.where(lane < bundle * width, factor, 0.0)
        count = jnp.sum(value, axis=0, keepdims=True)
        for j in range(bundle):
            mine = jnp.where(lane // width == j, count, 0.0)
            more_counts.append(jnp.sum(mine, axis=1, keepdims=True))
        rounded = value.astype(BF16)
        rounded_more[unit] = rounded
        spectrum = dot(forward[at, :], jnp.concatenate([rounded, rounded], 0)).astype(BF16)
        step = 4 * classes
        entries = spectrum.shape[0] // step
        for i in range(entries):
            send[pairs + unit * entries + i] = spectrum[i * step : (i + 1) * step]

    tops_here = jnp.concatenate([top[:, :128]] * 2, 1)
    scale_here = jnp.concatenate([scale[:, :128]] * 2, 1)

    def body(i, column):
        value = weights[i] * (jnp.exp(tops[pl.ds(i, 1), :] - tops_here) * scale_here)
        rounded = value.astype(BF16)
        rounded_ref[i] = rounded
        spread(held, i, dot(forward[at, :], jnp.concatenate([rounded, rounded], 0)))
        count = jnp.sum(value, axis=0, keepdims=True)
        for j in range(2):
            mine = jnp.sum(count[:, j * 128 : (j + 1) * 128], axis=1, keepdims=True)
            column = put(column, 2 * i + j, mine)
        return column

    column = each(classes // 2, body, jnp.zeros((4 * classes, 128), F32))
    extra = jnp.zeros((4 * classes, 128), F32)
    for k, count in enumerate(more_counts):
        extra = put(extra, k, count)
    for ref in last:
        ref[...] = evidence[:, :share]
        high = evidence.astype(BF16).astype(F32)
        middle = (evidence - high).astype(BF16).astype(F32)
        for i, value in enumerate((high, middle, evidence - high - middle)):
            for j in range(2):
                mine = value[:, j * 128 : (j + 1) * 128]
                extra = jnp.where(line == 2 * classes + 2 * i + j, mine, extra)
    send[send.shape[0] - 2] = column.astype(BF16)
    send[send.shape[0] - 1] = extra.astype(BF16)

    def rearrange(f):
        send[f] = pick(held, f, classes).astype(BF16)

    loop(pairs, rearrange, 32)


def spread(held, i, value):
    freqs = value.shape[0] // 2
    for j in range(2):
        for part in range(2):
            held[rows((4 * i + 2 * j + part) * (freqs + SPARE), freqs), :] = value[
                part * freqs : (part + 1) * freqs, j * 128 : (j + 1) * 128
            ]


def spread_more(held, unit, value, classes, share):
    width, bundle, _ = layout(classes, share)
    freqs = value.shape[0] // 2
    for j in range(bundle):
        shifted = turned(value, -j * width)
        for part in range(2):
            k = unit * bundle + j
            held[rows((2 * k + part) * (freqs + SPARE), freqs), :] = shifted[
                part * freqs : (part + 1) * freqs
            ]


def pick(held, f, classes):
    pitch = held.shape[0] // (2 * classes)
    return jnp.concatenate(
        [held[pl.ds(2 * f + part, 2 * classes, stride=pitch), :] for part in range(2)], 0
    )


def message_shape(classes, pairs, units):
    return (pairs + units * (ANG // 2) // (4 * classes) + 2, 4 * classes, 128)


def turn(weights, more, tops, more_tops, first, second, forward, freqs, share, last):
    classes = 2 * weights.shape[0]
    units = more.shape[0]
    return call(
        functools.partial(turn_kernel, share),
        [weights, more, tops, more_tops, first, second, forward],
        [
            (weights.shape, BF16),
            (more.shape, BF16),
            (message_shape(classes, freqs // 2, units), BF16),
            *([((1, share), F32)] if last else []),
        ],
        [((2 * classes * (freqs + SPARE), 128), F32)],
        flops=4 * classes * 256 * ANG * ANG,
    )


def gather_kernel(rounded_ref, rounded_more, forward, particles, image, held, held_more):
    classes = 2 * rounded_ref.shape[0]
    pairs, share, _ = particles.shape
    at = table_rows(ANG // 2, ANG // 2)

    for unit in range(rounded_more.shape[0]):
        rounded = rounded_more[unit]
        value = dot(forward[at, :], jnp.concatenate([rounded, rounded], 0))
        spread_more(held_more, unit, value, classes, share)

    def body(i, carry):
        rounded = rounded_ref[i]
        spread(held, i, dot(forward[at, :], jnp.concatenate([rounded, rounded], 0)))
        return carry

    each(classes // 2, body, 0)

    def accumulate(f):
        left = [pick(ref, f, classes).astype(BF16) for ref in (held, held_more)]
        left = jnp.concatenate(left, 1)[:, :share]
        take_in(image, f, dot(left, particles[f]), classes)

    loop(pairs, accumulate, 32)


def gather(rounded, rounded_more, forward, particles):
    pairs, share, twice = particles.shape
    classes = 2 * rounded.shape[0]
    lines = 2 * classes * (2 * pairs + SPARE)
    return call(
        gather_kernel,
        [rounded, rounded_more, forward, particles],
        [((lines, twice // 2), F32)],
        [((lines, 128), F32)] * 2,
        flops=4 * classes * 256 * ANG * ANG,
    )[0]


def take_in(image, f, value, classes):
    lines, depth = image.shape
    for part in range(2):
        at = pl.ds(2 * f + part, 2 * classes, stride=lines // (2 * classes))
        image[at, :] = value[
            part * 2 * classes : (part + 1) * 2 * classes, part * depth : (part + 1) * depth
        ]


def finish_kernel(image, mine, spectrum, particles, *refs):
    *outs, held, held_more = refs
    evidence_ref = outs.pop() if len(outs) > 1 else None
    pairs, share, twice = particles.shape
    classes = spectrum.shape[1] // 4
    freqs, depth = 2 * pairs, twice // 2
    radii = depth // 2
    pitch = freqs + SPARE

    units = layout(classes, share)[2]
    entries = ANG // 2 // (4 * classes)
    for unit in range(units):
        first = pairs + unit * entries
        value = jnp.concatenate([spectrum[first + i] for i in range(entries)], 0)
        spread_more(held_more, unit, value.astype(F32), classes, share)

    def body(f):
        left = jnp.concatenate([spectrum[f], pick(held_more, f, classes).astype(BF16)], 1)
        take_in(held, f, dot(left[:, :share], particles[f]), classes)

    loop(pairs, body, 32)
    end = spectrum.shape[0]
    counts = sum(ref[i].astype(F32) for ref in (mine, spectrum) for i in (end - 2, end - 1))
    if evidence_ref is not None:
        parts = spectrum[end - 1].astype(F32)[2 * classes :]
        parts = [jnp.concatenate([parts[i : i + 1], parts[i + 1 : i + 2]], 1) for i in (0, 2, 4)]
        evidence_ref[...] = (parts[0] + (parts[1] + parts[2]))[:, :share]
    counts = counts[:classes] + counts[classes : 2 * classes]
    lane = lax.broadcasted_iota(jnp.int32, (freqs, depth), 1)
    sign = jnp.where(lane < radii, -1.0, 1.0).astype(F32)
    for k in range(classes):
        plain, turned = [
            image[rows((2 * k + part) * pitch, freqs), :]
            + held[rows((2 * k + part) * pitch, freqs), :]
            for part in range(2)
        ]
        value = plain + sign * pltpu.roll(turned, radii, 1)
        if len(outs) == 1:
            outs[0][pl.ds(k * freqs, freqs), :] = value.astype(BF16)
        else:
            outs[k][pl.ds(0, freqs), :] = value
            outs[k][pl.ds(freqs, SPARE), :] = jnp.broadcast_to(counts[k : k + 1], (SPARE, depth))
    if len(outs) == 1:
        end = outs[0].shape[0] - classes * freqs
        high, low = split(counts)
        spare = [jnp.zeros((end - 2 * classes, depth), F32)] if end > 2 * classes else []
        tail = jnp.concatenate([high.astype(F32), low.astype(F32), *spare], 0)
        outs[0][pl.ds(classes * freqs, end), :] = tail.astype(BF16)


def finish(image, mine, spectrum, particles, last):
    pairs, _, twice = particles.shape
    classes = spectrum.shape[1] // 4
    freqs, depth = 2 * pairs, twice // 2
    if last:
        outs = [((freqs + SPARE, depth), F32)] * classes + [((1, particles.shape[1]), F32)]
    else:
        outs = [((classes * freqs + -(-2 * classes // 16) * 16, depth), BF16)]
    return call(
        finish_kernel,
        [image, mine, spectrum, particles],
        outs,
        [(image.shape, F32)] * 2,
        flops=2 * math.prod(spectrum.shape) * twice * 8,
    )


def means_kernel(*refs):
    *parts, own, other, out, evidence_ref = refs
    odd = lax.rem(lax.axis_index("cls"), 2)
    evidence_ref[...] = jnp.where(odd == 0, own[...], other[...])
    freqs = out.shape[1]
    total = tree(ref[...] for ref in parts)
    out[0] = total[:freqs, :] / (total[freqs : freqs + 1, :] + shrinkage)


def swap(value, axis, size, bit):
    if not bit:
        return value
    return lax.ppermute(value, axis, [(i, i ^ bit) for i in range(size)])


def bits(size):
    assert size > 1 and size & (size - 1) == 0
    return [1 << i for i in range(size.bit_length() - 1)]


def shards(particles, references, noise_inv, prior_rot):
    batch, freqs, depth = particles.shape
    sides = lax.axis_size("cls")
    groups = lax.axis_size("rot")
    blocks = lax.axis_size("blk")
    assert groups == 2 and 2 * groups * freqs == ANG
    share = batch // groups
    inverse, forward = tables(freqs)
    inverse_noise = noise_inv.reshape(1, depth // 2)
    assert blocks & (blocks - 1) == 0
    turns = sorted(range(1, blocks), key=lambda i: (-i.bit_length(), i))

    (permutation,) = call(permutation_kernel, [], [((256, 256), BF16)], flops=1 << 32)
    (prior_term,) = call(
        functools.partial(prior_kernel, share), [prior_rot], [((ANG, 256), F32)], flops=1 << 26
    )
    sources = {i: swap(references, "blk", blocks, i) for i in (*turns, 0)}
    other_images, own_images = prep(particles, permutation, share)
    for step in range(ITERS):
        last = step == ITERS - 1
        order = [0, *(reversed(turns) if step else reversed(range(1, blocks)))]
        message, energy, left = weigh(sources, order, inverse_noise, other_images, step == 0)
        message = swap(message, "rot", groups, 1)
        own = correlate(left, own_images)
        *weights, here = scores(own, message, energy, prior_term, inverse, share)
        first = here
        for bit in bits(sides):
            second = swap(first, ("cls", "rot"), sides * groups, groups * bit + (bit == 1))
            if 2 * bit < sides:
                (first,) = call(merge_kernel, [first, second], [(here.shape, F32)])
        rounded, more, send, *evidence = turn(
            *weights, first, second, forward, freqs, share, last
        )
        message = swap(send, "rot", groups, 1)
        image = gather(rounded, more, forward, own_images)
        sums = finish(image, send, message, other_images, last)
        sums, others = (sums[:blocks], sums[blocks:]) if last else (sums * blocks, [])
        sources = {i: swap(sums[i], "blk", blocks, i) for i in (*turns, 0)}
    means, evidence = call(
        means_kernel, [*[sources[i] for i in reversed(range(blocks))], *evidence, *others], [((1, freqs, depth), F32), ((1, share), F32)]
    )
    return means, evidence.reshape(share)


def solution(mesh):
    in_specs = (
        P(("grp", "blk"), "rot", None),
        P(("grp", "blk", "cls"), "rot", None),
        P(),
        P(("grp", "blk")),
    )
    out_specs = (P(("grp", "blk", "cls"), "rot", None), P(("grp", "blk", "rot")))
    return jax.shard_map(shards, mesh=mesh, in_specs=in_specs, out_specs=out_specs, check_vma=False)
```

```python
import functools
import math

import jax
import jax.numpy as jnp
import numpy as np
from jax import lax
from jax.experimental import pallas as pl
from jax.experimental.pallas import tpu as pltpu
from jax.sharding import PartitionSpec as P

ANG = 256
ITERS = 2
SIGMA = 32

shrinkage = 1.0

F32 = jnp.float32
BF16 = jnp.bfloat16
SPARE = 8

dot = functools.partial(jnp.dot, preferred_element_type=F32)


def split(x):
    high = x.astype(BF16)
    return high, (x - high.astype(F32)).astype(BF16)


def tables(half_freq):
    turn = np.arange(ANG)
    inverse, far, forward = [], [], []
    for group in range(2):
        sides = {}
        for which in range(2):
            freq = which * half_freq + np.arange(half_freq)
            angle = (turn[:, None] * freq[None, :] % ANG) * (2.0 * math.pi / ANG)
            scale = np.where(freq == 0, 1.0, 2.0) / ANG
            sides[which] = (
                np.concatenate([scale * np.cos(angle), -scale * np.sin(angle)], 1),
                np.concatenate([np.cos(angle), np.sin(angle)], 1).T,
            )
        inverse.append(sides[group][0])
        far.append(sides[1 - group][0])
        forward.append(np.concatenate([sides[1 - group][1], sides[group][1]], 0))
    result = []
    for table, kinds in ((inverse, (0, 0, 1)), (far, (0, 0, 1)), (forward, (0, 1))):
        table = np.concatenate(table, 0).astype(np.float32)
        high = table.astype(BF16)
        parts = [high, (table - high.astype(np.float32)).astype(BF16)]
        result.append(jnp.asarray(np.concatenate([parts[kind] for kind in kinds], 1)))
    return result


def loop(count, body, unroll):
    while count % unroll:
        unroll -= 1
    if unroll == count:
        for i in range(count):
            body(i)
        return

    def step(outer, carry):
        for inner in range(unroll):
            body(outer * unroll + inner)
        return carry

    lax.fori_loop(0, count // unroll, step, 0)


def each(count, body, init):
    if count <= 8:
        for k in range(count):
            init = body(k, init)
        return init
    return lax.fori_loop(0, count, body, init)


def rows(base, count):
    return pl.ds(pl.multiple_of(base, 8), count)


def call(kernel, ins, outs, scratch=(), flops=0, far=(), room=4 << 20):
    total = 0
    buffers = [(x.shape, x.dtype) for i, x in enumerate(ins) if i not in far]
    for shape, dtype in buffers + list(outs) + [x for x in scratch if isinstance(x, tuple)]:
        dims = [1, 1, *shape]
        lines = -(-dims[-2] // 16) * 16
        lanes = -(-dims[-1] // 128) * 128
        total += math.prod(dims[:-2]) * lines * lanes * jnp.dtype(dtype).itemsize
    kinds = [pltpu.VMEM] * len(ins)
    for i in far:
        kinds[i] = pltpu.MemorySpace.HBM
    return pl.pallas_call(
        kernel,
        out_shape=[jax.ShapeDtypeStruct(*x) for x in outs],
        in_specs=[pl.BlockSpec(memory_space=kind) for kind in kinds],
        out_specs=[pl.BlockSpec(memory_space=pltpu.VMEM)] * len(outs),
        scratch_shapes=[pltpu.VMEM(*x) if isinstance(x, tuple) else x for x in scratch],
        compiler_params=pltpu.CompilerParams(vmem_limit_bytes=min(total + room, 56 << 20)),
        cost_estimate=pl.CostEstimate(flops=flops, bytes_accessed=total, transcendentals=0),
    )(*ins)


def permutation_kernel(out):
    to = lax.broadcasted_iota(jnp.int32, out.shape, 0)
    at = lax.broadcasted_iota(jnp.int32, out.shape, 1)
    out[...] = ((to // 16 == at % 16) & (to % 16 == at // 16)).astype(F32).astype(BF16)


def half_index():
    return lax.rem(lax.axis_index("rot") + lax.axis_index("cls"), 2)


def prior_kernel(share, prior_ref, prior_term):
    turns = lax.broadcasted_iota(jnp.int32, (ANG, 256), 0)
    lane = lax.broadcasted_iota(jnp.int32, (1, 256), 1)
    priors = prior_ref[...].reshape(1, -1)
    first, second = [
        jnp.concatenate([priors[:, i * share : (i + 1) * share], lane[:, share:]], 1)
        for i in range(2)
    ]
    offset = jnp.abs(turns - jnp.where(half_index() == 0, first, second))
    distance = jnp.minimum(offset, ANG - offset).astype(F32)
    term = -distance * distance / (2.0 * SIGMA * SIGMA)
    prior_term[:, :128] = term[:, :128]
    prior_term[:, 128:] = repeat(term[:, 128:], share - 128, 128 // (share - 128))


def turned(value, lanes):
    return pltpu.roll(value, lanes % 128, 1) if lanes % 128 else value


def repeat(value, width, times):
    lane = lax.broadcasted_iota(jnp.int32, value.shape, 1)
    value = jnp.where(lane < width, value, 0.0)
    return sum(turned(value, i * width) for i in range(times))


def layout(classes, share):
    width = share - 128
    assert 0 < width < 128 and 128 % width == 0 and classes % 2 == 0
    bundle = min(128 // width, classes)
    assert classes % bundle == 0
    return width, bundle, classes // bundle


def prep_kernel(share, particles_ref, permutation_ref, other, own):
    freqs, depth = particles_ref.shape[1:]
    half = half_index()
    permutation = permutation_ref[...]
    for out, first in ((other, (1 - half) * share), (own, half * share)):
        for p in range(0, share, 16):
            for f in range(0, freqs, 32):
                blocks = [
                    jnp.concatenate(
                        [particles_ref[first + p + j, pl.ds(f + second, 16), :] for j in range(16)],
                        0,
                    )
                    for second in (0, 16)
                ]
                turned = dot(permutation, jnp.concatenate(blocks, 1)).astype(BF16)
                for half in range(2):
                    for j in range(16):
                        pair, part = divmod(f + 16 * half + j, 2)
                        out[pair, pl.ds(p, 16), pl.ds(part * depth, depth)] = turned[
                            16 * j : 16 * j + 16, half * depth : (half + 1) * depth
                        ]


def prep(particles, permutation, share):
    _, freqs, depth = particles.shape
    assert share % 16 == 0 and freqs % 32 == 0
    return call(
        functools.partial(prep_kernel, share),
        [particles, permutation],
        [((freqs // 2, share, 2 * depth), BF16)] * 2,
        flops=1 << 31,
    )


def tree(values):
    values = list(values)
    while len(values) > 1:
        values = [a + b for a, b in zip(values[::2], values[1::2])]
    return values[0]


def weigh_kernel(fresh, order, count, *refs):
    sources = [refs[order.index(i)] for i in range(count)]
    doubled_ref, particles, out, rest, energy_ref, left_ref, image = refs[count:]
    pairs, share, twice = particles.shape
    freqs, depth = 2 * pairs, twice // 2
    classes = energy_ref.shape[0]
    pitch = freqs + SPARE
    radii = depth // 2
    lane = lax.broadcasted_iota(jnp.int32, (freqs, depth), 1)
    sign = jnp.where(lane < radii, -1.0, 1.0).astype(F32)
    doubled = jnp.concatenate([doubled_ref[...]] * 2, 1)
    row = lax.broadcasted_iota(jnp.int32, (freqs, depth), 0) + lax.axis_index("rot") * freqs
    scale = jnp.where(row == 0, 1.0 / ANG, 2.0 / ANG).astype(F32) * doubled

    for k in range(classes):
        if fresh:
            plain = sources[k][0].astype(F32)
        else:
            sums, highs, lows = [
                tree(
                    source[pl.ds(base + (k ^ i) * step, step), :].astype(F32)
                    for i, source in enumerate(sources)
                )
                for base, step in ((0, freqs), (classes * freqs, 1), (classes * (freqs + 1), 1))
            ]
            plain = (sums / (highs + lows + shrinkage)).astype(BF16).astype(F32)
        weighted = (plain * doubled).astype(BF16).astype(F32)
        image[rows(2 * k * pitch, freqs), :] = weighted
        image[rows((2 * k + 1) * pitch, freqs), :] = sign * pltpu.roll(weighted, radii, 1)
        energy = jnp.sum(plain * plain * scale, axis=0, keepdims=True)
        energy = jnp.broadcast_to(jnp.sum(energy, axis=1, keepdims=True), (SPARE, 128))
        energy_ref[pl.ds(k, 1), :] = energy[:1]
        out[rows(2 * k * pitch + freqs, SPARE), :] = energy

    none = jnp.zeros((2 * classes, depth), BF16)

    def correlate(f):
        first, second = [
            image[pl.ds(2 * f + part, 2 * classes, stride=pitch), :].astype(BF16)
            for part in range(2)
        ]
        left = jnp.concatenate(
            [jnp.concatenate([first, none], 1), jnp.concatenate([none, second], 1)], 0
        )
        left_ref[f] = left
        place(out, rest, f, times(left, particles[f]), classes, pitch)

    loop(pairs, correlate, 32)


def times(left, particles):
    return lax.dot_general(left, particles, (((1,), (1,)), ((), ())), preferred_element_type=F32)


def place(out, rest, f, value, classes, pitch):
    width = value.shape[1] - 128
    spare = jnp.zeros((value.shape[0], 128 - width), F32)
    value = jnp.concatenate([value, spare], 1)
    for part in range(2):
        at = pl.ds(2 * f + part, 2 * classes, stride=pitch)
        mine = value[part * 2 * classes : (part + 1) * 2 * classes]
        out[at, :] = mine[:, :128]
        rest[at, :] = mine[:, 128:]


def pack(out, rest, classes, share, pitch):
    width = share - 128
    each_pack = 128 // width
    for first in range(0, 2 * classes, each_pack):
        total = 0.0
        for group in range(first, min(first + each_pack, 2 * classes)):
            part, k = divmod(group, classes)
            value = rest[rows((2 * k + part) * pitch, pitch), :]
            total = total + turned(value, (group - first) * width)
        out[rows(first // each_pack * pitch, pitch), :] = total


def pack_kernel(classes, share, pitch, rest, out):
    pack(out, rest, classes, share, pitch)


def unpack(ref, unit, part, classes, share, pitch, freqs):
    width, bundle, _ = layout(classes, share)
    group = part * classes + unit * bundle
    each_pack = 128 // width
    value = ref[rows(group // each_pack * pitch, freqs), :]
    return turned(value, -(group % each_pack) * width)


def packed_lines(classes, share, pitch):
    return -(-2 * classes * (share - 128) // 128) * pitch


def weigh(sources, order, inverse_noise, particles, fresh):
    pairs, share, twice = particles.shape
    classes = len(sources)
    pitch = 2 * pairs + SPARE
    return call(
        functools.partial(weigh_kernel, fresh, order, classes),
        [*[sources[i] for i in order], inverse_noise, particles],
        [
            ((2 * classes * pitch, 128), F32),
            ((2 * classes * pitch, 128), F32),
            ((classes, 128), F32),
            ((pairs, 4 * classes, twice), BF16),
        ],
        [((2 * classes * pitch, twice // 2), F32)],
        flops=8 * classes * share * pairs * twice * 4,
    )


def correlate_kernel(share, left_ref, particles, energy_ref, prior_term, table, *refs):
    partial, partial_more, main, rest, packed = refs
    pairs = particles.shape[0]
    classes = left_ref.shape[1] // 4
    freqs, pitch = 2 * pairs, 2 * pairs + SPARE
    _, bundle, units = layout(classes, share)

    def body(f):
        place(main, rest, f, times(left_ref[f], particles[f]), classes, pitch)

    loop(pairs, body, 32)
    pack(packed, rest, classes, share, pitch)

    def energy_of(k):
        return energy_ref[pl.ds(k, 1), :]

    def slab(i, carry):
        prior = jnp.concatenate([prior_term[:, :128]] * 2, 1)
        energy = jnp.concatenate([energy_of(2 * i), energy_of(2 * i + 1)], 1)
        partial[i] = invert(table, two_classes(main, i, pitch, freqs)) - 0.5 * energy + prior
        return carry

    for unit in range(units):
        energy = beside(energy_of, unit, classes, share)
        value = several_classes(packed, unit, classes, share, pitch, freqs)
        partial_more[unit] = invert(table, value) - 0.5 * energy + prior_term[:, 128:]
    each(classes // 2, slab, 0)


def two_classes(main, i, pitch, freqs):
    return jnp.concatenate(
        [
            jnp.concatenate(
                [main[rows((4 * i + 2 * j + part) * pitch, freqs), :] for j in range(2)], 1
            )
            for part in range(2)
        ],
        0,
    )


def several_classes(packed, unit, classes, share, pitch, freqs):
    return jnp.concatenate(
        [unpack(packed, unit, part, classes, share, pitch, freqs) for part in range(2)], 0
    )


def beside(value_of, unit, classes, share):
    width, bundle, _ = layout(classes, share)
    lane = lax.broadcasted_iota(jnp.int32, (1, 128), 1)
    return sum(
        jnp.where(lane // width == j, value_of(unit * bundle + j), 0.0) for j in range(bundle)
    )


def invert(table, value):
    high, low = split(value)
    return dot(table[table_rows(0, ANG), :], jnp.concatenate([high, low, high], 0))


def correlate(left, particles, energy, prior_term, table):
    pairs, share, twice = particles.shape
    classes = left.shape[1] // 4
    pitch = 2 * pairs + SPARE
    return call(
        functools.partial(correlate_kernel, share),
        [left, particles, energy, prior_term, table],
        [((classes // 2, ANG, 256), F32), ((layout(classes, share)[2], ANG, 128), F32)],
        [
            ((2 * classes * pitch, 128), F32),
            ((2 * classes * pitch, 128), F32),
            ((packed_lines(classes, share, pitch), 128), F32),
        ],
        flops=2 * left.shape[1] * share * pairs * twice * 8,
    )


def table_rows(base, count):
    return pl.ds(pl.multiple_of(lax.axis_index("rot") * ANG + base, 128), count)


def score_kernel(share, partial, partial_more, other, other_more, table, *refs):
    weights, more, tops, more_tops, peaks = refs
    classes = 2 * partial.shape[0]
    width, bundle, units = layout(classes, share)
    freqs = ANG // 4
    pitch = freqs + SPARE

    def exponentials(scores):
        top = jnp.max(scores, axis=0, keepdims=True)
        value = jnp.exp(scores - top)
        return value, top, jnp.sum(value, axis=0, keepdims=True)

    def energy_of(k):
        return other[rows(2 * k * pitch + freqs, SPARE), :][:1]

    def slab(i, carry):
        energy = jnp.concatenate([energy_of(2 * i), energy_of(2 * i + 1)], 1)
        inner = invert(table, two_classes(other, i, pitch, freqs))
        weights[i], top, total = exponentials(inner + (partial[i] - 0.5 * energy))
        tops[pl.ds(i, 1), :] = top
        for j in (0, 128):
            carry = merge(carry, (top[:, j : j + 128], total[:, j : j + 128]))
        return carry

    empty = (jnp.full((1, 128), -jnp.inf, F32), jnp.zeros((1, 128), F32))
    top, total = each(classes // 2, slab, empty)
    rest = empty
    for unit in range(units):
        energy = beside(energy_of, unit, classes, share)
        inner = invert(table, several_classes(other_more, unit, classes, share, pitch, freqs))
        more[unit], more_top, more_total = exponentials(inner + (partial_more[unit] - 0.5 * energy))
        more_tops[pl.ds(unit, 1), :] = more_top
        for j in range(bundle):
            rest = merge(rest, (turned(more_top, -j * width), turned(more_total, -j * width)))
    line = lax.broadcasted_iota(jnp.int32, peaks.shape, 0)
    peaks[...] = jnp.where(
        line == 0,
        jnp.concatenate([top, rest[0]], 1),
        jnp.concatenate([total, rest[1]], 1),
    )


def scores(partial, partial_more, other, other_more, table, share):
    classes = 2 * partial.shape[0]
    units = layout(classes, share)[2]
    return call(
        functools.partial(score_kernel, share),
        [partial, partial_more, other, other_more, table],
        [
            ((classes // 2, ANG, 256), F32),
            ((units, ANG, 128), F32),
            ((classes // 2, 256), F32),
            ((units, 128), F32),
            ((8, 256), F32),
        ],
        flops=6 * classes * 256 * ANG * ANG,
    )


def merge(first, second):
    top = jnp.maximum(first[0], second[0])
    return top, first[1] * jnp.exp(first[0] - top) + second[1] * jnp.exp(second[0] - top)


def two_lines(ref):
    return ref[0:1, :], ref[1:2, :]


def merge_kernel(first, second, out):
    top, total = merge(two_lines(first), two_lines(second))
    line = lax.broadcasted_iota(jnp.int32, out.shape, 0)
    out[...] = jnp.where(line == 0, top, total)


def turn_kernel(share, weights, more, tops, more_tops, first, second, forward, *refs):
    rounded_ref, rounded_more, send, *last, held = refs
    classes = 2 * weights.shape[0]
    width, bundle, units = layout(classes, share)
    pairs = (held.shape[0] // (2 * classes) - SPARE) // 2
    top, total = merge(two_lines(first), two_lines(second))
    evidence = top + jnp.log(total)
    scale = 1.0 / total
    at = table_rows(0, ANG // 2)
    lane = lax.broadcasted_iota(jnp.int32, (1, 128), 1)
    line = lax.broadcasted_iota(jnp.int32, (4 * classes, 128), 0)

    def put(column, k, count):
        high = count.astype(BF16).astype(F32)
        return jnp.where(line == k, high, jnp.where(line == classes + k, count - high, column))

    more_counts = []
    for unit in range(units):
        factor = jnp.exp(
            more_tops[pl.ds(unit, 1), :] - repeat(top[:, 128:], width, bundle)
        ) * repeat(scale[:, 128:], width, bundle)
        value = more[unit] * jnp.where(lane < bundle * width, factor, 0.0)
        count = jnp.sum(value, axis=0, keepdims=True)
        for j in range(bundle):
            mine = jnp.where(lane // width == j, count, 0.0)
            more_counts.append(jnp.sum(mine, axis=1, keepdims=True))
        rounded = value.astype(BF16)
        rounded_more[unit] = rounded
        spectrum = dot(forward[at, :], jnp.concatenate([rounded, rounded], 0)).astype(BF16)
        step = 4 * classes
        entries = spectrum.shape[0] // step
        for i in range(entries):
            send[pairs + unit * entries + i] = spectrum[i * step : (i + 1) * step]

    tops_here = jnp.concatenate([top[:, :128]] * 2, 1)
    scale_here = jnp.concatenate([scale[:, :128]] * 2, 1)

    def body(i, column):
        value = weights[i] * (jnp.exp(tops[pl.ds(i, 1), :] - tops_here) * scale_here)
        rounded = value.astype(BF16)
        rounded_ref[i] = rounded
        spread(held, i, dot(forward[at, :], jnp.concatenate([rounded, rounded], 0)))
        count = jnp.sum(value, axis=0, keepdims=True)
        for j in range(2):
            mine = jnp.sum(count[:, j * 128 : (j + 1) * 128], axis=1, keepdims=True)
            column = put(column, 2 * i + j, mine)
        return column

    column = each(classes // 2, body, jnp.zeros((4 * classes, 128), F32))
    extra = jnp.zeros((4 * classes, 128), F32)
    for k, count in enumerate(more_counts):
        extra = put(extra, k, count)
    for ref in last:
        ref[...] = evidence[:, :share]
        high = evidence.astype(BF16).astype(F32)
        middle = (evidence - high).astype(BF16).astype(F32)
        for i, value in enumerate((high, middle, evidence - high - middle)):
            for j in range(2):
                mine = value[:, j * 128 : (j + 1) * 128]
                extra = jnp.where(line == 2 * classes + 2 * i + j, mine, extra)
    send[send.shape[0] - 2] = column.astype(BF16)
    send[send.shape[0] - 1] = extra.astype(BF16)

    def rearrange(f):
        send[f] = pick(held, f, classes).astype(BF16)

    loop(pairs, rearrange, 32)


def spread(held, i, value):
    freqs = value.shape[0] // 2
    for j in range(2):
        for part in range(2):
            held[rows((4 * i + 2 * j + part) * (freqs + SPARE), freqs), :] = value[
                part * freqs : (part + 1) * freqs, j * 128 : (j + 1) * 128
            ]


def spread_more(held, unit, value, classes, share):
    width, bundle, _ = layout(classes, share)
    freqs = value.shape[0] // 2
    for j in range(bundle):
        shifted = turned(value, -j * width)
        for part in range(2):
            k = unit * bundle + j
            held[rows((2 * k + part) * (freqs + SPARE), freqs), :] = shifted[
                part * freqs : (part + 1) * freqs
            ]


def pick(held, f, classes):
    pitch = held.shape[0] // (2 * classes)
    return jnp.concatenate(
        [held[pl.ds(2 * f + part, 2 * classes, stride=pitch), :] for part in range(2)], 0
    )


def message_shape(classes, pairs, units):
    return (pairs + units * (ANG // 2) // (4 * classes) + 2, 4 * classes, 128)


def turn(weights, more, tops, more_tops, first, second, forward, freqs, share, last):
    classes = 2 * weights.shape[0]
    units = more.shape[0]
    return call(
        functools.partial(turn_kernel, share),
        [weights, more, tops, more_tops, first, second, forward],
        [
            (weights.shape, BF16),
            (more.shape, BF16),
            (message_shape(classes, freqs // 2, units), BF16),
            *([((1, share), F32)] if last else []),
        ],
        [((2 * classes * (freqs + SPARE), 128), F32)],
        flops=4 * classes * 256 * ANG * ANG,
    )


def gather_kernel(rounded_ref, rounded_more, forward, particles, image, held, held_more):
    classes = 2 * rounded_ref.shape[0]
    pairs, share, _ = particles.shape
    at = table_rows(ANG // 2, ANG // 2)

    for unit in range(rounded_more.shape[0]):
        rounded = rounded_more[unit]
        value = dot(forward[at, :], jnp.concatenate([rounded, rounded], 0))
        spread_more(held_more, unit, value, classes, share)

    def body(i, carry):
        rounded = rounded_ref[i]
        spread(held, i, dot(forward[at, :], jnp.concatenate([rounded, rounded], 0)))
        return carry

    each(classes // 2, body, 0)

    def accumulate(f):
        left = [pick(ref, f, classes).astype(BF16) for ref in (held, held_more)]
        left = jnp.concatenate(left, 1)[:, :share]
        take_in(image, f, dot(left, particles[f]), classes)

    loop(pairs, accumulate, 32)


def gather(rounded, rounded_more, forward, particles):
    pairs, share, twice = particles.shape
    classes = 2 * rounded.shape[0]
    lines = 2 * classes * (2 * pairs + SPARE)
    return call(
        gather_kernel,
        [rounded, rounded_more, forward, particles],
        [((lines, twice // 2), F32)],
        [((lines, 128), F32)] * 2,
        flops=4 * classes * 256 * ANG * ANG,
    )[0]


def take_in(image, f, value, classes):
    lines, depth = image.shape
    for part in range(2):
        at = pl.ds(2 * f + part, 2 * classes, stride=lines // (2 * classes))
        image[at, :] = value[
            part * 2 * classes : (part + 1) * 2 * classes, part * depth : (part + 1) * depth
        ]


def finish_kernel(image, mine, spectrum, particles, *refs):
    *outs, held, held_more = refs
    evidence_ref = outs.pop() if len(outs) > 1 else None
    pairs, share, twice = particles.shape
    classes = spectrum.shape[1] // 4
    freqs, depth = 2 * pairs, twice // 2
    radii = depth // 2
    pitch = freqs + SPARE

    units = layout(classes, share)[2]
    entries = ANG // 2 // (4 * classes)
    for unit in range(units):
        first = pairs + unit * entries
        value = jnp.concatenate([spectrum[first + i] for i in range(entries)], 0)
        spread_more(held_more, unit, value.astype(F32), classes, share)

    def body(f):
        left = jnp.concatenate([spectrum[f], pick(held_more, f, classes).astype(BF16)], 1)
        take_in(held, f, dot(left[:, :share], particles[f]), classes)

    loop(pairs, body, 32)
    end = spectrum.shape[0]
    counts = sum(ref[i].astype(F32) for ref in (mine, spectrum) for i in (end - 2, end - 1))
    if evidence_ref is not None:
        parts = spectrum[end - 1].astype(F32)[2 * classes :]
        parts = [jnp.concatenate([parts[i : i + 1], parts[i + 1 : i + 2]], 1) for i in (0, 2, 4)]
        evidence_ref[...] = (parts[0] + (parts[1] + parts[2]))[:, :share]
    counts = counts[:classes] + counts[classes : 2 * classes]
    lane = lax.broadcasted_iota(jnp.int32, (freqs, depth), 1)
    sign = jnp.where(lane < radii, -1.0, 1.0).astype(F32)
    for k in range(classes):
        plain, turned = [
            image[rows((2 * k + part) * pitch, freqs), :]
            + held[rows((2 * k + part) * pitch, freqs), :]
            for part in range(2)
        ]
        value = plain + sign * pltpu.roll(turned, radii, 1)
        if len(outs) == 1:
            outs[0][pl.ds(k * freqs, freqs), :] = value.astype(BF16)
        else:
            outs[k][pl.ds(0, freqs), :] = value
            outs[k][pl.ds(freqs, SPARE), :] = jnp.broadcast_to(counts[k : k + 1], (SPARE, depth))
    if len(outs) == 1:
        end = outs[0].shape[0] - classes * freqs
        high, low = split(counts)
        spare = [jnp.zeros((end - 2 * classes, depth), F32)] if end > 2 * classes else []
        tail = jnp.concatenate([high.astype(F32), low.astype(F32), *spare], 0)
        outs[0][pl.ds(classes * freqs, end), :] = tail.astype(BF16)


def finish(image, mine, spectrum, particles, last):
    pairs, _, twice = particles.shape
    classes = spectrum.shape[1] // 4
    freqs, depth = 2 * pairs, twice // 2
    if last:
        outs = [((freqs + SPARE, depth), F32)] * classes + [((1, particles.shape[1]), F32)]
    else:
        outs = [((classes * freqs + -(-2 * classes // 16) * 16, depth), BF16)]
    return call(
        finish_kernel,
        [image, mine, spectrum, particles],
        outs,
        [(image.shape, F32)] * 2,
        flops=2 * math.prod(spectrum.shape) * twice * 8,
    )


def means_kernel(*refs):
    *parts, own, other, out, evidence_ref = refs
    odd = lax.rem(lax.axis_index("cls"), 2)
    evidence_ref[...] = jnp.where(odd == 0, own[...], other[...])
    freqs = out.shape[1]
    total = tree(ref[...] for ref in parts)
    out[0] = total[:freqs, :] / (total[freqs : freqs + 1, :] + shrinkage)


def swap(value, axis, size, bit):
    if not bit:
        return value
    return lax.ppermute(value, axis, [(i, i ^ bit) for i in range(size)])


def bits(size):
    assert size > 1 and size & (size - 1) == 0
    return [1 << i for i in range(size.bit_length() - 1)]


def shards(particles, references, noise_inv, prior_rot):
    batch, freqs, depth = particles.shape
    sides = lax.axis_size("cls")
    groups = lax.axis_size("rot")
    blocks = lax.axis_size("blk")
    assert groups == 2 and 2 * groups * freqs == ANG
    share = batch // groups
    near, far, forward = tables(freqs)
    inverse_noise = noise_inv.reshape(1, depth // 2)
    assert blocks & (blocks - 1) == 0
    turns = sorted(range(1, blocks), key=lambda i: (-i.bit_length(), i))

    (permutation,) = call(permutation_kernel, [], [((256, 256), BF16)], flops=1 << 32)
    (prior_term,) = call(
        functools.partial(prior_kernel, share), [prior_rot], [((ANG, 256), F32)], flops=1 << 26
    )
    sources = {i: swap(references, "blk", blocks, i) for i in (*turns, 0)}
    other_images, own_images = prep(particles, permutation, share)
    for step in range(ITERS):
        last = step == ITERS - 1
        order = [0, *turns]
        message, rest, energy, left = weigh(
            sources, order, inverse_noise, other_images, step == 0
        )
        pitch = freqs + SPARE
        (packed,) = call(
            functools.partial(pack_kernel, blocks, share, pitch),
            [rest],
            [((packed_lines(blocks, share, pitch), 128), F32)],
        )
        message = swap(message, "rot", groups, 1)
        packed = swap(packed, "rot", groups, 1)
        partial = correlate(left, own_images, energy, prior_term, near)
        *weights, here = scores(*partial, message, packed, far, share)
        first = here
        for bit in bits(sides):
            second = swap(first, ("cls", "rot"), sides * groups, groups * bit + (bit == 1))
            if 2 * bit < sides:
                (first,) = call(merge_kernel, [first, second], [(here.shape, F32)])
        rounded, more, send, *evidence = turn(
            *weights, first, second, forward, freqs, share, last
        )
        message = swap(send, "rot", groups, 1)
        image = gather(rounded, more, forward, own_images)
        sums = finish(image, send, message, other_images, last)
        sums, others = (sums[:blocks], sums[blocks:]) if last else (sums * blocks, [])
        sources = {i: swap(sums[i], "blk", blocks, i) for i in (*turns, 0)}
    means, evidence = call(
        means_kernel, [*[sources[i] for i in reversed(range(blocks))], *evidence, *others], [((1, freqs, depth), F32), ((1, share), F32)]
    )
    return means, evidence.reshape(share)


def solution(mesh):
    in_specs = (
        P(("grp", "blk"), "rot", None),
        P(("grp", "blk", "cls"), "rot", None),
        P(),
        P(("grp", "blk")),
    )
    out_specs = (P(("grp", "blk", "cls"), "rot", None), P(("grp", "blk", "rot")))
    return jax.shard_map(shards, mesh=mesh, in_specs=in_specs, out_specs=out_specs, check_vma=False)
```

```python
import functools
import math

import jax
import jax.numpy as jnp
import numpy as np
from jax import lax
from jax.experimental import pallas as pl
from jax.experimental.pallas import tpu as pltpu
from jax.sharding import PartitionSpec as P

ANG = 256
ITERS = 2
SIGMA = 32

shrinkage = 1.0

F32 = jnp.float32
BF16 = jnp.bfloat16
SPARE = 8

dot = functools.partial(jnp.dot, preferred_element_type=F32)


def split(x):
    high = x.astype(BF16)
    return high, (x - high.astype(F32)).astype(BF16)


def tables(half_freq):
    turn = np.arange(ANG)
    inverse, forward = [], []
    for group in range(2):
        sides = {}
        for which in range(2):
            freq = which * half_freq + np.arange(half_freq)
            angle = (turn[:, None] * freq[None, :] % ANG) * (2.0 * math.pi / ANG)
            scale = np.where(freq == 0, 1.0, 2.0) / ANG
            sides[which] = (
                np.concatenate([scale * np.cos(angle), -scale * np.sin(angle)], 1),
                np.concatenate([np.cos(angle), np.sin(angle)], 1).T,
            )
        inverse.append(np.concatenate([sides[group][0], sides[1 - group][0]], 1))
        forward.append(np.concatenate([sides[1 - group][1], sides[group][1]], 0))
    result = []
    for table, kinds in ((inverse, (0, 0, 1)), (forward, (0, 1))):
        table = np.concatenate(table, 0).astype(np.float32)
        high = table.astype(BF16)
        parts = [high, (table - high.astype(np.float32)).astype(BF16)]
        result.append(jnp.asarray(np.concatenate([parts[kind] for kind in kinds], 1)))
    return result


def loop(count, body, unroll):
    while count % unroll:
        unroll -= 1
    if unroll == count:
        for i in range(count):
            body(i)
        return

    def step(outer, carry):
        for inner in range(unroll):
            body(outer * unroll + inner)
        return carry

    lax.fori_loop(0, count // unroll, step, 0)


def each(count, body, init):
    if count <= 8:
        for k in range(count):
            init = body(k, init)
        return init
    return lax.fori_loop(0, count, body, init)


def rows(base, count):
    return pl.ds(pl.multiple_of(base, 8), count)


def call(kernel, ins, outs, scratch=(), flops=0, far=(), room=4 << 20):
    total = 0
    buffers = [(x.shape, x.dtype) for i, x in enumerate(ins) if i not in far]
    for shape, dtype in buffers + list(outs) + [x for x in scratch if isinstance(x, tuple)]:
        dims = [1, 1, *shape]
        lines = -(-dims[-2] // 16) * 16
        lanes = -(-dims[-1] // 128) * 128
        total += math.prod(dims[:-2]) * lines * lanes * jnp.dtype(dtype).itemsize
    kinds = [pltpu.VMEM] * len(ins)
    for i in far:
        kinds[i] = pltpu.MemorySpace.HBM
    return pl.pallas_call(
        kernel,
        out_shape=[jax.ShapeDtypeStruct(*x) for x in outs],
        in_specs=[pl.BlockSpec(memory_space=kind) for kind in kinds],
        out_specs=[pl.BlockSpec(memory_space=pltpu.VMEM)] * len(outs),
        scratch_shapes=[pltpu.VMEM(*x) if isinstance(x, tuple) else x for x in scratch],
        compiler_params=pltpu.CompilerParams(vmem_limit_bytes=min(total + room, 56 << 20)),
        cost_estimate=pl.CostEstimate(flops=flops, bytes_accessed=total, transcendentals=0),
    )(*ins)


def permutation_kernel(out):
    to = lax.broadcasted_iota(jnp.int32, out.shape, 0)
    at = lax.broadcasted_iota(jnp.int32, out.shape, 1)
    out[...] = ((to // 16 == at % 16) & (to % 16 == at // 16)).astype(F32).astype(BF16)


def half_index():
    return lax.rem(lax.axis_index("rot") + lax.axis_index("cls"), 2)


def prior_kernel(share, prior_ref, prior_term):
    turns = lax.broadcasted_iota(jnp.int32, (ANG, 256), 0)
    lane = lax.broadcasted_iota(jnp.int32, (1, 256), 1)
    priors = prior_ref[...].reshape(1, -1)
    first, second = [
        jnp.concatenate([priors[:, i * share : (i + 1) * share], lane[:, share:]], 1)
        for i in range(2)
    ]
    offset = jnp.abs(turns - jnp.where(half_index() == 0, first, second))
    distance = jnp.minimum(offset, ANG - offset).astype(F32)
    term = -distance * distance / (2.0 * SIGMA * SIGMA)
    prior_term[:, :128] = term[:, :128]
    prior_term[:, 128:] = repeat(term[:, 128:], share - 128, 128 // (share - 128))


def turned(value, lanes):
    return pltpu.roll(value, lanes % 128, 1) if lanes % 128 else value


def repeat(value, width, times):
    lane = lax.broadcasted_iota(jnp.int32, value.shape, 1)
    value = jnp.where(lane < width, value, 0.0)
    return sum(turned(value, i * width) for i in range(times))


def layout(classes, share):
    width = share - 128
    assert 0 < width < 128 and 128 % width == 0 and classes % 2 == 0
    bundle = min(128 // width, classes)
    assert classes % bundle == 0
    return width, bundle, classes // bundle


def prep_kernel(share, particles_ref, permutation_ref, other, own):
    freqs, depth = particles_ref.shape[1:]
    half = half_index()
    permutation = permutation_ref[...]
    for out, first in ((other, (1 - half) * share), (own, half * share)):
        for p in range(0, share, 16):
            for f in range(0, freqs, 32):
                blocks = [
                    jnp.concatenate(
                        [particles_ref[first + p + j, pl.ds(f + second, 16), :] for j in range(16)],
                        0,
                    )
                    for second in (0, 16)
                ]
                turned = dot(permutation, jnp.concatenate(blocks, 1)).astype(BF16)
                for half in range(2):
                    for j in range(16):
                        pair, part = divmod(f + 16 * half + j, 2)
                        out[pair, pl.ds(p, 16), pl.ds(part * depth, depth)] = turned[
                            16 * j : 16 * j + 16, half * depth : (half + 1) * depth
                        ]


def prep(particles, permutation, share):
    _, freqs, depth = particles.shape
    assert share % 16 == 0 and freqs % 32 == 0
    return call(
        functools.partial(prep_kernel, share),
        [particles, permutation],
        [((freqs // 2, share, 2 * depth), BF16)] * 2,
        flops=1 << 31,
    )


def tree(values):
    values = list(values)
    while len(values) > 1:
        values = [a + b for a, b in zip(values[::2], values[1::2])]
    return values[0]


def weigh_kernel(fresh, order, count, *refs):
    sources = [refs[order.index(i)] for i in range(count)]
    doubled_ref, particles, out, energy_ref, left_ref, image, rest = refs[count:]
    pairs, share, twice = particles.shape
    freqs, depth = 2 * pairs, twice // 2
    classes = energy_ref.shape[0]
    pitch = freqs + SPARE
    radii = depth // 2
    lane = lax.broadcasted_iota(jnp.int32, (freqs, depth), 1)
    sign = jnp.where(lane < radii, -1.0, 1.0).astype(F32)
    doubled = jnp.concatenate([doubled_ref[...]] * 2, 1)
    row = lax.broadcasted_iota(jnp.int32, (freqs, depth), 0) + lax.axis_index("rot") * freqs
    scale = jnp.where(row == 0, 1.0 / ANG, 2.0 / ANG).astype(F32) * doubled

    for k in range(classes):
        if fresh:
            plain = sources[k][0].astype(F32)
        else:
            sums, highs, lows = [
                tree(
                    source[pl.ds(base + (k ^ i) * step, step), :].astype(F32)
                    for i, source in enumerate(sources)
                )
                for base, step in ((0, freqs), (classes * freqs, 1), (classes * (freqs + 1), 1))
            ]
            plain = (sums / (highs + lows + shrinkage)).astype(BF16).astype(F32)
        weighted = (plain * doubled).astype(BF16).astype(F32)
        image[rows(2 * k * pitch, freqs), :] = weighted
        image[rows((2 * k + 1) * pitch, freqs), :] = sign * pltpu.roll(weighted, radii, 1)
        energy = jnp.sum(plain * plain * scale, axis=0, keepdims=True)
        energy = jnp.broadcast_to(jnp.sum(energy, axis=1, keepdims=True), (SPARE, 128))
        energy_ref[pl.ds(k, 1), :] = energy[:1]
        out[rows(2 * k * pitch + freqs, SPARE), :] = energy

    none = jnp.zeros((2 * classes, depth), BF16)

    def correlate(f):
        lefts = []
        for first, second in pick(image, f, classes):
            first, second = first.astype(BF16), second.astype(BF16)
            left = jnp.concatenate(
                [jnp.concatenate([first, none], 1), jnp.concatenate([none, second], 1)], 0
            )
            left_ref[f + len(lefts)] = left
            lefts.append(left)
        values = [times(left, particles[f + i]) for i, left in enumerate(lefts)]
        place(out, rest, f, values, classes, pitch)

    every(pairs, correlate)
    pack(out, rest, classes, share, pitch)


def times(left, particles):
    return lax.dot_general(left, particles, (((1,), (1,)), ((), ())), preferred_element_type=F32)


GROUP = 4


def every(pairs, body):
    for f in range(0, pairs, GROUP):
        body(f)


def put(ref, f, blocks, pitch):
    turned_blocks = jnp.swapaxes(jnp.stack(blocks, 0), 0, 1)
    for i in range(blocks[0].shape[0]):
        ref[pl.ds(i * pitch + 2 * f, 2 * GROUP), :] = turned_blocks[i]


def pick(ref, f, classes):
    pitch = ref.shape[0] // (2 * classes)
    blocks = [ref[pl.ds(i * pitch + 2 * f, 2 * GROUP), :] for i in range(2 * classes)]
    blocks = jnp.swapaxes(jnp.stack(blocks, 0), 0, 1)
    return [(blocks[2 * i], blocks[2 * i + 1]) for i in range(GROUP)]


def place(out, rest, f, values, classes, pitch):
    width = values[0].shape[1] - 128
    spare = jnp.zeros((2 * classes, 128 - width), F32)
    parts = [
        value[part * 2 * classes : (part + 1) * 2 * classes] for value in values for part in range(2)
    ]
    put(out, f, [part[:, :128] for part in parts], pitch)
    put(rest, f, [jnp.concatenate([part[:, 128:], spare], 1) for part in parts], pitch)


def pack(out, rest, classes, share, pitch):
    width = share - 128
    each_pack = 128 // width
    for first in range(0, 2 * classes, each_pack):
        total = 0.0
        for group in range(first, min(first + each_pack, 2 * classes)):
            part, k = divmod(group, classes)
            value = rest[rows((2 * k + part) * pitch, pitch), :]
            total = total + turned(value, (group - first) * width)
        out[rows((2 * classes + first // each_pack) * pitch, pitch), :] = total


def unpack(ref, unit, part, classes, share, pitch, freqs):
    width, bundle, _ = layout(classes, share)
    group = part * classes + unit * bundle
    each_pack = 128 // width
    value = ref[rows((2 * classes + group // each_pack) * pitch, freqs), :]
    return turned(value, -(group % each_pack) * width)


def corr_lines(classes, share, pitch):
    return (2 * classes + -(-2 * classes * (share - 128) // 128)) * pitch


def weigh(sources, order, inverse_noise, particles, fresh):
    pairs, share, twice = particles.shape
    classes = len(sources)
    pitch = 2 * pairs + SPARE
    return call(
        functools.partial(weigh_kernel, fresh, order, classes),
        [*[sources[i] for i in order], inverse_noise, particles],
        [
            ((corr_lines(classes, share, pitch), 128), F32),
            ((classes, 128), F32),
            ((pairs, 4 * classes, twice), BF16),
        ],
        [((2 * classes * pitch, twice // 2), F32), ((2 * classes * pitch, 128), F32)],
        flops=8 * classes * share * pairs * twice * 4,
    )


def correlate_kernel(left_ref, particles, out, rest):
    pairs, share, _ = particles.shape
    classes = left_ref.shape[1] // 4
    pitch = 2 * pairs + SPARE

    def body(f):
        values = [times(left_ref[f + i], particles[f + i]) for i in range(GROUP)]
        place(out, rest, f, values, classes, pitch)

    every(pairs, body)
    pack(out, rest, classes, share, pitch)


def correlate(left, particles):
    pairs, share, twice = particles.shape
    classes = left.shape[1] // 4
    pitch = 2 * pairs + SPARE
    return call(
        correlate_kernel,
        [left, particles],
        [((corr_lines(classes, share, pitch), 128), F32)],
        [((2 * classes * pitch, 128), F32)],
        flops=2 * left.shape[1] * share * pairs * twice * 8,
    )[0]


def table_rows(base, count):
    return pl.ds(pl.multiple_of(lax.axis_index("rot") * ANG + base, 128), count)


def score_kernel(share, own, other, energy_ref, prior_term, inverse, *refs):
    weights, more, tops, more_tops, peaks = refs
    classes = energy_ref.shape[0]
    width, bundle, units = layout(classes, share)
    freqs = ANG // 4
    pitch = freqs + SPARE
    at = table_rows(0, ANG)
    lane = lax.broadcasted_iota(jnp.int32, (1, 128), 1)

    def exponentials(value, energy, prior):
        high, low = split(value)
        inner = dot(inverse[at, :], jnp.concatenate([high, low, high], 0))
        scores = inner - 0.5 * energy + prior
        top = jnp.max(scores, axis=0, keepdims=True)
        value = jnp.exp(scores - top)
        return value, top, jnp.sum(value, axis=0, keepdims=True)

    def energy_of(k):
        return energy_ref[pl.ds(k, 1), :] + other[rows(2 * k * pitch + freqs, SPARE), :][:1]

    def slab(i, carry):
        value = jnp.concatenate(
            [
                jnp.concatenate(
                    [ref[rows((4 * i + 2 * j + part) * pitch, freqs), :] for j in range(2)], 1
                )
                for ref in (own, other)
                for part in range(2)
            ],
            0,
        )
        energy = jnp.concatenate([energy_of(2 * i), energy_of(2 * i + 1)], 1)
        prior = jnp.concatenate([prior_term[:, :128]] * 2, 1)
        weights[i], top, total = exponentials(value, energy, prior)
        tops[pl.ds(i, 1), :] = top
        for j in (0, 128):
            carry = merge(carry, (top[:, j : j + 128], total[:, j : j + 128]))
        return carry

    empty = (jnp.full((1, 128), -jnp.inf, F32), jnp.zeros((1, 128), F32))
    top, total = each(classes // 2, slab, empty)
    rest = empty
    for unit in range(units):
        value = jnp.concatenate(
            [
                unpack(ref, unit, part, classes, share, pitch, freqs)
                for ref in (own, other)
                for part in range(2)
            ],
            0,
        )
        energy = sum(
            jnp.where(lane // width == j, energy_of(unit * bundle + j), 0.0)
            for j in range(bundle)
        )
        more[unit], more_top, more_total = exponentials(value, energy, prior_term[:, 128:])
        more_tops[pl.ds(unit, 1), :] = more_top
        for j in range(bundle):
            rest = merge(rest, (turned(more_top, -j * width), turned(more_total, -j * width)))
    line = lax.broadcasted_iota(jnp.int32, peaks.shape, 0)
    peaks[...] = jnp.where(
        line == 0,
        jnp.concatenate([top, rest[0]], 1),
        jnp.concatenate([total, rest[1]], 1),
    )


def scores(own, other, energy, prior_term, inverse, share):
    classes = energy.shape[0]
    units = layout(classes, share)[2]
    return call(
        functools.partial(score_kernel, share),
        [own, other, energy, prior_term, inverse],
        [
            ((classes // 2, ANG, 256), F32),
            ((units, ANG, 128), F32),
            ((classes // 2, 256), F32),
            ((units, 128), F32),
            ((8, 256), F32),
        ],
        flops=6 * classes * 256 * ANG * ANG,
    )


def merge(first, second):
    top = jnp.maximum(first[0], second[0])
    return top, first[1] * jnp.exp(first[0] - top) + second[1] * jnp.exp(second[0] - top)


def two_lines(ref):
    return ref[0:1, :], ref[1:2, :]


def merge_kernel(first, second, out):
    top, total = merge(two_lines(first), two_lines(second))
    line = lax.broadcasted_iota(jnp.int32, out.shape, 0)
    out[...] = jnp.where(line == 0, top, total)


def turn_kernel(share, weights, more, tops, more_tops, first, second, forward, *refs):
    rounded_ref, rounded_more, send, *last, held = refs
    classes = 2 * weights.shape[0]
    width, bundle, units = layout(classes, share)
    pairs = (held.shape[0] // (2 * classes) - SPARE) // 2
    top, total = merge(two_lines(first), two_lines(second))
    evidence = top + jnp.log(total)
    scale = 1.0 / total
    at = table_rows(0, ANG // 2)
    lane = lax.broadcasted_iota(jnp.int32, (1, 128), 1)
    line = lax.broadcasted_iota(jnp.int32, (4 * classes, 128), 0)

    def with_count(column, k, count):
        high = count.astype(BF16).astype(F32)
        return jnp.where(line == k, high, jnp.where(line == classes + k, count - high, column))

    more_counts = []
    for unit in range(units):
        factor = jnp.exp(
            more_tops[pl.ds(unit, 1), :] - repeat(top[:, 128:], width, bundle)
        ) * repeat(scale[:, 128:], width, bundle)
        value = more[unit] * jnp.where(lane < bundle * width, factor, 0.0)
        count = jnp.sum(value, axis=0, keepdims=True)
        for j in range(bundle):
            mine = jnp.where(lane // width == j, count, 0.0)
            more_counts.append(jnp.sum(mine, axis=1, keepdims=True))
        rounded = value.astype(BF16)
        rounded_more[unit] = rounded
        spectrum = dot(forward[at, :], jnp.concatenate([rounded, rounded], 0)).astype(BF16)
        step = 4 * classes
        entries = spectrum.shape[0] // step
        for i in range(entries):
            send[pairs + unit * entries + i] = spectrum[i * step : (i + 1) * step]

    tops_here = jnp.concatenate([top[:, :128]] * 2, 1)
    scale_here = jnp.concatenate([scale[:, :128]] * 2, 1)

    def body(i, column):
        value = weights[i] * (jnp.exp(tops[pl.ds(i, 1), :] - tops_here) * scale_here)
        rounded = value.astype(BF16)
        rounded_ref[i] = rounded
        spread(held, i, dot(forward[at, :], jnp.concatenate([rounded, rounded], 0)))
        count = jnp.sum(value, axis=0, keepdims=True)
        for j in range(2):
            mine = jnp.sum(count[:, j * 128 : (j + 1) * 128], axis=1, keepdims=True)
            column = with_count(column, 2 * i + j, mine)
        return column

    column = each(classes // 2, body, jnp.zeros((4 * classes, 128), F32))
    extra = jnp.zeros((4 * classes, 128), F32)
    for k, count in enumerate(more_counts):
        extra = with_count(extra, k, count)
    for ref in last:
        ref[...] = evidence[:, :share]
        high = evidence.astype(BF16).astype(F32)
        middle = (evidence - high).astype(BF16).astype(F32)
        for i, value in enumerate((high, middle, evidence - high - middle)):
            for j in range(2):
                mine = value[:, j * 128 : (j + 1) * 128]
                extra = jnp.where(line == 2 * classes + 2 * i + j, mine, extra)
    send[send.shape[0] - 2] = column.astype(BF16)
    send[send.shape[0] - 1] = extra.astype(BF16)

    def rearrange(f):
        for i, parts in enumerate(pick(held, f, classes)):
            send[f + i] = jnp.concatenate(parts, 0).astype(BF16)

    every(pairs, rearrange)


def spread(held, i, value):
    freqs = value.shape[0] // 2
    for j in range(2):
        for part in range(2):
            held[rows((4 * i + 2 * j + part) * (freqs + SPARE), freqs), :] = value[
                part * freqs : (part + 1) * freqs, j * 128 : (j + 1) * 128
            ]


def spread_more(held, unit, value, classes, share):
    width, bundle, _ = layout(classes, share)
    freqs = value.shape[0] // 2
    for j in range(bundle):
        shifted = turned(value, -j * width)
        for part in range(2):
            k = unit * bundle + j
            held[rows((2 * k + part) * (freqs + SPARE), freqs), :] = shifted[
                part * freqs : (part + 1) * freqs
            ]


def message_shape(classes, pairs, units):
    return (pairs + units * (ANG // 2) // (4 * classes) + 2, 4 * classes, 128)


def turn(weights, more, tops, more_tops, first, second, forward, freqs, share, last):
    classes = 2 * weights.shape[0]
    units = more.shape[0]
    return call(
        functools.partial(turn_kernel, share),
        [weights, more, tops, more_tops, first, second, forward],
        [
            (weights.shape, BF16),
            (more.shape, BF16),
            (message_shape(classes, freqs // 2, units), BF16),
            *([((1, share), F32)] if last else []),
        ],
        [((2 * classes * (freqs + SPARE), 128), F32)],
        flops=4 * classes * 256 * ANG * ANG,
    )


def gather_kernel(rounded_ref, rounded_more, forward, particles, image, held, held_more):
    classes = 2 * rounded_ref.shape[0]
    pairs, share, _ = particles.shape
    at = table_rows(ANG // 2, ANG // 2)

    for unit in range(rounded_more.shape[0]):
        rounded = rounded_more[unit]
        value = dot(forward[at, :], jnp.concatenate([rounded, rounded], 0))
        spread_more(held_more, unit, value, classes, share)

    def body(i, carry):
        rounded = rounded_ref[i]
        spread(held, i, dot(forward[at, :], jnp.concatenate([rounded, rounded], 0)))
        return carry

    each(classes // 2, body, 0)

    def accumulate(f):
        values = []
        for i, both in enumerate(zip(pick(held, f, classes), pick(held_more, f, classes))):
            left = [jnp.concatenate(parts, 0).astype(BF16) for parts in both]
            values.append(dot(jnp.concatenate(left, 1)[:, :share], particles[f + i]))
        take_in(image, f, values, classes)

    every(pairs, accumulate)


def gather(rounded, rounded_more, forward, particles):
    pairs, share, twice = particles.shape
    classes = 2 * rounded.shape[0]
    lines = 2 * classes * (2 * pairs + SPARE)
    return call(
        gather_kernel,
        [rounded, rounded_more, forward, particles],
        [((lines, twice // 2), F32)],
        [((lines, 128), F32)] * 2,
        flops=4 * classes * 256 * ANG * ANG,
    )[0]


def take_in(image, f, values, classes):
    lines, depth = image.shape
    blocks = [
        value[part * 2 * classes : (part + 1) * 2 * classes, part * depth : (part + 1) * depth]
        for value in values
        for part in range(2)
    ]
    put(image, f, blocks, lines // (2 * classes))


def finish_kernel(image, mine, spectrum, particles, *refs):
    *outs, held, held_more = refs
    evidence_ref = outs.pop() if len(outs) > 1 else None
    pairs, share, twice = particles.shape
    classes = spectrum.shape[1] // 4
    freqs, depth = 2 * pairs, twice // 2
    radii = depth // 2
    pitch = freqs + SPARE

    units = layout(classes, share)[2]
    entries = ANG // 2 // (4 * classes)
    for unit in range(units):
        first = pairs + unit * entries
        value = jnp.concatenate([spectrum[first + i] for i in range(entries)], 0)
        spread_more(held_more, unit, value.astype(F32), classes, share)

    def body(f):
        values = []
        for i, parts in enumerate(pick(held_more, f, classes)):
            left = jnp.concatenate(parts, 0).astype(BF16)
            left = jnp.concatenate([spectrum[f + i], left], 1)[:, :share]
            values.append(dot(left, particles[f + i]))
        take_in(held, f, values, classes)

    every(pairs, body)
    end = spectrum.shape[0]
    counts = sum(ref[i].astype(F32) for ref in (mine, spectrum) for i in (end - 2, end - 1))
    if evidence_ref is not None:
        parts = spectrum[end - 1].astype(F32)[2 * classes :]
        parts = [jnp.concatenate([parts[i : i + 1], parts[i + 1 : i + 2]], 1) for i in (0, 2, 4)]
        evidence_ref[...] = (parts[0] + (parts[1] + parts[2]))[:, :share]
    counts = counts[:classes] + counts[classes : 2 * classes]
    lane = lax.broadcasted_iota(jnp.int32, (freqs, depth), 1)
    sign = jnp.where(lane < radii, -1.0, 1.0).astype(F32)
    for k in range(classes):
        plain, turned = [
            image[rows((2 * k + part) * pitch, freqs), :]
            + held[rows((2 * k + part) * pitch, freqs), :]
            for part in range(2)
        ]
        value = plain + sign * pltpu.roll(turned, radii, 1)
        if len(outs) == 1:
            outs[0][pl.ds(k * freqs, freqs), :] = value.astype(BF16)
        else:
            outs[k][pl.ds(0, freqs), :] = value
            outs[k][pl.ds(freqs, SPARE), :] = jnp.broadcast_to(counts[k : k + 1], (SPARE, depth))
    if len(outs) == 1:
        end = outs[0].shape[0] - classes * freqs
        high, low = split(counts)
        spare = [jnp.zeros((end - 2 * classes, depth), F32)] if end > 2 * classes else []
        tail = jnp.concatenate([high.astype(F32), low.astype(F32), *spare], 0)
        outs[0][pl.ds(classes * freqs, end), :] = tail.astype(BF16)


def finish(image, mine, spectrum, particles, last):
    pairs, _, twice = particles.shape
    classes = spectrum.shape[1] // 4
    freqs, depth = 2 * pairs, twice // 2
    if last:
        outs = [((freqs + SPARE, depth), F32)] * classes + [((1, particles.shape[1]), F32)]
    else:
        outs = [((classes * freqs + -(-2 * classes // 16) * 16, depth), BF16)]
    return call(
        finish_kernel,
        [image, mine, spectrum, particles],
        outs,
        [(image.shape, F32)] * 2,
        flops=2 * math.prod(spectrum.shape) * twice * 8,
    )


def means_kernel(*refs):
    *parts, own, other, out, evidence_ref = refs
    odd = lax.rem(lax.axis_index("cls"), 2)
    evidence_ref[...] = jnp.where(odd == 0, own[...], other[...])
    freqs = out.shape[1]
    total = tree(ref[...] for ref in parts)
    out[0] = total[:freqs, :] / (total[freqs : freqs + 1, :] + shrinkage)


def swap(value, axis, size, bit):
    if not bit:
        return value
    return lax.ppermute(value, axis, [(i, i ^ bit) for i in range(size)])


def bits(size):
    assert size > 1 and size & (size - 1) == 0
    return [1 << i for i in range(size.bit_length() - 1)]


def shards(particles, references, noise_inv, prior_rot):
    batch, freqs, depth = particles.shape
    sides = lax.axis_size("cls")
    groups = lax.axis_size("rot")
    blocks = lax.axis_size("blk")
    assert groups == 2 and 2 * groups * freqs == ANG
    share = batch // groups
    inverse, forward = tables(freqs)
    inverse_noise = noise_inv.reshape(1, depth // 2)
    assert blocks & (blocks - 1) == 0
    turns = sorted(range(1, blocks), key=lambda i: (-i.bit_length(), i))

    (permutation,) = call(permutation_kernel, [], [((256, 256), BF16)], flops=1 << 32)
    (prior_term,) = call(
        functools.partial(prior_kernel, share), [prior_rot], [((ANG, 256), F32)], flops=1 << 26
    )
    sources = {i: swap(references, "blk", blocks, i) for i in (*turns, 0)}
    other_images, own_images = prep(particles, permutation, share)
    for step in range(ITERS):
        last = step == ITERS - 1
        order = [0, *(reversed(turns) if step else reversed(range(1, blocks)))]
        message, energy, left = weigh(sources, order, inverse_noise, other_images, step == 0)
        message = swap(message, "rot", groups, 1)
        own = correlate(left, own_images)
        *weights, here = scores(own, message, energy, prior_term, inverse, share)
        first = here
        for bit in bits(sides):
            second = swap(first, ("cls", "rot"), sides * groups, groups * bit + (bit == 1))
            if 2 * bit < sides:
                (first,) = call(merge_kernel, [first, second], [(here.shape, F32)])
        rounded, more, send, *evidence = turn(
            *weights, first, second, forward, freqs, share, last
        )
        message = swap(send, "rot", groups, 1)
        image = gather(rounded, more, forward, own_images)
        sums = finish(image, send, message, other_images, last)
        sums, others = (sums[:blocks], sums[blocks:]) if last else (sums * blocks, [])
        sources = {i: swap(sums[i], "blk", blocks, i) for i in (*turns, 0)}
    means, evidence = call(
        means_kernel, [*[sources[i] for i in reversed(range(blocks))], *evidence, *others], [((1, freqs, depth), F32), ((1, share), F32)]
    )
    return means, evidence.reshape(share)


def solution(mesh):
    in_specs = (
        P(("grp", "blk"), "rot", None),
        P(("grp", "blk", "cls"), "rot", None),
        P(),
        P(("grp", "blk")),
    )
    out_specs = (P(("grp", "blk", "cls"), "rot", None), P(("grp", "blk", "rot")))
    return jax.shard_map(shards, mesh=mesh, in_specs=in_specs, out_specs=out_specs, check_vma=False)
```

```python
import functools
import math

import jax
import jax.numpy as jnp
import numpy as np
from jax import lax
from jax.experimental import pallas as pl
from jax.experimental.pallas import tpu as pltpu
from jax.sharding import PartitionSpec as P

ANG = 256
ITERS = 2
SIGMA = 32

shrinkage = 1.0

F32 = jnp.float32
BF16 = jnp.bfloat16
SPARE = 8

dot = functools.partial(jnp.dot, preferred_element_type=F32)


def split(x):
    high = x.astype(BF16)
    return high, (x - high.astype(F32)).astype(BF16)


def tables(half_freq):
    turn = np.arange(ANG)
    inverse, forward = [], []
    for group in range(2):
        sides = {}
        for which in range(2):
            freq = which * half_freq + np.arange(half_freq)
            angle = (turn[:, None] * freq[None, :] % ANG) * (2.0 * math.pi / ANG)
            scale = np.where(freq == 0, 1.0, 2.0) / ANG
            sides[which] = (
                np.concatenate([scale * np.cos(angle), -scale * np.sin(angle)], 1),
                np.concatenate([np.cos(angle), np.sin(angle)], 1).T,
            )
        inverse.append(np.concatenate([sides[group][0], sides[1 - group][0]], 1))
        forward.append(np.concatenate([sides[1 - group][1], sides[group][1]], 0))
    result = []
    for table, kinds in ((inverse, (0, 0, 1)), (forward, (0, 1))):
        table = np.concatenate(table, 0).astype(np.float32)
        high = table.astype(BF16)
        parts = [high, (table - high.astype(np.float32)).astype(BF16)]
        result.append(jnp.asarray(np.concatenate([parts[kind] for kind in kinds], 1)))
    return result


def each(count, body, init):
    if count <= 8:
        for k in range(count):
            init = body(k, init)
        return init
    return lax.fori_loop(0, count, body, init)


def rows(base, count):
    return pl.ds(pl.multiple_of(base, 8), count)


def call(kernel, ins, outs, scratch=(), flops=0, far=(), room=4 << 20):
    total = 0
    buffers = [(x.shape, x.dtype) for i, x in enumerate(ins) if i not in far]
    for shape, dtype in buffers + list(outs) + [x for x in scratch if isinstance(x, tuple)]:
        dims = [1, 1, *shape]
        lines = -(-dims[-2] // 16) * 16
        lanes = -(-dims[-1] // 128) * 128
        total += math.prod(dims[:-2]) * lines * lanes * jnp.dtype(dtype).itemsize
    kinds = [pltpu.VMEM] * len(ins)
    for i in far:
        kinds[i] = pltpu.MemorySpace.HBM
    return pl.pallas_call(
        kernel,
        out_shape=[jax.ShapeDtypeStruct(*x) for x in outs],
        in_specs=[pl.BlockSpec(memory_space=kind) for kind in kinds],
        out_specs=[pl.BlockSpec(memory_space=pltpu.VMEM)] * len(outs),
        scratch_shapes=[pltpu.VMEM(*x) if isinstance(x, tuple) else x for x in scratch],
        compiler_params=pltpu.CompilerParams(vmem_limit_bytes=min(total + room, 56 << 20)),
        cost_estimate=pl.CostEstimate(flops=flops, bytes_accessed=total, transcendentals=0),
    )(*ins)


def permutation_kernel(out):
    to = lax.broadcasted_iota(jnp.int32, out.shape, 0)
    at = lax.broadcasted_iota(jnp.int32, out.shape, 1)
    out[...] = ((to // 16 == at % 16) & (to % 16 == at // 16)).astype(F32).astype(BF16)


def half_index():
    return lax.rem(lax.axis_index("rot") + lax.axis_index("cls"), 2)


def prior_kernel(share, prior_ref, prior_term):
    turns = lax.broadcasted_iota(jnp.int32, (ANG, 256), 0)
    lane = lax.broadcasted_iota(jnp.int32, (1, 256), 1)
    priors = prior_ref[...].reshape(1, -1)
    first, second = [
        jnp.concatenate([priors[:, i * share : (i + 1) * share], lane[:, share:]], 1)
        for i in range(2)
    ]
    offset = jnp.abs(turns - jnp.where(half_index() == 0, first, second))
    distance = jnp.minimum(offset, ANG - offset).astype(F32)
    term = -distance * distance / (2.0 * SIGMA * SIGMA)
    prior_term[:, :128] = term[:, :128]
    prior_term[:, 128:] = repeat(term[:, 128:], share - 128, 128 // (share - 128))


def turned(value, lanes):
    return pltpu.roll(value, lanes % 128, 1) if lanes % 128 else value


def repeat(value, width, times):
    lane = lax.broadcasted_iota(jnp.int32, value.shape, 1)
    value = jnp.where(lane < width, value, 0.0)
    return sum(turned(value, i * width) for i in range(times))


def layout(classes, share):
    width = share - 128
    assert 0 < width < 128 and 128 % width == 0 and classes % 2 == 0
    bundle = min(128 // width, classes)
    assert classes % bundle == 0
    return width, bundle, classes // bundle


def prep_kernel(share, particles_ref, permutation_ref, other, own):
    freqs, depth = particles_ref.shape[1:]
    half = half_index()
    permutation = permutation_ref[...]
    for out, first in ((other, (1 - half) * share), (own, half * share)):
        for p in range(0, share, 16):
            for f in range(0, freqs, 32):
                blocks = [
                    jnp.concatenate(
                        [particles_ref[first + p + j, pl.ds(f + second, 16), :] for j in range(16)],
                        0,
                    )
                    for second in (0, 16)
                ]
                turned = dot(permutation, jnp.concatenate(blocks, 1)).astype(BF16)
                for half in range(2):
                    for j in range(16):
                        pair, part = divmod(f + 16 * half + j, 2)
                        out[pair, pl.ds(p, 16), pl.ds(part * depth, depth)] = turned[
                            16 * j : 16 * j + 16, half * depth : (half + 1) * depth
                        ]


def prep(particles, permutation, share):
    _, freqs, depth = particles.shape
    assert share % 16 == 0 and freqs % 32 == 0
    return call(
        functools.partial(prep_kernel, share),
        [particles, permutation],
        [((freqs // 2, share, 2 * depth), BF16)] * 2,
        flops=1 << 31,
    )


def tree(values):
    values = list(values)
    while len(values) > 1:
        values = [a + b for a, b in zip(values[::2], values[1::2])]
    return values[0]


def weigh_kernel(fresh, order, count, *refs):
    sources = [refs[order.index(i)] for i in range(count)]
    doubled_ref, particles, out, energy_ref, left_ref, image = refs[count:]
    pairs, share, twice = particles.shape
    freqs, depth = 2 * pairs, twice // 2
    classes = energy_ref.shape[0]
    pitch = freqs + SPARE
    radii = depth // 2
    lane = lax.broadcasted_iota(jnp.int32, (freqs, depth), 1)
    sign = jnp.where(lane < radii, -1.0, 1.0).astype(F32)
    doubled = jnp.concatenate([doubled_ref[...]] * 2, 1)
    row = lax.broadcasted_iota(jnp.int32, (freqs, depth), 0) + lax.axis_index("rot") * freqs
    scale = jnp.where(row == 0, 1.0 / ANG, 2.0 / ANG).astype(F32) * doubled

    tails = []
    if not fresh:
        end = sources[0].shape[0] - classes * freqs
        tails = [source[pl.ds(classes * freqs, end), :].astype(F32) for source in sources]

    for k in range(classes):
        if fresh:
            plain = sources[k][0].astype(F32)
        else:
            sums = tree(
                source[pl.ds((k ^ i) * freqs, freqs), :].astype(F32)
                for i, source in enumerate(sources)
            )
            highs, lows = [
                tree(tail[base + (k ^ i) : base + (k ^ i) + 1] for i, tail in enumerate(tails))
                for base in (0, classes)
            ]
            plain = (sums / (highs + lows + shrinkage)).astype(BF16).astype(F32)
        weighted = (plain * doubled).astype(BF16).astype(F32)
        image[rows(2 * k * pitch, freqs), :] = weighted
        image[rows((2 * k + 1) * pitch, freqs), :] = sign * pltpu.roll(weighted, radii, 1)
        energy = jnp.sum(plain * plain * scale, axis=0, keepdims=True)
        energy = jnp.broadcast_to(jnp.sum(energy, axis=1, keepdims=True), (SPARE, 128))
        energy_ref[pl.ds(k, 1), :] = energy[:1]
        out[rows(2 * k * pitch + freqs, SPARE), :] = energy

    none = jnp.zeros((2 * classes, depth), BF16)

    def correlate(f):
        lefts = []
        for first, second in pick(image, f, classes):
            first, second = first.astype(BF16), second.astype(BF16)
            left = jnp.concatenate(
                [jnp.concatenate([first, none], 1), jnp.concatenate([none, second], 1)], 0
            )
            left_ref[f + len(lefts)] = left
            lefts.append(left)
        values = [times(left, particles[f + i]) for i, left in enumerate(lefts)]
        place(out, f, values, classes, pitch)

    every(pairs, correlate)


def times(left, particles):
    return lax.dot_general(left, particles, (((1,), (1,)), ((), ())), preferred_element_type=F32)


GROUP = 4


def every(pairs, body):
    for f in range(0, pairs, GROUP):
        body(f)


def put(ref, f, blocks, pitch):
    turned_blocks = jnp.swapaxes(jnp.stack(blocks, 0), 0, 1)
    for i in range(blocks[0].shape[0]):
        ref[pl.ds(i * pitch + 2 * f, 2 * GROUP), :] = turned_blocks[i]


def pick(ref, f, classes):
    pitch = ref.shape[0] // (2 * classes)
    blocks = [ref[pl.ds(i * pitch + 2 * f, 2 * GROUP), :] for i in range(2 * classes)]
    blocks = jnp.swapaxes(jnp.stack(blocks, 0), 0, 1)
    return [(blocks[2 * i], blocks[2 * i + 1]) for i in range(GROUP)]


def place(out, f, values, classes, pitch):
    width = values[0].shape[1] - 128
    each_pack = 128 // width
    spare = jnp.zeros((2 * classes, 128 - width), F32)
    parts = [
        value[part * 2 * classes : (part + 1) * 2 * classes] for value in values for part in range(2)
    ]
    put(out, f, [part[:, :128] for part in parts], pitch)
    more = [jnp.concatenate([part[:, 128:], spare], 1) for part in parts]
    more = jnp.swapaxes(jnp.stack(more, 0), 0, 1)
    for first in range(0, 2 * classes, each_pack):
        total = 0.0
        for group in range(first, min(first + each_pack, 2 * classes)):
            part, k = divmod(group, classes)
            total = total + turned(more[2 * k + part], (group - first) * width)
        at = (2 * classes + first // each_pack) * pitch + 2 * f
        out[pl.ds(at, 2 * GROUP), :] = total


def unpack(ref, unit, part, classes, share, pitch, freqs):
    width, bundle, _ = layout(classes, share)
    group = part * classes + unit * bundle
    each_pack = 128 // width
    value = ref[rows((2 * classes + group // each_pack) * pitch, freqs), :]
    return turned(value, -(group % each_pack) * width)


def corr_lines(classes, share, pitch):
    return (2 * classes + -(-2 * classes * (share - 128) // 128)) * pitch


def weigh(sources, order, inverse_noise, particles, fresh):
    pairs, share, twice = particles.shape
    classes = len(sources)
    pitch = 2 * pairs + SPARE
    return call(
        functools.partial(weigh_kernel, fresh, order, classes),
        [*[sources[i] for i in order], inverse_noise, particles],
        [
            ((corr_lines(classes, share, pitch), 128), F32),
            ((classes, 128), F32),
            ((pairs, 4 * classes, twice), BF16),
        ],
        [((2 * classes * pitch, twice // 2), F32)],
        flops=8 * classes * share * pairs * twice * 4,
    )


def correlate_kernel(left_ref, particles, out):
    pairs, share, _ = particles.shape
    classes = left_ref.shape[1] // 4
    pitch = 2 * pairs + SPARE

    def body(f):
        values = [times(left_ref[f + i], particles[f + i]) for i in range(GROUP)]
        place(out, f, values, classes, pitch)

    every(pairs, body)


def correlate(left, particles):
    pairs, share, twice = particles.shape
    classes = left.shape[1] // 4
    pitch = 2 * pairs + SPARE
    return call(
        correlate_kernel,
        [left, particles],
        [((corr_lines(classes, share, pitch), 128), F32)],
        flops=2 * left.shape[1] * share * pairs * twice * 8,
    )[0]


def table_rows(base, count):
    return pl.ds(pl.multiple_of(lax.axis_index("rot") * ANG + base, 128), count)


def score_kernel(share, own, other, energy_ref, prior_term, inverse, *refs):
    weights, more, tops, more_tops, peaks = refs
    classes = energy_ref.shape[0]
    width, bundle, units = layout(classes, share)
    freqs = ANG // 4
    pitch = freqs + SPARE
    at = table_rows(0, ANG)
    lane = lax.broadcasted_iota(jnp.int32, (1, 128), 1)

    def exponentials(value, energy, prior):
        high, low = split(value)
        inner = dot(inverse[at, :], jnp.concatenate([high, low, high], 0))
        scores = inner - 0.5 * energy + prior
        top = jnp.max(scores, axis=0, keepdims=True)
        value = jnp.exp(scores - top)
        return value, top, jnp.sum(value, axis=0, keepdims=True)

    def energy_of(k):
        return energy_ref[pl.ds(k, 1), :] + other[rows(2 * k * pitch + freqs, SPARE), :][:1]

    def slab(i, carry):
        value = jnp.concatenate(
            [
                jnp.concatenate(
                    [ref[rows((4 * i + 2 * j + part) * pitch, freqs), :] for j in range(2)], 1
                )
                for ref in (own, other)
                for part in range(2)
            ],
            0,
        )
        energy = jnp.concatenate([energy_of(2 * i), energy_of(2 * i + 1)], 1)
        prior = jnp.concatenate([prior_term[:, :128]] * 2, 1)
        weights[i], top, total = exponentials(value, energy, prior)
        tops[pl.ds(i, 1), :] = top
        for j in (0, 128):
            carry = merge(carry, (top[:, j : j + 128], total[:, j : j + 128]))
        return carry

    empty = (jnp.full((1, 128), -jnp.inf, F32), jnp.zeros((1, 128), F32))
    top, total = each(classes // 2, slab, empty)
    rest = empty
    for unit in range(units):
        value = jnp.concatenate(
            [
                unpack(ref, unit, part, classes, share, pitch, freqs)
                for ref in (own, other)
                for part in range(2)
            ],
            0,
        )
        energy = sum(
            jnp.where(lane // width == j, energy_of(unit * bundle + j), 0.0)
            for j in range(bundle)
        )
        more[unit], more_top, more_total = exponentials(value, energy, prior_term[:, 128:])
        more_tops[pl.ds(unit, 1), :] = more_top
        for j in range(bundle):
            rest = merge(rest, (turned(more_top, -j * width), turned(more_total, -j * width)))
    line = lax.broadcasted_iota(jnp.int32, peaks.shape, 0)
    peaks[...] = jnp.where(
        line == 0,
        jnp.concatenate([top, rest[0]], 1),
        jnp.concatenate([total, rest[1]], 1),
    )


def scores(own, other, energy, prior_term, inverse, share):
    classes = energy.shape[0]
    units = layout(classes, share)[2]
    return call(
        functools.partial(score_kernel, share),
        [own, other, energy, prior_term, inverse],
        [
            ((classes // 2, ANG, 256), F32),
            ((units, ANG, 128), F32),
            ((classes // 2, 256), F32),
            ((units, 128), F32),
            ((8, 256), F32),
        ],
        flops=6 * classes * 256 * ANG * ANG,
    )


def merge(first, second):
    top = jnp.maximum(first[0], second[0])
    return top, first[1] * jnp.exp(first[0] - top) + second[1] * jnp.exp(second[0] - top)


def two_lines(ref):
    return ref[0:1, :], ref[1:2, :]


def merge_kernel(first, second, out):
    top, total = merge(two_lines(first), two_lines(second))
    line = lax.broadcasted_iota(jnp.int32, out.shape, 0)
    out[...] = jnp.where(line == 0, top, total)


def turn_kernel(share, weights, more, tops, more_tops, first, second, forward, *refs):
    rounded_ref, rounded_more, send, *last, held = refs
    classes = 2 * weights.shape[0]
    width, bundle, units = layout(classes, share)
    pairs = (held.shape[0] // (2 * classes) - SPARE) // 2
    top, total = merge(two_lines(first), two_lines(second))
    evidence = top + jnp.log(total)
    scale = 1.0 / total
    at = table_rows(0, ANG // 2)
    lane = lax.broadcasted_iota(jnp.int32, (1, 128), 1)
    line = lax.broadcasted_iota(jnp.int32, (4 * classes, 128), 0)

    def with_count(column, k, count):
        high = count.astype(BF16).astype(F32)
        return jnp.where(line == k, high, jnp.where(line == classes + k, count - high, column))

    more_counts = []
    for unit in range(units):
        factor = jnp.exp(
            more_tops[pl.ds(unit, 1), :] - repeat(top[:, 128:], width, bundle)
        ) * repeat(scale[:, 128:], width, bundle)
        value = more[unit] * jnp.where(lane < bundle * width, factor, 0.0)
        count = jnp.sum(value, axis=0, keepdims=True)
        for j in range(bundle):
            mine = jnp.where(lane // width == j, count, 0.0)
            more_counts.append(jnp.sum(mine, axis=1, keepdims=True))
        rounded = value.astype(BF16)
        rounded_more[unit] = rounded
        spectrum = dot(forward[at, :], jnp.concatenate([rounded, rounded], 0)).astype(BF16)
        step = 4 * classes
        entries = spectrum.shape[0] // step
        for i in range(entries):
            send[pairs + unit * entries + i] = spectrum[i * step : (i + 1) * step]

    tops_here = jnp.concatenate([top[:, :128]] * 2, 1)
    scale_here = jnp.concatenate([scale[:, :128]] * 2, 1)

    def body(i, column):
        value = weights[i] * (jnp.exp(tops[pl.ds(i, 1), :] - tops_here) * scale_here)
        rounded = value.astype(BF16)
        rounded_ref[i] = rounded
        spread(held, i, dot(forward[at, :], jnp.concatenate([rounded, rounded], 0)))
        count = jnp.sum(value, axis=0, keepdims=True)
        for j in range(2):
            mine = jnp.sum(count[:, j * 128 : (j + 1) * 128], axis=1, keepdims=True)
            column = with_count(column, 2 * i + j, mine)
        return column

    column = each(classes // 2, body, jnp.zeros((4 * classes, 128), F32))
    extra = jnp.zeros((4 * classes, 128), F32)
    for k, count in enumerate(more_counts):
        extra = with_count(extra, k, count)
    for ref in last:
        ref[...] = evidence[:, :share]
        high = evidence.astype(BF16).astype(F32)
        middle = (evidence - high).astype(BF16).astype(F32)
        for i, value in enumerate((high, middle, evidence - high - middle)):
            for j in range(2):
                mine = value[:, j * 128 : (j + 1) * 128]
                extra = jnp.where(line == 2 * classes + 2 * i + j, mine, extra)
    send[send.shape[0] - 2] = column.astype(BF16)
    send[send.shape[0] - 1] = extra.astype(BF16)

    def rearrange(f):
        for i, parts in enumerate(pick(held, f, classes)):
            send[f + i] = jnp.concatenate(parts, 0).astype(BF16)

    every(pairs, rearrange)


def spread(held, i, value):
    freqs = value.shape[0] // 2
    for j in range(2):
        for part in range(2):
            held[rows((4 * i + 2 * j + part) * (freqs + SPARE), freqs), :] = value[
                part * freqs : (part + 1) * freqs, j * 128 : (j + 1) * 128
            ]


def spread_more(held, unit, value, classes, share):
    width, bundle, _ = layout(classes, share)
    freqs = value.shape[0] // 2
    for j in range(bundle):
        shifted = turned(value, -j * width)
        for part in range(2):
            k = unit * bundle + j
            held[rows((2 * k + part) * (freqs + SPARE), freqs), :] = shifted[
                part * freqs : (part + 1) * freqs
            ]


def message_shape(classes, pairs, units):
    return (pairs + units * (ANG // 2) // (4 * classes) + 2, 4 * classes, 128)


def turn(weights, more, tops, more_tops, first, second, forward, freqs, share, last):
    classes = 2 * weights.shape[0]
    units = more.shape[0]
    return call(
        functools.partial(turn_kernel, share),
        [weights, more, tops, more_tops, first, second, forward],
        [
            (weights.shape, BF16),
            (more.shape, BF16),
            (message_shape(classes, freqs // 2, units), BF16),
            *([((1, share), F32)] if last else []),
        ],
        [((2 * classes * (freqs + SPARE), 128), F32)],
        flops=4 * classes * 256 * ANG * ANG,
    )


def gather_kernel(rounded_ref, rounded_more, forward, particles, image, held, held_more):
    classes = 2 * rounded_ref.shape[0]
    pairs, share, _ = particles.shape
    at = table_rows(ANG // 2, ANG // 2)

    for unit in range(rounded_more.shape[0]):
        rounded = rounded_more[unit]
        value = dot(forward[at, :], jnp.concatenate([rounded, rounded], 0))
        spread_more(held_more, unit, value, classes, share)

    def body(i, carry):
        rounded = rounded_ref[i]
        spread(held, i, dot(forward[at, :], jnp.concatenate([rounded, rounded], 0)))
        return carry

    each(classes // 2, body, 0)

    def accumulate(f):
        values = []
        for i, both in enumerate(zip(pick(held, f, classes), pick(held_more, f, classes))):
            left = [jnp.concatenate(parts, 0).astype(BF16) for parts in both]
            values.append(dot(jnp.concatenate(left, 1)[:, :share], particles[f + i]))
        take_in(image, f, values, classes)

    every(pairs, accumulate)


def gather(rounded, rounded_more, forward, particles):
    pairs, share, twice = particles.shape
    classes = 2 * rounded.shape[0]
    lines = 2 * classes * (2 * pairs + SPARE)
    return call(
        gather_kernel,
        [rounded, rounded_more, forward, particles],
        [((lines, twice // 2), F32)],
        [((lines, 128), F32)] * 2,
        flops=4 * classes * 256 * ANG * ANG,
    )[0]


def take_in(image, f, values, classes):
    lines, depth = image.shape
    blocks = [
        value[part * 2 * classes : (part + 1) * 2 * classes, part * depth : (part + 1) * depth]
        for value in values
        for part in range(2)
    ]
    put(image, f, blocks, lines // (2 * classes))


def finish_kernel(image, mine, spectrum, particles, *refs):
    *outs, held = refs
    evidence_ref = outs.pop() if len(outs) > 1 else None
    pairs, share, twice = particles.shape
    classes = spectrum.shape[1] // 4
    freqs, depth = 2 * pairs, twice // 2
    radii = depth // 2
    pitch = freqs + SPARE

    width, bundle, units = layout(classes, share)
    step = 4 * classes
    entries = ANG // 2 // step

    def received(f):
        blocks = []
        for k in range(classes):
            unit, j = divmod(k, bundle)
            for part in range(2):
                entry, first = divmod(part * freqs + 2 * f, step)
                value = spectrum[pairs + unit * entries + entry].astype(F32)
                blocks.append(turned(value[first : first + 2 * GROUP], -j * width))
        blocks = jnp.swapaxes(jnp.stack(blocks, 0), 0, 1)
        return [(blocks[2 * i], blocks[2 * i + 1]) for i in range(GROUP)]

    def body(f):
        values = []
        for i, parts in enumerate(received(f)):
            left = jnp.concatenate(parts, 0).astype(BF16)
            left = jnp.concatenate([spectrum[f + i], left], 1)[:, :share]
            values.append(dot(left, particles[f + i]))
        take_in(held, f, values, classes)

    every(pairs, body)
    end = spectrum.shape[0]
    counts = sum(ref[i].astype(F32) for ref in (mine, spectrum) for i in (end - 2, end - 1))
    if evidence_ref is not None:
        parts = spectrum[end - 1].astype(F32)[2 * classes :]
        parts = [jnp.concatenate([parts[i : i + 1], parts[i + 1 : i + 2]], 1) for i in (0, 2, 4)]
        evidence_ref[...] = (parts[0] + (parts[1] + parts[2]))[:, :share]
    counts = counts[:classes] + counts[classes : 2 * classes]
    lane = lax.broadcasted_iota(jnp.int32, (freqs, depth), 1)
    sign = jnp.where(lane < radii, -1.0, 1.0).astype(F32)
    for k in range(classes):
        plain, crossed = [
            image[rows((2 * k + part) * pitch, freqs), :]
            + held[rows((2 * k + part) * pitch, freqs), :]
            for part in range(2)
        ]
        value = plain + sign * pltpu.roll(crossed, radii, 1)
        if len(outs) == 1:
            outs[0][pl.ds(k * freqs, freqs), :] = value.astype(BF16)
        else:
            outs[k][pl.ds(0, freqs), :] = value
            outs[k][pl.ds(freqs, SPARE), :] = jnp.broadcast_to(counts[k : k + 1], (SPARE, depth))
    if len(outs) == 1:
        end = outs[0].shape[0] - classes * freqs
        high, low = split(counts)
        spare = [jnp.zeros((end - 2 * classes, depth), F32)] if end > 2 * classes else []
        tail = jnp.concatenate([high.astype(F32), low.astype(F32), *spare], 0)
        outs[0][pl.ds(classes * freqs, end), :] = tail.astype(BF16)


def finish(image, mine, spectrum, particles, last):
    pairs, _, twice = particles.shape
    classes = spectrum.shape[1] // 4
    freqs, depth = 2 * pairs, twice // 2
    if last:
        outs = [((freqs + SPARE, depth), F32)] * classes + [((1, particles.shape[1]), F32)]
    else:
        outs = [((classes * freqs + -(-2 * classes // 16) * 16, depth), BF16)]
    return call(
        finish_kernel,
        [image, mine, spectrum, particles],
        outs,
        [(image.shape, F32)],
        flops=2 * math.prod(spectrum.shape) * twice * 8,
    )


def means_kernel(*refs):
    *parts, own, other, out, evidence_ref = refs
    odd = lax.rem(lax.axis_index("cls"), 2)
    evidence_ref[...] = jnp.where(odd == 0, own[...], other[...])
    freqs = out.shape[1]
    total = tree(ref[...] for ref in parts)
    out[0] = total[:freqs, :] / (total[freqs : freqs + 1, :] + shrinkage)


def swap(value, axis, size, bit):
    if not bit:
        return value
    return lax.ppermute(value, axis, [(i, i ^ bit) for i in range(size)])


def bits(size):
    assert size > 1 and size & (size - 1) == 0
    return [1 << i for i in range(size.bit_length() - 1)]


def shards(particles, references, noise_inv, prior_rot):
    batch, freqs, depth = particles.shape
    sides = lax.axis_size("cls")
    groups = lax.axis_size("rot")
    blocks = lax.axis_size("blk")
    assert groups == 2 and 2 * groups * freqs == ANG
    share = batch // groups
    inverse, forward = tables(freqs)
    inverse_noise = noise_inv.reshape(1, depth // 2)
    assert blocks & (blocks - 1) == 0
    turns = sorted(range(1, blocks), key=lambda i: (-i.bit_length(), i))

    (permutation,) = call(permutation_kernel, [], [((256, 256), BF16)], flops=1 << 32)
    (prior_term,) = call(
        functools.partial(prior_kernel, share), [prior_rot], [((ANG, 256), F32)], flops=1 << 26
    )
    sources = {i: swap(references, "blk", blocks, i) for i in (*turns, 0)}
    other_images, own_images = prep(particles, permutation, share)
    for step in range(ITERS):
        last = step == ITERS - 1
        order = [0, *(reversed(turns) if step else reversed(range(1, blocks)))]
        message, energy, left = weigh(sources, order, inverse_noise, other_images, step == 0)
        message = swap(message, "rot", groups, 1)
        own = correlate(left, own_images)
        *weights, here = scores(own, message, energy, prior_term, inverse, share)
        first = here
        for bit in bits(sides):
            second = swap(first, ("cls", "rot"), sides * groups, groups * bit + (bit == 1))
            if 2 * bit < sides:
                (first,) = call(merge_kernel, [first, second], [(here.shape, F32)])
        rounded, more, send, *evidence = turn(
            *weights, first, second, forward, freqs, share, last
        )
        message = swap(send, "rot", groups, 1)
        image = gather(rounded, more, forward, own_images)
        sums = finish(image, send, message, other_images, last)
        sums, others = (sums[:blocks], sums[blocks:]) if last else (sums * blocks, [])
        sources = {i: swap(sums[i], "blk", blocks, i) for i in (*turns, 0)}
    means, evidence = call(
        means_kernel, [*[sources[i] for i in reversed(range(blocks))], *evidence, *others], [((1, freqs, depth), F32), ((1, share), F32)]
    )
    return means, evidence.reshape(share)


def solution(mesh):
    in_specs = (
        P(("grp", "blk"), "rot", None),
        P(("grp", "blk", "cls"), "rot", None),
        P(),
        P(("grp", "blk")),
    )
    out_specs = (P(("grp", "blk", "cls"), "rot", None), P(("grp", "blk", "rot")))
    return jax.shard_map(shards, mesh=mesh, in_specs=in_specs, out_specs=out_specs, check_vma=False)
```

```python
import functools
import math

import jax
import jax.numpy as jnp
import numpy as np
from jax import lax
from jax.experimental import pallas as pl
from jax.experimental.pallas import tpu as pltpu
from jax.sharding import PartitionSpec as P

ANG = 256
ITERS = 2
SIGMA = 32

shrinkage = 1.0

F32 = jnp.float32
BF16 = jnp.bfloat16
SPARE = 8

dot = functools.partial(jnp.dot, preferred_element_type=F32)


def split(x):
    high = x.astype(BF16)
    return high, (x - high.astype(F32)).astype(BF16)


def tables(half_freq):
    turn = np.arange(ANG)
    inverse, forward = [], []
    for group in range(2):
        sides = {}
        for which in range(2):
            freq = which * half_freq + np.arange(half_freq)
            angle = (turn[:, None] * freq[None, :] % ANG) * (2.0 * math.pi / ANG)
            scale = np.where(freq == 0, 1.0, 2.0) / ANG
            sides[which] = (
                np.concatenate([scale * np.cos(angle), -scale * np.sin(angle)], 1),
                np.concatenate([np.cos(angle), np.sin(angle)], 1).T,
            )
        inverse.append(np.concatenate([sides[group][0], sides[1 - group][0]], 1))
        forward.append(np.concatenate([sides[1 - group][1], sides[group][1]], 0))
    result = []
    for table, kinds in ((inverse, (0, 0, 1)), (forward, (0, 1))):
        table = np.concatenate(table, 0).astype(np.float32)
        high = table.astype(BF16)
        parts = [high, (table - high.astype(np.float32)).astype(BF16)]
        result.append(jnp.asarray(np.concatenate([parts[kind] for kind in kinds], 1)))
    return result


def each(count, body, init):
    if count <= 8:
        for k in range(count):
            init = body(k, init)
        return init
    return lax.fori_loop(0, count, body, init)


def rows(base, count):
    return pl.ds(pl.multiple_of(base, 8), count)


def call(kernel, ins, outs, scratch=(), flops=0, far=(), room=4 << 20):
    total = 0
    buffers = [(x.shape, x.dtype) for i, x in enumerate(ins) if i not in far]
    for shape, dtype in buffers + list(outs) + [x for x in scratch if isinstance(x, tuple)]:
        dims = [1, 1, *shape]
        lines = -(-dims[-2] // 16) * 16
        lanes = -(-dims[-1] // 128) * 128
        total += math.prod(dims[:-2]) * lines * lanes * jnp.dtype(dtype).itemsize
    kinds = [pltpu.VMEM] * len(ins)
    for i in far:
        kinds[i] = pltpu.MemorySpace.HBM
    return pl.pallas_call(
        kernel,
        out_shape=[jax.ShapeDtypeStruct(*x) for x in outs],
        in_specs=[pl.BlockSpec(memory_space=kind) for kind in kinds],
        out_specs=[pl.BlockSpec(memory_space=pltpu.VMEM)] * len(outs),
        scratch_shapes=[pltpu.VMEM(*x) if isinstance(x, tuple) else x for x in scratch],
        compiler_params=pltpu.CompilerParams(vmem_limit_bytes=min(total + room, 56 << 20)),
        cost_estimate=pl.CostEstimate(flops=flops, bytes_accessed=total, transcendentals=0),
    )(*ins)


def permutation_kernel(out):
    to = lax.broadcasted_iota(jnp.int32, out.shape, 0)
    at = lax.broadcasted_iota(jnp.int32, out.shape, 1)
    out[...] = ((to // 16 == at % 16) & (to % 16 == at // 16)).astype(F32).astype(BF16)


def half_index():
    return lax.rem(lax.axis_index("rot") + lax.axis_index("cls"), 2)


def prior_kernel(share, prior_ref, prior_term):
    turns = lax.broadcasted_iota(jnp.int32, (ANG, 256), 0)
    lane = lax.broadcasted_iota(jnp.int32, (1, 256), 1)
    priors = prior_ref[...].reshape(1, -1)
    first, second = [
        jnp.concatenate([priors[:, i * share : (i + 1) * share], lane[:, share:]], 1)
        for i in range(2)
    ]
    offset = jnp.abs(turns - jnp.where(half_index() == 0, first, second))
    distance = jnp.minimum(offset, ANG - offset).astype(F32)
    term = -distance * distance / (2.0 * SIGMA * SIGMA)
    prior_term[:, :128] = term[:, :128]
    prior_term[:, 128:] = repeat(term[:, 128:], share - 128, 128 // (share - 128))


def turned(value, lanes):
    return pltpu.roll(value, lanes % 128, 1) if lanes % 128 else value


def repeat(value, width, times):
    lane = lax.broadcasted_iota(jnp.int32, value.shape, 1)
    value = jnp.where(lane < width, value, 0.0)
    return sum(turned(value, i * width) for i in range(times))


def layout(classes, share):
    width = share - 128
    assert 0 < width < 128 and 128 % width == 0 and classes % 2 == 0
    bundle = min(128 // width, classes)
    assert classes % bundle == 0
    return width, bundle, classes // bundle


def prep_kernel(share, particles_ref, permutation_ref, other, own):
    freqs, depth = particles_ref.shape[1:]
    half = half_index()
    permutation = permutation_ref[...]
    for out, first in ((other, (1 - half) * share), (own, half * share)):
        for p in range(0, share, 16):
            for f in range(0, freqs, 32):
                blocks = [
                    jnp.concatenate(
                        [particles_ref[first + p + j, pl.ds(f + second, 16), :] for j in range(16)],
                        0,
                    )
                    for second in (0, 16)
                ]
                turned = dot(permutation, jnp.concatenate(blocks, 1)).astype(BF16)
                for half in range(2):
                    for j in range(16):
                        pair, part = divmod(f + 16 * half + j, 2)
                        out[pair, pl.ds(p, 16), pl.ds(part * depth, depth)] = turned[
                            16 * j : 16 * j + 16, half * depth : (half + 1) * depth
                        ]


def prep(particles, permutation, share):
    _, freqs, depth = particles.shape
    assert share % 16 == 0 and freqs % 32 == 0
    return call(
        functools.partial(prep_kernel, share),
        [particles, permutation],
        [((freqs // 2, share, 2 * depth), BF16)] * 2,
        flops=1 << 31,
    )


def tree(values):
    values = list(values)
    while len(values) > 1:
        values = [a + b for a, b in zip(values[::2], values[1::2])]
    return values[0]


def weigh_kernel(fresh, order, count, *refs):
    sources = [refs[order.index(i)] for i in range(count)]
    doubled_ref, particles, out, energy_ref, left_ref, image = refs[count:]
    pairs, share, twice = particles.shape
    freqs, depth = 2 * pairs, twice // 2
    classes = energy_ref.shape[0]
    pitch = freqs + SPARE
    radii = depth // 2
    lane = lax.broadcasted_iota(jnp.int32, (freqs, depth), 1)
    sign = jnp.where(lane < radii, -1.0, 1.0).astype(F32)
    doubled = jnp.concatenate([doubled_ref[...]] * 2, 1)
    row = lax.broadcasted_iota(jnp.int32, (freqs, depth), 0) + lax.axis_index("rot") * freqs
    scale = jnp.where(row == 0, 1.0 / ANG, 2.0 / ANG).astype(F32) * doubled

    tails = []
    if not fresh:
        end = sources[0].shape[0] - classes * freqs
        tails = [source[pl.ds(classes * freqs, end), :].astype(F32) for source in sources]

    for k in range(classes):
        if fresh:
            plain = sources[k][0].astype(F32)
        else:
            sums = tree(
                source[pl.ds((k ^ i) * freqs, freqs), :].astype(F32)
                for i, source in enumerate(sources)
            )
            highs, lows = [
                tree(tail[base + (k ^ i) : base + (k ^ i) + 1] for i, tail in enumerate(tails))
                for base in (0, classes)
            ]
            plain = (sums / (highs + lows + shrinkage)).astype(BF16).astype(F32)
        weighted = (plain * doubled).astype(BF16).astype(F32)
        image[rows(2 * k * pitch, freqs), :] = weighted
        image[rows((2 * k + 1) * pitch, freqs), :] = sign * pltpu.roll(weighted, radii, 1)
        energy = jnp.sum(plain * plain * scale, axis=0, keepdims=True)
        energy = jnp.broadcast_to(jnp.sum(energy, axis=1, keepdims=True), (SPARE, 128))
        energy_ref[pl.ds(k, 1), :] = energy[:1]
        out[rows(2 * k * pitch + freqs, SPARE), :] = energy

    none = jnp.zeros((2 * classes, depth), BF16)

    def correlate(f):
        lefts = []
        for first, second in pick(image, f, classes):
            first, second = first.astype(BF16), second.astype(BF16)
            left = jnp.concatenate(
                [jnp.concatenate([first, none], 1), jnp.concatenate([none, second], 1)], 0
            )
            left_ref[f + len(lefts)] = left
            lefts.append(left)
        values = [times(left, particles[f + i]) for i, left in enumerate(lefts)]
        place(out, f, values, classes, pitch)

    every(pairs, correlate)


def times(left, particles):
    return lax.dot_general(left, particles, (((1,), (1,)), ((), ())), preferred_element_type=F32)


GROUP = 4


def every(pairs, body):
    for f in range(0, pairs, GROUP):
        body(f)


def put(ref, f, blocks, pitch):
    turned_blocks = jnp.swapaxes(jnp.stack(blocks, 0), 0, 1)
    for i in range(blocks[0].shape[0]):
        ref[pl.ds(i * pitch + 2 * f, 2 * GROUP), :] = turned_blocks[i]


def pick(ref, f, classes):
    pitch = ref.shape[0] // (2 * classes)
    blocks = [ref[pl.ds(i * pitch + 2 * f, 2 * GROUP), :] for i in range(2 * classes)]
    blocks = jnp.swapaxes(jnp.stack(blocks, 0), 0, 1)
    return [(blocks[2 * i], blocks[2 * i + 1]) for i in range(GROUP)]


def place(out, f, values, classes, pitch):
    width = values[0].shape[1] - 128
    each_pack = 128 // width
    spare = jnp.zeros((2 * classes, 128 - width), F32)
    parts = [
        value[part * 2 * classes : (part + 1) * 2 * classes] for value in values for part in range(2)
    ]
    put(out, f, [part[:, :128] for part in parts], pitch)
    more = [jnp.concatenate([part[:, 128:], spare], 1) for part in parts]
    more = jnp.swapaxes(jnp.stack(more, 0), 0, 1)
    for first in range(0, 2 * classes, each_pack):
        total = 0.0
        for group in range(first, min(first + each_pack, 2 * classes)):
            part, k = divmod(group, classes)
            total = total + turned(more[2 * k + part], (group - first) * width)
        at = (2 * classes + first // each_pack) * pitch + 2 * f
        out[pl.ds(at, 2 * GROUP), :] = total


def unpack(ref, unit, part, classes, share, pitch, freqs):
    width, bundle, _ = layout(classes, share)
    group = part * classes + unit * bundle
    each_pack = 128 // width
    value = ref[rows((2 * classes + group // each_pack) * pitch, freqs), :]
    return turned(value, -(group % each_pack) * width)


def corr_lines(classes, share, pitch):
    return (2 * classes + -(-2 * classes * (share - 128) // 128)) * pitch


def weigh(sources, order, inverse_noise, particles, fresh):
    pairs, share, twice = particles.shape
    classes = len(sources)
    pitch = 2 * pairs + SPARE
    return call(
        functools.partial(weigh_kernel, fresh, order, classes),
        [*[sources[i] for i in order], inverse_noise, particles],
        [
            ((corr_lines(classes, share, pitch), 128), F32),
            ((classes, 128), F32),
            ((pairs, 4 * classes, twice), BF16),
        ],
        [((2 * classes * pitch, twice // 2), F32)],
        flops=8 * classes * share * pairs * twice * 4,
    )


def correlate_kernel(left_ref, particles, out):
    pairs, share, _ = particles.shape
    classes = left_ref.shape[1] // 4
    pitch = 2 * pairs + SPARE

    def body(f):
        values = [times(left_ref[f + i], particles[f + i]) for i in range(GROUP)]
        place(out, f, values, classes, pitch)

    every(pairs, body)


def correlate(left, particles):
    pairs, share, twice = particles.shape
    classes = left.shape[1] // 4
    pitch = 2 * pairs + SPARE
    return call(
        correlate_kernel,
        [left, particles],
        [((corr_lines(classes, share, pitch), 128), F32)],
        flops=2 * left.shape[1] * share * pairs * twice * 8,
    )[0]


def table_rows(base, count):
    return pl.ds(pl.multiple_of(lax.axis_index("rot") * ANG + base, 128), count)


def score_kernel(share, own, other, energy_ref, prior_term, inverse, *refs):
    weights, more, tops, more_tops, peaks = refs
    classes = energy_ref.shape[0]
    width, bundle, units = layout(classes, share)
    freqs = ANG // 4
    pitch = freqs + SPARE
    at = table_rows(0, ANG)
    lane = lax.broadcasted_iota(jnp.int32, (1, 128), 1)

    def exponentials(value, energy, prior):
        high, low = split(value)
        inner = dot(inverse[at, :], jnp.concatenate([high, low, high], 0))
        scores = inner - 0.5 * energy + prior
        top = jnp.max(scores, axis=0, keepdims=True)
        value = jnp.exp(scores - top)
        return value, top, jnp.sum(value, axis=0, keepdims=True)

    def energy_of(k):
        return energy_ref[pl.ds(k, 1), :] + other[rows(2 * k * pitch + freqs, SPARE), :][:1]

    def slab(i, carry):
        value = jnp.concatenate(
            [
                jnp.concatenate(
                    [ref[rows((4 * i + 2 * j + part) * pitch, freqs), :] for j in range(2)], 1
                )
                for ref in (own, other)
                for part in range(2)
            ],
            0,
        )
        energy = jnp.concatenate([energy_of(2 * i), energy_of(2 * i + 1)], 1)
        prior = jnp.concatenate([prior_term[:, :128]] * 2, 1)
        weights[i], top, total = exponentials(value, energy, prior)
        tops[pl.ds(i, 1), :] = top
        for j in (0, 128):
            carry = merge(carry, (top[:, j : j + 128], total[:, j : j + 128]))
        return carry

    empty = (jnp.full((1, 128), -jnp.inf, F32), jnp.zeros((1, 128), F32))
    top, total = each(classes // 2, slab, empty)
    rest = empty
    for unit in range(units):
        value = jnp.concatenate(
            [
                unpack(ref, unit, part, classes, share, pitch, freqs)
                for ref in (own, other)
                for part in range(2)
            ],
            0,
        )
        energy = sum(
            jnp.where(lane // width == j, energy_of(unit * bundle + j), 0.0)
            for j in range(bundle)
        )
        more[unit], more_top, more_total = exponentials(value, energy, prior_term[:, 128:])
        more_tops[pl.ds(unit, 1), :] = more_top
        for j in range(bundle):
            rest = merge(rest, (turned(more_top, -j * width), turned(more_total, -j * width)))
    line = lax.broadcasted_iota(jnp.int32, peaks.shape, 0)
    peaks[...] = jnp.where(
        line == 0,
        jnp.concatenate([top, rest[0]], 1),
        jnp.concatenate([total, rest[1]], 1),
    )


def scores(own, other, energy, prior_term, inverse, share):
    classes = energy.shape[0]
    units = layout(classes, share)[2]
    return call(
        functools.partial(score_kernel, share),
        [own, other, energy, prior_term, inverse],
        [
            ((classes // 2, ANG, 256), F32),
            ((units, ANG, 128), F32),
            ((classes // 2, 256), F32),
            ((units, 128), F32),
            ((8, 256), F32),
        ],
        flops=6 * classes * 256 * ANG * ANG,
    )


def merge(first, second):
    top = jnp.maximum(first[0], second[0])
    return top, first[1] * jnp.exp(first[0] - top) + second[1] * jnp.exp(second[0] - top)


def two_lines(ref):
    return ref[0:1, :], ref[1:2, :]


def merge_kernel(first, second, out):
    top, total = merge(two_lines(first), two_lines(second))
    line = lax.broadcasted_iota(jnp.int32, out.shape, 0)
    out[...] = jnp.where(line == 0, top, total)


def turn_kernel(share, weights, more, tops, more_tops, first, second, forward, *refs):
    rounded_ref, rounded_more, send, *last, held = refs
    classes = 2 * weights.shape[0]
    width, bundle, units = layout(classes, share)
    pairs = (held.shape[0] // (2 * classes) - SPARE) // 2
    top, total = merge(two_lines(first), two_lines(second))
    evidence = top + jnp.log(total)
    scale = 1.0 / total
    at = table_rows(0, ANG // 2)
    lane = lax.broadcasted_iota(jnp.int32, (1, 128), 1)
    line = lax.broadcasted_iota(jnp.int32, (4 * classes, 128), 0)

    def with_count(column, k, count):
        high = count.astype(BF16).astype(F32)
        return jnp.where(line == k, high, jnp.where(line == classes + k, count - high, column))

    more_counts = []
    for unit in range(units):
        factor = jnp.exp(
            more_tops[pl.ds(unit, 1), :] - repeat(top[:, 128:], width, bundle)
        ) * repeat(scale[:, 128:], width, bundle)
        value = more[unit] * jnp.where(lane < bundle * width, factor, 0.0)
        count = jnp.sum(value, axis=0, keepdims=True)
        for j in range(bundle):
            mine = jnp.where(lane // width == j, count, 0.0)
            more_counts.append(jnp.sum(mine, axis=1, keepdims=True))
        rounded = value.astype(BF16)
        rounded_more[unit] = rounded
        spectrum = dot(forward[at, :], jnp.concatenate([rounded, rounded], 0)).astype(BF16)
        step = 4 * classes
        entries = spectrum.shape[0] // step
        for i in range(entries):
            send[pairs + unit * entries + i] = spectrum[i * step : (i + 1) * step]

    tops_here = jnp.concatenate([top[:, :128]] * 2, 1)
    scale_here = jnp.concatenate([scale[:, :128]] * 2, 1)

    def body(i, column):
        value = weights[i] * (jnp.exp(tops[pl.ds(i, 1), :] - tops_here) * scale_here)
        rounded = value.astype(BF16)
        rounded_ref[i] = rounded
        spread(held, i, dot(forward[at, :], jnp.concatenate([rounded, rounded], 0)))
        count = jnp.sum(value, axis=0, keepdims=True)
        for j in range(2):
            mine = jnp.sum(count[:, j * 128 : (j + 1) * 128], axis=1, keepdims=True)
            column = with_count(column, 2 * i + j, mine)
        return column

    column = each(classes // 2, body, jnp.zeros((4 * classes, 128), F32))
    extra = jnp.zeros((4 * classes, 128), F32)
    for k, count in enumerate(more_counts):
        extra = with_count(extra, k, count)
    for ref in last:
        ref[...] = evidence[:, :share]
        high = evidence.astype(BF16).astype(F32)
        middle = (evidence - high).astype(BF16).astype(F32)
        for i, value in enumerate((high, middle, evidence - high - middle)):
            for j in range(2):
                mine = value[:, j * 128 : (j + 1) * 128]
                extra = jnp.where(line == 2 * classes + 2 * i + j, mine, extra)
    send[send.shape[0] - 2] = column.astype(BF16)
    send[send.shape[0] - 1] = extra.astype(BF16)

    def rearrange(f):
        for i, parts in enumerate(pick(held, f, classes)):
            send[f + i] = jnp.concatenate(parts, 0).astype(BF16)

    every(pairs, rearrange)


def spread(held, i, value):
    freqs = value.shape[0] // 2
    for j in range(2):
        for part in range(2):
            held[rows((4 * i + 2 * j + part) * (freqs + SPARE), freqs), :] = value[
                part * freqs : (part + 1) * freqs, j * 128 : (j + 1) * 128
            ]


def spread_more(held, unit, value, classes, share):
    width, bundle, _ = layout(classes, share)
    freqs = value.shape[0] // 2
    for j in range(bundle):
        shifted = turned(value, -j * width)
        for part in range(2):
            k = unit * bundle + j
            held[rows((2 * k + part) * (freqs + SPARE), freqs), :] = shifted[
                part * freqs : (part + 1) * freqs
            ]


def message_shape(classes, pairs, units):
    return (pairs + units * (ANG // 2) // (4 * classes) + 2, 4 * classes, 128)


def turn(weights, more, tops, more_tops, first, second, forward, freqs, share, last):
    classes = 2 * weights.shape[0]
    units = more.shape[0]
    return call(
        functools.partial(turn_kernel, share),
        [weights, more, tops, more_tops, first, second, forward],
        [
            (weights.shape, BF16),
            (more.shape, BF16),
            (message_shape(classes, freqs // 2, units), BF16),
            *([((1, share), F32)] if last else []),
        ],
        [((2 * classes * (freqs + SPARE), 128), F32)],
        flops=4 * classes * 256 * ANG * ANG,
    )


def gather_kernel(rounded_ref, rounded_more, forward, particles, image, held, held_more):
    classes = 2 * rounded_ref.shape[0]
    pairs, share, _ = particles.shape
    at = table_rows(ANG // 2, ANG // 2)

    for unit in range(rounded_more.shape[0]):
        rounded = rounded_more[unit]
        value = dot(forward[at, :], jnp.concatenate([rounded, rounded], 0))
        spread_more(held_more, unit, value, classes, share)

    def body(i, carry):
        rounded = rounded_ref[i]
        spread(held, i, dot(forward[at, :], jnp.concatenate([rounded, rounded], 0)))
        return carry

    each(classes // 2, body, 0)

    def accumulate(f):
        values = []
        for i, both in enumerate(zip(pick(held, f, classes), pick(held_more, f, classes))):
            left = [jnp.concatenate(parts, 0).astype(BF16) for parts in both]
            values.append(dot(jnp.concatenate(left, 1)[:, :share], particles[f + i]))
        take_in(image, f, values, classes)

    every(pairs, accumulate)


def gather(rounded, rounded_more, forward, particles):
    pairs, share, twice = particles.shape
    classes = 2 * rounded.shape[0]
    lines = 2 * classes * (2 * pairs + SPARE)
    return call(
        gather_kernel,
        [rounded, rounded_more, forward, particles],
        [((lines, twice // 2), F32)],
        [((lines, 128), F32)] * 2,
        flops=4 * classes * 256 * ANG * ANG,
    )[0]


def take_in(image, f, values, classes):
    lines, depth = image.shape
    blocks = [
        value[part * 2 * classes : (part + 1) * 2 * classes, part * depth : (part + 1) * depth]
        for value in values
        for part in range(2)
    ]
    put(image, f, blocks, lines // (2 * classes))


def finish_kernel(image, mine, spectrum, particles, *refs):
    *outs, held = refs
    evidence_ref = outs.pop() if len(outs) > 1 else None
    pairs, share, twice = particles.shape
    classes = spectrum.shape[1] // 4
    freqs, depth = 2 * pairs, twice // 2
    radii = depth // 2
    pitch = freqs + SPARE

    width, bundle, units = layout(classes, share)
    step = 4 * classes
    entries = ANG // 2 // step

    def received(f):
        blocks = []
        for k in range(classes):
            unit, j = divmod(k, bundle)
            for part in range(2):
                entry, first = divmod(part * freqs + 2 * f, step)
                value = spectrum[pairs + unit * entries + entry].astype(F32)
                blocks.append(turned(value[first : first + 2 * GROUP], -j * width))
        blocks = jnp.swapaxes(jnp.stack(blocks, 0), 0, 1)
        return [(blocks[2 * i], blocks[2 * i + 1]) for i in range(GROUP)]

    def body(f):
        values = []
        for i, parts in enumerate(received(f)):
            left = jnp.concatenate(parts, 0).astype(BF16)
            left = jnp.concatenate([spectrum[f + i], left], 1)[:, :share]
            values.append(dot(left, particles[f + i]))
        take_in(held, f, values, classes)

    every(pairs, body)
    end = spectrum.shape[0]
    counts = sum(ref[i].astype(F32) for ref in (mine, spectrum) for i in (end - 2, end - 1))
    if evidence_ref is not None:
        parts = spectrum[end - 1].astype(F32)[2 * classes :]
        parts = [jnp.concatenate([parts[i : i + 1], parts[i + 1 : i + 2]], 1) for i in (0, 2, 4)]
        evidence_ref[...] = (parts[0] + (parts[1] + parts[2]))[:, :share]
    counts = counts[:classes] + counts[classes : 2 * classes]
    lane = lax.broadcasted_iota(jnp.int32, (freqs, depth), 1)
    sign = jnp.where(lane < radii, -1.0, 1.0).astype(F32)
    for k in range(classes):
        plain, crossed = [
            image[rows((2 * k + part) * pitch, freqs), :]
            + held[rows((2 * k + part) * pitch, freqs), :]
            for part in range(2)
        ]
        value = plain + sign * pltpu.roll(crossed, radii, 1)
        if len(outs) == 1:
            outs[0][pl.ds(k * freqs, freqs), :] = value.astype(BF16)
        else:
            outs[k][pl.ds(0, freqs), :] = value
            outs[k][pl.ds(freqs, SPARE), :] = jnp.broadcast_to(counts[k : k + 1], (SPARE, depth))
    if len(outs) == 1:
        end = outs[0].shape[0] - classes * freqs
        high, low = split(counts)
        spare = [jnp.zeros((end - 2 * classes, depth), F32)] if end > 2 * classes else []
        tail = jnp.concatenate([high.astype(F32), low.astype(F32), *spare], 0)
        outs[0][pl.ds(classes * freqs, end), :] = tail.astype(BF16)


def finish(image, mine, spectrum, particles, last):
    pairs, _, twice = particles.shape
    classes = spectrum.shape[1] // 4
    freqs, depth = 2 * pairs, twice // 2
    if last:
        outs = [((freqs + SPARE, depth), F32)] * classes + [((1, particles.shape[1]), F32)]
    else:
        outs = [((classes * freqs + -(-2 * classes // 16) * 16, depth), BF16)]
    return call(
        finish_kernel,
        [image, mine, spectrum, particles],
        outs,
        [(image.shape, F32)],
        flops=2 * math.prod(spectrum.shape) * twice * 8,
    )


def means_kernel(*refs):
    *parts, own, other, out, evidence_ref = refs
    odd = lax.rem(lax.axis_index("cls"), 2)
    evidence_ref[...] = jnp.where(odd == 0, own[...], other[...])
    freqs = out.shape[1]
    total = tree(ref[...] for ref in parts)
    out[0] = total[:freqs, :] / (total[freqs : freqs + 1, :] + shrinkage)


def swap(value, axis, size, bit):
    if not bit:
        return value
    return lax.ppermute(value, axis, [(i, i ^ bit) for i in range(size)])


def bits(size):
    assert size > 1 and size & (size - 1) == 0
    return [1 << i for i in range(size.bit_length() - 1)]


def shards(particles, references, noise_inv, prior_rot):
    batch, freqs, depth = particles.shape
    sides = lax.axis_size("cls")
    groups = lax.axis_size("rot")
    blocks = lax.axis_size("blk")
    assert groups == 2 and 2 * groups * freqs == ANG
    share = batch // groups
    inverse, forward = tables(freqs)
    inverse_noise = noise_inv.reshape(1, depth // 2)
    assert blocks & (blocks - 1) == 0
    turns = sorted(range(1, blocks), key=lambda i: (-i.bit_length(), i))

    (permutation,) = call(permutation_kernel, [], [((256, 256), BF16)], flops=1 << 32)
    (prior_term,) = call(
        functools.partial(prior_kernel, share), [prior_rot], [((ANG, 256), F32)], flops=1 << 26
    )
    sources = {i: swap(references, "blk", blocks, i) for i in (*turns, 0)}
    other_images, own_images = prep(particles, permutation, share)
    for step in range(ITERS):
        last = step == ITERS - 1
        order = list(range(blocks)) if step else [0, *reversed(range(1, blocks))]
        message, energy, left = weigh(sources, order, inverse_noise, other_images, step == 0)
        message = swap(message, "rot", groups, 1)
        own = correlate(left, own_images)
        *weights, here = scores(own, message, energy, prior_term, inverse, share)
        first = here
        for bit in bits(sides):
            second = swap(first, ("cls", "rot"), sides * groups, groups * bit + (bit == 1))
            if 2 * bit < sides:
                (first,) = call(merge_kernel, [first, second], [(here.shape, F32)])
        rounded, more, send, *evidence = turn(
            *weights, first, second, forward, freqs, share, last
        )
        message = swap(send, "rot", groups, 1)
        image = gather(rounded, more, forward, own_images)
        sums = finish(image, send, message, other_images, last)
        sums, others = (sums[:blocks], sums[blocks:]) if last else (sums * blocks, [])
        sources = {i: swap(sums[i], "blk", blocks, i) for i in (*turns, 0)}
    means, evidence = call(
        means_kernel, [*[sources[i] for i in reversed(range(blocks))], *evidence, *others], [((1, freqs, depth), F32), ((1, share), F32)]
    )
    return means, evidence.reshape(share)


def solution(mesh):
    in_specs = (
        P(("grp", "blk"), "rot", None),
        P(("grp", "blk", "cls"), "rot", None),
        P(),
        P(("grp", "blk")),
    )
    out_specs = (P(("grp", "blk", "cls"), "rot", None), P(("grp", "blk", "rot")))
    return jax.shard_map(shards, mesh=mesh, in_specs=in_specs, out_specs=out_specs, check_vma=False)
```

```python
import functools
import math

import jax
import jax.numpy as jnp
import numpy as np
from jax import lax
from jax.experimental import pallas as pl
from jax.experimental.pallas import tpu as pltpu
from jax.sharding import PartitionSpec as P

ANG = 256
ITERS = 2
SIGMA = 32

shrinkage = 1.0

F32 = jnp.float32
BF16 = jnp.bfloat16
SPARE = 8

dot = functools.partial(jnp.dot, preferred_element_type=F32)


def split(x):
    high = x.astype(BF16)
    return high, (x - high.astype(F32)).astype(BF16)


def tables(half_freq):
    turn = np.arange(ANG)
    near, far, forward = [], [], []
    for group in range(2):
        sides = {}
        for which in range(2):
            freq = which * half_freq + np.arange(half_freq)
            angle = (turn[:, None] * freq[None, :] % ANG) * (2.0 * math.pi / ANG)
            scale = np.where(freq == 0, 1.0, 2.0) / ANG
            sides[which] = (
                np.concatenate([scale * np.cos(angle), -scale * np.sin(angle)], 1),
                np.concatenate([np.cos(angle), np.sin(angle)], 1).T,
            )
        near.append(sides[group][0])
        far.append(sides[1 - group][0])
        forward.append(np.concatenate([sides[1 - group][1], sides[group][1]], 0))
    result = []
    for table, kinds in ((near, (0, 0, 1)), (far, (0, 0, 1)), (forward, (0, 1))):
        table = np.concatenate(table, 0).astype(np.float32)
        high = table.astype(BF16)
        parts = [high, (table - high.astype(np.float32)).astype(BF16)]
        result.append(jnp.asarray(np.concatenate([parts[kind] for kind in kinds], 1)))
    return result


def each(count, body, init):
    if count <= 8:
        for k in range(count):
            init = body(k, init)
        return init
    return lax.fori_loop(0, count, body, init)


def rows(base, count):
    return pl.ds(pl.multiple_of(base, 8), count)


def call(kernel, ins, outs, scratch=(), flops=0, far=(), room=4 << 20):
    total = 0
    buffers = [(x.shape, x.dtype) for i, x in enumerate(ins) if i not in far]
    for shape, dtype in buffers + list(outs) + [x for x in scratch if isinstance(x, tuple)]:
        dims = [1, 1, *shape]
        lines = -(-dims[-2] // 16) * 16
        lanes = -(-dims[-1] // 128) * 128
        total += math.prod(dims[:-2]) * lines * lanes * jnp.dtype(dtype).itemsize
    kinds = [pltpu.VMEM] * len(ins)
    for i in far:
        kinds[i] = pltpu.MemorySpace.HBM
    return pl.pallas_call(
        kernel,
        out_shape=[jax.ShapeDtypeStruct(*x) for x in outs],
        in_specs=[pl.BlockSpec(memory_space=kind) for kind in kinds],
        out_specs=[pl.BlockSpec(memory_space=pltpu.VMEM)] * len(outs),
        scratch_shapes=[pltpu.VMEM(*x) if isinstance(x, tuple) else x for x in scratch],
        compiler_params=pltpu.CompilerParams(vmem_limit_bytes=min(total + room, 56 << 20)),
        cost_estimate=pl.CostEstimate(flops=flops, bytes_accessed=total, transcendentals=0),
    )(*ins)


def permutation_kernel(out):
    to = lax.broadcasted_iota(jnp.int32, out.shape, 0)
    at = lax.broadcasted_iota(jnp.int32, out.shape, 1)
    out[...] = ((to // 16 == at % 16) & (to % 16 == at // 16)).astype(F32).astype(BF16)


def half_index():
    return lax.rem(lax.axis_index("rot") + lax.axis_index("cls"), 2)


def prior_kernel(share, prior_ref, prior_term):
    turns = lax.broadcasted_iota(jnp.int32, (ANG, 256), 0)
    lane = lax.broadcasted_iota(jnp.int32, (1, 256), 1)
    priors = prior_ref[...].reshape(1, -1)
    first, second = [
        jnp.concatenate([priors[:, i * share : (i + 1) * share], lane[:, share:]], 1)
        for i in range(2)
    ]
    offset = jnp.abs(turns - jnp.where(half_index() == 0, first, second))
    distance = jnp.minimum(offset, ANG - offset).astype(F32)
    term = -distance * distance / (2.0 * SIGMA * SIGMA)
    prior_term[:, :128] = term[:, :128]
    prior_term[:, 128:] = repeat(term[:, 128:], share - 128, 128 // (share - 128))


def turned(value, lanes):
    return pltpu.roll(value, lanes % 128, 1) if lanes % 128 else value


def repeat(value, width, times):
    lane = lax.broadcasted_iota(jnp.int32, value.shape, 1)
    value = jnp.where(lane < width, value, 0.0)
    return sum(turned(value, i * width) for i in range(times))


def layout(classes, share):
    width = share - 128
    assert 0 < width < 128 and 128 % width == 0 and classes % 2 == 0
    bundle = min(128 // width, classes)
    assert classes % bundle == 0
    return width, bundle, classes // bundle


def prep_kernel(share, particles_ref, permutation_ref, other, own):
    freqs, depth = particles_ref.shape[1:]
    half = half_index()
    permutation = permutation_ref[...]
    for out, first in ((other, (1 - half) * share), (own, half * share)):
        for p in range(0, share, 16):
            for f in range(0, freqs, 32):
                blocks = [
                    jnp.concatenate(
                        [particles_ref[first + p + j, pl.ds(f + second, 16), :] for j in range(16)],
                        0,
                    )
                    for second in (0, 16)
                ]
                turned = dot(permutation, jnp.concatenate(blocks, 1)).astype(BF16)
                for half in range(2):
                    for j in range(16):
                        pair, part = divmod(f + 16 * half + j, 2)
                        out[pair, pl.ds(p, 16), pl.ds(part * depth, depth)] = turned[
                            16 * j : 16 * j + 16, half * depth : (half + 1) * depth
                        ]


def prep(particles, permutation, share):
    _, freqs, depth = particles.shape
    assert share % 16 == 0 and freqs % 32 == 0
    return call(
        functools.partial(prep_kernel, share),
        [particles, permutation],
        [((freqs // 2, share, 2 * depth), BF16)] * 2,
        flops=1 << 31,
    )


def tree(values):
    values = list(values)
    while len(values) > 1:
        values = [a + b for a, b in zip(values[::2], values[1::2])]
    return values[0]


def weigh_kernel(fresh, order, count, *refs):
    sources = [refs[order.index(i)] for i in range(count)]
    doubled_ref, particles, out, energy_ref, left_ref, image = refs[count:]
    pairs, share, twice = particles.shape
    freqs, depth = 2 * pairs, twice // 2
    classes = energy_ref.shape[0]
    pitch = freqs + SPARE
    radii = depth // 2
    lane = lax.broadcasted_iota(jnp.int32, (freqs, depth), 1)
    sign = jnp.where(lane < radii, -1.0, 1.0).astype(F32)
    doubled = jnp.concatenate([doubled_ref[...]] * 2, 1)
    row = lax.broadcasted_iota(jnp.int32, (freqs, depth), 0) + lax.axis_index("rot") * freqs
    scale = jnp.where(row == 0, 1.0 / ANG, 2.0 / ANG).astype(F32) * doubled

    tails = []
    if not fresh:
        end = sources[0].shape[0] - classes * freqs
        tails = [source[pl.ds(classes * freqs, end), :].astype(F32) for source in sources]

    for k in range(classes):
        if fresh:
            plain = sources[k][0].astype(F32)
        else:
            sums = tree(
                source[pl.ds((k ^ i) * freqs, freqs), :].astype(F32)
                for i, source in enumerate(sources)
            )
            highs, lows = [
                tree(tail[base + (k ^ i) : base + (k ^ i) + 1] for i, tail in enumerate(tails))
                for base in (0, classes)
            ]
            plain = (sums / (highs + lows + shrinkage)).astype(BF16).astype(F32)
        weighted = (plain * doubled).astype(BF16).astype(F32)
        image[rows(2 * k * pitch, freqs), :] = weighted
        image[rows((2 * k + 1) * pitch, freqs), :] = sign * pltpu.roll(weighted, radii, 1)
        energy = jnp.sum(plain * plain * scale, axis=0, keepdims=True)
        energy = jnp.broadcast_to(jnp.sum(energy, axis=1, keepdims=True), (SPARE, 128))
        energy_ref[pl.ds(k, 1), :] = energy[:1]
        out[rows(2 * k * pitch + freqs, SPARE), :] = energy

    none = jnp.zeros((2 * classes, depth), BF16)

    def correlate(f):
        lefts = []
        for first, second in pick(image, f, classes):
            first, second = first.astype(BF16), second.astype(BF16)
            left = jnp.concatenate(
                [jnp.concatenate([first, none], 1), jnp.concatenate([none, second], 1)], 0
            )
            left_ref[f + len(lefts)] = left
            lefts.append(left)
        values = [times(left, particles[f + i]) for i, left in enumerate(lefts)]
        place(out, f, values, classes, pitch)

    every(pairs, correlate)


def times(left, particles):
    return lax.dot_general(left, particles, (((1,), (1,)), ((), ())), preferred_element_type=F32)


GROUP = 4


def every(pairs, body):
    for f in range(0, pairs, GROUP):
        body(f)


def put(ref, f, blocks, pitch):
    turned_blocks = jnp.swapaxes(jnp.stack(blocks, 0), 0, 1)
    for i in range(blocks[0].shape[0]):
        ref[pl.ds(i * pitch + 2 * f, 2 * GROUP), :] = turned_blocks[i]


def pick(ref, f, classes):
    pitch = ref.shape[0] // (2 * classes)
    blocks = [ref[pl.ds(i * pitch + 2 * f, 2 * GROUP), :] for i in range(2 * classes)]
    blocks = jnp.swapaxes(jnp.stack(blocks, 0), 0, 1)
    return [(blocks[2 * i], blocks[2 * i + 1]) for i in range(GROUP)]


def place(out, f, values, classes, pitch):
    width = values[0].shape[1] - 128
    each_pack = 128 // width
    spare = jnp.zeros((2 * classes, 128 - width), F32)
    parts = [
        value[part * 2 * classes : (part + 1) * 2 * classes] for value in values for part in range(2)
    ]
    put(out, f, [part[:, :128] for part in parts], pitch)
    more = [jnp.concatenate([part[:, 128:], spare], 1) for part in parts]
    more = jnp.swapaxes(jnp.stack(more, 0), 0, 1)
    for first in range(0, 2 * classes, each_pack):
        total = 0.0
        for group in range(first, min(first + each_pack, 2 * classes)):
            part, k = divmod(group, classes)
            total = total + turned(more[2 * k + part], (group - first) * width)
        at = (2 * classes + first // each_pack) * pitch + 2 * f
        out[pl.ds(at, 2 * GROUP), :] = total


def unpack(ref, unit, part, classes, share, pitch, freqs):
    width, bundle, _ = layout(classes, share)
    group = part * classes + unit * bundle
    each_pack = 128 // width
    value = ref[rows((2 * classes + group // each_pack) * pitch, freqs), :]
    return turned(value, -(group % each_pack) * width)


def corr_lines(classes, share, pitch):
    return (2 * classes + -(-2 * classes * (share - 128) // 128)) * pitch


def weigh(sources, order, inverse_noise, particles, fresh):
    pairs, share, twice = particles.shape
    classes = len(sources)
    pitch = 2 * pairs + SPARE
    return call(
        functools.partial(weigh_kernel, fresh, order, classes),
        [*[sources[i] for i in order], inverse_noise, particles],
        [
            ((corr_lines(classes, share, pitch), 128), F32),
            ((classes, 128), F32),
            ((pairs, 4 * classes, twice), BF16),
        ],
        [((2 * classes * pitch, twice // 2), F32)],
        flops=8 * classes * share * pairs * twice * 4,
    )


def correlate_kernel(left_ref, particles, energy_ref, prior_term, table, *refs):
    partial, partial_more, field = refs
    pairs, share, _ = particles.shape
    classes = left_ref.shape[1] // 4
    freqs, pitch = 2 * pairs, 2 * pairs + SPARE

    def body(f):
        values = [times(left_ref[f + i], particles[f + i]) for i in range(GROUP)]
        place(field, f, values, classes, pitch)

    every(pairs, body)

    def energy_of(k):
        return energy_ref[pl.ds(k, 1), :]

    def slab(i, carry):
        prior = jnp.concatenate([prior_term[:, :128]] * 2, 1)
        energy = jnp.concatenate([energy_of(2 * i), energy_of(2 * i + 1)], 1)
        partial[i] = invert(table, two_classes(field, i, pitch, freqs)) - 0.5 * energy + prior
        return carry

    each(classes // 2, slab, 0)
    for unit in range(partial_more.shape[0]):
        energy = beside(energy_of, unit, classes, share)
        value = several_classes(field, unit, classes, share, pitch, freqs)
        partial_more[unit] = invert(table, value) - 0.5 * energy + prior_term[:, 128:]


def two_classes(field, i, pitch, freqs):
    parts = [
        [field[rows((4 * i + 2 * j + part) * pitch, freqs), :] for j in range(2)]
        for part in range(2)
    ]
    return jnp.concatenate([jnp.concatenate(part, 1) for part in parts], 0)


def several_classes(field, unit, classes, share, pitch, freqs):
    return jnp.concatenate(
        [unpack(field, unit, part, classes, share, pitch, freqs) for part in range(2)], 0
    )


def beside(value_of, unit, classes, share):
    width, bundle, _ = layout(classes, share)
    lane = lax.broadcasted_iota(jnp.int32, (1, 128), 1)
    return sum(
        jnp.where(lane // width == j, value_of(unit * bundle + j), 0.0) for j in range(bundle)
    )


def invert(table, value):
    high, low = split(value)
    return dot(table[table_rows(0, ANG), :], jnp.concatenate([high, low, high], 0))


def correlate(left, particles, energy, prior_term, table):
    pairs, share, twice = particles.shape
    classes = left.shape[1] // 4
    pitch = 2 * pairs + SPARE
    return call(
        correlate_kernel,
        [left, particles, energy, prior_term, table],
        [((classes // 2, ANG, 256), F32), ((layout(classes, share)[2], ANG, 128), F32)],
        [((corr_lines(classes, share, pitch), 128), F32)],
        flops=2 * left.shape[1] * share * pairs * twice * 8,
    )


def table_rows(base, count):
    return pl.ds(pl.multiple_of(lax.axis_index("rot") * ANG + base, 128), count)


def score_kernel(share, partial, partial_more, other, table, *refs):
    weights, more, tops, more_tops, peaks = refs
    classes = 2 * partial.shape[0]
    width, bundle, units = layout(classes, share)
    freqs = ANG // 4
    pitch = freqs + SPARE

    def exponentials(scores):
        top = jnp.max(scores, axis=0, keepdims=True)
        value = jnp.exp(scores - top)
        return value, top, jnp.sum(value, axis=0, keepdims=True)

    def energy_of(k):
        return other[rows(2 * k * pitch + freqs, SPARE), :][:1]

    def slab(i, carry):
        energy = jnp.concatenate([energy_of(2 * i), energy_of(2 * i + 1)], 1)
        inner = invert(table, two_classes(other, i, pitch, freqs))
        weights[i], top, total = exponentials(inner + (partial[i] - 0.5 * energy))
        tops[pl.ds(i, 1), :] = top
        for j in (0, 128):
            carry = merge(carry, (top[:, j : j + 128], total[:, j : j + 128]))
        return carry

    empty = (jnp.full((1, 128), -jnp.inf, F32), jnp.zeros((1, 128), F32))
    top, total = each(classes // 2, slab, empty)
    rest = empty
    for unit in range(units):
        energy = beside(energy_of, unit, classes, share)
        inner = invert(table, several_classes(other, unit, classes, share, pitch, freqs))
        more[unit], more_top, more_total = exponentials(inner + (partial_more[unit] - 0.5 * energy))
        more_tops[pl.ds(unit, 1), :] = more_top
        for j in range(bundle):
            rest = merge(rest, (turned(more_top, -j * width), turned(more_total, -j * width)))
    line = lax.broadcasted_iota(jnp.int32, peaks.shape, 0)
    peaks[...] = jnp.where(
        line == 0,
        jnp.concatenate([top, rest[0]], 1),
        jnp.concatenate([total, rest[1]], 1),
    )


def scores(partial, partial_more, other, table, share):
    classes = 2 * partial.shape[0]
    units = layout(classes, share)[2]
    return call(
        functools.partial(score_kernel, share),
        [partial, partial_more, other, table],
        [
            ((classes // 2, ANG, 256), F32),
            ((units, ANG, 128), F32),
            ((classes // 2, 256), F32),
            ((units, 128), F32),
            ((8, 256), F32),
        ],
        flops=6 * classes * 256 * ANG * ANG,
    )


def merge(first, second):
    top = jnp.maximum(first[0], second[0])
    return top, first[1] * jnp.exp(first[0] - top) + second[1] * jnp.exp(second[0] - top)


def two_lines(ref):
    return ref[0:1, :], ref[1:2, :]


def merge_kernel(first, second, out):
    top, total = merge(two_lines(first), two_lines(second))
    line = lax.broadcasted_iota(jnp.int32, out.shape, 0)
    out[...] = jnp.where(line == 0, top, total)


def turn_kernel(share, weights, more, tops, more_tops, first, second, forward, *refs):
    rounded_ref, rounded_more, send, *last, held = refs
    classes = 2 * weights.shape[0]
    width, bundle, units = layout(classes, share)
    pairs = (held.shape[0] // (2 * classes) - SPARE) // 2
    top, total = merge(two_lines(first), two_lines(second))
    evidence = top + jnp.log(total)
    scale = 1.0 / total
    at = table_rows(0, ANG // 2)
    lane = lax.broadcasted_iota(jnp.int32, (1, 128), 1)
    line = lax.broadcasted_iota(jnp.int32, (4 * classes, 128), 0)

    def with_count(column, k, count):
        high = count.astype(BF16).astype(F32)
        return jnp.where(line == k, high, jnp.where(line == classes + k, count - high, column))

    more_counts = []
    for unit in range(units):
        factor = jnp.exp(
            more_tops[pl.ds(unit, 1), :] - repeat(top[:, 128:], width, bundle)
        ) * repeat(scale[:, 128:], width, bundle)
        value = more[unit] * jnp.where(lane < bundle * width, factor, 0.0)
        count = jnp.sum(value, axis=0, keepdims=True)
        for j in range(bundle):
            mine = jnp.where(lane // width == j, count, 0.0)
            more_counts.append(jnp.sum(mine, axis=1, keepdims=True))
        rounded = value.astype(BF16)
        rounded_more[unit] = rounded
        spectrum = dot(forward[at, :], jnp.concatenate([rounded, rounded], 0)).astype(BF16)
        step = 4 * classes
        entries = spectrum.shape[0] // step
        for i in range(entries):
            send[pairs + unit * entries + i] = spectrum[i * step : (i + 1) * step]

    tops_here = jnp.concatenate([top[:, :128]] * 2, 1)
    scale_here = jnp.concatenate([scale[:, :128]] * 2, 1)

    def body(i, column):
        value = weights[i] * (jnp.exp(tops[pl.ds(i, 1), :] - tops_here) * scale_here)
        rounded = value.astype(BF16)
        rounded_ref[i] = rounded
        spread(held, i, dot(forward[at, :], jnp.concatenate([rounded, rounded], 0)))
        count = jnp.sum(value, axis=0, keepdims=True)
        for j in range(2):
            mine = jnp.sum(count[:, j * 128 : (j + 1) * 128], axis=1, keepdims=True)
            column = with_count(column, 2 * i + j, mine)
        return column

    column = each(classes // 2, body, jnp.zeros((4 * classes, 128), F32))
    extra = jnp.zeros((4 * classes, 128), F32)
    for k, count in enumerate(more_counts):
        extra = with_count(extra, k, count)
    for ref in last:
        ref[...] = evidence[:, :share]
        high = evidence.astype(BF16).astype(F32)
        middle = (evidence - high).astype(BF16).astype(F32)
        for i, value in enumerate((high, middle, evidence - high - middle)):
            for j in range(2):
                mine = value[:, j * 128 : (j + 1) * 128]
                extra = jnp.where(line == 2 * classes + 2 * i + j, mine, extra)
    send[send.shape[0] - 2] = column.astype(BF16)
    send[send.shape[0] - 1] = extra.astype(BF16)

    def rearrange(f):
        for i, parts in enumerate(pick(held, f, classes)):
            send[f + i] = jnp.concatenate(parts, 0).astype(BF16)

    every(pairs, rearrange)


def spread(held, i, value):
    freqs = value.shape[0] // 2
    for j in range(2):
        for part in range(2):
            held[rows((4 * i + 2 * j + part) * (freqs + SPARE), freqs), :] = value[
                part * freqs : (part + 1) * freqs, j * 128 : (j + 1) * 128
            ]


def spread_more(held, unit, value, classes, share):
    width, bundle, _ = layout(classes, share)
    freqs = value.shape[0] // 2
    for j in range(bundle):
        shifted = turned(value, -j * width)
        for part in range(2):
            k = unit * bundle + j
            held[rows((2 * k + part) * (freqs + SPARE), freqs), :] = shifted[
                part * freqs : (part + 1) * freqs
            ]


def message_shape(classes, pairs, units):
    return (pairs + units * (ANG // 2) // (4 * classes) + 2, 4 * classes, 128)


def turn(weights, more, tops, more_tops, first, second, forward, freqs, share, last):
    classes = 2 * weights.shape[0]
    units = more.shape[0]
    return call(
        functools.partial(turn_kernel, share),
        [weights, more, tops, more_tops, first, second, forward],
        [
            (weights.shape, BF16),
            (more.shape, BF16),
            (message_shape(classes, freqs // 2, units), BF16),
            *([((1, share), F32)] if last else []),
        ],
        [((2 * classes * (freqs + SPARE), 128), F32)],
        flops=4 * classes * 256 * ANG * ANG,
    )


def gather_kernel(rounded_ref, rounded_more, forward, particles, image, held, held_more):
    classes = 2 * rounded_ref.shape[0]
    pairs, share, _ = particles.shape
    at = table_rows(ANG // 2, ANG // 2)

    for unit in range(rounded_more.shape[0]):
        rounded = rounded_more[unit]
        value = dot(forward[at, :], jnp.concatenate([rounded, rounded], 0))
        spread_more(held_more, unit, value, classes, share)

    def body(i, carry):
        rounded = rounded_ref[i]
        spread(held, i, dot(forward[at, :], jnp.concatenate([rounded, rounded], 0)))
        return carry

    each(classes // 2, body, 0)

    def accumulate(f):
        values = []
        for i, both in enumerate(zip(pick(held, f, classes), pick(held_more, f, classes))):
            left = [jnp.concatenate(parts, 0).astype(BF16) for parts in both]
            values.append(dot(jnp.concatenate(left, 1)[:, :share], particles[f + i]))
        take_in(image, f, values, classes)

    every(pairs, accumulate)


def gather(rounded, rounded_more, forward, particles):
    pairs, share, twice = particles.shape
    classes = 2 * rounded.shape[0]
    lines = 2 * classes * (2 * pairs + SPARE)
    return call(
        gather_kernel,
        [rounded, rounded_more, forward, particles],
        [((lines, twice // 2), F32)],
        [((lines, 128), F32)] * 2,
        flops=4 * classes * 256 * ANG * ANG,
    )[0]


def take_in(image, f, values, classes):
    lines, depth = image.shape
    blocks = [
        value[part * 2 * classes : (part + 1) * 2 * classes, part * depth : (part + 1) * depth]
        for value in values
        for part in range(2)
    ]
    put(image, f, blocks, lines // (2 * classes))


def finish_kernel(image, mine, spectrum, particles, *refs):
    *outs, held = refs
    evidence_ref = outs.pop() if len(outs) > 1 else None
    pairs, share, twice = particles.shape
    classes = spectrum.shape[1] // 4
    freqs, depth = 2 * pairs, twice // 2
    radii = depth // 2
    pitch = freqs + SPARE

    width, bundle, units = layout(classes, share)
    step = 4 * classes
    entries = ANG // 2 // step

    def received(f):
        blocks = []
        for k in range(classes):
            unit, j = divmod(k, bundle)
            for part in range(2):
                entry, first = divmod(part * freqs + 2 * f, step)
                value = spectrum[pairs + unit * entries + entry].astype(F32)
                blocks.append(turned(value[first : first + 2 * GROUP], -j * width))
        blocks = jnp.swapaxes(jnp.stack(blocks, 0), 0, 1)
        return [(blocks[2 * i], blocks[2 * i + 1]) for i in range(GROUP)]

    def body(f):
        values = []
        for i, parts in enumerate(received(f)):
            left = jnp.concatenate(parts, 0).astype(BF16)
            left = jnp.concatenate([spectrum[f + i], left], 1)[:, :share]
            values.append(dot(left, particles[f + i]))
        take_in(held, f, values, classes)

    every(pairs, body)
    end = spectrum.shape[0]
    counts = sum(ref[i].astype(F32) for ref in (mine, spectrum) for i in (end - 2, end - 1))
    if evidence_ref is not None:
        parts = spectrum[end - 1].astype(F32)[2 * classes :]
        parts = [jnp.concatenate([parts[i : i + 1], parts[i + 1 : i + 2]], 1) for i in (0, 2, 4)]
        evidence_ref[...] = (parts[0] + (parts[1] + parts[2]))[:, :share]
    counts = counts[:classes] + counts[classes : 2 * classes]
    lane = lax.broadcasted_iota(jnp.int32, (freqs, depth), 1)
    sign = jnp.where(lane < radii, -1.0, 1.0).astype(F32)
    for k in range(classes):
        plain, crossed = [
            image[rows((2 * k + part) * pitch, freqs), :]
            + held[rows((2 * k + part) * pitch, freqs), :]
            for part in range(2)
        ]
        value = plain + sign * pltpu.roll(crossed, radii, 1)
        if len(outs) == 1:
            outs[0][pl.ds(k * freqs, freqs), :] = value.astype(BF16)
        else:
            outs[k][pl.ds(0, freqs), :] = value
            outs[k][pl.ds(freqs, SPARE), :] = jnp.broadcast_to(counts[k : k + 1], (SPARE, depth))
    if len(outs) == 1:
        end = outs[0].shape[0] - classes * freqs
        high, low = split(counts)
        spare = [jnp.zeros((end - 2 * classes, depth), F32)] if end > 2 * classes else []
        tail = jnp.concatenate([high.astype(F32), low.astype(F32), *spare], 0)
        outs[0][pl.ds(classes * freqs, end), :] = tail.astype(BF16)


def finish(image, mine, spectrum, particles, last):
    pairs, _, twice = particles.shape
    classes = spectrum.shape[1] // 4
    freqs, depth = 2 * pairs, twice // 2
    if last:
        outs = [((freqs + SPARE, depth), F32)] * classes + [((1, particles.shape[1]), F32)]
    else:
        outs = [((classes * freqs + -(-2 * classes // 16) * 16, depth), BF16)]
    return call(
        finish_kernel,
        [image, mine, spectrum, particles],
        outs,
        [(image.shape, F32)],
        flops=2 * math.prod(spectrum.shape) * twice * 8,
    )


def means_kernel(*refs):
    *parts, own, other, out, evidence_ref = refs
    odd = lax.rem(lax.axis_index("cls"), 2)
    evidence_ref[...] = jnp.where(odd == 0, own[...], other[...])
    freqs = out.shape[1]
    total = tree(ref[...] for ref in parts)
    out[0] = total[:freqs, :] / (total[freqs : freqs + 1, :] + shrinkage)


def swap(value, axis, size, bit):
    if not bit:
        return value
    return lax.ppermute(value, axis, [(i, i ^ bit) for i in range(size)])


def bits(size):
    assert size > 1 and size & (size - 1) == 0
    return [1 << i for i in range(size.bit_length() - 1)]


def shards(particles, references, noise_inv, prior_rot):
    batch, freqs, depth = particles.shape
    sides = lax.axis_size("cls")
    groups = lax.axis_size("rot")
    blocks = lax.axis_size("blk")
    assert groups == 2 and 2 * groups * freqs == ANG
    share = batch // groups
    near, far, forward = tables(freqs)
    inverse_noise = noise_inv.reshape(1, depth // 2)
    assert blocks & (blocks - 1) == 0
    turns = sorted(range(1, blocks), key=lambda i: (-i.bit_length(), i))

    (permutation,) = call(permutation_kernel, [], [((256, 256), BF16)], flops=1 << 32)
    (prior_term,) = call(
        functools.partial(prior_kernel, share), [prior_rot], [((ANG, 256), F32)], flops=1 << 26
    )
    sources = {i: swap(references, "blk", blocks, i) for i in (*turns, 0)}
    other_images, own_images = prep(particles, permutation, share)
    for step in range(ITERS):
        last = step == ITERS - 1
        order = [0, *(reversed(turns) if step else reversed(range(1, blocks)))]
        message, energy, left = weigh(sources, order, inverse_noise, other_images, step == 0)
        message = swap(message, "rot", groups, 1)
        partial = correlate(left, own_images, energy, prior_term, near)
        *weights, here = scores(*partial, message, far, share)
        first = here
        for bit in bits(sides):
            second = swap(first, ("cls", "rot"), sides * groups, groups * bit + (bit == 1))
            if 2 * bit < sides:
                (first,) = call(merge_kernel, [first, second], [(here.shape, F32)])
        rounded, more, send, *evidence = turn(
            *weights, first, second, forward, freqs, share, last
        )
        message = swap(send, "rot", groups, 1)
        image = gather(rounded, more, forward, own_images)
        sums = finish(image, send, message, other_images, last)
        sums, others = (sums[:blocks], sums[blocks:]) if last else (sums * blocks, [])
        sources = {i: swap(sums[i], "blk", blocks, i) for i in (*turns, 0)}
    means, evidence = call(
        means_kernel, [*[sources[i] for i in reversed(range(blocks))], *evidence, *others], [((1, freqs, depth), F32), ((1, share), F32)]
    )
    return means, evidence.reshape(share)


def solution(mesh):
    in_specs = (
        P(("grp", "blk"), "rot", None),
        P(("grp", "blk", "cls"), "rot", None),
        P(),
        P(("grp", "blk")),
    )
    out_specs = (P(("grp", "blk", "cls"), "rot", None), P(("grp", "blk", "rot")))
    return jax.shard_map(shards, mesh=mesh, in_specs=in_specs, out_specs=out_specs, check_vma=False)
```

```python
import functools
import math

import jax
import jax.numpy as jnp
import numpy as np
from jax import lax
from jax.experimental import pallas as pl
from jax.experimental.pallas import tpu as pltpu
from jax.sharding import PartitionSpec as P

ANG = 256
ITERS = 2
SIGMA = 32

shrinkage = 1.0

F32 = jnp.float32
BF16 = jnp.bfloat16
SPARE = 8

dot = functools.partial(jnp.dot, preferred_element_type=F32)


def split(x):
    high = x.astype(BF16)
    return high, (x - high.astype(F32)).astype(BF16)


def tables(half_freq):
    turn = np.arange(ANG)
    near, far, forward = [], [], []
    for group in range(2):
        sides = {}
        for which in range(2):
            freq = which * half_freq + np.arange(half_freq)
            angle = (turn[:, None] * freq[None, :] % ANG) * (2.0 * math.pi / ANG)
            scale = np.where(freq == 0, 1.0, 2.0) / ANG
            sides[which] = (
                np.concatenate([scale * np.cos(angle), -scale * np.sin(angle)], 1),
                np.concatenate([np.cos(angle), np.sin(angle)], 1).T,
            )
        near.append(sides[group][0])
        far.append(sides[1 - group][0])
        forward.append(np.concatenate([sides[1 - group][1], sides[group][1]], 0))
    result = []
    for table, kinds in ((near, (0, 0, 1)), (far, (0, 0, 1)), (forward, (0, 1))):
        table = np.concatenate(table, 0).astype(np.float32)
        high = table.astype(BF16)
        parts = [high, (table - high.astype(np.float32)).astype(BF16)]
        result.append(jnp.asarray(np.concatenate([parts[kind] for kind in kinds], 1)))
    return result


def each(count, body, init):
    if count <= 8:
        for k in range(count):
            init = body(k, init)
        return init
    return lax.fori_loop(0, count, body, init)


def rows(base, count):
    return pl.ds(pl.multiple_of(base, 8), count)


def call(kernel, ins, outs, scratch=(), flops=0, far=(), room=4 << 20):
    total = 0
    buffers = [(x.shape, x.dtype) for i, x in enumerate(ins) if i not in far]
    for shape, dtype in buffers + list(outs) + [x for x in scratch if isinstance(x, tuple)]:
        dims = [1, 1, *shape]
        lines = -(-dims[-2] // 16) * 16
        lanes = -(-dims[-1] // 128) * 128
        total += math.prod(dims[:-2]) * lines * lanes * jnp.dtype(dtype).itemsize
    kinds = [pltpu.VMEM] * len(ins)
    for i in far:
        kinds[i] = pltpu.MemorySpace.HBM
    return pl.pallas_call(
        kernel,
        out_shape=[jax.ShapeDtypeStruct(*x) for x in outs],
        in_specs=[pl.BlockSpec(memory_space=kind) for kind in kinds],
        out_specs=[pl.BlockSpec(memory_space=pltpu.VMEM)] * len(outs),
        scratch_shapes=[pltpu.VMEM(*x) if isinstance(x, tuple) else x for x in scratch],
        compiler_params=pltpu.CompilerParams(vmem_limit_bytes=min(total + room, 56 << 20)),
        cost_estimate=pl.CostEstimate(flops=flops, bytes_accessed=total, transcendentals=0),
    )(*ins)


def permutation_kernel(out):
    to = lax.broadcasted_iota(jnp.int32, out.shape, 0)
    at = lax.broadcasted_iota(jnp.int32, out.shape, 1)
    out[...] = ((to // 16 == at % 16) & (to % 16 == at // 16)).astype(F32).astype(BF16)


def half_index():
    return lax.rem(lax.axis_index("rot") + lax.axis_index("cls"), 2)


def prior_kernel(share, prior_ref, prior_term):
    turns = lax.broadcasted_iota(jnp.int32, (ANG, 256), 0)
    lane = lax.broadcasted_iota(jnp.int32, (1, 256), 1)
    priors = prior_ref[...].reshape(1, -1)
    first, second = [
        jnp.concatenate([priors[:, i * share : (i + 1) * share], lane[:, share:]], 1)
        for i in range(2)
    ]
    offset = jnp.abs(turns - jnp.where(half_index() == 0, first, second))
    distance = jnp.minimum(offset, ANG - offset).astype(F32)
    term = -distance * distance / (2.0 * SIGMA * SIGMA)
    prior_term[:, :128] = term[:, :128]
    prior_term[:, 128:] = repeat(term[:, 128:], share - 128, 128 // (share - 128))


def turned(value, lanes):
    return pltpu.roll(value, lanes % 128, 1) if lanes % 128 else value


def repeat(value, width, times):
    lane = lax.broadcasted_iota(jnp.int32, value.shape, 1)
    value = jnp.where(lane < width, value, 0.0)
    return sum(turned(value, i * width) for i in range(times))


def layout(classes, share):
    width = share - 128
    assert 0 < width < 128 and 128 % width == 0 and classes % 2 == 0
    bundle = min(128 // width, classes)
    assert classes % bundle == 0
    return width, bundle, classes // bundle


def prep_kernel(share, particles_ref, permutation_ref, prior_ref, other, own, prior_term):
    freqs, depth = particles_ref.shape[1:]
    half = half_index()
    prior_kernel(share, prior_ref, prior_term)
    permutation = permutation_ref[...]
    for out, first in ((other, (1 - half) * share), (own, half * share)):
        for p in range(0, share, 16):
            for f in range(0, freqs, 32):
                blocks = [
                    jnp.concatenate(
                        [particles_ref[first + p + j, pl.ds(f + second, 16), :] for j in range(16)],
                        0,
                    )
                    for second in (0, 16)
                ]
                turned = dot(permutation, jnp.concatenate(blocks, 1)).astype(BF16)
                for half in range(2):
                    for j in range(16):
                        pair, part = divmod(f + 16 * half + j, 2)
                        out[pair, pl.ds(p, 16), pl.ds(part * depth, depth)] = turned[
                            16 * j : 16 * j + 16, half * depth : (half + 1) * depth
                        ]


def prep(particles, permutation, prior_rot, share):
    _, freqs, depth = particles.shape
    assert share % 16 == 0 and freqs % 32 == 0
    return call(
        functools.partial(prep_kernel, share),
        [particles, permutation, prior_rot],
        [((freqs // 2, share, 2 * depth), BF16)] * 2 + [((ANG, 256), F32)],
        flops=1 << 31,
    )


def tree(values):
    values = list(values)
    while len(values) > 1:
        values = [a + b for a, b in zip(values[::2], values[1::2])]
    return values[0]


def weigh_kernel(fresh, order, count, *refs):
    sources = [refs[order.index(i)] for i in range(count)]
    doubled_ref, particles, out, energy_ref, left_ref, image = refs[count:]
    pairs, share, twice = particles.shape
    freqs, depth = 2 * pairs, twice // 2
    classes = energy_ref.shape[0]
    pitch = freqs + SPARE
    radii = depth // 2
    lane = lax.broadcasted_iota(jnp.int32, (freqs, depth), 1)
    sign = jnp.where(lane < radii, -1.0, 1.0).astype(F32)
    doubled = jnp.concatenate([doubled_ref[...]] * 2, 1)
    row = lax.broadcasted_iota(jnp.int32, (freqs, depth), 0) + lax.axis_index("rot") * freqs
    scale = jnp.where(row == 0, 1.0 / ANG, 2.0 / ANG).astype(F32) * doubled

    tails = []
    if not fresh:
        end = sources[0].shape[0] - classes * freqs
        tails = [source[pl.ds(classes * freqs, end), :].astype(F32) for source in sources]

    for k in range(classes):
        if fresh:
            plain = sources[k][0].astype(F32)
        else:
            sums = tree(
                source[pl.ds((k ^ i) * freqs, freqs), :].astype(F32)
                for i, source in enumerate(sources)
            )
            highs, lows = [
                tree(tail[base + (k ^ i) : base + (k ^ i) + 1] for i, tail in enumerate(tails))
                for base in (0, classes)
            ]
            plain = (sums / (highs + lows + shrinkage)).astype(BF16).astype(F32)
        weighted = (plain * doubled).astype(BF16).astype(F32)
        image[rows(2 * k * pitch, freqs), :] = weighted
        image[rows((2 * k + 1) * pitch, freqs), :] = sign * pltpu.roll(weighted, radii, 1)
        energy = jnp.sum(plain * plain * scale, axis=0, keepdims=True)
        energy = jnp.broadcast_to(jnp.sum(energy, axis=1, keepdims=True), (SPARE, 128))
        energy_ref[pl.ds(k, 1), :] = energy[:1]
        out[rows(2 * k * pitch + freqs, SPARE), :] = energy

    none = jnp.zeros((2 * classes, depth), BF16)

    def correlate(f):
        lefts = []
        for first, second in pick(image, f, classes):
            first, second = first.astype(BF16), second.astype(BF16)
            left = jnp.concatenate(
                [jnp.concatenate([first, none], 1), jnp.concatenate([none, second], 1)], 0
            )
            left_ref[f + len(lefts)] = left
            lefts.append(left)
        values = [times(left, particles[f + i]) for i, left in enumerate(lefts)]
        place(out, f, values, classes, pitch)

    every(pairs, correlate)


def times(left, particles):
    return lax.dot_general(left, particles, (((1,), (1,)), ((), ())), preferred_element_type=F32)


GROUP = 4


def every(pairs, body):
    for f in range(0, pairs, GROUP):
        body(f)


def put(ref, f, blocks, pitch):
    turned_blocks = jnp.swapaxes(jnp.stack(blocks, 0), 0, 1)
    for i in range(blocks[0].shape[0]):
        ref[pl.ds(i * pitch + 2 * f, 2 * GROUP), :] = turned_blocks[i]


def pick(ref, f, classes):
    pitch = ref.shape[0] // (2 * classes)
    blocks = [ref[pl.ds(i * pitch + 2 * f, 2 * GROUP), :] for i in range(2 * classes)]
    blocks = jnp.swapaxes(jnp.stack(blocks, 0), 0, 1)
    return [(blocks[2 * i], blocks[2 * i + 1]) for i in range(GROUP)]


def place(out, f, values, classes, pitch):
    width = values[0].shape[1] - 128
    each_pack = 128 // width
    spare = jnp.zeros((2 * classes, 128 - width), F32)
    parts = [
        value[part * 2 * classes : (part + 1) * 2 * classes] for value in values for part in range(2)
    ]
    put(out, f, [part[:, :128] for part in parts], pitch)
    more = [jnp.concatenate([part[:, 128:], spare], 1) for part in parts]
    more = jnp.swapaxes(jnp.stack(more, 0), 0, 1)
    for first in range(0, 2 * classes, each_pack):
        total = 0.0
        for group in range(first, min(first + each_pack, 2 * classes)):
            part, k = divmod(group, classes)
            total = total + turned(more[2 * k + part], (group - first) * width)
        at = (2 * classes + first // each_pack) * pitch + 2 * f
        out[pl.ds(at, 2 * GROUP), :] = total


def unpack(ref, unit, part, classes, share, pitch, freqs):
    width, bundle, _ = layout(classes, share)
    group = part * classes + unit * bundle
    each_pack = 128 // width
    value = ref[rows((2 * classes + group // each_pack) * pitch, freqs), :]
    return turned(value, -(group % each_pack) * width)


def corr_lines(classes, share, pitch):
    return (2 * classes + -(-2 * classes * (share - 128) // 128)) * pitch


def weigh(sources, order, inverse_noise, particles, fresh):
    pairs, share, twice = particles.shape
    classes = len(sources)
    pitch = 2 * pairs + SPARE
    return call(
        functools.partial(weigh_kernel, fresh, order, classes),
        [*[sources[i] for i in order], inverse_noise, particles],
        [
            ((corr_lines(classes, share, pitch), 128), F32),
            ((classes, 128), F32),
            ((pairs, 4 * classes, twice), BF16),
        ],
        [((2 * classes * pitch, twice // 2), F32)],
        flops=8 * classes * share * pairs * twice * 4,
    )


def correlate_kernel(left_ref, particles, energy_ref, prior_term, table, *refs):
    partial, partial_more, field = refs
    pairs, share, _ = particles.shape
    classes = left_ref.shape[1] // 4
    freqs, pitch = 2 * pairs, 2 * pairs + SPARE

    def body(f):
        values = [times(left_ref[f + i], particles[f + i]) for i in range(GROUP)]
        place(field, f, values, classes, pitch)

    every(pairs, body)

    def energy_of(k):
        return energy_ref[pl.ds(k, 1), :]

    def slab(i, carry):
        prior = jnp.concatenate([prior_term[:, :128]] * 2, 1)
        energy = jnp.concatenate([energy_of(2 * i), energy_of(2 * i + 1)], 1)
        partial[i] = invert(table, two_classes(field, i, pitch, freqs)) - 0.5 * energy + prior
        return carry

    each(classes // 2, slab, 0)
    for unit in range(partial_more.shape[0]):
        energy = beside(energy_of, unit, classes, share)
        value = several_classes(field, unit, classes, share, pitch, freqs)
        partial_more[unit] = invert(table, value) - 0.5 * energy + prior_term[:, 128:]


def two_classes(field, i, pitch, freqs):
    parts = [
        [field[rows((4 * i + 2 * j + part) * pitch, freqs), :] for j in range(2)]
        for part in range(2)
    ]
    return jnp.concatenate([jnp.concatenate(part, 1) for part in parts], 0)


def several_classes(field, unit, classes, share, pitch, freqs):
    return jnp.concatenate(
        [unpack(field, unit, part, classes, share, pitch, freqs) for part in range(2)], 0
    )


def beside(value_of, unit, classes, share):
    width, bundle, _ = layout(classes, share)
    lane = lax.broadcasted_iota(jnp.int32, (1, 128), 1)
    return sum(
        jnp.where(lane // width == j, value_of(unit * bundle + j), 0.0) for j in range(bundle)
    )


def invert(table, value):
    high, low = split(value)
    return dot(table[table_rows(0, ANG), :], jnp.concatenate([high, low, high], 0))


def correlate(left, particles, energy, prior_term, table):
    pairs, share, twice = particles.shape
    classes = left.shape[1] // 4
    pitch = 2 * pairs + SPARE
    return call(
        correlate_kernel,
        [left, particles, energy, prior_term, table],
        [((classes // 2, ANG, 256), F32), ((layout(classes, share)[2], ANG, 128), F32)],
        [((corr_lines(classes, share, pitch), 128), F32)],
        flops=2 * left.shape[1] * share * pairs * twice * 8,
    )


def table_rows(base, count):
    return pl.ds(pl.multiple_of(lax.axis_index("rot") * ANG + base, 128), count)


def score_kernel(share, partial, partial_more, other, table, *refs):
    weights, more, tops, more_tops, peaks = refs
    classes = 2 * partial.shape[0]
    width, bundle, units = layout(classes, share)
    freqs = ANG // 4
    pitch = freqs + SPARE

    def exponentials(scores):
        top = jnp.max(scores, axis=0, keepdims=True)
        value = jnp.exp(scores - top)
        return value, top, jnp.sum(value, axis=0, keepdims=True)

    def energy_of(k):
        return other[rows(2 * k * pitch + freqs, SPARE), :][:1]

    def slab(i, carry):
        energy = jnp.concatenate([energy_of(2 * i), energy_of(2 * i + 1)], 1)
        inner = invert(table, two_classes(other, i, pitch, freqs))
        weights[i], top, total = exponentials(inner + (partial[i] - 0.5 * energy))
        tops[pl.ds(i, 1), :] = top
        for j in (0, 128):
            carry = merge(carry, (top[:, j : j + 128], total[:, j : j + 128]))
        return carry

    empty = (jnp.full((1, 128), -jnp.inf, F32), jnp.zeros((1, 128), F32))
    top, total = each(classes // 2, slab, empty)
    rest = empty
    for unit in range(units):
        energy = beside(energy_of, unit, classes, share)
        inner = invert(table, several_classes(other, unit, classes, share, pitch, freqs))
        more[unit], more_top, more_total = exponentials(inner + (partial_more[unit] - 0.5 * energy))
        more_tops[pl.ds(unit, 1), :] = more_top
        for j in range(bundle):
            rest = merge(rest, (turned(more_top, -j * width), turned(more_total, -j * width)))
    line = lax.broadcasted_iota(jnp.int32, peaks.shape, 0)
    peaks[...] = jnp.where(
        line == 0,
        jnp.concatenate([top, rest[0]], 1),
        jnp.concatenate([total, rest[1]], 1),
    )


def scores(partial, partial_more, other, table, share):
    classes = 2 * partial.shape[0]
    units = layout(classes, share)[2]
    return call(
        functools.partial(score_kernel, share),
        [partial, partial_more, other, table],
        [
            ((classes // 2, ANG, 256), F32),
            ((units, ANG, 128), F32),
            ((classes // 2, 256), F32),
            ((units, 128), F32),
            ((8, 256), F32),
        ],
        flops=6 * classes * 256 * ANG * ANG,
    )


def merge(first, second):
    top = jnp.maximum(first[0], second[0])
    return top, first[1] * jnp.exp(first[0] - top) + second[1] * jnp.exp(second[0] - top)


def two_lines(ref):
    return ref[0:1, :], ref[1:2, :]


def merge_kernel(first, second, out):
    top, total = merge(two_lines(first), two_lines(second))
    line = lax.broadcasted_iota(jnp.int32, out.shape, 0)
    out[...] = jnp.where(line == 0, top, total)


def turn_kernel(share, weights, more, tops, more_tops, first, second, forward, *refs):
    rounded_ref, rounded_more, send, *last, held = refs
    classes = 2 * weights.shape[0]
    width, bundle, units = layout(classes, share)
    pairs = (held.shape[0] // (2 * classes) - SPARE) // 2
    top, total = merge(two_lines(first), two_lines(second))
    evidence = top + jnp.log(total)
    scale = 1.0 / total
    at = table_rows(0, ANG // 2)
    lane = lax.broadcasted_iota(jnp.int32, (1, 128), 1)
    line = lax.broadcasted_iota(jnp.int32, (4 * classes, 128), 0)

    def with_count(column, k, count):
        high = count.astype(BF16).astype(F32)
        return jnp.where(line == k, high, jnp.where(line == classes + k, count - high, column))

    more_counts = []
    for unit in range(units):
        factor = jnp.exp(
            more_tops[pl.ds(unit, 1), :] - repeat(top[:, 128:], width, bundle)
        ) * repeat(scale[:, 128:], width, bundle)
        value = more[unit] * jnp.where(lane < bundle * width, factor, 0.0)
        count = jnp.sum(value, axis=0, keepdims=True)
        for j in range(bundle):
            mine = jnp.where(lane // width == j, count, 0.0)
            more_counts.append(jnp.sum(mine, axis=1, keepdims=True))
        rounded = value.astype(BF16)
        rounded_more[unit] = rounded
        spectrum = dot(forward[at, :], jnp.concatenate([rounded, rounded], 0)).astype(BF16)
        step = 4 * classes
        entries = spectrum.shape[0] // step
        for i in range(entries):
            send[pairs + unit * entries + i] = spectrum[i * step : (i + 1) * step]

    tops_here = jnp.concatenate([top[:, :128]] * 2, 1)
    scale_here = jnp.concatenate([scale[:, :128]] * 2, 1)

    def body(i, column):
        value = weights[i] * (jnp.exp(tops[pl.ds(i, 1), :] - tops_here) * scale_here)
        rounded = value.astype(BF16)
        rounded_ref[i] = rounded
        spread(held, i, dot(forward[at, :], jnp.concatenate([rounded, rounded], 0)))
        count = jnp.sum(value, axis=0, keepdims=True)
        for j in range(2):
            mine = jnp.sum(count[:, j * 128 : (j + 1) * 128], axis=1, keepdims=True)
            column = with_count(column, 2 * i + j, mine)
        return column

    column = each(classes // 2, body, jnp.zeros((4 * classes, 128), F32))
    extra = jnp.zeros((4 * classes, 128), F32)
    for k, count in enumerate(more_counts):
        extra = with_count(extra, k, count)
    for ref in last:
        ref[...] = evidence[:, :share]
        high = evidence.astype(BF16).astype(F32)
        middle = (evidence - high).astype(BF16).astype(F32)
        for i, value in enumerate((high, middle, evidence - high - middle)):
            for j in range(2):
                mine = value[:, j * 128 : (j + 1) * 128]
                extra = jnp.where(line == 2 * classes + 2 * i + j, mine, extra)
    send[send.shape[0] - 2] = column.astype(BF16)
    send[send.shape[0] - 1] = extra.astype(BF16)

    def rearrange(f):
        for i, parts in enumerate(pick(held, f, classes)):
            send[f + i] = jnp.concatenate(parts, 0).astype(BF16)

    every(pairs, rearrange)


def spread(held, i, value):
    freqs = value.shape[0] // 2
    for j in range(2):
        for part in range(2):
            held[rows((4 * i + 2 * j + part) * (freqs + SPARE), freqs), :] = value[
                part * freqs : (part + 1) * freqs, j * 128 : (j + 1) * 128
            ]


def spread_more(held, unit, value, classes, share):
    width, bundle, _ = layout(classes, share)
    freqs = value.shape[0] // 2
    for j in range(bundle):
        shifted = turned(value, -j * width)
        for part in range(2):
            k = unit * bundle + j
            held[rows((2 * k + part) * (freqs + SPARE), freqs), :] = shifted[
                part * freqs : (part + 1) * freqs
            ]


def message_shape(classes, pairs, units):
    return (pairs + units * (ANG // 2) // (4 * classes) + 2, 4 * classes, 128)


def turn(weights, more, tops, more_tops, first, second, forward, freqs, share, last):
    classes = 2 * weights.shape[0]
    units = more.shape[0]
    return call(
        functools.partial(turn_kernel, share),
        [weights, more, tops, more_tops, first, second, forward],
        [
            (weights.shape, BF16),
            (more.shape, BF16),
            (message_shape(classes, freqs // 2, units), BF16),
            *([((1, share), F32)] if last else []),
        ],
        [((2 * classes * (freqs + SPARE), 128), F32)],
        flops=4 * classes * 256 * ANG * ANG,
    )


def gather_kernel(rounded_ref, rounded_more, forward, particles, image, held, held_more):
    classes = 2 * rounded_ref.shape[0]
    pairs, share, _ = particles.shape
    at = table_rows(ANG // 2, ANG // 2)

    for unit in range(rounded_more.shape[0]):
        rounded = rounded_more[unit]
        value = dot(forward[at, :], jnp.concatenate([rounded, rounded], 0))
        spread_more(held_more, unit, value, classes, share)

    def body(i, carry):
        rounded = rounded_ref[i]
        spread(held, i, dot(forward[at, :], jnp.concatenate([rounded, rounded], 0)))
        return carry

    each(classes // 2, body, 0)

    def accumulate(f):
        values = []
        for i, both in enumerate(zip(pick(held, f, classes), pick(held_more, f, classes))):
            left = [jnp.concatenate(parts, 0).astype(BF16) for parts in both]
            values.append(dot(jnp.concatenate(left, 1)[:, :share], particles[f + i]))
        take_in(image, f, values, classes)

    every(pairs, accumulate)


def gather(rounded, rounded_more, forward, particles):
    pairs, share, twice = particles.shape
    classes = 2 * rounded.shape[0]
    lines = 2 * classes * (2 * pairs + SPARE)
    return call(
        gather_kernel,
        [rounded, rounded_more, forward, particles],
        [((lines, twice // 2), F32)],
        [((lines, 128), F32)] * 2,
        flops=4 * classes * 256 * ANG * ANG,
    )[0]


def take_in(image, f, values, classes):
    lines, depth = image.shape
    blocks = [
        value[part * 2 * classes : (part + 1) * 2 * classes, part * depth : (part + 1) * depth]
        for value in values
        for part in range(2)
    ]
    put(image, f, blocks, lines // (2 * classes))


def finish_kernel(image, mine, spectrum, particles, *refs):
    *outs, held = refs
    evidence_ref = outs.pop() if len(outs) > 1 else None
    pairs, share, twice = particles.shape
    classes = spectrum.shape[1] // 4
    freqs, depth = 2 * pairs, twice // 2
    radii = depth // 2
    pitch = freqs + SPARE

    width, bundle, units = layout(classes, share)
    step = 4 * classes
    entries = ANG // 2 // step

    def received(f):
        blocks = []
        for k in range(classes):
            unit, j = divmod(k, bundle)
            for part in range(2):
                entry, first = divmod(part * freqs + 2 * f, step)
                value = spectrum[pairs + unit * entries + entry].astype(F32)
                blocks.append(turned(value[first : first + 2 * GROUP], -j * width))
        blocks = jnp.swapaxes(jnp.stack(blocks, 0), 0, 1)
        return [(blocks[2 * i], blocks[2 * i + 1]) for i in range(GROUP)]

    def body(f):
        values = []
        for i, parts in enumerate(received(f)):
            left = jnp.concatenate(parts, 0).astype(BF16)
            left = jnp.concatenate([spectrum[f + i], left], 1)[:, :share]
            values.append(dot(left, particles[f + i]))
        take_in(held, f, values, classes)

    every(pairs, body)
    end = spectrum.shape[0]
    counts = sum(ref[i].astype(F32) for ref in (mine, spectrum) for i in (end - 2, end - 1))
    if evidence_ref is not None:
        parts = spectrum[end - 1].astype(F32)[2 * classes :]
        parts = [jnp.concatenate([parts[i : i + 1], parts[i + 1 : i + 2]], 1) for i in (0, 2, 4)]
        evidence_ref[...] = (parts[0] + (parts[1] + parts[2]))[:, :share]
    counts = counts[:classes] + counts[classes : 2 * classes]
    lane = lax.broadcasted_iota(jnp.int32, (freqs, depth), 1)
    sign = jnp.where(lane < radii, -1.0, 1.0).astype(F32)
    for k in range(classes):
        plain, crossed = [
            image[rows((2 * k + part) * pitch, freqs), :]
            + held[rows((2 * k + part) * pitch, freqs), :]
            for part in range(2)
        ]
        value = plain + sign * pltpu.roll(crossed, radii, 1)
        if len(outs) == 1:
            outs[0][pl.ds(k * freqs, freqs), :] = value.astype(BF16)
        else:
            outs[k][pl.ds(0, freqs), :] = value
            outs[k][pl.ds(freqs, SPARE), :] = jnp.broadcast_to(counts[k : k + 1], (SPARE, depth))
    if len(outs) == 1:
        end = outs[0].shape[0] - classes * freqs
        high, low = split(counts)
        spare = [jnp.zeros((end - 2 * classes, depth), F32)] if end > 2 * classes else []
        tail = jnp.concatenate([high.astype(F32), low.astype(F32), *spare], 0)
        outs[0][pl.ds(classes * freqs, end), :] = tail.astype(BF16)


def finish(image, mine, spectrum, particles, last):
    pairs, _, twice = particles.shape
    classes = spectrum.shape[1] // 4
    freqs, depth = 2 * pairs, twice // 2
    if last:
        outs = [((freqs + SPARE, depth), F32)] * classes + [((1, particles.shape[1]), F32)]
    else:
        outs = [((classes * freqs + -(-2 * classes // 16) * 16, depth), BF16)]
    return call(
        finish_kernel,
        [image, mine, spectrum, particles],
        outs,
        [(image.shape, F32)],
        flops=2 * math.prod(spectrum.shape) * twice * 8,
    )


def means_kernel(*refs):
    *parts, own, other, out, evidence_ref = refs
    odd = lax.rem(lax.axis_index("cls"), 2)
    evidence_ref[...] = jnp.where(odd == 0, own[...], other[...])
    freqs = out.shape[1]
    total = tree(ref[...] for ref in parts)
    out[0] = total[:freqs, :] / (total[freqs : freqs + 1, :] + shrinkage)


def swap(value, axis, size, bit):
    if not bit:
        return value
    return lax.ppermute(value, axis, [(i, i ^ bit) for i in range(size)])


def bits(size):
    assert size > 1 and size & (size - 1) == 0
    return [1 << i for i in range(size.bit_length() - 1)]


def shards(particles, references, noise_inv, prior_rot):
    batch, freqs, depth = particles.shape
    sides = lax.axis_size("cls")
    groups = lax.axis_size("rot")
    blocks = lax.axis_size("blk")
    assert groups == 2 and 2 * groups * freqs == ANG
    share = batch // groups
    near, far, forward = tables(freqs)
    inverse_noise = noise_inv.reshape(1, depth // 2)
    assert blocks & (blocks - 1) == 0
    turns = sorted(range(1, blocks), key=lambda i: (-i.bit_length(), i))

    (permutation,) = call(permutation_kernel, [], [((256, 256), BF16)], flops=1 << 32)
    sources = {i: swap(references, "blk", blocks, i) for i in (*turns, 0)}
    other_images, own_images, prior_term = prep(particles, permutation, prior_rot, share)
    for step in range(ITERS):
        last = step == ITERS - 1
        order = [0, *(reversed(turns) if step else reversed(range(1, blocks)))]
        message, energy, left = weigh(sources, order, inverse_noise, other_images, step == 0)
        message = swap(message, "rot", groups, 1)
        partial = correlate(left, own_images, energy, prior_term, near)
        *weights, here = scores(*partial, message, far, share)
        first = here
        for bit in bits(sides):
            second = swap(first, ("cls", "rot"), sides * groups, groups * bit + (bit == 1))
            if 2 * bit < sides:
                (first,) = call(merge_kernel, [first, second], [(here.shape, F32)])
        rounded, more, send, *evidence = turn(
            *weights, first, second, forward, freqs, share, last
        )
        message = swap(send, "rot", groups, 1)
        image = gather(rounded, more, forward, own_images)
        sums = finish(image, send, message, other_images, last)
        sums, others = (sums[:blocks], sums[blocks:]) if last else (sums * blocks, [])
        sources = {i: swap(sums[i], "blk", blocks, i) for i in (*turns, 0)}
    means, evidence = call(
        means_kernel, [*[sources[i] for i in reversed(range(blocks))], *evidence, *others], [((1, freqs, depth), F32), ((1, share), F32)]
    )
    return means, evidence.reshape(share)


def solution(mesh):
    in_specs = (
        P(("grp", "blk"), "rot", None),
        P(("grp", "blk", "cls"), "rot", None),
        P(),
        P(("grp", "blk")),
    )
    out_specs = (P(("grp", "blk", "cls"), "rot", None), P(("grp", "blk", "rot")))
    return jax.shard_map(shards, mesh=mesh, in_specs=in_specs, out_specs=out_specs, check_vma=False)
```

```python
import functools
import math

import jax
import jax.numpy as jnp
import numpy as np
from jax import lax
from jax.experimental import pallas as pl
from jax.experimental.pallas import tpu as pltpu
from jax.sharding import PartitionSpec as P

ANG = 256
ITERS = 2
SIGMA = 32

shrinkage = 1.0

F32 = jnp.float32
BF16 = jnp.bfloat16
SPARE = 8

dot = functools.partial(jnp.dot, preferred_element_type=F32)


def split(x):
    high = x.astype(BF16)
    return high, (x - high.astype(F32)).astype(BF16)


def tables(half_freq):
    turn = np.arange(ANG)
    near, far, forward = [], [], []
    for group in range(2):
        sides = {}
        for which in range(2):
            freq = which * half_freq + np.arange(half_freq)
            angle = (turn[:, None] * freq[None, :] % ANG) * (2.0 * math.pi / ANG)
            scale = np.where(freq == 0, 1.0, 2.0) / ANG
            sides[which] = (
                np.concatenate([scale * np.cos(angle), -scale * np.sin(angle)], 1),
                np.concatenate([np.cos(angle), np.sin(angle)], 1).T,
            )
        near.append(sides[group][0])
        far.append(sides[1 - group][0])
        forward.append(np.concatenate([sides[1 - group][1], sides[group][1]], 0))
    result = []
    for table, kinds in ((near, (0, 0, 1)), (far, (0, 0, 1)), (forward, (0, 1))):
        table = np.concatenate(table, 0).astype(np.float32)
        high = table.astype(BF16)
        parts = [high, (table - high.astype(np.float32)).astype(BF16)]
        result.append(jnp.asarray(np.concatenate([parts[kind] for kind in kinds], 1)))
    return result


def each(count, body, init):
    if count <= 8:
        for k in range(count):
            init = body(k, init)
        return init
    return lax.fori_loop(0, count, body, init)


def rows(base, count):
    return pl.ds(pl.multiple_of(base, 8), count)


def call(kernel, ins, outs, scratch=(), flops=0, far=(), room=4 << 20):
    total = 0
    buffers = [(x.shape, x.dtype) for i, x in enumerate(ins) if i not in far]
    for shape, dtype in buffers + list(outs) + [x for x in scratch if isinstance(x, tuple)]:
        dims = [1, 1, *shape]
        lines = -(-dims[-2] // 16) * 16
        lanes = -(-dims[-1] // 128) * 128
        total += math.prod(dims[:-2]) * lines * lanes * jnp.dtype(dtype).itemsize
    kinds = [pltpu.VMEM] * len(ins)
    for i in far:
        kinds[i] = pltpu.MemorySpace.HBM
    return pl.pallas_call(
        kernel,
        out_shape=[jax.ShapeDtypeStruct(*x) for x in outs],
        in_specs=[pl.BlockSpec(memory_space=kind) for kind in kinds],
        out_specs=[pl.BlockSpec(memory_space=pltpu.VMEM)] * len(outs),
        scratch_shapes=[pltpu.VMEM(*x) if isinstance(x, tuple) else x for x in scratch],
        compiler_params=pltpu.CompilerParams(vmem_limit_bytes=min(total + room, 56 << 20)),
        cost_estimate=pl.CostEstimate(flops=flops, bytes_accessed=total, transcendentals=0),
    )(*ins)


def permutation_kernel(out):
    to = lax.broadcasted_iota(jnp.int32, out.shape, 0)
    at = lax.broadcasted_iota(jnp.int32, out.shape, 1)
    out[...] = ((to // 16 == at % 16) & (to % 16 == at // 16)).astype(F32).astype(BF16)


def half_index():
    return lax.rem(lax.axis_index("rot") + lax.axis_index("cls"), 2)


def prior_kernel(share, prior_ref, prior_term):
    turns = lax.broadcasted_iota(jnp.int32, (ANG, 256), 0)
    lane = lax.broadcasted_iota(jnp.int32, (1, 256), 1)
    priors = prior_ref[...].reshape(1, -1)
    first, second = [
        jnp.concatenate([priors[:, i * share : (i + 1) * share], lane[:, share:]], 1)
        for i in range(2)
    ]
    offset = jnp.abs(turns - jnp.where(half_index() == 0, first, second))
    distance = jnp.minimum(offset, ANG - offset).astype(F32)
    term = -distance * distance / (2.0 * SIGMA * SIGMA)
    prior_term[:, :128] = term[:, :128]
    prior_term[:, 128:] = repeat(term[:, 128:], share - 128, 128 // (share - 128))


def turned(value, lanes):
    return pltpu.roll(value, lanes % 128, 1) if lanes % 128 else value


def repeat(value, width, times):
    lane = lax.broadcasted_iota(jnp.int32, value.shape, 1)
    value = jnp.where(lane < width, value, 0.0)
    return sum(turned(value, i * width) for i in range(times))


def layout(classes, share):
    width = share - 128
    assert 0 < width < 128 and 128 % width == 0 and classes % 2 == 0
    bundle = min(128 // width, classes)
    assert classes % bundle == 0
    return width, bundle, classes // bundle


def prep_kernel(share, particles_ref, permutation_ref, prior_ref, other, own, prior_term):
    freqs, depth = particles_ref.shape[1:]
    half = half_index()
    prior_kernel(share, prior_ref, prior_term)
    permutation = permutation_ref[...]
    for out, first in ((other, (1 - half) * share), (own, half * share)):
        for p in range(0, share, 16):
            for f in range(0, freqs, 32):
                blocks = [
                    jnp.concatenate(
                        [particles_ref[first + p + j, pl.ds(f + second, 16), :] for j in range(16)],
                        0,
                    )
                    for second in (0, 16)
                ]
                turned = dot(permutation, jnp.concatenate(blocks, 1)).astype(BF16)
                for half in range(2):
                    for j in range(16):
                        pair, part = divmod(f + 16 * half + j, 2)
                        out[pair, pl.ds(p, 16), pl.ds(part * depth, depth)] = turned[
                            16 * j : 16 * j + 16, half * depth : (half + 1) * depth
                        ]


def prep(particles, permutation, prior_rot, share):
    _, freqs, depth = particles.shape
    assert share % 16 == 0 and freqs % 32 == 0
    return call(
        functools.partial(prep_kernel, share),
        [particles, permutation, prior_rot],
        [((freqs // 2, share, 2 * depth), BF16)] * 2 + [((ANG, 256), F32)],
        flops=1 << 31,
    )


def tree(values):
    values = list(values)
    while len(values) > 1:
        values = [a + b for a, b in zip(values[::2], values[1::2])]
    return values[0]


def weigh_kernel(fresh, order, count, *refs):
    sources = [refs[order.index(i)] for i in range(count)]
    doubled_ref, particles, out, energy_ref, left_ref, image = refs[count:]
    pairs, share, twice = particles.shape
    freqs, depth = 2 * pairs, twice // 2
    classes = energy_ref.shape[0]
    pitch = freqs
    radii = depth // 2
    lane = lax.broadcasted_iota(jnp.int32, (freqs, depth), 1)
    sign = jnp.where(lane < radii, -1.0, 1.0).astype(F32)
    doubled = jnp.concatenate([doubled_ref[...]] * 2, 1)
    row = lax.broadcasted_iota(jnp.int32, (freqs, depth), 0) + lax.axis_index("rot") * freqs
    scale = jnp.where(row == 0, 1.0 / ANG, 2.0 / ANG).astype(F32) * doubled

    tails = []
    if not fresh:
        end = sources[0].shape[0] - classes * freqs
        tails = [source[pl.ds(classes * freqs, end), :].astype(F32) for source in sources]

    energies = [jnp.zeros((SPARE, 128), F32)] * -(-classes // SPARE)
    for k in range(classes):
        if fresh:
            plain = sources[k][0].astype(F32)
        else:
            sums = tree(
                source[pl.ds((k ^ i) * freqs, freqs), :].astype(F32)
                for i, source in enumerate(sources)
            )
            highs, lows = [
                tree(tail[base + (k ^ i) : base + (k ^ i) + 1] for i, tail in enumerate(tails))
                for base in (0, classes)
            ]
            plain = (sums / (highs + lows + shrinkage)).astype(BF16).astype(F32)
        weighted = (plain * doubled).astype(BF16).astype(F32)
        image[rows(2 * k * pitch, freqs), :] = weighted
        image[rows((2 * k + 1) * pitch, freqs), :] = sign * pltpu.roll(weighted, radii, 1)
        energy = jnp.sum(plain * plain * scale, axis=0, keepdims=True)
        energy = jnp.broadcast_to(jnp.sum(energy, axis=1, keepdims=True), (SPARE, 128))
        line = lax.broadcasted_iota(jnp.int32, (SPARE, 128), 0)
        energies[k // SPARE] = jnp.where(line == k % SPARE, energy, energies[k // SPARE])
        energy_ref[pl.ds(k, 1), :] = energy[:1]

    for i, energy in enumerate(energies):
        out[pl.ds(out.shape[0] - (len(energies) - i) * SPARE, SPARE), :] = energy
    none = jnp.zeros((2 * classes, depth), BF16)

    def correlate(f):
        lefts = []
        for first, second in pick(image, f, classes):
            first, second = first.astype(BF16), second.astype(BF16)
            left = jnp.concatenate(
                [jnp.concatenate([first, none], 1), jnp.concatenate([none, second], 1)], 0
            )
            left_ref[f + len(lefts)] = left
            lefts.append(left)
        values = [times(left, particles[f + i]) for i, left in enumerate(lefts)]
        place(out, f, values, classes, pitch)

    every(pairs, correlate)


def times(left, particles):
    return lax.dot_general(left, particles, (((1,), (1,)), ((), ())), preferred_element_type=F32)


GROUP = 4


def every(pairs, body):
    for f in range(0, pairs, GROUP):
        body(f)


def put(ref, f, blocks, pitch):
    turned_blocks = jnp.swapaxes(jnp.stack(blocks, 0), 0, 1)
    for i in range(blocks[0].shape[0]):
        ref[pl.ds(i * pitch + 2 * f, 2 * GROUP), :] = turned_blocks[i]


def pick(ref, f, classes):
    pitch = ref.shape[0] // (2 * classes)
    blocks = [ref[pl.ds(i * pitch + 2 * f, 2 * GROUP), :] for i in range(2 * classes)]
    blocks = jnp.swapaxes(jnp.stack(blocks, 0), 0, 1)
    return [(blocks[2 * i], blocks[2 * i + 1]) for i in range(GROUP)]


def place(out, f, values, classes, pitch):
    width = values[0].shape[1] - 128
    each_pack = 128 // width
    spare = jnp.zeros((2 * classes, 128 - width), F32)
    parts = [
        value[part * 2 * classes : (part + 1) * 2 * classes] for value in values for part in range(2)
    ]
    put(out, f, [part[:, :128] for part in parts], pitch)
    more = [jnp.concatenate([part[:, 128:], spare], 1) for part in parts]
    more = jnp.swapaxes(jnp.stack(more, 0), 0, 1)
    for first in range(0, 2 * classes, each_pack):
        total = 0.0
        for group in range(first, min(first + each_pack, 2 * classes)):
            part, k = divmod(group, classes)
            total = total + turned(more[2 * k + part], (group - first) * width)
        at = (2 * classes + first // each_pack) * pitch + 2 * f
        out[pl.ds(at, 2 * GROUP), :] = total


def unpack(ref, unit, part, classes, share, pitch, freqs):
    width, bundle, _ = layout(classes, share)
    group = part * classes + unit * bundle
    each_pack = 128 // width
    value = ref[rows((2 * classes + group // each_pack) * pitch, freqs), :]
    return turned(value, -(group % each_pack) * width)


def corr_lines(classes, share, pitch):
    packs = -(-2 * classes * (share - 128) // 128)
    return (2 * classes + packs) * pitch + -(-classes // SPARE) * SPARE


def weigh(sources, order, inverse_noise, particles, fresh):
    pairs, share, twice = particles.shape
    classes = len(sources)
    pitch = 2 * pairs
    return call(
        functools.partial(weigh_kernel, fresh, order, classes),
        [*[sources[i] for i in order], inverse_noise, particles],
        [
            ((corr_lines(classes, share, pitch), 128), F32),
            ((classes, 128), F32),
            ((pairs, 4 * classes, twice), BF16),
        ],
        [((2 * classes * pitch, twice // 2), F32)],
        flops=8 * classes * share * pairs * twice * 4,
    )


def correlate_kernel(left_ref, particles, energy_ref, prior_term, table, *refs):
    partial, partial_more, field = refs
    pairs, share, _ = particles.shape
    classes = left_ref.shape[1] // 4
    freqs = pitch = 2 * pairs

    def body(f):
        values = [times(left_ref[f + i], particles[f + i]) for i in range(GROUP)]
        place(field, f, values, classes, pitch)

    every(pairs, body)

    def energy_of(k):
        return energy_ref[pl.ds(k, 1), :]

    def slab(i, carry):
        prior = jnp.concatenate([prior_term[:, :128]] * 2, 1)
        energy = jnp.concatenate([energy_of(2 * i), energy_of(2 * i + 1)], 1)
        partial[i] = invert(table, two_classes(field, i, pitch, freqs)) - 0.5 * energy + prior
        return carry

    each(classes // 2, slab, 0)
    for unit in range(partial_more.shape[0]):
        energy = beside(energy_of, unit, classes, share)
        value = several_classes(field, unit, classes, share, pitch, freqs)
        partial_more[unit] = invert(table, value) - 0.5 * energy + prior_term[:, 128:]


def two_classes(field, i, pitch, freqs):
    parts = [
        [field[rows((4 * i + 2 * j + part) * pitch, freqs), :] for j in range(2)]
        for part in range(2)
    ]
    return jnp.concatenate([jnp.concatenate(part, 1) for part in parts], 0)


def several_classes(field, unit, classes, share, pitch, freqs):
    return jnp.concatenate(
        [unpack(field, unit, part, classes, share, pitch, freqs) for part in range(2)], 0
    )


def beside(value_of, unit, classes, share):
    width, bundle, _ = layout(classes, share)
    lane = lax.broadcasted_iota(jnp.int32, (1, 128), 1)
    return sum(
        jnp.where(lane // width == j, value_of(unit * bundle + j), 0.0) for j in range(bundle)
    )


def invert(table, value):
    high, low = split(value)
    return dot(table[table_rows(0, ANG), :], jnp.concatenate([high, low, high], 0))


def correlate(left, particles, energy, prior_term, table):
    pairs, share, twice = particles.shape
    classes = left.shape[1] // 4
    pitch = 2 * pairs
    return call(
        correlate_kernel,
        [left, particles, energy, prior_term, table],
        [((classes // 2, ANG, 256), F32), ((layout(classes, share)[2], ANG, 128), F32)],
        [((corr_lines(classes, share, pitch), 128), F32)],
        flops=2 * left.shape[1] * share * pairs * twice * 8,
    )


def table_rows(base, count):
    return pl.ds(pl.multiple_of(lax.axis_index("rot") * ANG + base, 128), count)


def score_kernel(share, partial, partial_more, other, table, *refs):
    weights, more, tops, more_tops, peaks = refs
    classes = 2 * partial.shape[0]
    width, bundle, units = layout(classes, share)
    freqs = ANG // 4
    pitch = freqs

    def exponentials(scores):
        top = jnp.max(scores, axis=0, keepdims=True)
        value = jnp.exp(scores - top)
        return value, top, jnp.sum(value, axis=0, keepdims=True)

    def energy_of(k):
        return other[pl.ds(other.shape[0] - -(-classes // SPARE) * SPARE + k, 1), :]

    def slab(i, carry):
        energy = jnp.concatenate([energy_of(2 * i), energy_of(2 * i + 1)], 1)
        inner = invert(table, two_classes(other, i, pitch, freqs))
        weights[i], top, total = exponentials(inner + (partial[i] - 0.5 * energy))
        tops[pl.ds(i, 1), :] = top
        for j in (0, 128):
            carry = merge(carry, (top[:, j : j + 128], total[:, j : j + 128]))
        return carry

    empty = (jnp.full((1, 128), -jnp.inf, F32), jnp.zeros((1, 128), F32))
    top, total = each(classes // 2, slab, empty)
    rest = empty
    for unit in range(units):
        energy = beside(energy_of, unit, classes, share)
        inner = invert(table, several_classes(other, unit, classes, share, pitch, freqs))
        more[unit], more_top, more_total = exponentials(inner + (partial_more[unit] - 0.5 * energy))
        more_tops[pl.ds(unit, 1), :] = more_top
        for j in range(bundle):
            rest = merge(rest, (turned(more_top, -j * width), turned(more_total, -j * width)))
    line = lax.broadcasted_iota(jnp.int32, peaks.shape, 0)
    peaks[...] = jnp.where(
        line == 0,
        jnp.concatenate([top, rest[0]], 1),
        jnp.concatenate([total, rest[1]], 1),
    )


def scores(partial, partial_more, other, table, share):
    classes = 2 * partial.shape[0]
    units = layout(classes, share)[2]
    return call(
        functools.partial(score_kernel, share),
        [partial, partial_more, other, table],
        [
            ((classes // 2, ANG, 256), F32),
            ((units, ANG, 128), F32),
            ((classes // 2, 256), F32),
            ((units, 128), F32),
            ((8, 256), F32),
        ],
        flops=6 * classes * 256 * ANG * ANG,
    )


def merge(first, second):
    top = jnp.maximum(first[0], second[0])
    return top, first[1] * jnp.exp(first[0] - top) + second[1] * jnp.exp(second[0] - top)


def two_lines(ref):
    return ref[0:1, :], ref[1:2, :]


def merge_kernel(first, second, out):
    top, total = merge(two_lines(first), two_lines(second))
    line = lax.broadcasted_iota(jnp.int32, out.shape, 0)
    out[...] = jnp.where(line == 0, top, total)


def turn_kernel(share, weights, more, tops, more_tops, first, second, forward, *refs):
    rounded_ref, rounded_more, send, *last, held = refs
    classes = 2 * weights.shape[0]
    width, bundle, units = layout(classes, share)
    pairs = held.shape[0] // (2 * classes) // 2
    top, total = merge(two_lines(first), two_lines(second))
    evidence = top + jnp.log(total)
    scale = 1.0 / total
    at = table_rows(0, ANG // 2)
    lane = lax.broadcasted_iota(jnp.int32, (1, 128), 1)
    line = lax.broadcasted_iota(jnp.int32, (4 * classes, 128), 0)

    def with_count(column, k, count):
        high = count.astype(BF16).astype(F32)
        return jnp.where(line == k, high, jnp.where(line == classes + k, count - high, column))

    more_counts = []
    for unit in range(units):
        factor = jnp.exp(
            more_tops[pl.ds(unit, 1), :] - repeat(top[:, 128:], width, bundle)
        ) * repeat(scale[:, 128:], width, bundle)
        value = more[unit] * jnp.where(lane < bundle * width, factor, 0.0)
        count = jnp.sum(value, axis=0, keepdims=True)
        for j in range(bundle):
            mine = jnp.where(lane // width == j, count, 0.0)
            more_counts.append(jnp.sum(mine, axis=1, keepdims=True))
        rounded = value.astype(BF16)
        rounded_more[unit] = rounded
        spectrum = dot(forward[at, :], jnp.concatenate([rounded, rounded], 0)).astype(BF16)
        step = 4 * classes
        entries = spectrum.shape[0] // step
        for i in range(entries):
            send[pairs + unit * entries + i] = spectrum[i * step : (i + 1) * step]

    tops_here = jnp.concatenate([top[:, :128]] * 2, 1)
    scale_here = jnp.concatenate([scale[:, :128]] * 2, 1)

    def body(i, column):
        value = weights[i] * (jnp.exp(tops[pl.ds(i, 1), :] - tops_here) * scale_here)
        rounded = value.astype(BF16)
        rounded_ref[i] = rounded
        spread(held, i, dot(forward[at, :], jnp.concatenate([rounded, rounded], 0)))
        count = jnp.sum(value, axis=0, keepdims=True)
        for j in range(2):
            mine = jnp.sum(count[:, j * 128 : (j + 1) * 128], axis=1, keepdims=True)
            column = with_count(column, 2 * i + j, mine)
        return column

    column = each(classes // 2, body, jnp.zeros((4 * classes, 128), F32))
    extra = jnp.zeros((4 * classes, 128), F32)
    for k, count in enumerate(more_counts):
        extra = with_count(extra, k, count)
    for ref in last:
        ref[...] = evidence[:, :share]
        high = evidence.astype(BF16).astype(F32)
        middle = (evidence - high).astype(BF16).astype(F32)
        for i, value in enumerate((high, middle, evidence - high - middle)):
            for j in range(2):
                mine = value[:, j * 128 : (j + 1) * 128]
                extra = jnp.where(line == 2 * classes + 2 * i + j, mine, extra)
    send[send.shape[0] - 2] = column.astype(BF16)
    send[send.shape[0] - 1] = extra.astype(BF16)

    def rearrange(f):
        for i, parts in enumerate(pick(held, f, classes)):
            send[f + i] = jnp.concatenate(parts, 0).astype(BF16)

    every(pairs, rearrange)


def spread(held, i, value):
    freqs = value.shape[0] // 2
    for j in range(2):
        for part in range(2):
            held[rows((4 * i + 2 * j + part) * freqs, freqs), :] = value[
                part * freqs : (part + 1) * freqs, j * 128 : (j + 1) * 128
            ]


def spread_more(held, unit, value, classes, share):
    width, bundle, _ = layout(classes, share)
    freqs = value.shape[0] // 2
    for j in range(bundle):
        shifted = turned(value, -j * width)
        for part in range(2):
            k = unit * bundle + j
            held[rows((2 * k + part) * freqs, freqs), :] = shifted[
                part * freqs : (part + 1) * freqs
            ]


def message_shape(classes, pairs, units):
    return (pairs + units * (ANG // 2) // (4 * classes) + 2, 4 * classes, 128)


def turn(weights, more, tops, more_tops, first, second, forward, freqs, share, last):
    classes = 2 * weights.shape[0]
    units = more.shape[0]
    return call(
        functools.partial(turn_kernel, share),
        [weights, more, tops, more_tops, first, second, forward],
        [
            (weights.shape, BF16),
            (more.shape, BF16),
            (message_shape(classes, freqs // 2, units), BF16),
            *([((1, share), F32)] if last else []),
        ],
        [((2 * classes * freqs, 128), F32)],
        flops=4 * classes * 256 * ANG * ANG,
    )


def gather_kernel(rounded_ref, rounded_more, forward, particles, image, held, held_more):
    classes = 2 * rounded_ref.shape[0]
    pairs, share, _ = particles.shape
    at = table_rows(ANG // 2, ANG // 2)

    for unit in range(rounded_more.shape[0]):
        rounded = rounded_more[unit]
        value = dot(forward[at, :], jnp.concatenate([rounded, rounded], 0))
        spread_more(held_more, unit, value, classes, share)

    def body(i, carry):
        rounded = rounded_ref[i]
        spread(held, i, dot(forward[at, :], jnp.concatenate([rounded, rounded], 0)))
        return carry

    each(classes // 2, body, 0)

    def accumulate(f):
        values = []
        for i, both in enumerate(zip(pick(held, f, classes), pick(held_more, f, classes))):
            left = [jnp.concatenate(parts, 0).astype(BF16) for parts in both]
            values.append(dot(jnp.concatenate(left, 1)[:, :share], particles[f + i]))
        take_in(image, f, values, classes)

    every(pairs, accumulate)


def gather(rounded, rounded_more, forward, particles):
    pairs, share, twice = particles.shape
    classes = 2 * rounded.shape[0]
    lines = 2 * classes * 2 * pairs
    return call(
        gather_kernel,
        [rounded, rounded_more, forward, particles],
        [((lines, twice // 2), F32)],
        [((lines, 128), F32)] * 2,
        flops=4 * classes * 256 * ANG * ANG,
    )[0]


def take_in(image, f, values, classes):
    lines, depth = image.shape
    blocks = [
        value[part * 2 * classes : (part + 1) * 2 * classes, part * depth : (part + 1) * depth]
        for value in values
        for part in range(2)
    ]
    put(image, f, blocks, lines // (2 * classes))


def finish_kernel(image, mine, spectrum, particles, *refs):
    *outs, held = refs
    evidence_ref = outs.pop() if len(outs) > 1 else None
    pairs, share, twice = particles.shape
    classes = spectrum.shape[1] // 4
    freqs, depth = 2 * pairs, twice // 2
    radii = depth // 2
    pitch = freqs

    width, bundle, units = layout(classes, share)
    step = 4 * classes
    entries = ANG // 2 // step

    def received(f):
        blocks = []
        for k in range(classes):
            unit, j = divmod(k, bundle)
            for part in range(2):
                entry, first = divmod(part * freqs + 2 * f, step)
                value = spectrum[pairs + unit * entries + entry].astype(F32)
                blocks.append(turned(value[first : first + 2 * GROUP], -j * width))
        blocks = jnp.swapaxes(jnp.stack(blocks, 0), 0, 1)
        return [(blocks[2 * i], blocks[2 * i + 1]) for i in range(GROUP)]

    def body(f):
        values = []
        for i, parts in enumerate(received(f)):
            left = jnp.concatenate(parts, 0).astype(BF16)
            left = jnp.concatenate([spectrum[f + i], left], 1)[:, :share]
            values.append(dot(left, particles[f + i]))
        take_in(held, f, values, classes)

    every(pairs, body)
    end = spectrum.shape[0]
    counts = sum(ref[i].astype(F32) for ref in (mine, spectrum) for i in (end - 2, end - 1))
    if evidence_ref is not None:
        parts = spectrum[end - 1].astype(F32)[2 * classes :]
        parts = [jnp.concatenate([parts[i : i + 1], parts[i + 1 : i + 2]], 1) for i in (0, 2, 4)]
        evidence_ref[...] = (parts[0] + (parts[1] + parts[2]))[:, :share]
    counts = counts[:classes] + counts[classes : 2 * classes]
    lane = lax.broadcasted_iota(jnp.int32, (freqs, depth), 1)
    sign = jnp.where(lane < radii, -1.0, 1.0).astype(F32)
    for k in range(classes):
        plain, crossed = [
            image[rows((2 * k + part) * pitch, freqs), :]
            + held[rows((2 * k + part) * pitch, freqs), :]
            for part in range(2)
        ]
        value = plain + sign * pltpu.roll(crossed, radii, 1)
        if len(outs) == 1:
            outs[0][pl.ds(k * freqs, freqs), :] = value.astype(BF16)
        else:
            outs[k][pl.ds(0, freqs), :] = value
            outs[k][pl.ds(freqs, SPARE), :] = jnp.broadcast_to(counts[k : k + 1], (SPARE, depth))
    if len(outs) == 1:
        end = outs[0].shape[0] - classes * freqs
        high, low = split(counts)
        spare = [jnp.zeros((end - 2 * classes, depth), F32)] if end > 2 * classes else []
        tail = jnp.concatenate([high.astype(F32), low.astype(F32), *spare], 0)
        outs[0][pl.ds(classes * freqs, end), :] = tail.astype(BF16)


def finish(image, mine, spectrum, particles, last):
    pairs, _, twice = particles.shape
    classes = spectrum.shape[1] // 4
    freqs, depth = 2 * pairs, twice // 2
    if last:
        outs = [((freqs + SPARE, depth), F32)] * classes + [((1, particles.shape[1]), F32)]
    else:
        outs = [((classes * freqs + -(-2 * classes // 16) * 16, depth), BF16)]
    return call(
        finish_kernel,
        [image, mine, spectrum, particles],
        outs,
        [(image.shape, F32)],
        flops=2 * math.prod(spectrum.shape) * twice * 8,
    )


def means_kernel(*refs):
    *parts, own, other, out, evidence_ref = refs
    odd = lax.rem(lax.axis_index("cls"), 2)
    evidence_ref[...] = jnp.where(odd == 0, own[...], other[...])
    freqs = out.shape[1]
    total = tree(ref[...] for ref in parts)
    out[0] = total[:freqs, :] / (total[freqs : freqs + 1, :] + shrinkage)


def swap(value, axis, size, bit):
    if not bit:
        return value
    return lax.ppermute(value, axis, [(i, i ^ bit) for i in range(size)])


def bits(size):
    assert size > 1 and size & (size - 1) == 0
    return [1 << i for i in range(size.bit_length() - 1)]


def shards(particles, references, noise_inv, prior_rot):
    batch, freqs, depth = particles.shape
    sides = lax.axis_size("cls")
    groups = lax.axis_size("rot")
    blocks = lax.axis_size("blk")
    assert groups == 2 and 2 * groups * freqs == ANG
    share = batch // groups
    near, far, forward = tables(freqs)
    inverse_noise = noise_inv.reshape(1, depth // 2)
    assert blocks & (blocks - 1) == 0
    turns = sorted(range(1, blocks), key=lambda i: (-i.bit_length(), i))

    (permutation,) = call(permutation_kernel, [], [((256, 256), BF16)], flops=1 << 32)
    sources = {i: swap(references, "blk", blocks, i) for i in (*turns, 0)}
    other_images, own_images, prior_term = prep(particles, permutation, prior_rot, share)
    for step in range(ITERS):
        last = step == ITERS - 1
        order = [0, *(reversed(turns) if step else reversed(range(1, blocks)))]
        message, energy, left = weigh(sources, order, inverse_noise, other_images, step == 0)
        message = swap(message, "rot", groups, 1)
        partial = correlate(left, own_images, energy, prior_term, near)
        *weights, here = scores(*partial, message, far, share)
        first = here
        for bit in bits(sides):
            second = swap(first, ("cls", "rot"), sides * groups, groups * bit + (bit == 1))
            if 2 * bit < sides:
                (first,) = call(merge_kernel, [first, second], [(here.shape, F32)])
        rounded, more, send, *evidence = turn(
            *weights, first, second, forward, freqs, share, last
        )
        message = swap(send, "rot", groups, 1)
        image = gather(rounded, more, forward, own_images)
        sums = finish(image, send, message, other_images, last)
        sums, others = (sums[:blocks], sums[blocks:]) if last else (sums * blocks, [])
        sources = {i: swap(sums[i], "blk", blocks, i) for i in (*turns, 0)}
    means, evidence = call(
        means_kernel, [*[sources[i] for i in reversed(range(blocks))], *evidence, *others], [((1, freqs, depth), F32), ((1, share), F32)]
    )
    return means, evidence.reshape(share)


def solution(mesh):
    in_specs = (
        P(("grp", "blk"), "rot", None),
        P(("grp", "blk", "cls"), "rot", None),
        P(),
        P(("grp", "blk")),
    )
    out_specs = (P(("grp", "blk", "cls"), "rot", None), P(("grp", "blk", "rot")))
    return jax.shard_map(shards, mesh=mesh, in_specs=in_specs, out_specs=out_specs, check_vma=False)
```

```python
import functools
import math

import jax
import jax.numpy as jnp
import numpy as np
from jax import lax
from jax.experimental import pallas as pl
from jax.experimental.pallas import tpu as pltpu
from jax.sharding import PartitionSpec as P

ANG = 256
ITERS = 2
SIGMA = 32

shrinkage = 1.0

F32 = jnp.float32
BF16 = jnp.bfloat16
SPARE = 8

dot = functools.partial(jnp.dot, preferred_element_type=F32)


def split(x):
    high = x.astype(BF16)
    return high, (x - high.astype(F32)).astype(BF16)


def tables(half_freq):
    turn = np.arange(ANG)
    near, far, forward = [], [], []
    for group in range(2):
        sides = {}
        for which in range(2):
            freq = which * half_freq + np.arange(half_freq)
            angle = (turn[:, None] * freq[None, :] % ANG) * (2.0 * math.pi / ANG)
            scale = np.where(freq == 0, 1.0, 2.0) / ANG
            sides[which] = (
                np.concatenate([scale * np.cos(angle), -scale * np.sin(angle)], 1),
                np.concatenate([np.cos(angle), np.sin(angle)], 1).T,
            )
        near.append(sides[group][0])
        far.append(sides[1 - group][0])
        forward.append(np.concatenate([sides[1 - group][1], sides[group][1]], 0))
    result = []
    for table, kinds in ((near, (0, 0, 1)), (far, (0, 0, 1)), (forward, (0, 1))):
        table = np.concatenate(table, 0).astype(np.float32)
        high = table.astype(BF16)
        parts = [high, (table - high.astype(np.float32)).astype(BF16)]
        result.append(jnp.asarray(np.concatenate([parts[kind] for kind in kinds], 1)))
    return result


def each(count, body, init):
    if count <= 8:
        for k in range(count):
            init = body(k, init)
        return init
    return lax.fori_loop(0, count, body, init)


def rows(base, count):
    return pl.ds(pl.multiple_of(base, 8), count)


def call(kernel, ins, outs, scratch=(), flops=0, far=(), room=4 << 20):
    total = 0
    buffers = [(x.shape, x.dtype) for i, x in enumerate(ins) if i not in far]
    for shape, dtype in buffers + list(outs) + [x for x in scratch if isinstance(x, tuple)]:
        dims = [1, 1, *shape]
        lines = -(-dims[-2] // 16) * 16
        lanes = -(-dims[-1] // 128) * 128
        total += math.prod(dims[:-2]) * lines * lanes * jnp.dtype(dtype).itemsize
    kinds = [pltpu.VMEM] * len(ins)
    for i in far:
        kinds[i] = pltpu.MemorySpace.HBM
    return pl.pallas_call(
        kernel,
        out_shape=[jax.ShapeDtypeStruct(*x) for x in outs],
        in_specs=[pl.BlockSpec(memory_space=kind) for kind in kinds],
        out_specs=[pl.BlockSpec(memory_space=pltpu.VMEM)] * len(outs),
        scratch_shapes=[pltpu.VMEM(*x) if isinstance(x, tuple) else x for x in scratch],
        compiler_params=pltpu.CompilerParams(vmem_limit_bytes=min(total + room, 56 << 20)),
        cost_estimate=pl.CostEstimate(flops=flops, bytes_accessed=total, transcendentals=0),
    )(*ins)


def permutation_kernel(out):
    to = lax.broadcasted_iota(jnp.int32, out.shape, 0)
    at = lax.broadcasted_iota(jnp.int32, out.shape, 1)
    out[...] = ((to // 16 == at % 16) & (to % 16 == at // 16)).astype(F32).astype(BF16)


def half_index():
    return lax.rem(lax.axis_index("rot") + lax.axis_index("cls"), 2)


def prior_kernel(share, prior_ref, prior_term):
    turns = lax.broadcasted_iota(jnp.int32, (ANG, 256), 0)
    lane = lax.broadcasted_iota(jnp.int32, (1, 256), 1)
    priors = prior_ref[...].reshape(1, -1)
    first, second = [
        jnp.concatenate([priors[:, i * share : (i + 1) * share], lane[:, share:]], 1)
        for i in range(2)
    ]
    offset = jnp.abs(turns - jnp.where(half_index() == 0, first, second))
    distance = jnp.minimum(offset, ANG - offset).astype(F32)
    term = -distance * distance / (2.0 * SIGMA * SIGMA)
    prior_term[:, :128] = term[:, :128]
    prior_term[:, 128:] = repeat(term[:, 128:], share - 128, 128 // (share - 128))


def turned(value, lanes):
    return pltpu.roll(value, lanes % 128, 1) if lanes % 128 else value


def repeat(value, width, times):
    lane = lax.broadcasted_iota(jnp.int32, value.shape, 1)
    value = jnp.where(lane < width, value, 0.0)
    return sum(turned(value, i * width) for i in range(times))


def layout(classes, share):
    width = share - 128
    assert 0 < width < 128 and 128 % width == 0 and classes % 2 == 0
    bundle = min(128 // width, classes)
    assert classes % bundle == 0
    return width, bundle, classes // bundle


def prep_kernel(share, particles_ref, permutation_ref, prior_ref, other, own, prior_term):
    freqs, depth = particles_ref.shape[1:]
    half = half_index()
    prior_kernel(share, prior_ref, prior_term)
    permutation = permutation_ref[...]
    for out, first in ((other, (1 - half) * share), (own, half * share)):
        for p in range(0, share, 16):
            for f in range(0, freqs, 32):
                blocks = [
                    jnp.concatenate(
                        [particles_ref[first + p + j, pl.ds(f + second, 16), :] for j in range(16)],
                        0,
                    )
                    for second in (0, 16)
                ]
                turned = dot(permutation, jnp.concatenate(blocks, 1)).astype(BF16)
                for half in range(2):
                    for j in range(16):
                        pair, part = divmod(f + 16 * half + j, 2)
                        out[pair, pl.ds(p, 16), pl.ds(part * depth, depth)] = turned[
                            16 * j : 16 * j + 16, half * depth : (half + 1) * depth
                        ]


def prep(particles, permutation, prior_rot, share):
    _, freqs, depth = particles.shape
    assert share % 16 == 0 and freqs % 32 == 0
    return call(
        functools.partial(prep_kernel, share),
        [particles, permutation, prior_rot],
        [((freqs // 2, share, 2 * depth), BF16)] * 2 + [((ANG, 256), F32)],
        flops=1 << 31,
    )


def tree(values):
    values = list(values)
    while len(values) > 1:
        values = [a + b for a, b in zip(values[::2], values[1::2])]
    return values[0]


def weigh_kernel(fresh, order, count, *refs):
    sources = [refs[order.index(i)] for i in range(count)]
    doubled_ref, particles, out, energy_ref, left_ref, image = refs[count:]
    pairs, share, twice = particles.shape
    freqs, depth = 2 * pairs, twice // 2
    classes = energy_ref.shape[0]
    pitch = freqs
    radii = depth // 2
    lane = lax.broadcasted_iota(jnp.int32, (freqs, depth), 1)
    sign = jnp.where(lane < radii, -1.0, 1.0).astype(F32)
    doubled = jnp.concatenate([doubled_ref[...]] * 2, 1)
    row = lax.broadcasted_iota(jnp.int32, (freqs, depth), 0) + lax.axis_index("rot") * freqs
    scale = jnp.where(row == 0, 1.0 / ANG, 2.0 / ANG).astype(F32) * doubled

    tails = []
    if not fresh:
        end = sources[0].shape[0] - classes * freqs
        tails = [source[pl.ds(classes * freqs, end), :].astype(F32) for source in sources]

    energies = [jnp.zeros((SPARE, 128), F32)] * -(-classes // SPARE)
    for k in range(classes):
        if fresh:
            plain = sources[k][0].astype(F32)
        else:
            sums = tree(
                source[pl.ds((k ^ i) * freqs, freqs), :].astype(F32)
                for i, source in enumerate(sources)
            )
            highs, lows = [
                tree(tail[base + (k ^ i) : base + (k ^ i) + 1] for i, tail in enumerate(tails))
                for base in (0, classes)
            ]
            plain = (sums * (1.0 / (highs + lows + shrinkage))).astype(BF16).astype(F32)
        weighted = (plain * doubled).astype(BF16).astype(F32)
        image[rows(2 * k * pitch, freqs), :] = weighted
        image[rows((2 * k + 1) * pitch, freqs), :] = sign * pltpu.roll(weighted, radii, 1)
        energy = jnp.sum(plain * plain * scale, axis=0, keepdims=True)
        energy = jnp.broadcast_to(jnp.sum(energy, axis=1, keepdims=True), (SPARE, 128))
        line = lax.broadcasted_iota(jnp.int32, (SPARE, 128), 0)
        energies[k // SPARE] = jnp.where(line == k % SPARE, energy, energies[k // SPARE])
        energy_ref[pl.ds(k, 1), :] = energy[:1]

    for i, energy in enumerate(energies):
        out[pl.ds(out.shape[0] - (len(energies) - i) * SPARE, SPARE), :] = energy
    none = jnp.zeros((2 * classes, depth), BF16)

    def correlate(f):
        lefts = []
        for first, second in pick(image, f, classes):
            first, second = first.astype(BF16), second.astype(BF16)
            left = jnp.concatenate(
                [jnp.concatenate([first, none], 1), jnp.concatenate([none, second], 1)], 0
            )
            left_ref[f + len(lefts)] = left
            lefts.append(left)
        values = [times(left, particles[f + i]) for i, left in enumerate(lefts)]
        place(out, f, values, classes, pitch)

    every(pairs, correlate)


def times(left, particles):
    return lax.dot_general(left, particles, (((1,), (1,)), ((), ())), preferred_element_type=F32)


GROUP = 4


def every(pairs, body):
    for f in range(0, pairs, GROUP):
        body(f)


def put(ref, f, blocks, pitch):
    turned_blocks = jnp.swapaxes(jnp.stack(blocks, 0), 0, 1)
    for i in range(blocks[0].shape[0]):
        ref[pl.ds(i * pitch + 2 * f, 2 * GROUP), :] = turned_blocks[i]


def pick(ref, f, classes):
    pitch = ref.shape[0] // (2 * classes)
    blocks = [ref[pl.ds(i * pitch + 2 * f, 2 * GROUP), :] for i in range(2 * classes)]
    blocks = jnp.swapaxes(jnp.stack(blocks, 0), 0, 1)
    return [(blocks[2 * i], blocks[2 * i + 1]) for i in range(GROUP)]


def place(out, f, values, classes, pitch):
    width = values[0].shape[1] - 128
    each_pack = 128 // width
    spare = jnp.zeros((2 * classes, 128 - width), F32)
    parts = [
        value[part * 2 * classes : (part + 1) * 2 * classes] for value in values for part in range(2)
    ]
    put(out, f, [part[:, :128] for part in parts], pitch)
    more = [jnp.concatenate([part[:, 128:], spare], 1) for part in parts]
    more = jnp.swapaxes(jnp.stack(more, 0), 0, 1)
    for first in range(0, 2 * classes, each_pack):
        total = 0.0
        for group in range(first, min(first + each_pack, 2 * classes)):
            part, k = divmod(group, classes)
            total = total + turned(more[2 * k + part], (group - first) * width)
        at = (2 * classes + first // each_pack) * pitch + 2 * f
        out[pl.ds(at, 2 * GROUP), :] = total


def unpack(ref, unit, part, classes, share, pitch, freqs):
    width, bundle, _ = layout(classes, share)
    group = part * classes + unit * bundle
    each_pack = 128 // width
    value = ref[rows((2 * classes + group // each_pack) * pitch, freqs), :]
    return turned(value, -(group % each_pack) * width)


def corr_lines(classes, share, pitch):
    packs = -(-2 * classes * (share - 128) // 128)
    return (2 * classes + packs) * pitch + -(-classes // SPARE) * SPARE


def weigh(sources, order, inverse_noise, particles, fresh):
    pairs, share, twice = particles.shape
    classes = len(sources)
    pitch = 2 * pairs
    return call(
        functools.partial(weigh_kernel, fresh, order, classes),
        [*[sources[i] for i in order], inverse_noise, particles],
        [
            ((corr_lines(classes, share, pitch), 128), F32),
            ((classes, 128), F32),
            ((pairs, 4 * classes, twice), BF16),
        ],
        [((2 * classes * pitch, twice // 2), F32)],
        flops=8 * classes * share * pairs * twice * 4,
    )


def correlate_kernel(left_ref, particles, energy_ref, prior_term, table, *refs):
    partial, partial_more, field = refs
    pairs, share, _ = particles.shape
    classes = left_ref.shape[1] // 4
    freqs = pitch = 2 * pairs

    def body(f):
        values = [times(left_ref[f + i], particles[f + i]) for i in range(GROUP)]
        place(field, f, values, classes, pitch)

    every(pairs, body)

    def energy_of(k):
        return energy_ref[pl.ds(k, 1), :]

    def slab(i, carry):
        prior = jnp.concatenate([prior_term[:, :128]] * 2, 1)
        energy = jnp.concatenate([energy_of(2 * i), energy_of(2 * i + 1)], 1)
        partial[i] = invert(table, two_classes(field, i, pitch, freqs)) - 0.5 * energy + prior
        return carry

    each(classes // 2, slab, 0)
    for unit in range(partial_more.shape[0]):
        energy = beside(energy_of, unit, classes, share)
        value = several_classes(field, unit, classes, share, pitch, freqs)
        partial_more[unit] = invert(table, value) - 0.5 * energy + prior_term[:, 128:]


def two_classes(field, i, pitch, freqs):
    parts = [
        [field[rows((4 * i + 2 * j + part) * pitch, freqs), :] for j in range(2)]
        for part in range(2)
    ]
    return jnp.concatenate([jnp.concatenate(part, 1) for part in parts], 0)


def several_classes(field, unit, classes, share, pitch, freqs):
    return jnp.concatenate(
        [unpack(field, unit, part, classes, share, pitch, freqs) for part in range(2)], 0
    )


def beside(value_of, unit, classes, share):
    width, bundle, _ = layout(classes, share)
    lane = lax.broadcasted_iota(jnp.int32, (1, 128), 1)
    return sum(
        jnp.where(lane // width == j, value_of(unit * bundle + j), 0.0) for j in range(bundle)
    )


def invert(table, value):
    high, low = split(value)
    return dot(table[table_rows(0, ANG), :], jnp.concatenate([high, low, high], 0))


def correlate(left, particles, energy, prior_term, table):
    pairs, share, twice = particles.shape
    classes = left.shape[1] // 4
    pitch = 2 * pairs
    return call(
        correlate_kernel,
        [left, particles, energy, prior_term, table],
        [((classes // 2, ANG, 256), F32), ((layout(classes, share)[2], ANG, 128), F32)],
        [((corr_lines(classes, share, pitch), 128), F32)],
        flops=2 * left.shape[1] * share * pairs * twice * 8,
    )


def table_rows(base, count):
    return pl.ds(pl.multiple_of(lax.axis_index("rot") * ANG + base, 128), count)


def score_kernel(share, partial, partial_more, other, table, *refs):
    weights, more, tops, more_tops, peaks = refs
    classes = 2 * partial.shape[0]
    width, bundle, units = layout(classes, share)
    freqs = ANG // 4
    pitch = freqs

    def exponentials(scores):
        top = jnp.max(scores, axis=0, keepdims=True)
        value = jnp.exp(scores - top)
        return value, top, jnp.sum(value, axis=0, keepdims=True)

    def energy_of(k):
        return other[pl.ds(other.shape[0] - -(-classes // SPARE) * SPARE + k, 1), :]

    def slab(i, carry):
        energy = jnp.concatenate([energy_of(2 * i), energy_of(2 * i + 1)], 1)
        inner = invert(table, two_classes(other, i, pitch, freqs))
        weights[i], top, total = exponentials(inner + (partial[i] - 0.5 * energy))
        tops[pl.ds(i, 1), :] = top
        for j in (0, 128):
            carry = merge(carry, (top[:, j : j + 128], total[:, j : j + 128]))
        return carry

    empty = (jnp.full((1, 128), -jnp.inf, F32), jnp.zeros((1, 128), F32))
    top, total = each(classes // 2, slab, empty)
    rest = empty
    for unit in range(units):
        energy = beside(energy_of, unit, classes, share)
        inner = invert(table, several_classes(other, unit, classes, share, pitch, freqs))
        more[unit], more_top, more_total = exponentials(inner + (partial_more[unit] - 0.5 * energy))
        more_tops[pl.ds(unit, 1), :] = more_top
        for j in range(bundle):
            rest = merge(rest, (turned(more_top, -j * width), turned(more_total, -j * width)))
    line = lax.broadcasted_iota(jnp.int32, peaks.shape, 0)
    peaks[...] = jnp.where(
        line == 0,
        jnp.concatenate([top, rest[0]], 1),
        jnp.concatenate([total, rest[1]], 1),
    )


def scores(partial, partial_more, other, table, share):
    classes = 2 * partial.shape[0]
    units = layout(classes, share)[2]
    return call(
        functools.partial(score_kernel, share),
        [partial, partial_more, other, table],
        [
            ((classes // 2, ANG, 256), F32),
            ((units, ANG, 128), F32),
            ((classes // 2, 256), F32),
            ((units, 128), F32),
            ((8, 256), F32),
        ],
        flops=6 * classes * 256 * ANG * ANG,
    )


def merge(first, second):
    top = jnp.maximum(first[0], second[0])
    return top, first[1] * jnp.exp(first[0] - top) + second[1] * jnp.exp(second[0] - top)


def two_lines(ref):
    return ref[0:1, :], ref[1:2, :]


def merge_kernel(first, second, out):
    top, total = merge(two_lines(first), two_lines(second))
    line = lax.broadcasted_iota(jnp.int32, out.shape, 0)
    out[...] = jnp.where(line == 0, top, total)


def turn_kernel(share, weights, more, tops, more_tops, first, second, forward, *refs):
    rounded_ref, rounded_more, send, *last, held = refs
    classes = 2 * weights.shape[0]
    width, bundle, units = layout(classes, share)
    pairs = held.shape[0] // (2 * classes) // 2
    top, total = merge(two_lines(first), two_lines(second))
    evidence = top + jnp.log(total)
    scale = 1.0 / total
    at = table_rows(0, ANG // 2)
    lane = lax.broadcasted_iota(jnp.int32, (1, 128), 1)
    line = lax.broadcasted_iota(jnp.int32, (4 * classes, 128), 0)

    def with_count(column, k, count):
        high = count.astype(BF16).astype(F32)
        return jnp.where(line == k, high, jnp.where(line == classes + k, count - high, column))

    more_counts = []
    for unit in range(units):
        factor = jnp.exp(
            more_tops[pl.ds(unit, 1), :] - repeat(top[:, 128:], width, bundle)
        ) * repeat(scale[:, 128:], width, bundle)
        value = more[unit] * jnp.where(lane < bundle * width, factor, 0.0)
        count = jnp.sum(value, axis=0, keepdims=True)
        for j in range(bundle):
            mine = jnp.where(lane // width == j, count, 0.0)
            more_counts.append(jnp.sum(mine, axis=1, keepdims=True))
        rounded = value.astype(BF16)
        rounded_more[unit] = rounded
        spectrum = dot(forward[at, :], jnp.concatenate([rounded, rounded], 0)).astype(BF16)
        step = 4 * classes
        entries = spectrum.shape[0] // step
        for i in range(entries):
            send[pairs + unit * entries + i] = spectrum[i * step : (i + 1) * step]

    tops_here = jnp.concatenate([top[:, :128]] * 2, 1)
    scale_here = jnp.concatenate([scale[:, :128]] * 2, 1)

    def body(i, column):
        value = weights[i] * (jnp.exp(tops[pl.ds(i, 1), :] - tops_here) * scale_here)
        rounded = value.astype(BF16)
        rounded_ref[i] = rounded
        spread(held, i, dot(forward[at, :], jnp.concatenate([rounded, rounded], 0)))
        count = jnp.sum(value, axis=0, keepdims=True)
        for j in range(2):
            mine = jnp.sum(count[:, j * 128 : (j + 1) * 128], axis=1, keepdims=True)
            column = with_count(column, 2 * i + j, mine)
        return column

    column = each(classes // 2, body, jnp.zeros((4 * classes, 128), F32))
    extra = jnp.zeros((4 * classes, 128), F32)
    for k, count in enumerate(more_counts):
        extra = with_count(extra, k, count)
    for ref in last:
        ref[...] = evidence[:, :share]
        high = evidence.astype(BF16).astype(F32)
        middle = (evidence - high).astype(BF16).astype(F32)
        for i, value in enumerate((high, middle, evidence - high - middle)):
            for j in range(2):
                mine = value[:, j * 128 : (j + 1) * 128]
                extra = jnp.where(line == 2 * classes + 2 * i + j, mine, extra)
    send[send.shape[0] - 2] = column.astype(BF16)
    send[send.shape[0] - 1] = extra.astype(BF16)

    def rearrange(f):
        for i, parts in enumerate(pick(held, f, classes)):
            send[f + i] = jnp.concatenate(parts, 0).astype(BF16)

    every(pairs, rearrange)


def spread(held, i, value):
    freqs = value.shape[0] // 2
    for j in range(2):
        for part in range(2):
            held[rows((4 * i + 2 * j + part) * freqs, freqs), :] = value[
                part * freqs : (part + 1) * freqs, j * 128 : (j + 1) * 128
            ]


def spread_more(held, unit, value, classes, share):
    width, bundle, _ = layout(classes, share)
    freqs = value.shape[0] // 2
    for j in range(bundle):
        shifted = turned(value, -j * width)
        for part in range(2):
            k = unit * bundle + j
            held[rows((2 * k + part) * freqs, freqs), :] = shifted[
                part * freqs : (part + 1) * freqs
            ]


def message_shape(classes, pairs, units):
    return (pairs + units * (ANG // 2) // (4 * classes) + 2, 4 * classes, 128)


def turn(weights, more, tops, more_tops, first, second, forward, freqs, share, last):
    classes = 2 * weights.shape[0]
    units = more.shape[0]
    return call(
        functools.partial(turn_kernel, share),
        [weights, more, tops, more_tops, first, second, forward],
        [
            (weights.shape, BF16),
            (more.shape, BF16),
            (message_shape(classes, freqs // 2, units), BF16),
            *([((1, share), F32)] if last else []),
        ],
        [((2 * classes * freqs, 128), F32)],
        flops=4 * classes * 256 * ANG * ANG,
    )


def gather_kernel(rounded_ref, rounded_more, forward, particles, image, held, held_more):
    classes = 2 * rounded_ref.shape[0]
    pairs, share, _ = particles.shape
    at = table_rows(ANG // 2, ANG // 2)

    for unit in range(rounded_more.shape[0]):
        rounded = rounded_more[unit]
        value = dot(forward[at, :], jnp.concatenate([rounded, rounded], 0))
        spread_more(held_more, unit, value, classes, share)

    def body(i, carry):
        rounded = rounded_ref[i]
        spread(held, i, dot(forward[at, :], jnp.concatenate([rounded, rounded], 0)))
        return carry

    each(classes // 2, body, 0)

    def accumulate(f):
        values = []
        for i, both in enumerate(zip(pick(held, f, classes), pick(held_more, f, classes))):
            left = [jnp.concatenate(parts, 0).astype(BF16) for parts in both]
            values.append(dot(jnp.concatenate(left, 1)[:, :share], particles[f + i]))
        take_in(image, f, values, classes)

    every(pairs, accumulate)


def gather(rounded, rounded_more, forward, particles):
    pairs, share, twice = particles.shape
    classes = 2 * rounded.shape[0]
    lines = 2 * classes * 2 * pairs
    return call(
        gather_kernel,
        [rounded, rounded_more, forward, particles],
        [((lines, twice // 2), F32)],
        [((lines, 128), F32)] * 2,
        flops=4 * classes * 256 * ANG * ANG,
    )[0]


def take_in(image, f, values, classes):
    lines, depth = image.shape
    blocks = [
        value[part * 2 * classes : (part + 1) * 2 * classes, part * depth : (part + 1) * depth]
        for value in values
        for part in range(2)
    ]
    put(image, f, blocks, lines // (2 * classes))


def finish_kernel(image, mine, spectrum, particles, *refs):
    *outs, held = refs
    evidence_ref = outs.pop() if len(outs) > 1 else None
    pairs, share, twice = particles.shape
    classes = spectrum.shape[1] // 4
    freqs, depth = 2 * pairs, twice // 2
    radii = depth // 2
    pitch = freqs

    width, bundle, units = layout(classes, share)
    step = 4 * classes
    entries = ANG // 2 // step

    def received(f):
        blocks = []
        for k in range(classes):
            unit, j = divmod(k, bundle)
            for part in range(2):
                entry, first = divmod(part * freqs + 2 * f, step)
                value = spectrum[pairs + unit * entries + entry].astype(F32)
                blocks.append(turned(value[first : first + 2 * GROUP], -j * width))
        blocks = jnp.swapaxes(jnp.stack(blocks, 0), 0, 1)
        return [(blocks[2 * i], blocks[2 * i + 1]) for i in range(GROUP)]

    def body(f):
        values = []
        for i, parts in enumerate(received(f)):
            left = jnp.concatenate(parts, 0).astype(BF16)
            left = jnp.concatenate([spectrum[f + i], left], 1)[:, :share]
            values.append(dot(left, particles[f + i]))
        take_in(held, f, values, classes)

    every(pairs, body)
    end = spectrum.shape[0]
    counts = sum(ref[i].astype(F32) for ref in (mine, spectrum) for i in (end - 2, end - 1))
    if evidence_ref is not None:
        parts = spectrum[end - 1].astype(F32)[2 * classes :]
        parts = [jnp.concatenate([parts[i : i + 1], parts[i + 1 : i + 2]], 1) for i in (0, 2, 4)]
        evidence_ref[...] = (parts[0] + (parts[1] + parts[2]))[:, :share]
    counts = counts[:classes] + counts[classes : 2 * classes]
    lane = lax.broadcasted_iota(jnp.int32, (freqs, depth), 1)
    sign = jnp.where(lane < radii, -1.0, 1.0).astype(F32)
    for k in range(classes):
        plain, crossed = [
            image[rows((2 * k + part) * pitch, freqs), :]
            + held[rows((2 * k + part) * pitch, freqs), :]
            for part in range(2)
        ]
        value = plain + sign * pltpu.roll(crossed, radii, 1)
        if len(outs) == 1:
            outs[0][pl.ds(k * freqs, freqs), :] = value.astype(BF16)
        else:
            outs[k][pl.ds(0, freqs), :] = value
            outs[k][pl.ds(freqs, SPARE), :] = jnp.broadcast_to(counts[k : k + 1], (SPARE, depth))
    if len(outs) == 1:
        end = outs[0].shape[0] - classes * freqs
        high, low = split(counts)
        spare = [jnp.zeros((end - 2 * classes, depth), F32)] if end > 2 * classes else []
        tail = jnp.concatenate([high.astype(F32), low.astype(F32), *spare], 0)
        outs[0][pl.ds(classes * freqs, end), :] = tail.astype(BF16)


def finish(image, mine, spectrum, particles, last):
    pairs, _, twice = particles.shape
    classes = spectrum.shape[1] // 4
    freqs, depth = 2 * pairs, twice // 2
    if last:
        outs = [((freqs + SPARE, depth), F32)] * classes + [((1, particles.shape[1]), F32)]
    else:
        outs = [((classes * freqs + -(-2 * classes // 16) * 16, depth), BF16)]
    return call(
        finish_kernel,
        [image, mine, spectrum, particles],
        outs,
        [(image.shape, F32)],
        flops=2 * math.prod(spectrum.shape) * twice * 8,
    )


def means_kernel(*refs):
    *parts, own, other, out, evidence_ref = refs
    odd = lax.rem(lax.axis_index("cls"), 2)
    evidence_ref[...] = jnp.where(odd == 0, own[...], other[...])
    freqs = out.shape[1]
    total = tree(ref[...] for ref in parts)
    out[0] = total[:freqs, :] / (total[freqs : freqs + 1, :] + shrinkage)


def swap(value, axis, size, bit):
    if not bit:
        return value
    return lax.ppermute(value, axis, [(i, i ^ bit) for i in range(size)])


def bits(size):
    assert size > 1 and size & (size - 1) == 0
    return [1 << i for i in range(size.bit_length() - 1)]


def shards(particles, references, noise_inv, prior_rot):
    batch, freqs, depth = particles.shape
    sides = lax.axis_size("cls")
    groups = lax.axis_size("rot")
    blocks = lax.axis_size("blk")
    assert groups == 2 and 2 * groups * freqs == ANG
    share = batch // groups
    near, far, forward = tables(freqs)
    inverse_noise = noise_inv.reshape(1, depth // 2)
    assert blocks & (blocks - 1) == 0
    turns = sorted(range(1, blocks), key=lambda i: (-i.bit_length(), i))

    (permutation,) = call(permutation_kernel, [], [((256, 256), BF16)], flops=1 << 32)
    sources = {i: swap(references, "blk", blocks, i) for i in (*turns, 0)}
    other_images, own_images, prior_term = prep(particles, permutation, prior_rot, share)
    for step in range(ITERS):
        last = step == ITERS - 1
        order = [0, *(reversed(turns) if step else reversed(range(1, blocks)))]
        message, energy, left = weigh(sources, order, inverse_noise, other_images, step == 0)
        message = swap(message, "rot", groups, 1)
        partial = correlate(left, own_images, energy, prior_term, near)
        *weights, here = scores(*partial, message, far, share)
        first = here
        for bit in bits(sides):
            second = swap(first, ("cls", "rot"), sides * groups, groups * bit + (bit == 1))
            if 2 * bit < sides:
                (first,) = call(merge_kernel, [first, second], [(here.shape, F32)])
        rounded, more, send, *evidence = turn(
            *weights, first, second, forward, freqs, share, last
        )
        message = swap(send, "rot", groups, 1)
        image = gather(rounded, more, forward, own_images)
        sums = finish(image, send, message, other_images, last)
        sums, others = (sums[:blocks], sums[blocks:]) if last else (sums * blocks, [])
        sources = {i: swap(sums[i], "blk", blocks, i) for i in (*turns, 0)}
    means, evidence = call(
        means_kernel, [*[sources[i] for i in reversed(range(blocks))], *evidence, *others], [((1, freqs, depth), F32), ((1, share), F32)]
    )
    return means, evidence.reshape(share)


def solution(mesh):
    in_specs = (
        P(("grp", "blk"), "rot", None),
        P(("grp", "blk", "cls"), "rot", None),
        P(),
        P(("grp", "blk")),
    )
    out_specs = (P(("grp", "blk", "cls"), "rot", None), P(("grp", "blk", "rot")))
    return jax.shard_map(shards, mesh=mesh, in_specs=in_specs, out_specs=out_specs, check_vma=False)
```
